32 devices in a mesh: fsdp: 2 (over x), heads: 4 (over z), tensor: 4 (over y, core).
Axes of the slice: x: 2, y: 2, z: 4, core: 2. Of those that a mesh axis runs over, the one named last changes fastest.
Arguments:
- tokens: bfloat16 [8, 256, 768], P(('fsdp', 'tensor')), may hold values from -6 to 6
- valid_mask: int32 [8, 256], P(('fsdp', 'tensor')), may hold values from 0 to 1, as said below
- routes: int32 [8, 256, 2], P('fsdp'), may hold values from 0 to 31, all different within a row; in each aligned block of 1024 rows (0 to 1023, 1024 to 2047, ..., all dimensions but the last counted through in order) at most 128 rows name the same one
- teacher: bfloat16 [8, 256, 768], P(('fsdp', 'tensor')), may hold values from -6 to 6
- gain_one: bfloat16 [768], P(('fsdp', 'tensor')), may hold values from 0.099609375 to 1.8984375
- qkv_weight: bfloat16 [768, 12, 192], P(('fsdp', 'tensor'), 'heads'), may hold values from -0.3125 to 0.3125
- out_weight: bfloat16 [12, 64, 768], P('heads', None, ('fsdp', 'tensor')), may hold values from -1 to 1
- gain_two: bfloat16 [768], P(('fsdp', 'tensor')), may hold values from 0.099609375 to 1.8984375
- router_weight: bfloat16 [768, 32], P(('fsdp', 'tensor')), may hold values from -0.109375 to 0.109375
- expert_up: bfloat16 [32, 768, 3072], P('heads', 'fsdp', 'tensor'), may hold values from -0.21875 to 0.21875
- expert_down: bfloat16 [32, 3072, 768], P('heads', 'tensor', 'fsdp'), may hold values from -3.5 to 3.5
Outputs:
- result: bfloat16 [8, 256, 768], P(('fsdp', 'tensor'))
- loss_terms: float32 [8], P(('fsdp', 'tensor'))
- tokens_grad: float32 [8, 256, 768], P(('fsdp', 'tensor'))
- gain_one_grad: float32 [768], P(('fsdp', 'tensor'))
- qkv_grad: float32 [768, 12, 192], P(('fsdp', 'tensor'), 'heads')
- out_weight_grad: float32 [12, 64, 768], P('heads', None, ('fsdp', 'tensor'))
- gain_two_grad: float32 [768], P(('fsdp', 'tensor'))
- router_grad: float32 [768, 32], P(('fsdp', 'tensor'))
- expert_up_grad: float32 [32, 768, 3072], P('heads', 'fsdp', 'tensor')
- expert_down_grad: float32 [32, 3072, 768], P('heads', 'tensor', 'fsdp')
The draws below stay inside these ranges and needn't reach their ends.
Inputs may be any that keep to these rules, and one draw needn't show every extreme that they name: `valid_mask`: an image's valid tokens are its first ones, 1 to 197 of them; some image has exactly 197. `routes`: each row names 2 different experts. In the 1024 rows of each index of fsdp no expert is named more than 128 times, a bound that some block reaches.
All inputs are finite; a program needn't handle non-finite values.
Results may differ from the reference program's by a relative error of at most 0.012.
The reference program's roundings to bfloat16 on the way count: a program that leaves them out, or rounds other values in their place, can miss the bound.
Values may be sent and summed in bfloat16 or wider, within the bound.
A program may use at most 192 MiB of HBM per device.

```python
import math
import jax
import jax.numpy as jnp
import numpy as np
from jax import lax

D = 768
HEADS = 12
HDIM = 64
EXPERTS = 32
FF = 3072
TOPK = 2
SEQ = 256
VALID = 197
IMAGES = 8
GROUP_TOK = 1024
CAP = 128
TOKENS = 2048


def draw_valid_mask(key, part):
    image_index = jnp.arange(IMAGES, dtype=jnp.int32)
    shortest = max(VALID // 3, 1)
    baseline = shortest + (VALID - shortest) * image_index // max(IMAGES - 1, 1)
    spread = max(VALID // 8, 1)
    jitter = jax.random.randint(key, (IMAGES,), -spread, spread + 1)
    lengths = jnp.clip(baseline + jitter, 1, VALID)
    lengths = jnp.where(image_index == IMAGES - 1, VALID, lengths)
    position = jnp.arange(SEQ, dtype=jnp.int32)
    return (position[None, :] < lengths[:, None]).astype(jnp.int32)


def block_levels(stream_key, extent, cuts, smallest, top_value):
    level = 1.0
    for dim, blocks in cuts:
        heights = jax.random.uniform(jax.random.fold_in(jax.random.fold_in(stream_key, 6), dim), (blocks,), jnp.float32, smallest / len(cuts), top_value / len(cuts))
        level = level * jnp.repeat(jnp.exp(heights), extent[dim] // blocks).reshape((-1,) + (1,) * (len(extent) - 1 - dim))
    return level


def shared_out(own_key, own, number, rows, amount, top, bound, skew):
    ranking = jax.random.permutation(own_key, amount)
    crowded, usual = shares(amount, rows * top, bound, skew, True), shares(amount, rows * top, bound, skew, False)
    places = jnp.arange(amount)

    def named(sizes, offset_by):
        used = int((sizes > 0).sum())
        fixed = max(1, used // 4)
        moved = fixed + (places - fixed + offset_by * (used - fixed)) % max(1, amount - fixed)
        return jnp.zeros((amount,), jnp.int32).at[ranking[jnp.where(places < fixed, places, moved)]].set(jnp.asarray(sizes, jnp.int32))

    sizes = jnp.where(number % 4 == 0, named(crowded, number // 4), named(usual, number - number // 4 - 1))
    mixed = jax.random.permutation(jax.random.fold_in(own, 3), amount)
    source_of, taker = mixed[0:amount // 2 * 2:2], mixed[1:amount // 2 * 2:2]
    slack = jnp.minimum(sizes[source_of] - 1, bound - sizes[taker]) // 2
    slack = jnp.where((source_of == ranking[0]) | (taker == ranking[0]) | (sizes[taker] == 0), 0, jnp.maximum(slack, 0))
    moved = jax.random.randint(jax.random.fold_in(own, 4), (amount // 2,), 0, 1 << 20) % (slack + 1)
    sizes = sizes.at[source_of].add(-moved).at[taker].add(moved)
    members = jnp.searchsorted(jnp.cumsum(sizes), jnp.arange(rows * top), side="right").astype(jnp.int32)
    grid = members.reshape(top, rows).T
    grid = grid[jax.random.permutation(jax.random.fold_in(own, 1), rows)]
    offset_by = jax.random.randint(jax.random.fold_in(own, 2), (rows, 1), 0, top)
    return jnp.take_along_axis(grid, (jnp.arange(top)[None, :] + offset_by) % top, axis=1)


def shares(number_of, total, limit, lean, full):
    weights = [(1 << 20) // math.isqrt(rank ** lean) + 1 for rank in range(1, number_of + 1)]
    largest = limit if full else min(limit, max(-(-total // number_of), total * weights[0] // sum(weights)))
    least = 1 if total - largest >= number_of - 1 else 0
    holding, surplus = [largest] + [least] * (number_of - 1), total - largest - least * (number_of - 1)
    while surplus > 0:
        free = [i for i in range(1, number_of) if holding[i] < largest] or [i for i in range(1, number_of) if holding[i] < limit]
        mass, budget = sum([weights[i] for i in free]), surplus
        for i in free:
            addition = min(limit - holding[i], max(1, budget * weights[i] // mass), surplus)
            holding[i] = holding[i] + addition
            surplus = surplus - addition
    return np.array(holding)


def noise(own_key, shape, scale, reach, split=(), held_as=jnp.bfloat16):
    entries = jax.random.normal(own_key, shape, jnp.float32) * scale
    if len(split) > 0:
        entries = block_levels(own_key, shape, split, -0.22, 0.18) * entries
    return jnp.clip(entries, min=-reach, max=reach).astype(held_as)


def setup_inputs(seed: int = 0) -> dict:
    arg_keys = jax.random.split(jax.random.key(seed), 12)
    tokens = noise(arg_keys[0], (IMAGES, SEQ, D), 1.0, 6.0, ((0, 8),))
    valid_mask = draw_valid_mask(jax.random.fold_in(arg_keys[11], 71), 0)
    routes_keys = jax.random.split(jax.random.fold_in(arg_keys[2], 1), IMAGES * SEQ // GROUP_TOK)
    routes_turns = jax.random.permutation(jax.random.fold_in(arg_keys[2], 3), IMAGES * SEQ // GROUP_TOK)
    routes = jax.vmap(lambda own, number: shared_out(jax.random.fold_in(arg_keys[2], 2), own, number, GROUP_TOK, EXPERTS, TOPK, CAP, 2))(routes_keys, routes_turns).reshape((IMAGES, SEQ, TOPK))
    teacher = noise(arg_keys[3], (IMAGES, SEQ, D), 1.0, 6.0, ((0, 8),))
    gain_one = jnp.clip(1.0 + 0.18 * jax.random.normal(arg_keys[4], (D,), jnp.float32), 0.099609375, 1.8984375).astype(jnp.bfloat16)
    qkv_weight = noise(arg_keys[5], (D, HEADS, 3 * HDIM), (D // 2) ** -0.5, 0.3125, ((0, 8), (1, 4)))
    out_weight = noise(arg_keys[6], (HEADS, HDIM, D), (HEADS * HDIM * 8 // VALID) ** -0.5, 1.0, ((0, 4), (2, 8)))
    gain_two = jnp.clip(1.0 + 0.18 * jax.random.normal(arg_keys[7], (D,), jnp.float32), 0.099609375, 1.8984375).astype(jnp.bfloat16)
    router_weight = noise(arg_keys[8], (D, EXPERTS), (4 * D) ** -0.5, 0.109375, ((0, 8),))
    expert_up = noise(arg_keys[9], (EXPERTS, D, FF), D ** -0.5, 0.21875, ((0, 4), (1, 2), (2, 4)))
    expert_down = noise(arg_keys[10], (EXPERTS, FF, D), (max(FF // 1024, 1)) ** -0.5, 3.5, ((0, 4), (1, 4), (2, 2)))
    return {"tokens": tokens, "valid_mask": valid_mask, "routes": routes, "teacher": teacher, "gain_one": gain_one, "qkv_weight": qkv_weight, "out_weight": out_weight, "gain_two": gain_two, "router_weight": router_weight, "expert_up": expert_up, "expert_down": expert_down}


EPSILON = 1e-06
MASKED = -1e+30
FULL_ACCURACY = lax.Precision.HIGHEST

@jax.custom_vjp
def low(v):
    return lax.optimization_barrier(v.astype(jnp.bfloat16)).astype(jnp.float32)

@jax.custom_vjp
def low_back(v):
    return v

def low_keep(v):
    return (low(v), None)

def low_pass(kept, grad):
    return (grad,)

def back_keep(v):
    return (v, None)

def back_low(kept, grad):
    return (low(grad),)
low.defvjp(low_keep, low_pass)
low_back.defvjp(back_keep, back_low)

def normalize(values, gain_vector):
    center = values - lax.optimization_barrier(jnp.mean(values, -1, keepdims=True))
    variance = lax.optimization_barrier(jnp.mean(center * center, -1, keepdims=True))
    return center * lax.rsqrt(variance + EPSILON) * gain_vector

def attend_block(block, valid_block, gain_a, qkv_full, output_complete):
    first_in = low(normalize(block, gain_a))
    projected = low_back(low(jnp.einsum('bsd,dhe->bshe', first_in, qkv_full, precision=FULL_ACCURACY)))
    queries = projected[..., :HDIM]
    key_rows = projected[..., HDIM:2 * HDIM]
    values = projected[..., 2 * HDIM:]
    scores = low_back(jnp.einsum('bqhe,bkhe->bhqk', queries, key_rows, precision=FULL_ACCURACY) * HDIM ** (-0.5))
    scores = jnp.where(valid_block[:, None, None, :], scores, MASKED)
    peak_score = lax.optimization_barrier(jnp.max(scores, -1, keepdims=True))
    exp_scores = jnp.exp(scores - peak_score)
    attention = low(exp_scores / lax.optimization_barrier(jnp.sum(exp_scores, -1, keepdims=True)))
    combined_heads = low_back(low(jnp.einsum('bhqk,bkhe->bqhe', attention, values, precision=FULL_ACCURACY)))
    return jnp.einsum('pmjz,jzv->pmv', combined_heads, output_complete, precision=FULL_ACCURACY)

def expert_group(rows, picks, router_full, up_full, down_full):
    logits = low_back(jnp.dot(rows, router_full, precision=FULL_ACCURACY))
    peak_logit = lax.optimization_barrier(jnp.max(logits, -1, keepdims=True))
    exponent_logits = jnp.exp(logits - peak_logit)
    router_probs = exponent_logits / lax.optimization_barrier(jnp.sum(exponent_logits, -1, keepdims=True))
    expert_ids = jnp.arange(EXPERTS).astype(jnp.int32)
    picked_hot = (picks[:, :, None] == expert_ids[None, None, :]).astype(router_probs.dtype)
    gate_weight_values = lax.optimization_barrier(jnp.sum(router_probs[:, None, :] * picked_hot, -1))
    flat_routes = picks.reshape(GROUP_TOK * TOPK).astype(jnp.int32)
    route_hot = (flat_routes[:, None] == expert_ids[None, :]).astype(jnp.int32)
    earlier = jnp.cumsum(route_hot, 0).astype(jnp.int32) - route_hot
    slot_index = lax.optimization_barrier(jnp.sum(earlier * route_hot, 1)).astype(jnp.int32)
    target = (flat_routes * CAP + slot_index).astype(jnp.int32)
    owner_row = (jnp.arange(GROUP_TOK * TOPK) // TOPK).astype(jnp.int32)
    source = jnp.zeros((EXPERTS * CAP,), jnp.int32).at[target].set(owner_row)
    buffer = rows[source].reshape(EXPERTS, CAP, D)
    before_gelu = low_back(jnp.einsum('ecd,edf->ecf', buffer, up_full, precision=FULL_ACCURACY))
    hidden = low(jax.nn.gelu(before_gelu, approximate=False))
    expert_out = low_back(jnp.einsum('ecf,efd->ecd', hidden, down_full, precision=FULL_ACCURACY)).reshape(EXPERTS * CAP, D)
    picked = expert_out[target].reshape(GROUP_TOK, TOPK, D)
    return lax.optimization_barrier(jnp.sum(gate_weight_values[..., None] * picked, 1))

def reference(tokens, valid_mask, routes, teacher, gain_one, qkv_weight, out_weight, gain_two, router_weight, expert_up, expert_down):
    valid_rows = valid_mask.astype(jnp.float32)
    valid_total = jnp.sum(valid_rows)
    target_rows = teacher.astype(jnp.float32)
    block_images = math.gcd(IMAGES, max(1, 4096 // SEQ))
    valid_blocks = (valid_mask > 0).reshape(IMAGES // block_images, block_images, SEQ)
    group_count = IMAGES * SEQ // GROUP_TOK
    route_groups = routes.reshape(group_count, GROUP_TOK, TOPK)

    def forward(inputs, gain_a, qkv_full, output_complete, gain_b, router_full, up_full, down_full):
        blocks = inputs.reshape(IMAGES // block_images, block_images, SEQ, D)

        def attend_step(carry, item):
            return (carry, jax.checkpoint(attend_block)(item[0], item[1], gain_a, qkv_full, output_complete))
        carry_one, attended = lax.scan(attend_step, jnp.zeros((), jnp.float32), (blocks, valid_blocks))
        residual = inputs + low_back(attended.reshape(IMAGES, SEQ, D))
        second_in = low(normalize(residual, gain_b))
        groups = second_in.reshape(group_count, GROUP_TOK, D)

        def expert_step(carry, item):
            return (carry, jax.checkpoint(expert_group)(item[0], item[1], router_full, up_full, down_full))
        carry_two, expert_sum = lax.scan(expert_step, jnp.zeros((), jnp.float32), (groups, route_groups))
        final = residual + low_back(expert_sum.reshape(IMAGES, SEQ, D))
        difference = (final - target_rows) * valid_rows[..., None]
        squares = lax.optimization_barrier(jnp.sum(difference * difference, axis=(1, 2)))
        per_image = squares * (IMAGES / (valid_total * D))
        scaled = jnp.sum(squares) / (valid_total * D) * (TOKENS * D * 0.5)
        return (scaled, (final, per_image))
    primals = (tokens.astype(jnp.float32), gain_one.astype(jnp.float32), qkv_weight.astype(jnp.float32), out_weight.astype(jnp.float32), gain_two.astype(jnp.float32), router_weight.astype(jnp.float32), expert_up.astype(jnp.float32), expert_down.astype(jnp.float32))
    scaled, pullback, extras = jax.vjp(forward, *primals, has_aux=True)
    grads = pullback(jnp.ones((), jnp.float32))
    return (extras[0].astype(jnp.bfloat16), extras[1], grads[0], grads[1], grads[2], grads[3], grads[4], grads[5], grads[6], grads[7])
```

```python
import functools

import jax
import jax.numpy as jnp
from jax import lax
from jax.experimental import pallas as pl
from jax.experimental.pallas import tpu as pltpu
from jax.sharding import PartitionSpec as P

FSDP, HEADS, TENSOR = "fsdp", "heads", "tensor"
EPSILON = 1e-06
MASKED = -1e30
ROOT_HALF = 0.7071067811865476
DENSITY = 0.3989422804014327


def normalize(values):
    center = values - jnp.mean(values, -1, keepdims=True)
    inv_std = lax.rsqrt(jnp.mean(center * center, -1, keepdims=True) + EPSILON)
    return (center * inv_std, inv_std)


def norm_back(gradient, normed, inv_std, gain_vector):
    weighted = gradient * gain_vector
    gain_grad = jnp.sum(gradient * normed, axis=(0, 1))
    inner = (
        weighted
        - jnp.mean(weighted, -1, keepdims=True)
        - normed * jnp.mean(weighted * normed, -1, keepdims=True)
    )
    return (inner * inv_std, gain_grad)


def scores_of(queries, key_rows, keys_ok, score_scale):
    raw_scores = (
        jnp.einsum("iqhe,ikhe->ihqk", queries, key_rows, preferred_element_type=jnp.float32)
        * score_scale
    )
    return jnp.where(keys_ok, raw_scores, MASKED)


def gather_weights(
    gain_one, qkv_weight, out_weight, gain_two, router_weight, expert_up, expert_down
):
    dense_set = (
        lax.all_gather(qkv_weight, (FSDP, TENSOR), axis=0, tiled=True),
        lax.all_gather(out_weight, (FSDP, TENSOR), axis=2, tiled=True),
        lax.all_gather(router_weight, (FSDP, TENSOR), axis=0, tiled=True),
        lax.all_gather(gain_one, (FSDP, TENSOR), axis=0, tiled=True),
        lax.all_gather(gain_two, (FSDP, TENSOR), axis=0, tiled=True),
    )
    expert_set = (
        lax.all_gather(expert_up, FSDP, axis=1, tiled=True),
        lax.all_gather(expert_down, FSDP, axis=2, tiled=True),
    )
    return (dense_set, expert_set)


def reduce_expert_grads(up_grad, down_grad):
    return (
        lax.psum_scatter(up_grad, FSDP, scatter_dimension=1, tiled=True),
        lax.psum_scatter(down_grad, FSDP, scatter_dimension=2, tiled=True),
    )


def general(
    tokens,
    valid_mask,
    routes,
    teacher,
    gain_one,
    qkv_weight,
    out_weight,
    gain_two,
    router_weight,
    expert_up,
    expert_down,
):
    valid_total = lax.psum(jnp.sum(valid_mask.astype(jnp.float32)), (FSDP, TENSOR))
    dense_set, expert_set = gather_weights(
        gain_one, qkv_weight, out_weight, gain_two, router_weight, expert_up, expert_down
    )
    qkv_full, output_complete, router_full, gain_a, gain_b = dense_set
    up_full, down_full = expert_set
    image_count, token_slots, model_width = tokens.shape
    head_dim = qkv_full.shape[2] // 3
    local_experts = expert_up.shape[0]
    tensor_size = lax.axis_size(TENSOR)
    group_images = image_count * tensor_size
    group_rows = group_images * token_slots
    top_choices = routes.shape[2]
    expert_count = local_experts * lax.axis_size(HEADS)
    capacity = 2 * top_choices * group_rows // expert_count
    slot_count = local_experts * capacity
    total_tokens = image_count * token_slots * lax.axis_size(FSDP) * tensor_size
    total_images = image_count * lax.axis_size(FSDP) * tensor_size
    score_scale = head_dim ** (-0.5)
    inputs = tokens.astype(jnp.float32)
    normed_one, spread_one = normalize(inputs)
    first_in = (normed_one * gain_a.astype(jnp.float32)).astype(jnp.bfloat16)
    projected = jnp.einsum(
        "isd,dhe->ishe", first_in, qkv_full, preferred_element_type=jnp.float32
    ).astype(jnp.bfloat16)
    queries = projected[..., :head_dim]
    key_rows = projected[..., head_dim : 2 * head_dim]
    values = projected[..., 2 * head_dim :]
    keys_ok = (valid_mask > 0)[:, None, None, :]
    scores = scores_of(queries, key_rows, keys_ok, score_scale)
    peak_score = jnp.max(scores, -1, keepdims=True)
    exp_scores = jnp.exp(scores - peak_score)
    score_total = jnp.sum(exp_scores, -1, keepdims=True)
    logarithm_total = peak_score + jnp.log(score_total)
    attention = (exp_scores / score_total).astype(jnp.bfloat16)
    combined_heads = jnp.einsum(
        "ihqk,ikhe->iqhe", attention, values, preferred_element_type=jnp.float32
    ).astype(jnp.bfloat16)
    attn_part = jnp.einsum(
        "iqhe,hed->iqd", combined_heads, output_complete, preferred_element_type=jnp.float32
    )
    attended = lax.psum(attn_part, HEADS)
    residual = inputs + attended
    normed_two, spread_two = normalize(residual)
    second_in = (normed_two * gain_b.astype(jnp.float32)).astype(jnp.bfloat16)
    group_in = lax.all_gather(second_in, TENSOR, axis=0, tiled=True)
    rows_in = group_in.reshape(group_rows, model_width)
    logits = jnp.dot(rows_in, router_full, preferred_element_type=jnp.float32)
    peak_logit = jnp.max(logits, -1, keepdims=True)
    exponent_logits = jnp.exp(logits - peak_logit)
    router_probs = exponent_logits / jnp.sum(exponent_logits, -1, keepdims=True)
    expert_ids = jnp.arange(expert_count, dtype=jnp.int32)
    route_pairs = routes.reshape(group_rows, top_choices)
    picked_hot = (route_pairs[:, :, None] == expert_ids[None, None, :]).astype(jnp.float32)
    gate_weight_values = jnp.sum(router_probs[:, None, :] * picked_hot, -1)
    flat_routes = route_pairs.reshape(group_rows * top_choices)
    route_hot = (flat_routes[:, None] == expert_ids[None, :]).astype(jnp.int32)
    order = jnp.arange(group_rows * top_choices, dtype=jnp.int32)
    before = (order[None, :] < order[:, None]).astype(jnp.bfloat16)
    earlier = jnp.dot(
        before, route_hot.astype(jnp.bfloat16), preferred_element_type=jnp.float32
    ).astype(jnp.int32)
    slot_index = jnp.sum(earlier * route_hot, 1)
    first_expert = lax.axis_index(HEADS) * local_experts
    is_local = (flat_routes >= first_expert) & (flat_routes < first_expert + local_experts)
    target = jnp.where(is_local, (flat_routes - first_expert) * capacity + slot_index, slot_count)
    owner_row = jnp.arange(group_rows * top_choices, dtype=jnp.int32) // top_choices
    source = jnp.zeros((slot_count,), jnp.int32).at[target].set(owner_row, mode="drop")
    slot_gate = (
        jnp.zeros((slot_count,), jnp.float32)
        .at[target]
        .set(gate_weight_values.reshape(-1), mode="drop")
    )
    slot_pick = jnp.minimum(target, slot_count - 1)
    retain_mask = is_local.astype(jnp.float32)
    dispatched = rows_in[source].reshape(local_experts, capacity, model_width)
    before_gelu = jnp.einsum(
        "ecd,edf->ecf", dispatched, up_full, preferred_element_type=jnp.float32
    )
    hidden = jax.nn.gelu(before_gelu, approximate=False).astype(jnp.bfloat16)
    expert_out = jnp.einsum(
        "ecf,efd->ecd", hidden, down_full, preferred_element_type=jnp.float32
    ).reshape(slot_count, model_width)
    weighted = expert_out * slot_gate[:, None]
    moe_part = jnp.sum(
        (weighted[slot_pick] * retain_mask[:, None]).reshape(group_rows, top_choices, model_width),
        1,
    )
    moe_part = moe_part.reshape(group_images, token_slots, model_width)
    expert_sum = lax.psum(
        lax.psum_scatter(moe_part, TENSOR, scatter_dimension=0, tiled=True), HEADS
    )
    final = residual + expert_sum
    valid_rows = valid_mask.astype(jnp.float32)[..., None]
    difference = (final - teacher.astype(jnp.float32)) * valid_rows
    loss_terms = jnp.sum(difference * difference, axis=(1, 2)) * (
        total_images / (valid_total * model_width)
    )
    final_grad = difference * (total_tokens / valid_total)
    dense_set, expert_set = gather_weights(
        gain_one, qkv_weight, out_weight, gain_two, router_weight, expert_up, expert_down
    )
    qkv_full, output_complete, router_full, gain_a, gain_b = dense_set
    up_full, down_full = expert_set
    moe_grad = final_grad.astype(jnp.bfloat16)
    group_grad = lax.all_gather(moe_grad, TENSOR, axis=0, tiled=True).reshape(
        group_rows, model_width
    )
    slot_grad = group_grad[source].astype(jnp.float32)
    gate_slot_grad = jnp.sum(slot_grad * expert_out, -1)
    out_grad = (
        (slot_grad * slot_gate[:, None])
        .astype(jnp.bfloat16)
        .reshape(local_experts, capacity, model_width)
    )
    expert_down_grad = jnp.einsum(
        "ecf,ecd->efd", hidden, out_grad, preferred_element_type=jnp.float32
    )
    hidden_grad = jnp.einsum(
        "ecd,efd->ecf", out_grad, down_full, preferred_element_type=jnp.float32
    )
    normal_cdf = 0.5 * (1.0 + lax.erf(before_gelu * ROOT_HALF))
    slope = normal_cdf + before_gelu * DENSITY * jnp.exp(-0.5 * before_gelu * before_gelu)
    pre_grad = (hidden_grad * slope).astype(jnp.bfloat16)
    expert_up_grad = jnp.einsum(
        "ecd,ecf->edf", dispatched, pre_grad, preferred_element_type=jnp.float32
    )
    row_grad = jnp.einsum(
        "ecf,edf->ecd", pre_grad, up_full, preferred_element_type=jnp.float32
    ).reshape(slot_count, model_width)
    rows_part = jnp.sum(
        (row_grad[slot_pick] * retain_mask[:, None]).reshape(group_rows, top_choices, model_width),
        1,
    )
    rows_part = rows_part.reshape(group_images, token_slots, model_width)
    gate_part = (gate_slot_grad[slot_pick] * retain_mask).reshape(
        group_images, token_slots, top_choices
    )
    rows_share, gate_share = (
        lax.psum_scatter(rows_part, TENSOR, scatter_dimension=0, tiled=True),
        lax.psum_scatter(gate_part, TENSOR, scatter_dimension=0, tiled=True),
    )
    second_grad, gate_grad = lax.psum((rows_share, gate_share), HEADS)
    own_start = lax.axis_index(TENSOR) * image_count * token_slots
    own_rows = image_count * token_slots
    own_probs = lax.dynamic_slice_in_dim(router_probs, own_start, own_rows, 0).reshape(
        image_count, token_slots, expert_count
    )
    own_hot = lax.dynamic_slice_in_dim(picked_hot, own_start, own_rows, 0).reshape(
        image_count, token_slots, top_choices, expert_count
    )
    prob_grad = jnp.sum(gate_grad[..., None] * own_hot, 2)
    logit_grad = (
        own_probs * (prob_grad - jnp.sum(own_probs * prob_grad, -1, keepdims=True))
    ).astype(jnp.bfloat16)
    router_grad = jnp.einsum(
        "isd,ise->de", second_in, logit_grad, preferred_element_type=jnp.float32
    )
    second_grad = second_grad + jnp.einsum(
        "ise,de->isd", logit_grad, router_full, preferred_element_type=jnp.float32
    )
    residual_norm, gain_two_grad = norm_back(
        second_grad, normed_two, spread_two, gain_b.astype(jnp.float32)
    )
    residual_grad = final_grad + residual_norm
    attended_output_gradient = residual_grad.astype(jnp.bfloat16)
    out_weight_grad = jnp.einsum(
        "iqhe,iqd->hed",
        combined_heads,
        attended_output_gradient,
        preferred_element_type=jnp.float32,
    )
    mixed_grad = jnp.einsum(
        "iqd,hed->iqhe",
        attended_output_gradient,
        output_complete,
        preferred_element_type=jnp.float32,
    ).astype(jnp.bfloat16)
    scores = scores_of(queries, key_rows, keys_ok, score_scale)
    probs = jnp.exp(scores - logarithm_total)
    probs_low = probs.astype(jnp.bfloat16)
    prob_part = jnp.einsum(
        "iqhe,ikhe->ihqk", mixed_grad, values, preferred_element_type=jnp.float32
    )
    score_grad = (probs * (prob_part - jnp.sum(probs * prob_part, -1, keepdims=True))).astype(
        jnp.bfloat16
    )
    query_grad = (
        jnp.einsum("ihqk,ikhe->iqhe", score_grad, key_rows, preferred_element_type=jnp.float32)
        * score_scale
    )
    key_grad = (
        jnp.einsum("ihqk,iqhe->ikhe", score_grad, queries, preferred_element_type=jnp.float32)
        * score_scale
    )
    value_grad = jnp.einsum(
        "ihqk,iqhe->ikhe", probs_low, mixed_grad, preferred_element_type=jnp.float32
    )
    projected_grad = jnp.concatenate([query_grad, key_grad, value_grad], -1).astype(jnp.bfloat16)
    qkv_grad = jnp.einsum(
        "isd,ishe->dhe", first_in, projected_grad, preferred_element_type=jnp.float32
    )
    first_part = jnp.einsum(
        "ishe,dhe->isd", projected_grad, qkv_full, preferred_element_type=jnp.float32
    )
    first_grad = lax.psum(first_part, HEADS)
    input_norm, gain_one_grad = norm_back(
        first_grad, normed_one, spread_one, gain_a.astype(jnp.float32)
    )
    tokens_grad = residual_grad + input_norm
    dense_grads = (
        lax.psum_scatter(qkv_grad, (FSDP, TENSOR), scatter_dimension=0, tiled=True),
        lax.psum_scatter(out_weight_grad, (FSDP, TENSOR), scatter_dimension=2, tiled=True),
        lax.psum_scatter(router_grad, (FSDP, TENSOR), scatter_dimension=0, tiled=True),
        lax.psum_scatter(gain_one_grad, (FSDP, TENSOR), scatter_dimension=0, tiled=True),
        lax.psum_scatter(gain_two_grad, (FSDP, TENSOR), scatter_dimension=0, tiled=True),
    )
    expert_grads = reduce_expert_grads(expert_up_grad, expert_down_grad)
    return (
        final.astype(jnp.bfloat16),
        loss_terms,
        tokens_grad,
        dense_grads[3],
        dense_grads[0],
        dense_grads[1],
        dense_grads[4],
        dense_grads[2],
        expert_grads[0],
        expert_grads[1],
    )


MESH = pl.DeviceIdType.MESH
LOW = jnp.bfloat16
WIDE = jnp.float32


class Links:
    def __init__(self, send_sems, recv_sems):
        self.send_sems, self.recv_sems = send_sems, recv_sems
        self.copies = []

    def send(self, src, dst, device):
        k = len(self.copies)
        copy = pltpu.make_async_remote_copy(
            src_ref=src,
            dst_ref=dst,
            send_sem=self.send_sems.at[k],
            recv_sem=self.recv_sems.at[k],
            device_id=device,
            device_id_type=MESH,
        )
        copy.start()
        self.copies.append(copy)
        return copy

    def drain(self):
        for copy in self.copies:
            copy.wait_send()


class Place:
    def __init__(self, heads):
        self.f = lax.axis_index(FSDP)
        t = lax.axis_index(TENSOR)
        self.y, self.c = t // 2, lax.rem(t, 2)
        self.z = lax.axis_index(HEADS)
        self.heads = heads
        self.x_peer = {FSDP: 1 - self.f}
        self.y_peer = {TENSOR: 2 * (1 - self.y) + self.c}
        self.core_peer = {TENSOR: 2 * self.y + 1 - self.c}
        self.z_peers = [{HEADS: lax.rem(self.z + k, heads)} for k in range(1, heads)]
        self.plane_peers = []
        for a in range(2):
            for k in range(4):
                if a or k:
                    where = {TENSOR: lax.rem(t + k, 4)}
                    if a:
                        where[FSDP] = 1 - self.f
                    self.plane_peers.append(where)

    def image(self, df, dy, dc):
        f = 1 - self.f if df else self.f
        y = 1 - self.y if dy else self.y
        c = 1 - self.c if dc else self.c
        return f * 4 + 2 * y + c

    def greet(self, devices):
        barrier = pltpu.get_barrier_semaphore()
        for device in devices:
            pl.semaphore_signal(barrier, inc=1, device_id=device, device_id_type=MESH)
        pl.semaphore_wait(barrier, len(devices))

    def axis_peers(self):
        return [self.x_peer, self.y_peer, self.core_peer]


class PlaneGather:
    def __init__(self, links, place, first, second, whole):
        self.links, self.place = links, place
        self.first, self.second, self.whole = first, second, whole

    def go(self, part, image, device):
        return self.links.send(part(image), part(image), device)

    def start(self):
        p, me = self.place, self.place.image(0, 0, 0)
        self.xa = self.go(self.first, me, p.x_peer)
        self.yb = self.go(self.second, me, p.y_peer)
        self.own = self.go(self.whole, me, p.core_peer)
        self.xb = self.go(self.second, me, p.x_peer)
        self.ya = self.go(self.first, me, p.y_peer)

    def forward(self):
        p = self.place
        self.xa.wait_recv()
        self.fa = self.go(self.first, p.image(1, 0, 0), p.y_peer)
        self.yb.wait_recv()
        self.fb = self.go(self.second, p.image(0, 1, 0), p.x_peer)

    def share(self):
        p = self.place
        self.xb.wait_recv()
        self.c1 = self.go(self.whole, p.image(1, 0, 0), p.core_peer)
        self.ya.wait_recv()
        self.c2 = self.go(self.whole, p.image(0, 1, 0), p.core_peer)

    def finish(self):
        p = self.place
        self.fa.wait_recv()
        self.fb.wait_recv()
        self.c3 = self.go(self.whole, p.image(1, 1, 0), p.core_peer)
        for copy in (self.own, self.c1, self.c2, self.c3):
            copy.wait_recv()

    def run(self):
        self.start()
        self.forward()
        self.share()
        self.finish()


GATHER_COPIES = 10


def in_rows(rows, step, body):
    def one(i, carry):
        body(pl.ds(pl.multiple_of(i * step, step), step))
        return carry

    lax.fori_loop(0, rows // step, one, 0)


class PlaneSum:
    def __init__(self, links, place, part, core_in, xa, ya, yb, xb, cut, step):
        self.links, self.place, self.part, self.core_in = links, place, part, core_in
        self.xa, self.ya, self.yb, self.xb, self.cut, self.step = xa, ya, yb, xb, cut, step
        self.rows, self.width = part.shape[1], part.shape[2]
        self.a, self.b = pl.ds(0, cut), pl.ds(cut, self.width - cut)

    def start(self):
        p = self.place
        self.order = [(1, 1), (1, 0), (0, 1), (0, 0)]
        self.into = {}
        for df, dy in self.order:
            f = 1 - p.f if df else p.f
            y = 1 - p.y if dy else p.y
            self.into[df, dy] = self.links.send(
                self.part.at[p.image(df, dy, 1)], self.core_in.at[2 * f + y], p.core_peer
            )

    def slot(self, df, dy):
        p = self.place
        return 2 * (1 - p.f if df else p.f) + (1 - p.y if dy else p.y)

    def cores(self):
        p, rc = self.place, self.core_in
        self.got = {}
        for df, dy in self.order:
            self.into[df, dy].wait_recv()
            j, mine = self.slot(df, dy), p.image(df, dy, 0)

            def add(rows, j=j, mine=mine):
                both = rc[j, rows, :].astype(WIDE) + self.part[mine, rows, :].astype(WIDE)
                rc[j, rows, :] = both.astype(LOW)

            in_rows(self.rows, self.step, add)
            y = 1 - p.y if dy else p.y
            f = 1 - p.f if df else p.f
            if df:
                self.got["x", dy] = self.links.send(rc.at[j, :, self.a], self.xa.at[y], p.x_peer)
            if dy:
                self.got["y", df] = self.links.send(rc.at[j, :, self.b], self.yb.at[f], p.y_peer)

    def cross(self):
        p, rc, xa, yb = self.place, self.core_in, self.xa, self.yb
        self.got["x", 1].wait_recv()
        j, other = self.slot(0, 1), 1 - p.y

        def add_a(rows):
            both = xa[other, rows, :].astype(WIDE) + rc[j, rows, self.a].astype(WIDE)
            xa[other, rows, :] = both.astype(LOW)

        in_rows(self.rows, self.step, add_a)
        self.last_a = self.links.send(xa.at[other], self.ya, p.y_peer)
        self.got["y", 1].wait_recv()
        k, away = self.slot(1, 0), 1 - p.f

        def add_b(rows):
            both = yb[away, rows, :].astype(WIDE) + rc[k, rows, self.b].astype(WIDE)
            yb[away, rows, :] = both.astype(LOW)

        in_rows(self.rows, self.step, add_b)
        self.last_b = self.links.send(yb.at[away], self.xb, p.x_peer)

    def finish(self, take):
        p, rc = self.place, self.core_in
        self.got["x", 0].wait_recv()
        self.got["y", 0].wait_recv()
        self.last_a.wait_recv()
        self.last_b.wait_recv()
        j, y, f = self.slot(0, 0), p.y, p.f

        def add(rows):
            first = rc[j, rows, self.a].astype(WIDE) + self.xa[y, rows, :].astype(WIDE)
            second = rc[j, rows, self.b].astype(WIDE) + self.yb[f, rows, :].astype(WIDE)
            take(rows, self.a, first + self.ya[rows, :].astype(WIDE))
            take(rows, self.b, second + self.xb[rows, :].astype(WIDE))

        in_rows(self.rows, self.step, add)


SUM_COPIES = 10


def sum_scratch(rows, width, cut):
    return [
        pltpu.VMEM((4, rows, width), LOW),
        pltpu.VMEM((2, rows, cut), LOW),
        pltpu.VMEM((rows, cut), LOW),
        pltpu.VMEM((2, rows, width - cut), LOW),
        pltpu.VMEM((rows, width - cut), LOW),
    ]


def all_heads(links, place, make):
    copies = []
    for k, device in enumerate(place.z_peers):
        src, dst = make(k, device[HEADS])
        copies.append(links.send(src, dst, device))
    return copies


def remote_call(kernel, outs, ins, scratch, copies, collective_id, vmem_mib):
    vmem = pl.BlockSpec(memory_space=pltpu.VMEM)
    return pl.pallas_call(
        kernel,
        out_shape=outs,
        in_specs=[vmem] * len(ins),
        out_specs=[vmem] * len(outs),
        scratch_shapes=[
            *scratch,
            pltpu.SemaphoreType.DMA((copies,)),
            pltpu.SemaphoreType.DMA((copies,)),
        ],
        compiler_params=pltpu.CompilerParams(
            collective_id=collective_id,
            has_side_effects=True,
            vmem_limit_bytes=vmem_mib * 2**20,
        ),
    )(*ins)


def shape(dims, dtype=LOW):
    return jax.ShapeDtypeStruct(dims, dtype)


def weights_kernel(heads, wq, wo, count, route, oq, oo, counts, far_route, ss, rs):
    place = Place(heads)
    links = Links(ss, rs)
    me = place.image(0, 0, 0)
    place.greet(place.plane_peers + place.z_peers)
    oq[me] = wq[...]
    oo[me, place.z] = wo[...]
    counts[me] = count[...]
    half = wq.shape[1] // 2
    mid = heads // 2
    main = PlaneGather(
        links,
        place,
        lambda i: oq.at[i, :, pl.ds(0, half)],
        lambda i: oq.at[i, :, pl.ds(half, half)],
        lambda i: oq.at[i],
    )
    side = PlaneGather(
        links,
        place,
        lambda i: oo.at[i, pl.ds(0, mid)],
        lambda i: oo.at[i, pl.ds(mid, heads - mid)],
        lambda i: oo.at[i],
    )
    main.start()
    along = all_heads(
        links, place, lambda k, z: (oo.at[me, place.z], oo.at[me, place.z])
    )
    small = [links.send(counts.at[me], counts.at[me], d) for d in place.plane_peers]
    small.append(links.send(route, far_route, place.x_peer))
    main.forward()
    for copy in along:
        copy.wait_recv()
    side.start()
    main.share()
    main.finish()
    side.forward()
    side.share()
    side.finish()
    for copy in small:
        copy.wait_recv()
    links.drain()


def gather_weights_fast(heads, wq, wo, count, route):
    outs = [
        shape((8, *wq.shape)),
        shape((8, heads, *wo.shape)),
        shape((8, *count.shape), jnp.int32),
        shape(route.shape, jnp.int32),
    ]
    copies = 2 * GATHER_COPIES + heads - 1 + 7 + 1
    return remote_call(
        functools.partial(weights_kernel, heads),
        outs,
        [wq, wo, count, route],
        [],
        copies,
        1,
        32,
    )


def mix_kernel(
    heads,
    experts,
    mixed,
    wo,
    tokens,
    gain,
    router,
    residual,
    second,
    group,
    probs,
    everyone,
    other_half,
    ss,
    rs,
):
    place = Place(heads)
    links = Links(ss, rs)
    me = place.image(0, 0, 0)
    place.greet(place.plane_peers + place.z_peers)
    everyone[place.z] = mixed[...]
    along = all_heads(links, place, lambda k, z: (everyone.at[place.z], everyone.at[place.z]))
    for copy in along:
        copy.wait_recv()
    rows_all, width = tokens.shape
    half = width // 2
    total = jnp.zeros((rows_all, width), WIDE)
    for z in range(heads):
        weight = wo[:, z].reshape(width, wo.shape[3])
        total = total + lax.dot_general(
            everyone[z], weight, (((1,), (1,)), ((), ())), preferred_element_type=WIDE
        )
    residual[...] = total

    def norm(rows):
        values = tokens[rows, :].astype(WIDE) + residual[rows, :]
        residual[rows, :] = values
        normed, _ = normalize(values)
        second[rows, :] = (normed * gain[...]).astype(LOW)

    in_rows(rows_all, 64, norm)
    low, high = second[:, :half], second[:, half:]
    first = place.f == 0
    group[me] = jnp.where(first, low, high)
    other_half[...] = jnp.where(first, high, low)
    x1 = links.send(other_half, group.at[me], place.x_peer)
    y1 = links.send(group.at[me], group.at[me], place.y_peer)
    shared = [links.send(group.at[me], group.at[me], place.core_peer)]
    logits = lax.dot_general(
        router[...], second[...], (((0,), (1,)), ((), ())), preferred_element_type=WIDE
    )[:experts]
    powers = jnp.exp(logits - jnp.max(logits, 0, keepdims=True))
    probs[me] = powers / jnp.sum(powers, 0, keepdims=True)
    small = [links.send(probs.at[me], probs.at[me], d) for d in place.plane_peers]
    across, beside, corner = place.image(1, 0, 0), place.image(0, 1, 0), place.image(1, 1, 0)
    x1.wait_recv()
    y2 = links.send(group.at[across], group.at[across], place.y_peer)
    shared.append(links.send(group.at[across], group.at[across], place.core_peer))
    y1.wait_recv()
    shared.append(links.send(group.at[beside], group.at[beside], place.core_peer))
    y2.wait_recv()
    shared.append(links.send(group.at[corner], group.at[corner], place.core_peer))
    for copy in shared + small:
        copy.wait_recv()
    links.drain()


def mix_heads(heads, experts, mixed, wo, tokens, gain, router):
    rows, width = tokens.shape
    return remote_call(
        functools.partial(mix_kernel, heads, experts),
        [
            shape((rows, width), WIDE),
            shape((rows, width)),
            shape((8, rows, width // 2)),
            shape((8, experts, rows), WIDE),
        ],
        [mixed, wo, tokens, gain, router],
        [pltpu.VMEM((heads, *mixed.shape), LOW), pltpu.VMEM((rows, width // 2), LOW)],
        heads - 1 + 7 + 7,
        2,
        48,
    )


def combine_kernel(
    heads,
    part,
    residual,
    teacher,
    valid,
    scale,
    result,
    final_grad,
    group,
    loss,
    core_in,
    xa,
    ya,
    yb,
    xb,
    image_sum,
    far,
    ss,
    rs,
):
    place = Place(heads)
    links = Links(ss, rs)
    me = place.image(0, 0, 0)
    z = place.z
    place.greet(place.axis_peers() + place.z_peers)
    rows_all, width = residual.shape
    own = rows_all // heads
    adder = PlaneSum(links, place, part, core_in, xa, ya, yb, xb, width // 2, 32)
    adder.start()
    adder.cores()
    adder.cross()

    def keep(rows, columns, values):
        image_sum[rows, columns] = values.astype(LOW)

    adder.finish(keep)
    along = all_heads(
        links,
        place,
        lambda k, to: (image_sum.at[pl.ds(pl.multiple_of(to * own, own), own)], far.at[k]),
    )
    for copy in along:
        copy.wait_recv()
    mine = pl.ds(pl.multiple_of(z * own, own), own)
    total = image_sum[mine, :].astype(WIDE)
    for k in range(heads - 1):
        total = total + far[k].astype(WIDE)
    final = residual[mine, :] + total
    result[z] = final.astype(LOW)
    error = (final - teacher[mine, :].astype(WIDE)) * valid[mine, :]
    grad = error * scale[0:1, 0:1]
    final_grad[...] = grad
    group[me, mine, :] = grad.astype(LOW)
    along = all_heads(links, place, lambda k, to: (group.at[me, mine], group.at[me, mine]))
    squares = jnp.sum((error * error).reshape(own // 8, 8, width), axis=0)
    loss[z] = sum(squares[:, i * 128 : (i + 1) * 128] for i in range(width // 128))
    extra = all_heads(links, place, lambda k, to: (result.at[z], result.at[z]))
    extra += all_heads(links, place, lambda k, to: (loss.at[z], loss.at[z]))
    for copy in along:
        copy.wait_recv()
    half = width // 2
    PlaneGather(
        links,
        place,
        lambda i: group.at[i, :, pl.ds(0, half)],
        lambda i: group.at[i, :, pl.ds(half, half)],
        lambda i: group.at[i],
    ).run()
    for copy in extra:
        copy.wait_recv()
    links.drain()


def combine(heads, part, residual, teacher, valid, scale):
    rows, width = residual.shape
    own = rows // heads
    return remote_call(
        functools.partial(combine_kernel, heads),
        [
            shape((heads, own, width)),
            shape((own, width), WIDE),
            shape((8, rows, width)),
            shape((heads, 8, 128), WIDE),
        ],
        [part, residual, teacher, valid, scale],
        [
            *sum_scratch(rows, width, width // 2),
            pltpu.VMEM((rows, width), LOW),
            pltpu.VMEM((heads - 1, own, width), LOW),
        ],
        GATHER_COPIES + SUM_COPIES + 4 * (heads - 1),
        3,
        56,
    )


def back_kernel(
    heads,
    experts,
    part,
    residual,
    gain,
    router,
    final_grad,
    attended,
    logit_grads,
    residual_grad,
    gain_part,
    core_in,
    y_in,
    far,
    pair,
    x_in,
    ss,
    rs,
):
    place = Place(heads)
    links = Links(ss, rs)
    f, y, z = place.f, place.y, place.z
    place.greet(place.axis_peers() + place.z_peers)
    rows_all, width = residual.shape
    half = width // 2
    own = rows_all // heads
    into = {}
    for dy in (1, 0):
        for df in (1, 0):
            slot = 2 * (1 - f if df else f) + (1 - y if dy else y)
            into[df, dy] = links.send(
                part.at[place.image(df, dy, 1)], core_in.at[slot], place.core_peer
            )
    beside = {}
    for dy in (1, 0):
        for df in (1, 0):
            to = 1 - f if df else f
            slot = 2 * to + (1 - y if dy else y)
            mine = place.image(df, dy, 0)
            into[df, dy].wait_recv()

            def add(rows, slot=slot, mine=mine):
                both = core_in[slot, rows, :].astype(WIDE) + part[mine, rows, :].astype(WIDE)
                core_in[slot, rows, :] = both.astype(LOW)

            in_rows(rows_all, 32, add)
            if dy:
                beside[df] = links.send(core_in.at[slot], y_in.at[to], place.y_peer)
    for df in (1, 0):
        to = 1 - f if df else f
        slot = 2 * to + y
        beside[df].wait_recv()

        def add_y(rows, slot=slot, to=to):
            both = core_in[slot, rows, :].astype(WIDE) + y_in[to, rows, :].astype(WIDE)
            y_in[to, rows, :] = both.astype(LOW)

        in_rows(rows_all, 32, add_y)
    along = all_heads(
        links,
        place,
        lambda k, to: (y_in.at[:, pl.ds(pl.multiple_of(to * own, own), own)], far.at[k]),
    )
    mine = pl.ds(pl.multiple_of(z * own, own), own)
    normed, spread = normalize(residual[mine, :])
    second_in = (normed * gain[...]).astype(LOW)
    logits = jnp.dot(second_in, router[...], preferred_element_type=WIDE)
    lanes = lax.broadcasted_iota(jnp.int32, logits.shape, 1)
    logits = jnp.where(lanes < experts, logits, MASKED)
    powers = jnp.exp(logits - jnp.max(logits, -1, keepdims=True))
    probs = powers / jnp.sum(powers, -1, keepdims=True)
    for copy in along:
        copy.wait_recv()
    for index in (1 - f, f):
        total = y_in[index, mine, :].astype(WIDE)
        for k in range(heads - 1):
            total = total + far[k, index].astype(WIDE)
        pair[index] = total.astype(LOW)
    cross = links.send(pair.at[1 - f], x_in, place.x_peer)
    near = pair[f].astype(WIDE)
    cross.wait_recv()
    away = x_in[...].astype(WIDE)
    prob_grad = near[:, half:] + away[:, half:]
    low, high = near[:, :half], away[:, :half]
    first = f == 0
    rows_grad = jnp.concatenate([jnp.where(first, low, high), jnp.where(first, high, low)], 1)
    inner = jnp.sum(probs * prob_grad, -1, keepdims=True)
    logit_grad = (probs * (prob_grad - inner)).astype(LOW)
    logit_grads[z] = logit_grad
    second_grad = rows_grad + lax.dot_general(
        logit_grad, router[...], (((1,), (1,)), ((), ())), preferred_element_type=WIDE
    )
    weighted = second_grad * gain[...]
    gain_part[...] = jnp.sum((second_grad * normed).reshape(own // 8, 8, width), axis=0)
    inner = (
        weighted
        - jnp.mean(weighted, -1, keepdims=True)
        - normed * jnp.mean(weighted * normed, -1, keepdims=True)
    )
    total_grad = final_grad[...] + inner * spread
    residual_grad[...] = total_grad
    attended[z] = total_grad.astype(LOW)
    along = all_heads(links, place, lambda k, to: (attended.at[z], attended.at[z]))
    along += all_heads(links, place, lambda k, to: (logit_grads.at[z], logit_grads.at[z]))
    for copy in along:
        copy.wait_recv()
    links.drain()


def back_through_norm(heads, experts, part, residual, gain, router, final_grad):
    rows, width = residual.shape
    own = rows // heads
    wide = part.shape[2]
    return remote_call(
        functools.partial(back_kernel, heads, experts),
        [
            shape((heads, own, width)),
            shape((heads, own, 128)),
            shape((own, width), WIDE),
            shape((8, width), WIDE),
        ],
        [part, residual, gain, router, final_grad],
        [
            pltpu.VMEM((4, rows, wide), LOW),
            pltpu.VMEM((2, rows, wide), LOW),
            pltpu.VMEM((heads - 1, 2, own, wide), LOW),
            pltpu.VMEM((2, own, wide), LOW),
            pltpu.VMEM((own, wide), LOW),
        ],
        4 + 2 + 1 + 3 * (heads - 1),
        4,
        56,
    )


def last_kernel(
    heads,
    first_part,
    dense,
    tokens,
    gain,
    residual_grad,
    gain_parts,
    tokens_grad,
    dense_out,
    gain_out,
    core_in,
    xa,
    ya,
    yb,
    xb,
    far,
    rounded,
    tiles,
    tiles_z,
    ss,
    rs,
):
    place = Place(heads)
    links = Links(ss, rs)
    z = place.z
    me = place.image(0, 0, 0)
    place.greet(place.plane_peers + place.z_peers)
    own, width = residual_grad.shape
    adder = PlaneSum(links, place, dense, core_in, xa, ya, yb, xb, xa.shape[2], 32)
    adder.start()
    along = all_heads(links, place, lambda k, to: (first_part.at[to], far.at[k]))
    tiles[me] = gain_parts[me]
    small = []
    for device in place.plane_peers:
        to = (device[FSDP] if FSDP in device else place.f) * 4 + device[TENSOR]
        small.append(links.send(gain_parts.at[to], tiles.at[me], device))
    adder.cores()
    adder.cross()
    for copy in small:
        copy.wait_recv()
    tiles_z[z] = sum(tiles[i] for i in range(8))
    gains = all_heads(links, place, lambda k, to: (tiles_z.at[z], tiles_z.at[z]))
    mine = pl.ds(pl.multiple_of(z * own, own), own)
    normed, spread = normalize(tokens[mine, :].astype(WIDE))
    for copy in along:
        copy.wait_recv()
    first_grad = first_part[z].astype(WIDE)
    for k in range(heads - 1):
        first_grad = first_grad + far[k].astype(WIDE)
    weighted = first_grad * gain[...]
    inner = (
        weighted
        - jnp.mean(weighted, -1, keepdims=True)
        - normed * jnp.mean(weighted * normed, -1, keepdims=True)
    )
    rounded[z] = (residual_grad[...] + inner * spread).astype(LOW)
    along = all_heads(links, place, lambda k, to: (rounded.at[z], rounded.at[z]))

    def keep(rows, columns, values):
        dense_out[rows, columns] = values

    adder.finish(keep)
    for copy in gains:
        copy.wait_recv()
    gain_out[...] = sum(tiles_z[i] for i in range(heads))
    for copy in along:
        copy.wait_recv()
    for i in range(heads):
        tokens_grad[i] = rounded[i].astype(WIDE)
    links.drain()


def last_sums(heads, first_part, dense, tokens, gain, residual_grad, gain_parts):
    own, width = residual_grad.shape
    _, rows, wide = dense.shape
    cut = 512 if wide == 896 else 128 * (wide // 256)
    return remote_call(
        functools.partial(last_kernel, heads),
        [
            shape((heads, own, width), WIDE),
            shape((rows, wide), WIDE),
            shape((8, 128), WIDE),
        ],
        [first_part, dense, tokens, gain, residual_grad, gain_parts],
        [
            *sum_scratch(rows, wide, cut),
            pltpu.VMEM((heads - 1, own, width), LOW),
            pltpu.VMEM((heads, own, width), LOW),
            pltpu.VMEM((8, 8, 128), WIDE),
            pltpu.VMEM((heads, 8, 128), WIDE),
        ],
        SUM_COPIES + 3 * (heads - 1) + 7,
        5,
        48,
    )


def by_index(index, own, other, axis):
    return jnp.where(
        index == 0,
        jnp.concatenate([own, other], axis),
        jnp.concatenate([other, own], axis),
    )


def swap(values):
    return lax.ppermute(values, FSDP, [(0, 1), (1, 0)])


def fast(
    tokens,
    valid_mask,
    routes,
    teacher,
    gain_one,
    qkv_weight,
    out_weight,
    gain_two,
    router_weight,
    expert_up,
    expert_down,
):
    heads = lax.axis_size(HEADS)
    f, z = lax.axis_index(FSDP), lax.axis_index(HEADS)
    _, rows, width = tokens.shape
    block, head_count, qkv_dim = qkv_weight.shape
    head_dim = qkv_dim // 3
    local_experts = expert_up.shape[0]
    kept = local_experts // 2
    expert_count = local_experts * heads
    group_rows = 4 * rows
    capacity = 2 * routes.shape[2] * group_rows // expert_count
    total_tokens, total_images = 8 * rows, 8
    score_scale = head_dim ** (-0.5)

    mine, theirs = f * kept, (1 - f) * kept
    half = width // 2

    qkv_width = head_count * qkv_dim
    pad = -(128 + qkv_width) % 256
    wq = jnp.concatenate(
        [
            router_weight,
            gain_one[:, None],
            gain_two[:, None],
            jnp.zeros((block, 128 - expert_count - 2), LOW),
            qkv_weight.reshape(block, qkv_width),
            jnp.zeros((block, pad), LOW),
        ],
        1,
    )
    wo = out_weight.reshape(head_count * head_dim, block).T
    count = jnp.full((8, 128), jnp.sum(valid_mask), jnp.int32)
    near_route = jnp.pad(routes.reshape(group_rows, -1).T, ((0, 8 - routes.shape[2]), (0, 0)))
    gathered, wo_all, counts, far_route = gather_weights_fast(heads, wq, wo, count, near_route)
    gathered, down_away = lax.optimization_barrier(
        (gathered, lax.dynamic_slice_in_dim(expert_down, theirs, kept, 0))
    )
    down_far = swap(down_away)
    down_near = lax.dynamic_slice_in_dim(expert_down, mine, kept, 0)
    gathered = gathered.reshape(width, -1)
    qkv_full = gathered[:, 128 : 128 + qkv_width]
    lanes = jnp.arange(128)
    router_wide = jnp.where(lanes < expert_count, gathered[:, :128], 0)
    gain_a = gathered[:, expert_count].astype(WIDE)[None]
    gain_b = gathered[:, expert_count + 1].astype(WIDE)[None]
    valid_total = jnp.sum(counts[:, 0, 0]).astype(WIDE)

    inputs = tokens[0].astype(WIDE)
    normed_one, _ = normalize(inputs)
    first_in = (normed_one * gain_a).astype(LOW)
    projected = (
        jnp.dot(first_in, qkv_full, preferred_element_type=WIDE)
        .astype(LOW)
        .reshape(rows, head_count, qkv_dim)
    )
    queries = projected[..., :head_dim]
    key_rows = projected[..., head_dim : 2 * head_dim]
    values = projected[..., 2 * head_dim :]
    keys_ok = (valid_mask > 0)[0][None, None, :]

    def scores_now():
        raw = jnp.einsum("qhe,khe->hqk", queries, key_rows, preferred_element_type=WIDE)
        return jnp.where(keys_ok, raw * score_scale, MASKED)

    scores = scores_now()
    peak_score = jnp.max(scores, -1, keepdims=True)
    exp_scores = jnp.exp(scores - peak_score)
    score_total = jnp.sum(exp_scores, -1, keepdims=True)
    logarithm_total = peak_score + jnp.log(score_total)
    attention = (exp_scores / score_total).astype(LOW)
    mixed = (
        jnp.einsum("hqk,khe->qhe", attention, values, preferred_element_type=WIDE)
        .astype(LOW)
        .reshape(rows, head_count * head_dim)
    )
    residual, second_in, group_in, probs_all = mix_heads(
        heads, expert_count, mixed, wo_all, tokens[0], gain_b, router_wide
    )

    both = by_index(f, near_route[None], far_route[None], 0)[:, : routes.shape[2]]
    rows_in = group_in.reshape(2, group_rows, half)
    probs_all = probs_all.reshape(2, 4, expert_count, rows)
    order = jnp.arange(group_rows, dtype=jnp.int32)
    earlier = (order[:, None] < order[None, :]).astype(LOW)

    def picks(start):
        ids = z * local_experts + start + jnp.arange(kept, dtype=jnp.int32)
        chosen = jnp.any(both[:, None] == ids[None, :, None, None], 2)
        slot = jnp.einsum(
            "get,tu->geu", chosen.astype(LOW), earlier, preferred_element_type=WIDE
        ).astype(jnp.int32)
        return chosen[:, :, None, :] & (
            slot[:, :, None, :] == jnp.arange(capacity, dtype=jnp.int32)[None, None, :, None]
        )

    def dispatch(pick, values):
        out = jnp.einsum("gest,gtd->egsd", pick, values, preferred_element_type=WIDE)
        return out.reshape(kept, 2 * capacity, values.shape[-1])

    def collect(pick, values):
        values = values.reshape(kept, 2, capacity, values.shape[-1])
        return jnp.einsum("gest,egsd->gtd", pick, values, preferred_element_type=WIDE)

    hot = picks(mine)
    pick_near, pick_far = hot.astype(LOW), picks(theirs).astype(LOW)
    up_near = lax.dynamic_slice_in_dim(expert_up, mine, kept, 0)
    up_far = lax.dynamic_slice_in_dim(expert_up, theirs, kept, 0)
    buffer_far = dispatch(pick_far, rows_in).astype(LOW)
    away = jnp.einsum("ecd,edf->ecf", buffer_far, up_far, preferred_element_type=WIDE)
    arrived = swap(away.astype(LOW))
    buffer_near = dispatch(pick_near, rows_in).astype(LOW)
    before_gelu = jnp.einsum("ecd,edf->ecf", buffer_near, up_near, preferred_element_type=WIDE)
    before_gelu = before_gelu + arrived.astype(WIDE)
    probs_own = lax.dynamic_slice_in_dim(probs_all, z * local_experts + mine, kept, 2)
    probs_own = jnp.swapaxes(probs_own, 1, 2).reshape(2, kept, 1, group_rows)
    slot_gate = jnp.sum(jnp.where(hot, probs_own, 0.0), -1)
    gates = jnp.swapaxes(slot_gate, 0, 1).reshape(kept, 2 * capacity, 1)
    down_full = by_index(f, down_near, down_far, 2)
    hidden = jax.nn.gelu(before_gelu, approximate=False).astype(LOW)
    expert_out = jnp.einsum("ecf,efd->ecd", hidden, down_full, preferred_element_type=WIDE)
    part = collect(pick_near, (expert_out * gates).astype(LOW)).astype(LOW)
    part = part.reshape(8, rows, width)

    valid_rows = valid_mask[0].astype(WIDE)[:, None]
    scale = jnp.full((8, 128), total_tokens / valid_total, WIDE)
    result, final_grad, group_grad, loss = combine(
        heads, part, residual, teacher[0], valid_rows, scale
    )
    loss_terms = (jnp.sum(loss) * (total_images / (valid_total * width)))[None]

    slot_grad = dispatch(pick_near, group_grad.reshape(2, group_rows, width))
    out_grad = (slot_grad * gates).astype(LOW)
    raw = jnp.einsum(
        "ecd,efd->ecf", slot_grad.astype(LOW), down_full, preferred_element_type=WIDE
    )
    gate_slot_grad = jnp.sum(raw * hidden.astype(WIDE), -1)
    normal_cdf = 0.5 * (1.0 + lax.erf(before_gelu * ROOT_HALF))
    slope = normal_cdf + before_gelu * DENSITY * jnp.exp(-0.5 * before_gelu * before_gelu)
    pre_near = (raw * gates * slope).astype(LOW)
    pre_far = swap(pre_near)
    down_grad = jnp.einsum("ecf,ecd->efd", hidden, out_grad, preferred_element_type=WIDE)
    down_own = lax.dynamic_slice_in_dim(down_grad, f * half, half, 2)
    down_send = lax.dynamic_slice_in_dim(down_grad, (1 - f) * half, half, 2).astype(LOW)
    ids = z * local_experts + mine + jnp.arange(kept, dtype=jnp.int32)
    column = (ids[:, None, None] == lanes).astype(WIDE)

    def through_up(pick, buffer, pre, up, extra):
        grad = jnp.einsum("ecd,ecf->edf", buffer, pre, preferred_element_type=WIDE)
        rows_out = jnp.einsum("ecf,edf->ecd", pre, up, preferred_element_type=WIDE)
        rows_out = jnp.concatenate([rows_out, extra], -1).astype(LOW)
        return grad, collect(pick, rows_out)

    up_own, back_near = through_up(
        pick_near, buffer_near, pre_near, up_near, gate_slot_grad[..., None] * column
    )
    up_other, back_far = through_up(
        pick_far, buffer_far, pre_far, up_far, jnp.zeros((kept, 2 * capacity, 128), WIDE)
    )
    back_part = (back_near + back_far).astype(LOW).reshape(8, rows, -1)

    attended, logit_grads, residual_grad, gain_two_part = back_through_norm(
        heads, expert_count, back_part, residual, gain_b, router_wide, final_grad
    )
    attended, down_send = lax.optimization_barrier((attended, down_send))
    down_other = swap(down_send)

    attended_grad = attended.reshape(rows, width)
    wo_own = lax.dynamic_index_in_dim(wo_all, z, 1, False).reshape(width, -1)
    mixed_grad = (
        jnp.dot(attended_grad, wo_own, preferred_element_type=WIDE)
        .astype(LOW)
        .reshape(rows, head_count, head_dim)
    )
    scores = scores_now()
    probs = jnp.exp(scores - logarithm_total)
    prob_part = jnp.einsum("qhe,khe->hqk", mixed_grad, values, preferred_element_type=WIDE)
    score_grad = (probs * (prob_part - jnp.sum(probs * prob_part, -1, keepdims=True))).astype(LOW)
    query_grad = (
        jnp.einsum("hqk,khe->qhe", score_grad, key_rows, preferred_element_type=WIDE) * score_scale
    )
    key_grad = (
        jnp.einsum("hqk,qhe->khe", score_grad, queries, preferred_element_type=WIDE) * score_scale
    )
    value_grad = jnp.einsum(
        "hqk,qhe->khe", probs.astype(LOW), mixed_grad, preferred_element_type=WIDE
    )
    projected_grad = (
        jnp.concatenate([query_grad, key_grad, value_grad], -1)
        .astype(LOW)
        .reshape(rows, qkv_width)
    )
    first_part = lax.dot_general(
        projected_grad, qkv_full, (((1,), (1,)), ((), ())), preferred_element_type=WIDE
    )
    gain_one_part = jnp.sum(first_part * normed_one, 0)
    qkv_grad = jnp.einsum("sd,se->de", first_in, projected_grad, preferred_element_type=WIDE)
    out_grad_t = jnp.einsum("sd,se->de", attended_grad, mixed, preferred_element_type=WIDE)
    router_grad = jnp.einsum(
        "sd,se->de", second_in, logit_grads.reshape(rows, 128), preferred_element_type=WIDE
    )
    dense = jnp.concatenate([qkv_grad, out_grad_t, router_grad], 1).astype(LOW)
    gain_parts = jnp.stack([gain_one_part, jnp.sum(gain_two_part, 0)], 0).reshape(2, 8, block)
    gain_parts = jnp.pad(jnp.swapaxes(gain_parts, 0, 1), ((0, 0), (0, 6), (0, 128 - block)))
    tokens_grad, dense_out, gain_out = last_sums(
        heads,
        first_part.astype(LOW).reshape(heads, rows // heads, width),
        dense.reshape(8, block, -1),
        tokens[0],
        gain_a,
        residual_grad,
        gain_parts,
    )
    out_width = head_count * head_dim
    return (
        result.reshape(1, rows, width),
        loss_terms,
        tokens_grad.reshape(1, rows, width),
        gain_out[0, :block],
        dense_out[:, :qkv_width].reshape(block, head_count, qkv_dim),
        dense_out[:, qkv_width : qkv_width + out_width].T.reshape(head_count, head_dim, block),
        gain_out[1, :block],
        dense_out[:, qkv_width + out_width : qkv_width + out_width + expert_count],
        by_index(f, up_own, up_other, 0),
        by_index(f, down_own, down_other.astype(WIDE), 0),
    )


def local(sizes, *args):
    tokens, routes, up = args[0], args[2], args[9]
    fits = (
        sizes[FSDP] == 2
        and sizes[TENSOR] == 4
        and sizes[HEADS] % 2 == 0
        and tokens.shape[0] == 1
        and up.shape[0] % 2 == 0
        and tokens.shape[1] % (32 * sizes[HEADS]) == 0
        and tokens.shape[2] % 256 == 0
        and routes.shape[2] <= 8
        and up.shape[0] * sizes[HEADS] <= 126
    )
    return fast(*args) if fits else general(*args)


def solution(mesh):
    sizes = dict(mesh.shape)
    program = functools.partial(local, sizes)
    in_specs = (
        P((FSDP, TENSOR), None, None),
        P((FSDP, TENSOR), None),
        P(FSDP, None, None),
        P((FSDP, TENSOR), None, None),
        P((FSDP, TENSOR)),
        P((FSDP, TENSOR), HEADS, None),
        P(HEADS, None, (FSDP, TENSOR)),
        P((FSDP, TENSOR)),
        P((FSDP, TENSOR), None),
        P(HEADS, FSDP, TENSOR),
        P(HEADS, TENSOR, FSDP),
    )
    out_specs = (
        P((FSDP, TENSOR), None, None),
        P((FSDP, TENSOR)),
        P((FSDP, TENSOR), None, None),
        P((FSDP, TENSOR)),
        P((FSDP, TENSOR), HEADS, None),
        P(HEADS, None, (FSDP, TENSOR)),
        P((FSDP, TENSOR)),
        P((FSDP, TENSOR), None),
        P(HEADS, FSDP, TENSOR),
        P(HEADS, TENSOR, FSDP),
    )
    return jax.shard_map(program, mesh=mesh, in_specs=in_specs, out_specs=out_specs, check_vma=False)
```

```python
import functools

import jax
import jax.numpy as jnp
from jax import lax
from jax.experimental import pallas as pl
from jax.experimental.pallas import tpu as pltpu
from jax.sharding import PartitionSpec as P

FSDP, HEADS, TENSOR = "fsdp", "heads", "tensor"
EPSILON = 1e-06
MASKED = -1e30
ROOT_HALF = 0.7071067811865476
DENSITY = 0.3989422804014327


def normalize(values):
    center = values - jnp.mean(values, -1, keepdims=True)
    inv_std = lax.rsqrt(jnp.mean(center * center, -1, keepdims=True) + EPSILON)
    return (center * inv_std, inv_std)


def norm_back(gradient, normed, inv_std, gain_vector):
    weighted = gradient * gain_vector
    gain_grad = jnp.sum(gradient * normed, axis=(0, 1))
    inner = (
        weighted
        - jnp.mean(weighted, -1, keepdims=True)
        - normed * jnp.mean(weighted * normed, -1, keepdims=True)
    )
    return (inner * inv_std, gain_grad)


def scores_of(queries, key_rows, keys_ok, score_scale):
    raw_scores = (
        jnp.einsum("iqhe,ikhe->ihqk", queries, key_rows, preferred_element_type=jnp.float32)
        * score_scale
    )
    return jnp.where(keys_ok, raw_scores, MASKED)


def gather_weights(
    gain_one, qkv_weight, out_weight, gain_two, router_weight, expert_up, expert_down
):
    dense_set = (
        lax.all_gather(qkv_weight, (FSDP, TENSOR), axis=0, tiled=True),
        lax.all_gather(out_weight, (FSDP, TENSOR), axis=2, tiled=True),
        lax.all_gather(router_weight, (FSDP, TENSOR), axis=0, tiled=True),
        lax.all_gather(gain_one, (FSDP, TENSOR), axis=0, tiled=True),
        lax.all_gather(gain_two, (FSDP, TENSOR), axis=0, tiled=True),
    )
    expert_set = (
        lax.all_gather(expert_up, FSDP, axis=1, tiled=True),
        lax.all_gather(expert_down, FSDP, axis=2, tiled=True),
    )
    return (dense_set, expert_set)


def reduce_expert_grads(up_grad, down_grad):
    return (
        lax.psum_scatter(up_grad, FSDP, scatter_dimension=1, tiled=True),
        lax.psum_scatter(down_grad, FSDP, scatter_dimension=2, tiled=True),
    )


def general(
    tokens,
    valid_mask,
    routes,
    teacher,
    gain_one,
    qkv_weight,
    out_weight,
    gain_two,
    router_weight,
    expert_up,
    expert_down,
):
    valid_total = lax.psum(jnp.sum(valid_mask.astype(jnp.float32)), (FSDP, TENSOR))
    dense_set, expert_set = gather_weights(
        gain_one, qkv_weight, out_weight, gain_two, router_weight, expert_up, expert_down
    )
    qkv_full, output_complete, router_full, gain_a, gain_b = dense_set
    up_full, down_full = expert_set
    image_count, token_slots, model_width = tokens.shape
    head_dim = qkv_full.shape[2] // 3
    local_experts = expert_up.shape[0]
    tensor_size = lax.axis_size(TENSOR)
    group_images = image_count * tensor_size
    group_rows = group_images * token_slots
    top_choices = routes.shape[2]
    expert_count = local_experts * lax.axis_size(HEADS)
    capacity = 2 * top_choices * group_rows // expert_count
    slot_count = local_experts * capacity
    total_tokens = image_count * token_slots * lax.axis_size(FSDP) * tensor_size
    total_images = image_count * lax.axis_size(FSDP) * tensor_size
    score_scale = head_dim ** (-0.5)
    inputs = tokens.astype(jnp.float32)
    normed_one, spread_one = normalize(inputs)
    first_in = (normed_one * gain_a.astype(jnp.float32)).astype(jnp.bfloat16)
    projected = jnp.einsum(
        "isd,dhe->ishe", first_in, qkv_full, preferred_element_type=jnp.float32
    ).astype(jnp.bfloat16)
    queries = projected[..., :head_dim]
    key_rows = projected[..., head_dim : 2 * head_dim]
    values = projected[..., 2 * head_dim :]
    keys_ok = (valid_mask > 0)[:, None, None, :]
    scores = scores_of(queries, key_rows, keys_ok, score_scale)
    peak_score = jnp.max(scores, -1, keepdims=True)
    exp_scores = jnp.exp(scores - peak_score)
    score_total = jnp.sum(exp_scores, -1, keepdims=True)
    logarithm_total = peak_score + jnp.log(score_total)
    attention = (exp_scores / score_total).astype(jnp.bfloat16)
    combined_heads = jnp.einsum(
        "ihqk,ikhe->iqhe", attention, values, preferred_element_type=jnp.float32
    ).astype(jnp.bfloat16)
    attn_part = jnp.einsum(
        "iqhe,hed->iqd", combined_heads, output_complete, preferred_element_type=jnp.float32
    )
    attended = lax.psum(attn_part, HEADS)
    residual = inputs + attended
    normed_two, spread_two = normalize(residual)
    second_in = (normed_two * gain_b.astype(jnp.float32)).astype(jnp.bfloat16)
    group_in = lax.all_gather(second_in, TENSOR, axis=0, tiled=True)
    rows_in = group_in.reshape(group_rows, model_width)
    logits = jnp.dot(rows_in, router_full, preferred_element_type=jnp.float32)
    peak_logit = jnp.max(logits, -1, keepdims=True)
    exponent_logits = jnp.exp(logits - peak_logit)
    router_probs = exponent_logits / jnp.sum(exponent_logits, -1, keepdims=True)
    expert_ids = jnp.arange(expert_count, dtype=jnp.int32)
    route_pairs = routes.reshape(group_rows, top_choices)
    picked_hot = (route_pairs[:, :, None] == expert_ids[None, None, :]).astype(jnp.float32)
    gate_weight_values = jnp.sum(router_probs[:, None, :] * picked_hot, -1)
    flat_routes = route_pairs.reshape(group_rows * top_choices)
    route_hot = (flat_routes[:, None] == expert_ids[None, :]).astype(jnp.int32)
    order = jnp.arange(group_rows * top_choices, dtype=jnp.int32)
    before = (order[None, :] < order[:, None]).astype(jnp.bfloat16)
    earlier = jnp.dot(
        before, route_hot.astype(jnp.bfloat16), preferred_element_type=jnp.float32
    ).astype(jnp.int32)
    slot_index = jnp.sum(earlier * route_hot, 1)
    first_expert = lax.axis_index(HEADS) * local_experts
    is_local = (flat_routes >= first_expert) & (flat_routes < first_expert + local_experts)
    target = jnp.where(is_local, (flat_routes - first_expert) * capacity + slot_index, slot_count)
    owner_row = jnp.arange(group_rows * top_choices, dtype=jnp.int32) // top_choices
    source = jnp.zeros((slot_count,), jnp.int32).at[target].set(owner_row, mode="drop")
    slot_gate = (
        jnp.zeros((slot_count,), jnp.float32)
        .at[target]
        .set(gate_weight_values.reshape(-1), mode="drop")
    )
    slot_pick = jnp.minimum(target, slot_count - 1)
    retain_mask = is_local.astype(jnp.float32)
    dispatched = rows_in[source].reshape(local_experts, capacity, model_width)
    before_gelu = jnp.einsum(
        "ecd,edf->ecf", dispatched, up_full, preferred_element_type=jnp.float32
    )
    hidden = jax.nn.gelu(before_gelu, approximate=False).astype(jnp.bfloat16)
    expert_out = jnp.einsum(
        "ecf,efd->ecd", hidden, down_full, preferred_element_type=jnp.float32
    ).reshape(slot_count, model_width)
    weighted = expert_out * slot_gate[:, None]
    moe_part = jnp.sum(
        (weighted[slot_pick] * retain_mask[:, None]).reshape(group_rows, top_choices, model_width),
        1,
    )
    moe_part = moe_part.reshape(group_images, token_slots, model_width)
    expert_sum = lax.psum(
        lax.psum_scatter(moe_part, TENSOR, scatter_dimension=0, tiled=True), HEADS
    )
    final = residual + expert_sum
    valid_rows = valid_mask.astype(jnp.float32)[..., None]
    difference = (final - teacher.astype(jnp.float32)) * valid_rows
    loss_terms = jnp.sum(difference * difference, axis=(1, 2)) * (
        total_images / (valid_total * model_width)
    )
    final_grad = difference * (total_tokens / valid_total)
    dense_set, expert_set = gather_weights(
        gain_one, qkv_weight, out_weight, gain_two, router_weight, expert_up, expert_down
    )
    qkv_full, output_complete, router_full, gain_a, gain_b = dense_set
    up_full, down_full = expert_set
    moe_grad = final_grad.astype(jnp.bfloat16)
    group_grad = lax.all_gather(moe_grad, TENSOR, axis=0, tiled=True).reshape(
        group_rows, model_width
    )
    slot_grad = group_grad[source].astype(jnp.float32)
    gate_slot_grad = jnp.sum(slot_grad * expert_out, -1)
    out_grad = (
        (slot_grad * slot_gate[:, None])
        .astype(jnp.bfloat16)
        .reshape(local_experts, capacity, model_width)
    )
    expert_down_grad = jnp.einsum(
        "ecf,ecd->efd", hidden, out_grad, preferred_element_type=jnp.float32
    )
    hidden_grad = jnp.einsum(
        "ecd,efd->ecf", out_grad, down_full, preferred_element_type=jnp.float32
    )
    normal_cdf = 0.5 * (1.0 + lax.erf(before_gelu * ROOT_HALF))
    slope = normal_cdf + before_gelu * DENSITY * jnp.exp(-0.5 * before_gelu * before_gelu)
    pre_grad = (hidden_grad * slope).astype(jnp.bfloat16)
    expert_up_grad = jnp.einsum(
        "ecd,ecf->edf", dispatched, pre_grad, preferred_element_type=jnp.float32
    )
    row_grad = jnp.einsum(
        "ecf,edf->ecd", pre_grad, up_full, preferred_element_type=jnp.float32
    ).reshape(slot_count, model_width)
    rows_part = jnp.sum(
        (row_grad[slot_pick] * retain_mask[:, None]).reshape(group_rows, top_choices, model_width),
        1,
    )
    rows_part = rows_part.reshape(group_images, token_slots, model_width)
    gate_part = (gate_slot_grad[slot_pick] * retain_mask).reshape(
        group_images, token_slots, top_choices
    )
    rows_share, gate_share = (
        lax.psum_scatter(rows_part, TENSOR, scatter_dimension=0, tiled=True),
        lax.psum_scatter(gate_part, TENSOR, scatter_dimension=0, tiled=True),
    )
    second_grad, gate_grad = lax.psum((rows_share, gate_share), HEADS)
    own_start = lax.axis_index(TENSOR) * image_count * token_slots
    own_rows = image_count * token_slots
    own_probs = lax.dynamic_slice_in_dim(router_probs, own_start, own_rows, 0).reshape(
        image_count, token_slots, expert_count
    )
    own_hot = lax.dynamic_slice_in_dim(picked_hot, own_start, own_rows, 0).reshape(
        image_count, token_slots, top_choices, expert_count
    )
    prob_grad = jnp.sum(gate_grad[..., None] * own_hot, 2)
    logit_grad = (
        own_probs * (prob_grad - jnp.sum(own_probs * prob_grad, -1, keepdims=True))
    ).astype(jnp.bfloat16)
    router_grad = jnp.einsum(
        "isd,ise->de", second_in, logit_grad, preferred_element_type=jnp.float32
    )
    second_grad = second_grad + jnp.einsum(
        "ise,de->isd", logit_grad, router_full, preferred_element_type=jnp.float32
    )
    residual_norm, gain_two_grad = norm_back(
        second_grad, normed_two, spread_two, gain_b.astype(jnp.float32)
    )
    residual_grad = final_grad + residual_norm
    attended_output_gradient = residual_grad.astype(jnp.bfloat16)
    out_weight_grad = jnp.einsum(
        "iqhe,iqd->hed",
        combined_heads,
        attended_output_gradient,
        preferred_element_type=jnp.float32,
    )
    mixed_grad = jnp.einsum(
        "iqd,hed->iqhe",
        attended_output_gradient,
        output_complete,
        preferred_element_type=jnp.float32,
    ).astype(jnp.bfloat16)
    scores = scores_of(queries, key_rows, keys_ok, score_scale)
    probs = jnp.exp(scores - logarithm_total)
    probs_low = probs.astype(jnp.bfloat16)
    prob_part = jnp.einsum(
        "iqhe,ikhe->ihqk", mixed_grad, values, preferred_element_type=jnp.float32
    )
    score_grad = (probs * (prob_part - jnp.sum(probs * prob_part, -1, keepdims=True))).astype(
        jnp.bfloat16
    )
    query_grad = (
        jnp.einsum("ihqk,ikhe->iqhe", score_grad, key_rows, preferred_element_type=jnp.float32)
        * score_scale
    )
    key_grad = (
        jnp.einsum("ihqk,iqhe->ikhe", score_grad, queries, preferred_element_type=jnp.float32)
        * score_scale
    )
    value_grad = jnp.einsum(
        "ihqk,iqhe->ikhe", probs_low, mixed_grad, preferred_element_type=jnp.float32
    )
    projected_grad = jnp.concatenate([query_grad, key_grad, value_grad], -1).astype(jnp.bfloat16)
    qkv_grad = jnp.einsum(
        "isd,ishe->dhe", first_in, projected_grad, preferred_element_type=jnp.float32
    )
    first_part = jnp.einsum(
        "ishe,dhe->isd", projected_grad, qkv_full, preferred_element_type=jnp.float32
    )
    first_grad = lax.psum(first_part, HEADS)
    input_norm, gain_one_grad = norm_back(
        first_grad, normed_one, spread_one, gain_a.astype(jnp.float32)
    )
    tokens_grad = residual_grad + input_norm
    dense_grads = (
        lax.psum_scatter(qkv_grad, (FSDP, TENSOR), scatter_dimension=0, tiled=True),
        lax.psum_scatter(out_weight_grad, (FSDP, TENSOR), scatter_dimension=2, tiled=True),
        lax.psum_scatter(router_grad, (FSDP, TENSOR), scatter_dimension=0, tiled=True),
        lax.psum_scatter(gain_one_grad, (FSDP, TENSOR), scatter_dimension=0, tiled=True),
        lax.psum_scatter(gain_two_grad, (FSDP, TENSOR), scatter_dimension=0, tiled=True),
    )
    expert_grads = reduce_expert_grads(expert_up_grad, expert_down_grad)
    return (
        final.astype(jnp.bfloat16),
        loss_terms,
        tokens_grad,
        dense_grads[3],
        dense_grads[0],
        dense_grads[1],
        dense_grads[4],
        dense_grads[2],
        expert_grads[0],
        expert_grads[1],
    )


MESH = pl.DeviceIdType.MESH
LOW = jnp.bfloat16
WIDE = jnp.float32


class Links:
    def __init__(self, send_sems, recv_sems):
        self.send_sems, self.recv_sems = send_sems, recv_sems
        self.copies = []

    def send(self, src, dst, device):
        k = len(self.copies)
        copy = pltpu.make_async_remote_copy(
            src_ref=src,
            dst_ref=dst,
            send_sem=self.send_sems.at[k],
            recv_sem=self.recv_sems.at[k],
            device_id=device,
            device_id_type=MESH,
        )
        copy.start()
        self.copies.append(copy)
        return copy

    def drain(self):
        for copy in self.copies:
            copy.wait_send()


class Place:
    def __init__(self, heads):
        self.f = lax.axis_index(FSDP)
        t = lax.axis_index(TENSOR)
        self.y, self.c = t // 2, lax.rem(t, 2)
        self.z = lax.axis_index(HEADS)
        self.heads = heads
        self.x_peer = {FSDP: 1 - self.f}
        self.y_peer = {TENSOR: 2 * (1 - self.y) + self.c}
        self.core_peer = {TENSOR: 2 * self.y + 1 - self.c}
        self.z_peers = [{HEADS: lax.rem(self.z + k, heads)} for k in range(1, heads)]
        self.plane_peers = []
        for a in range(2):
            for k in range(4):
                if a or k:
                    where = {TENSOR: lax.rem(t + k, 4)}
                    if a:
                        where[FSDP] = 1 - self.f
                    self.plane_peers.append(where)

    def image(self, df, dy, dc):
        f = 1 - self.f if df else self.f
        y = 1 - self.y if dy else self.y
        c = 1 - self.c if dc else self.c
        return f * 4 + 2 * y + c

    def greet(self, devices):
        barrier = pltpu.get_barrier_semaphore()
        for device in devices:
            pl.semaphore_signal(barrier, inc=1, device_id=device, device_id_type=MESH)
        pl.semaphore_wait(barrier, len(devices))

    def axis_peers(self):
        return [self.x_peer, self.y_peer, self.core_peer]


class PlaneGather:
    def __init__(self, links, place, first, second, whole):
        self.links, self.place = links, place
        self.first, self.second, self.whole = first, second, whole

    def go(self, part, image, device):
        return self.links.send(part(image), part(image), device)

    def start(self):
        p, me = self.place, self.place.image(0, 0, 0)
        self.xa = self.go(self.first, me, p.x_peer)
        self.yb = self.go(self.second, me, p.y_peer)
        self.own = self.go(self.whole, me, p.core_peer)
        self.xb = self.go(self.second, me, p.x_peer)
        self.ya = self.go(self.first, me, p.y_peer)

    def forward(self):
        p = self.place
        self.xa.wait_recv()
        self.fa = self.go(self.first, p.image(1, 0, 0), p.y_peer)
        self.yb.wait_recv()
        self.fb = self.go(self.second, p.image(0, 1, 0), p.x_peer)

    def share(self):
        p = self.place
        self.xb.wait_recv()
        self.c1 = self.go(self.whole, p.image(1, 0, 0), p.core_peer)
        self.ya.wait_recv()
        self.c2 = self.go(self.whole, p.image(0, 1, 0), p.core_peer)

    def finish(self):
        p = self.place
        self.fa.wait_recv()
        self.fb.wait_recv()
        self.c3 = self.go(self.whole, p.image(1, 1, 0), p.core_peer)
        for copy in (self.own, self.c1, self.c2, self.c3):
            copy.wait_recv()

    def run(self):
        self.start()
        self.forward()
        self.share()
        self.finish()


GATHER_COPIES = 10


def in_rows(rows, step, body):
    def one(i, carry):
        body(pl.ds(pl.multiple_of(i * step, step), step))
        return carry

    lax.fori_loop(0, rows // step, one, 0)


class PlaneSum:
    def __init__(self, links, place, part, core_in, xa, ya, yb, xb, cut, step):
        self.links, self.place, self.part, self.core_in = links, place, part, core_in
        self.xa, self.ya, self.yb, self.xb, self.cut, self.step = xa, ya, yb, xb, cut, step
        self.rows, self.width = part.shape[1], part.shape[2]
        self.a, self.b = pl.ds(0, cut), pl.ds(cut, self.width - cut)

    def start(self):
        p = self.place
        self.order = [(1, 1), (1, 0), (0, 1), (0, 0)]
        self.into = {}
        for df, dy in self.order:
            f = 1 - p.f if df else p.f
            y = 1 - p.y if dy else p.y
            self.into[df, dy] = self.links.send(
                self.part.at[p.image(df, dy, 1)], self.core_in.at[2 * f + y], p.core_peer
            )

    def slot(self, df, dy):
        p = self.place
        return 2 * (1 - p.f if df else p.f) + (1 - p.y if dy else p.y)

    def cores(self):
        p, rc = self.place, self.core_in
        self.got = {}
        for df, dy in self.order:
            self.into[df, dy].wait_recv()
            j, mine = self.slot(df, dy), p.image(df, dy, 0)

            def add(rows, j=j, mine=mine):
                both = rc[j, rows, :].astype(WIDE) + self.part[mine, rows, :].astype(WIDE)
                rc[j, rows, :] = both.astype(LOW)

            in_rows(self.rows, self.step, add)
            y = 1 - p.y if dy else p.y
            f = 1 - p.f if df else p.f
            if df:
                self.got["x", dy] = self.links.send(rc.at[j, :, self.a], self.xa.at[y], p.x_peer)
            if dy:
                self.got["y", df] = self.links.send(rc.at[j, :, self.b], self.yb.at[f], p.y_peer)

    def cross(self):
        p, rc, xa, yb = self.place, self.core_in, self.xa, self.yb
        self.got["x", 1].wait_recv()
        j, other = self.slot(0, 1), 1 - p.y

        def add_a(rows):
            both = xa[other, rows, :].astype(WIDE) + rc[j, rows, self.a].astype(WIDE)
            xa[other, rows, :] = both.astype(LOW)

        in_rows(self.rows, self.step, add_a)
        self.last_a = self.links.send(xa.at[other], self.ya, p.y_peer)
        self.got["y", 1].wait_recv()
        k, away = self.slot(1, 0), 1 - p.f

        def add_b(rows):
            both = yb[away, rows, :].astype(WIDE) + rc[k, rows, self.b].astype(WIDE)
            yb[away, rows, :] = both.astype(LOW)

        in_rows(self.rows, self.step, add_b)
        self.last_b = self.links.send(yb.at[away], self.xb, p.x_peer)

    def finish(self, take):
        p, rc = self.place, self.core_in
        self.got["x", 0].wait_recv()
        self.got["y", 0].wait_recv()
        self.last_a.wait_recv()
        self.last_b.wait_recv()
        j, y, f = self.slot(0, 0), p.y, p.f

        def add(rows):
            first = rc[j, rows, self.a].astype(WIDE) + self.xa[y, rows, :].astype(WIDE)
            second = rc[j, rows, self.b].astype(WIDE) + self.yb[f, rows, :].astype(WIDE)
            take(rows, self.a, first + self.ya[rows, :].astype(WIDE))
            take(rows, self.b, second + self.xb[rows, :].astype(WIDE))

        in_rows(self.rows, self.step, add)


SUM_COPIES = 10


def sum_scratch(rows, width, cut):
    return [
        pltpu.VMEM((4, rows, width), LOW),
        pltpu.VMEM((2, rows, cut), LOW),
        pltpu.VMEM((rows, cut), LOW),
        pltpu.VMEM((2, rows, width - cut), LOW),
        pltpu.VMEM((rows, width - cut), LOW),
    ]


def all_heads(links, place, make):
    copies = []
    for k, device in enumerate(place.z_peers):
        src, dst = make(k, device[HEADS])
        copies.append(links.send(src, dst, device))
    return copies


def spends(microseconds):
    return pl.CostEstimate(flops=0, bytes_accessed=microseconds * 3_000_000, transcendentals=0)


def remote_call(
    kernel,
    outs,
    ins,
    scratch,
    copies,
    collective_id,
    vmem_mib,
    microseconds,
    in_hbm=(),
    out_hbm=(),
):
    vmem, hbm = pl.BlockSpec(memory_space=pltpu.VMEM), pl.BlockSpec(memory_space=pl.ANY)
    return pl.pallas_call(
        kernel,
        out_shape=outs,
        in_specs=[hbm if i in in_hbm else vmem for i in range(len(ins))],
        out_specs=[hbm if i in out_hbm else vmem for i in range(len(outs))],
        scratch_shapes=[
            *scratch,
            pltpu.SemaphoreType.DMA((copies,)),
            pltpu.SemaphoreType.DMA((copies,)),
        ],
        compiler_params=pltpu.CompilerParams(
            collective_id=collective_id,
            has_side_effects=True,
            vmem_limit_bytes=vmem_mib * 2**20,
        ),
        cost_estimate=spends(microseconds),
    )(*ins)


def shape(dims, dtype=LOW):
    return jax.ShapeDtypeStruct(dims, dtype)


def weights_kernel(heads, wq, wo, count, route, oq, oo, counts, far_route, ss, rs):
    place = Place(heads)
    links = Links(ss, rs)
    me = place.image(0, 0, 0)
    place.greet(place.plane_peers + place.z_peers)
    oq[me] = wq[...]
    oo[me, place.z] = wo[...]
    counts[me] = count[...]
    half = wq.shape[1] // 2
    mid = heads // 2
    main = PlaneGather(
        links,
        place,
        lambda i: oq.at[i, :, pl.ds(0, half)],
        lambda i: oq.at[i, :, pl.ds(half, half)],
        lambda i: oq.at[i],
    )
    side = PlaneGather(
        links,
        place,
        lambda i: oo.at[i, pl.ds(0, mid)],
        lambda i: oo.at[i, pl.ds(mid, heads - mid)],
        lambda i: oo.at[i],
    )
    main.start()
    along = all_heads(
        links, place, lambda k, z: (oo.at[me, place.z], oo.at[me, place.z])
    )
    small = [links.send(counts.at[me], counts.at[me], d) for d in place.plane_peers]
    small.append(links.send(route, far_route, place.x_peer))
    main.forward()
    for copy in along:
        copy.wait_recv()
    side.start()
    main.share()
    main.finish()
    side.forward()
    side.share()
    side.finish()
    for copy in small:
        copy.wait_recv()
    links.drain()


def gather_weights_fast(heads, wq, wo, count, route):
    outs = [
        shape((8, *wq.shape)),
        shape((8, heads, *wo.shape)),
        shape((8, *count.shape), jnp.int32),
        shape(route.shape, jnp.int32),
    ]
    copies = 2 * GATHER_COPIES + heads - 1 + 7 + 1
    return remote_call(
        functools.partial(weights_kernel, heads),
        outs,
        [wq, wo, count, route],
        [],
        copies,
        1,
        32,
        20,
    )


def mix_kernel(
    heads,
    experts,
    skip,
    mixed,
    wo,
    tokens,
    gain,
    router,
    near_route,
    far_route,
    down,
    residual,
    second,
    group,
    probs,
    slots,
    arrived,
    everyone,
    other_half,
    ss,
    rs,
):
    place = Place(heads)
    links = Links(ss, rs)
    me = place.image(0, 0, 0)
    place.greet(place.plane_peers + place.z_peers)
    everyone[place.z] = mixed[...]
    along = all_heads(links, place, lambda k, z: (everyone.at[place.z], everyone.at[place.z]))
    local_experts = slots.shape[0] // 2
    ids = place.z * local_experts + lax.broadcasted_iota(jnp.int32, (local_experts, 1), 0)
    first = place.f == 0
    near, far = near_route[...], far_route[...]
    both = [jnp.where(first, near, far), jnp.where(first, far, near)]
    chosen = jnp.concatenate([(r[0:1] == ids) | (r[1:2] == ids) for r in both], 0)
    count = chosen.astype(WIDE)
    before = lax.broadcasted_iota(jnp.int32, (128, 128), 0)
    before = (before < lax.broadcasted_iota(jnp.int32, (128, 128), 1)).astype(LOW)
    running = jnp.zeros((2 * local_experts, 1), WIDE)
    for b in range(slots.shape[1] // 128):
        columns = slice(b * 128, (b + 1) * 128)
        here = count[:, columns]
        slot = dot(here.astype(LOW), before) + running
        slots[:, columns] = jnp.where(chosen[:, columns], slot, -1.0).astype(jnp.int32)
        running = running + jnp.sum(here, -1, keepdims=True)
    for copy in along:
        copy.wait_recv()
    rows_all, width = tokens.shape
    half = width // 2
    total = jnp.zeros((rows_all, width), WIDE)
    for z in range(heads):
        weight = wo[:, z].reshape(width, wo.shape[3])
        total = total + lax.dot_general(
            everyone[z], weight, (((1,), (1,)), ((), ())), preferred_element_type=WIDE
        )
    residual[...] = total

    def norm(rows):
        values = tokens[rows, :].astype(WIDE) + residual[rows, :]
        residual[rows, :] = values
        normed, _ = normalize(values)
        second[rows, :] = (normed * gain[...]).astype(LOW)

    in_rows(rows_all, 64, norm)
    low, high = second[:, :half], second[:, half:]
    group[me] = jnp.where(first, low, high)
    other_half[...] = jnp.where(first, high, low)
    x1 = links.send(other_half, group.at[me], place.x_peer)
    theirs = pl.ds((1 - place.f) * (local_experts // 2) + skip, arrived.shape[0])
    bulk = links.send(down.at[theirs], arrived, place.x_peer)
    y1 = links.send(group.at[me], group.at[me], place.y_peer)
    shared = [links.send(group.at[me], group.at[me], place.core_peer)]
    logits = lax.dot_general(
        router[...], second[...], (((0,), (1,)), ((), ())), preferred_element_type=WIDE
    )[:experts]
    powers = jnp.exp(logits - jnp.max(logits, 0, keepdims=True))
    probs[me] = powers / jnp.sum(powers, 0, keepdims=True)
    small = [links.send(probs.at[me], probs.at[me], d) for d in place.plane_peers]
    across, beside, corner = place.image(1, 0, 0), place.image(0, 1, 0), place.image(1, 1, 0)
    x1.wait_recv()
    y2 = links.send(group.at[across], group.at[across], place.y_peer)
    shared.append(links.send(group.at[across], group.at[across], place.core_peer))
    y1.wait_recv()
    shared.append(links.send(group.at[beside], group.at[beside], place.core_peer))
    y2.wait_recv()
    shared.append(links.send(group.at[corner], group.at[corner], place.core_peer))
    for copy in shared + small + [bulk]:
        copy.wait_recv()
    links.drain()


def mix_heads(
    heads, experts, skip, mixed, wo, tokens, gain, router, near_route, far_route, down
):
    rows, width = tokens.shape
    late = down.shape[0] // 2 - skip
    return remote_call(
        functools.partial(mix_kernel, heads, experts, skip),
        [
            shape((rows, width), WIDE),
            shape((rows, width)),
            shape((8, rows, width // 2)),
            shape((8, experts, rows), WIDE),
            shape((2 * experts // heads, near_route.shape[1]), jnp.int32),
            shape((late, *down.shape[1:])),
        ],
        [mixed, wo, tokens, gain, router, near_route, far_route, down],
        [pltpu.VMEM((heads, *mixed.shape), LOW), pltpu.VMEM((rows, width // 2), LOW)],
        heads - 1 + 7 + 8,
        2,
        48,
        26,
        in_hbm=(7,),
        out_hbm=(5,),
    )


class ChunkSum:
    def __init__(self, links, place, part, columns, core_in, xa, ya, yb, xb):
        self.links, self.place, self.part, self.columns = links, place, part, columns
        self.core_in, self.xa, self.ya, self.yb, self.xb = core_in, xa, ya, yb, xb
        self.rows, self.half = core_in.shape[2], core_in.shape[3] // 2
        self.a, self.b = pl.ds(0, self.half), pl.ds(self.half, self.half)

    def start(self):
        p = self.place
        self.into = self.links.send(
            self.part.at[:, :, 1 - p.c, :, self.columns], self.core_in, p.core_peer
        )

    def cores(self):
        p, rc = self.place, self.core_in
        self.into.wait_recv()

        def add(rows):
            here = self.part[:, :, p.c, rows, self.columns].astype(WIDE)
            rc[:, :, rows, :] = (rc[:, :, rows, :].astype(WIDE) + here).astype(LOW)

        in_rows(self.rows, 32, add)
        self.to_x = self.links.send(rc.at[1 - p.f, :, :, self.a], self.xa, p.x_peer)
        self.to_y = self.links.send(rc.at[:, 1 - p.y, :, self.b], self.yb, p.y_peer)

    def cross(self):
        p, rc, xa, yb = self.place, self.core_in, self.xa, self.yb
        self.to_x.wait_recv()
        y, f = 1 - p.y, 1 - p.f

        def add_a(rows):
            both = xa[y, rows, :].astype(WIDE) + rc[p.f, y, rows, self.a].astype(WIDE)
            xa[y, rows, :] = both.astype(LOW)

        in_rows(self.rows, 64, add_a)
        self.last_a = self.links.send(xa.at[y], self.ya, p.y_peer)
        self.to_y.wait_recv()

        def add_b(rows):
            both = yb[f, rows, :].astype(WIDE) + rc[f, p.y, rows, self.b].astype(WIDE)
            yb[f, rows, :] = both.astype(LOW)

        in_rows(self.rows, 64, add_b)
        self.last_b = self.links.send(yb.at[f], self.xb, p.x_peer)

    def finish(self, take):
        p, rc = self.place, self.core_in
        self.last_a.wait_recv()
        self.last_b.wait_recv()

        def add(rows):
            first = rc[p.f, p.y, rows, self.a].astype(WIDE) + self.xa[p.y, rows, :].astype(WIDE)
            second = rc[p.f, p.y, rows, self.b].astype(WIDE) + self.yb[p.f, rows, :].astype(WIDE)
            take(rows, 0, first + self.ya[rows, :].astype(WIDE))
            take(rows, 1, second + self.xb[rows, :].astype(WIDE))

        in_rows(self.rows, 64, add)


def skewed(chunks, stages):
    for step in range(chunks + len(stages) - 1):
        for k in range(chunks):
            if 0 <= step - k < len(stages):
                stages[step - k](k)


def combine_kernel(
    heads,
    chunks,
    part,
    residual,
    teacher,
    valid,
    scale,
    result,
    final_grad,
    group,
    loss,
    core_in,
    xa,
    ya,
    yb,
    xb,
    image_sum,
    far,
    ss,
    rs,
):
    place = Place(heads)
    links = Links(ss, rs)
    me = place.image(0, 0, 0)
    z = place.z
    place.greet(place.axis_peers() + place.z_peers)
    rows_all, width = residual.shape
    own = rows_all // heads
    wide = width // chunks
    half = wide // 2
    mine = pl.ds(pl.multiple_of(z * own, own), own)
    columns = [pl.ds(k * wide, wide) for k in range(chunks)]
    adders = [
        ChunkSum(
            links,
            place,
            part,
            columns[k],
            core_in.at[k],
            xa.at[k],
            ya.at[k],
            yb.at[k],
            xb.at[k],
        )
        for k in range(chunks)
    ]
    for adder in adders:
        adder.start()
    along, spread, squares = {}, {}, []
    gathers = [
        PlaneGather(
            links,
            place,
            lambda i, k=k: group.at[i, :, pl.ds(k * wide, half)],
            lambda i, k=k: group.at[i, :, pl.ds(k * wide + half, half)],
            lambda i, k=k: group.at[i, :, columns[k]],
        )
        for k in range(chunks)
    ]

    def to_heads(k):
        def keep(rows, part_of, values):
            image_sum[k, rows, pl.ds(part_of * half, half)] = values.astype(LOW)

        adders[k].finish(keep)
        along[k] = all_heads(
            links,
            place,
            lambda n, to: (
                image_sum.at[k, pl.ds(pl.multiple_of(to * own, own), own)],
                far.at[k, n],
            ),
        )

    def final(k):
        for copy in along[k]:
            copy.wait_recv()
        total = image_sum[k, mine, :].astype(WIDE)
        for n in range(heads - 1):
            total = total + far[k, n].astype(WIDE)
        values = residual[mine, columns[k]] + total
        result[z, :, columns[k]] = values.astype(LOW)
        error = (values - teacher[mine, columns[k]].astype(WIDE)) * valid[mine, :]
        grad = error * scale[0:1, 0:1]
        final_grad[:, columns[k]] = grad
        group[me, mine, columns[k]] = grad.astype(LOW)
        block = group.at[me, mine, columns[k]]
        spread[k] = all_heads(links, place, lambda n, to: (block, block))
        square = jnp.sum((error * error).reshape(own // 8, 8, wide), axis=0)
        squares.extend(square[:, i * 128 : (i + 1) * 128] for i in range(wide // 128))

    def to_plane(k):
        for copy in spread[k]:
            copy.wait_recv()
        gathers[k].start()

    def forward(k):
        gathers[k].forward()
        gathers[k].share()

    skewed(
        chunks,
        [
            lambda k: adders[k].cores(),
            lambda k: adders[k].cross(),
            to_heads,
            final,
            to_plane,
            forward,
        ],
    )
    loss[z] = sum(squares)
    extra = all_heads(links, place, lambda k, to: (result.at[z], result.at[z]))
    extra += all_heads(links, place, lambda k, to: (loss.at[z], loss.at[z]))
    for gather in gathers:
        gather.finish()
    for copy in extra:
        copy.wait_recv()
    links.drain()


def combine(heads, part, residual, teacher, valid, scale):
    rows, width = residual.shape
    own = rows // heads
    chunks = width // 256
    return remote_call(
        functools.partial(combine_kernel, heads, chunks),
        [
            shape((heads, own, width)),
            shape((own, width), WIDE),
            shape((8, rows, width)),
            shape((heads, 8, 128), WIDE),
        ],
        [part, residual, teacher, valid, scale],
        [
            pltpu.VMEM((chunks, 2, 2, rows, 256), LOW),
            pltpu.VMEM((chunks, 2, rows, 128), LOW),
            pltpu.VMEM((chunks, rows, 128), LOW),
            pltpu.VMEM((chunks, 2, rows, 128), LOW),
            pltpu.VMEM((chunks, rows, 128), LOW),
            pltpu.VMEM((chunks, rows, 256), LOW),
            pltpu.VMEM((chunks, heads - 1, own, 256), LOW),
        ],
        chunks * (5 + GATHER_COPIES + 2 * (heads - 1)) + 2 * (heads - 1),
        3,
        28,
        50,
    )


def back_kernel(
    heads,
    chunks,
    part,
    gates_a,
    gates_b,
    residual,
    gain,
    router,
    probs,
    final_grad,
    attended,
    logit_grads,
    residual_grad,
    gain_part,
    core_in,
    y_in,
    far,
    pair,
    x_in,
    gate_own,
    gate_in,
    gate_sum,
    gate_all,
    logit_rows,
    ss,
    rs,
):
    place = Place(heads)
    links = Links(ss, rs)
    f, y, z = place.f, place.y, place.z
    t = 2 * y + place.c
    tensor_peers = [{TENSOR: lax.rem(t + k, 4)} for k in range(1, 4)]
    owners = [
        {FSDP: 1 - f if a else f, HEADS: lax.rem(z + k, heads)}
        for k in range(heads)
        for a in range(2)
        if a or k
    ]
    place.greet(tensor_peers + owners)
    rows_all, width = residual.shape
    half = width // 2
    own = rows_all // heads
    into, beside, along, cross = {}, {}, {}, {}
    for k in range(chunks):
        source = part.at[:, :, 1 - place.c, :, pl.ds(k * 128, 128)]
        into[k] = links.send(source, core_in.at[k], place.core_peer)
    cut = gates_a.shape[1]
    gate_own[:, :cut] = gates_a[...]
    gate_own[:, cut:] = gates_b[...]
    gate_in[t] = gate_own[...]
    shared = [links.send(gate_own, gate_in.at[t], d) for d in tensor_peers]
    mine = pl.ds(pl.multiple_of(z * own, own), own)

    def to_y(k):
        into[k].wait_recv()
        rc = core_in.at[k]

        def add(rows):
            here = part[:, :, place.c, rows, pl.ds(k * 128, 128)].astype(WIDE)
            rc[:, :, rows, :] = (rc[:, :, rows, :].astype(WIDE) + here).astype(LOW)

        in_rows(rows_all, 32, add)
        beside[k] = links.send(rc.at[:, 1 - y], y_in.at[k], place.y_peer)

    def to_heads(k):
        beside[k].wait_recv()

        def add(rows):
            both = y_in[k, :, rows, :].astype(WIDE) + core_in[k, :, y, rows, :].astype(WIDE)
            y_in[k, :, rows, :] = both.astype(LOW)

        in_rows(rows_all, 64, add)
        along[k] = all_heads(
            links,
            place,
            lambda n, to: (
                y_in.at[k, :, pl.ds(pl.multiple_of(to * own, own), own)],
                far.at[k, n],
            ),
        )

    def to_x(k):
        for copy in along[k]:
            copy.wait_recv()
        total = y_in[k, :, mine, :].astype(WIDE)
        for n in range(heads - 1):
            total = total + far[k, n].astype(WIDE)
        pair[k] = total.astype(LOW)
        cross[k] = links.send(pair.at[k, 1 - f], x_in.at[k], place.x_peer)

    to_y(0)
    for copy in shared:
        copy.wait_recv()
    gate_sum[...] = sum(gate_in[k] for k in range(4))
    kept = gate_sum.shape[1]
    rows_of = pl.ds(pl.multiple_of(t * rows_all, rows_all), rows_all)
    gate_all[z, f] = gate_sum[f, :, rows_of]
    spread = [
        links.send(gate_sum.at[d[FSDP], :, rows_of], gate_all.at[z, f], d) for d in owners
    ]
    to_y(1)
    to_heads(0)
    for k in range(2, chunks):
        to_y(k)
        to_heads(k - 1)
        to_x(k - 2)
    for copy in spread:
        copy.wait_recv()
    chances = probs[...]
    prob_grad = gate_all[...].reshape(2 * heads * kept, rows_all)
    logit_grad = chances * (prob_grad - jnp.sum(chances * prob_grad, 0, keepdims=True))
    logit_grads[...] = logit_grad.astype(LOW)
    logit_rows[...] = dot(logit_grads[...], router[...], (0, 0))
    normed, spread_two = normalize(residual[mine, :])
    to_heads(chunks - 1)
    to_x(chunks - 2)
    to_x(chunks - 1)
    near = jnp.concatenate([pair[k, f].astype(WIDE) for k in range(chunks)], 1)
    for k in range(chunks):
        cross[k].wait_recv()
    away = jnp.concatenate([x_in[k].astype(WIDE) for k in range(chunks)], 1)
    first = f == 0
    rows_grad = jnp.concatenate([jnp.where(first, near, away), jnp.where(first, away, near)], 1)
    second_grad = rows_grad + logit_rows[mine, :]
    weighted = second_grad * gain[...]
    gain_part[...] = jnp.sum((second_grad * normed).reshape(own // 8, 8, width), axis=0)
    inner = (
        weighted
        - jnp.mean(weighted, -1, keepdims=True)
        - normed * jnp.mean(weighted * normed, -1, keepdims=True)
    )
    total_grad = final_grad[...] + inner * spread_two
    residual_grad[...] = total_grad
    attended[z] = total_grad.astype(LOW)
    for copy in all_heads(links, place, lambda k, to: (attended.at[z], attended.at[z])):
        copy.wait_recv()
    links.drain()


def back_through_norm(heads, part, gates_a, gates_b, residual, gain, router, probs, final_grad):
    rows, width = residual.shape
    own = rows // heads
    chunks = width // 256
    kept = gates_a.shape[1] + gates_b.shape[1]
    group_rows = gates_a.shape[2]
    return remote_call(
        functools.partial(back_kernel, heads, chunks),
        [
            shape((heads, own, width)),
            shape(probs.shape),
            shape((own, width), WIDE),
            shape((8, width), WIDE),
        ],
        [part, gates_a, gates_b, residual, gain, router, probs, final_grad],
        [
            pltpu.VMEM((chunks, 2, 2, rows, 128), LOW),
            pltpu.VMEM((chunks, 2, rows, 128), LOW),
            pltpu.VMEM((chunks, heads - 1, 2, own, 128), LOW),
            pltpu.VMEM((chunks, 2, own, 128), LOW),
            pltpu.VMEM((chunks, own, 128), LOW),
            pltpu.VMEM((2, kept, group_rows), WIDE),
            pltpu.VMEM((4, 2, kept, group_rows), WIDE),
            pltpu.VMEM((2, kept, group_rows), WIDE),
            pltpu.VMEM((heads, 2, kept, rows), WIDE),
            pltpu.VMEM((rows, width), WIDE),
        ],
        chunks * (3 + heads - 1) + 3 + 2 * heads - 1 + heads - 1,
        4,
        20,
        40,
    )


def last_kernel(
    heads,
    first_part,
    dense,
    tokens,
    gain,
    residual_grad,
    gain_parts,
    tokens_grad,
    dense_out,
    gain_out,
    core_in,
    xa,
    ya,
    yb,
    xb,
    far,
    rounded,
    tiles,
    tiles_z,
    ss,
    rs,
):
    place = Place(heads)
    links = Links(ss, rs)
    z = place.z
    me = place.image(0, 0, 0)
    place.greet(place.plane_peers + place.z_peers)
    own, width = residual_grad.shape
    adder = PlaneSum(links, place, dense, core_in, xa, ya, yb, xb, xa.shape[2], 32)
    adder.start()
    along = all_heads(links, place, lambda k, to: (first_part.at[to], far.at[k]))
    tiles[me] = gain_parts[me]
    small = []
    for device in place.plane_peers:
        to = (device[FSDP] if FSDP in device else place.f) * 4 + device[TENSOR]
        small.append(links.send(gain_parts.at[to], tiles.at[me], device))
    adder.cores()
    adder.cross()
    for copy in small:
        copy.wait_recv()
    tiles_z[z] = sum(tiles[i] for i in range(8))
    gains = all_heads(links, place, lambda k, to: (tiles_z.at[z], tiles_z.at[z]))
    mine = pl.ds(pl.multiple_of(z * own, own), own)
    normed, spread = normalize(tokens[mine, :].astype(WIDE))
    for copy in along:
        copy.wait_recv()
    first_grad = first_part[z].astype(WIDE)
    for k in range(heads - 1):
        first_grad = first_grad + far[k].astype(WIDE)
    weighted = first_grad * gain[...]
    inner = (
        weighted
        - jnp.mean(weighted, -1, keepdims=True)
        - normed * jnp.mean(weighted * normed, -1, keepdims=True)
    )
    rounded[z] = (residual_grad[...] + inner * spread).astype(LOW)
    along = all_heads(links, place, lambda k, to: (rounded.at[z], rounded.at[z]))

    def keep(rows, columns, values):
        dense_out[rows, columns] = values

    adder.finish(keep)
    for copy in gains:
        copy.wait_recv()
    gain_out[...] = sum(tiles_z[i] for i in range(heads))
    for copy in along:
        copy.wait_recv()
    for i in range(heads):
        tokens_grad[i] = rounded[i].astype(WIDE)
    links.drain()


def last_sums(heads, first_part, dense, tokens, gain, residual_grad, gain_parts):
    own, width = residual_grad.shape
    _, rows, wide = dense.shape
    cut = 512 if wide == 896 else 128 * (wide // 256)
    return remote_call(
        functools.partial(last_kernel, heads),
        [
            shape((heads, own, width), WIDE),
            shape((rows, wide), WIDE),
            shape((8, 128), WIDE),
        ],
        [first_part, dense, tokens, gain, residual_grad, gain_parts],
        [
            *sum_scratch(rows, wide, cut),
            pltpu.VMEM((heads - 1, own, width), LOW),
            pltpu.VMEM((heads, own, width), LOW),
            pltpu.VMEM((8, 8, 128), WIDE),
            pltpu.VMEM((heads, 8, 128), WIDE),
        ],
        SUM_COPIES + 3 * (heads - 1) + 7,
        5,
        48,
        25,
    )


def local_call(
    kernel, grid, scalars, ins, outs, scratch=(), vmem_mib=28, aliases=None, microseconds=5
):
    def spec(array, block, index):
        if block is None:
            dims = array.shape
            return pl.BlockSpec(dims, lambda i, s, n=len(dims): (0,) * n)
        if block is pl.ANY:
            return pl.BlockSpec(memory_space=pl.ANY)
        return pl.BlockSpec(block, index)

    return pl.pallas_call(
        kernel,
        out_shape=[o[0] for o in outs],
        grid_spec=pltpu.PrefetchScalarGridSpec(
            num_scalar_prefetch=1,
            grid=(grid,),
            in_specs=[spec(*a) for a in ins],
            out_specs=[spec(*o) for o in outs],
            scratch_shapes=list(scratch),
        ),
        input_output_aliases=aliases or {},
        compiler_params=pltpu.CompilerParams(vmem_limit_bytes=vmem_mib * 2**20),
        cost_estimate=spends(microseconds),
    )(scalars, *[a[0] for a in ins])


def per_expert(dims, skip=0):
    return (1, *dims), lambda i, s: (i + skip, 0, 0)


def held_expert(dims, which, skip=0):
    return (1, *dims), lambda i, s: (s[which] + i + skip, 0, 0)


def slot_block(dims, skip=0):
    return (2, *dims), lambda i, s: (0, i + skip, 0)


def dot(a, b, over=(1, 0)):
    return lax.dot_general(a, b, (((over[0],), (over[1],)), ((), ())), preferred_element_type=WIDE)


def one_hot(slots, row, capacity):
    places = lax.broadcasted_iota(jnp.int32, (capacity, slots.shape[1]), 0)
    return places == slots[pl.ds(row, 1), :]


def far_up_kernel(skip, s, slots, x, up, pick, buffer, away):
    i, local_experts = pl.program_id(0) + skip, slots.shape[0] // 2
    capacity = pick.shape[1]
    for g in range(2):
        hot = one_hot(slots, g * local_experts + s[1] + i, capacity).astype(LOW)
        pick[g] = hot
        buffer[0, pl.ds(g * capacity, capacity), :] = dot(hot, x[g]).astype(LOW)
    away[0] = dot(buffer[0], up[0]).astype(LOW)


def near_up_kernel(s, slots, x, up, probs, pick, buffer, own, gates):
    i, local_experts = pl.program_id(0), slots.shape[0] // 2
    capacity = pick.shape[1]
    expert = s[3] + i
    for g in range(2):
        hot = one_hot(slots, g * local_experts + s[0] + i, capacity)
        chances = jnp.concatenate([probs[4 * g + k, pl.ds(expert, 1), :] for k in range(4)], 1)
        rows = pl.ds(g * capacity, capacity)
        gates[0, rows, :] = jnp.sum(jnp.where(hot, chances, 0.0), -1, keepdims=True)
        pick[g] = hot.astype(LOW)
        buffer[0, rows, :] = dot(hot.astype(LOW), x[g]).astype(LOW)
    own[0] = dot(buffer[0], up[0])


def down_kernel(last, s, own, arrived, gates, near, far, *refs):
    if last:
        before, pick, hidden, slope, part, weighted = refs
    else:
        hidden, slope, weighted = refs
    i = pl.program_id(0)
    half = near.shape[2]
    capacity = own.shape[1] // 2
    values = own[0] + arrived[0].astype(WIDE)
    cdf = 0.5 * (1.0 + lax.erf(values * ROOT_HALF))
    hidden[0] = (values * cdf).astype(LOW)
    slope[0] = cdf + values * DENSITY * jnp.exp(-0.5 * values * values)
    for weight, f in ((near, s[2]), (far, 1 - s[2])):
        out = (dot(hidden[0], weight[0]) * gates[0]).astype(LOW)
        columns = pl.ds(pl.multiple_of(f * half, half), half)
        for g in range(2):
            rows = pl.ds(pl.multiple_of(i * capacity, capacity), capacity)
            weighted[g, rows, columns] = out[g * capacity : (g + 1) * capacity]

    if last:

        @pl.when(i == pl.num_programs(0) - 1)
        def _():
            cut = before.shape[1]
            for g in range(2):
                total = dot(pick[g, :cut], before[g], (0, 0))
                part[g] = (total + dot(pick[g, cut:], weighted[g], (0, 0))).astype(LOW)


def hidden_back_kernel(
    s, pick, grads, near, far, hidden, slope, gates, pre, out_grad, gate_rows, rows
):
    i = pl.program_id(0)
    half = near.shape[2]
    capacity = pick.shape[1]
    for g in range(2):
        rows[pl.ds(g * capacity, capacity), :] = dot(pick[g], grads[g]).astype(LOW)
    first = pl.ds(pl.multiple_of(s[2] * half, half), half)
    second = pl.ds(pl.multiple_of((1 - s[2]) * half, half), half)
    raw = dot(rows[:, first], near[0], (1, 1)) + dot(rows[:, second], far[0], (1, 1))
    pre[0] = (raw * gates[0] * slope[0]).astype(LOW)
    out_grad[0] = (rows[...].astype(WIDE) * gates[0]).astype(LOW)
    gate_grad = jnp.sum(raw * hidden[0].astype(WIDE), -1, keepdims=True)
    for g in range(2):
        terms = gate_grad[g * capacity : (g + 1) * capacity] * pick[g].astype(WIDE)
        gate_rows[g, pl.ds(i, 1), :] = jnp.sum(terms, 0, keepdims=True)


def down_grad_kernel(s, hidden, out_grad, *refs):
    kept_grad, sent_grad = refs[-2:]
    half = kept_grad.shape[2]
    first = pl.ds(pl.multiple_of(s[2] * half, half), half)
    second = pl.ds(pl.multiple_of((1 - s[2]) * half, half), half)
    kept_grad[0] = dot(hidden[0], out_grad[0, :, first], (0, 0))
    sent_grad[0] = dot(hidden[0], out_grad[0, :, second], (0, 0)).astype(LOW)


def up_back_kernel(s, buffer, pre, up, *refs):
    grad, rows_out = refs[-2:]
    capacity = rows_out.shape[1]
    grad[0] = dot(buffer[0], pre[0], (0, 0))
    back = dot(pre[0], up[0], (1, 1)).astype(LOW)
    for g in range(2):
        rows_out[g] = back[g * capacity : (g + 1) * capacity]


def far_up_last_kernel(s, buffer, pre, up, rows_near, before, pick_near, pick_far, held, grad, part, rows_far):
    i = pl.program_id(0)
    capacity = buffer.shape[1] // 2
    grad[0] = dot(buffer[0], pre[0], (0, 0))
    back = dot(pre[0], up[0], (1, 1)).astype(LOW)
    for g in range(2):
        rows = pl.ds(pl.multiple_of(i * capacity, capacity), capacity)
        rows_far[g, rows, :] = back[g * capacity : (g + 1) * capacity]

    @pl.when(i == pl.num_programs(0) - 1)
    def _():
        cut = before.shape[1]
        for g in range(2):
            near = dot(pick_near[g], rows_near[g], (0, 0))
            far = dot(pick_far[g, :cut], before[g], (0, 0))
            far = far + dot(pick_far[g, cut:], rows_far[g], (0, 0))
            part[g] = (near + far).astype(LOW)


def widen_kernel(s, arrived, held, grad):
    grad[0] = arrived[0].astype(WIDE)


def swap(values):
    return lax.ppermute(values, FSDP, [(0, 1), (1, 0)])


def fast(
    tokens,
    valid_mask,
    routes,
    teacher,
    gain_one,
    qkv_weight,
    out_weight,
    gain_two,
    router_weight,
    expert_up,
    expert_down,
):
    heads = lax.axis_size(HEADS)
    f, z = lax.axis_index(FSDP), lax.axis_index(HEADS)
    _, rows, width = tokens.shape
    block, head_count, qkv_dim = qkv_weight.shape
    head_dim = qkv_dim // 3
    local_experts = expert_up.shape[0]
    kept = local_experts // 2
    expert_count = local_experts * heads
    group_rows = 4 * rows
    capacity = 2 * routes.shape[2] * group_rows // expert_count
    total_tokens, total_images = 8 * rows, 8
    score_scale = head_dim ** (-0.5)

    mine, theirs = f * kept, (1 - f) * kept
    half = width // 2
    first_chunk, second_chunk = kept // 4, kept // 2
    down_a = lax.dynamic_slice_in_dim(expert_down, theirs, first_chunk, 0)
    down_a, qkv_weight = lax.optimization_barrier((down_a, qkv_weight))
    down_a = swap(down_a)

    qkv_width = head_count * qkv_dim
    pad = -(128 + qkv_width) % 256
    wq = jnp.concatenate(
        [
            router_weight,
            gain_one[:, None],
            gain_two[:, None],
            jnp.zeros((block, 128 - expert_count - 2), LOW),
            qkv_weight.reshape(block, qkv_width),
            jnp.zeros((block, pad), LOW),
        ],
        1,
    )
    wo = out_weight.reshape(head_count * head_dim, block).T
    count = jnp.full((8, 128), jnp.sum(valid_mask), jnp.int32)
    near_route = jnp.pad(routes.reshape(group_rows, -1).T, ((0, 8 - routes.shape[2]), (0, 0)))
    count, down_a = lax.optimization_barrier((count, down_a))
    gathered, wo_all, counts, far_route = gather_weights_fast(heads, wq, wo, count, near_route)
    gathered, down_b = lax.optimization_barrier(
        (gathered, lax.dynamic_slice_in_dim(expert_down, theirs + first_chunk, second_chunk, 0))
    )
    down_b = swap(down_b)
    gathered = gathered.reshape(width, -1)
    qkv_full = gathered[:, 128 : 128 + qkv_width]
    lanes = jnp.arange(128)
    router_wide = jnp.where(lanes < expert_count, gathered[:, :128], 0)
    gain_a = gathered[:, expert_count].astype(WIDE)[None]
    gain_b = gathered[:, expert_count + 1].astype(WIDE)[None]
    valid_total = jnp.sum(counts[:, 0, 0]).astype(WIDE)

    inputs = tokens[0].astype(WIDE)
    normed_one, _ = normalize(inputs)
    first_in = (normed_one * gain_a).astype(LOW)
    projected = (
        jnp.dot(first_in, qkv_full, preferred_element_type=WIDE)
        .astype(LOW)
        .reshape(rows, head_count, qkv_dim)
    )
    queries = projected[..., :head_dim]
    key_rows = projected[..., head_dim : 2 * head_dim]
    values = projected[..., 2 * head_dim :]
    keys_ok = (valid_mask > 0)[0][None, None, :]

    def scores_now():
        raw = jnp.einsum("qhe,khe->hqk", queries, key_rows, preferred_element_type=WIDE)
        return jnp.where(keys_ok, raw * score_scale, MASKED)

    scores = scores_now()
    peak_score = jnp.max(scores, -1, keepdims=True)
    exp_scores = jnp.exp(scores - peak_score)
    score_total = jnp.sum(exp_scores, -1, keepdims=True)
    logarithm_total = peak_score + jnp.log(score_total)
    attention = (exp_scores / score_total).astype(LOW)
    mixed = (
        jnp.einsum("hqk,khe->qhe", attention, values, preferred_element_type=WIDE)
        .astype(LOW)
        .reshape(rows, head_count * head_dim)
    )
    residual, second_in, group_in, probs_all, slots, down_c = mix_heads(
        heads,
        expert_count,
        first_chunk + second_chunk,
        mixed,
        wo_all,
        tokens[0],
        gain_b,
        router_wide,
        near_route,
        far_route,
        expert_down,
    )
    group_in, down_b = lax.optimization_barrier((group_in, down_b))

    hidden_width = expert_up.shape[2]
    pair = 2 * capacity
    scalars = jnp.stack([mine, theirs, f, z * local_experts + mine]).astype(jnp.int32)
    rows_in = group_in.reshape(2, group_rows, half)
    a_pick = shape((2, kept * capacity, group_rows)), *slot_block((capacity, group_rows))
    a_buffer = shape((kept, pair, half)), *per_expert((pair, half))
    near_up = expert_up, *held_expert((half, hidden_width), 0)
    part_size = kept // 2
    a_hidden = per_expert((pair, hidden_width))
    halves = (0, part_size)
    picks_far, buffers_far, arrived = [], [], []
    for skip in halves:
        pick, buffer, away = local_call(
            functools.partial(far_up_kernel, skip),
            part_size,
            scalars,
            [
                (slots, None, None),
                (rows_in, None, None),
                (expert_up, *held_expert((half, hidden_width), 1, skip)),
            ],
            [
                (
                    shape((2, part_size * capacity, group_rows)),
                    *slot_block((capacity, group_rows)),
                ),
                (shape((part_size, pair, half)), *per_expert((pair, half))),
                (shape((part_size, pair, hidden_width)), *a_hidden),
            ],
        )
        away, scalars = lax.optimization_barrier((away, scalars))
        picks_far.append(pick)
        buffers_far.append(buffer)
        arrived.append(swap(away))
    down_far = jnp.concatenate([down_a, down_b, down_c], 0)
    pick_near, buffer_near, own, gates = local_call(
        near_up_kernel,
        kept,
        scalars,
        [(slots, None, None), (rows_in, None, None), near_up, (probs_all, None, None)],
        [
            a_pick,
            a_buffer,
            (shape((kept, pair, hidden_width), WIDE), *per_expert((pair, hidden_width))),
            (shape((kept, pair, 1), WIDE), *per_expert((pair, 1))),
        ],
    )
    hiddens, slopes, weighted = [], [], []
    for n, skip in enumerate(halves):
        ins = [
            (own, *per_expert((pair, hidden_width), skip)),
            (arrived[n], *a_hidden),
            (gates, *per_expert((pair, 1), skip)),
            (expert_down, *held_expert((hidden_width, half), 0, skip)),
            (down_far, *per_expert((hidden_width, half), skip)),
        ]
        outs = [
            (shape((part_size, pair, hidden_width)), *a_hidden),
            (shape((part_size, pair, hidden_width), WIDE), *a_hidden),
        ]
        rows_shape = (2, part_size * capacity, width)
        last = n == 1
        if last:
            ins += [(weighted[0], None, None), (pick_near, None, None)]
            outs.append((shape((2, group_rows, width)), None, None))
        else:
            outs.append((shape(rows_shape), None, None))
        scratch = [pltpu.VMEM(rows_shape, LOW)] if last else []
        hidden, slope, out = local_call(
            functools.partial(down_kernel, last), part_size, scalars, ins, outs, scratch
        )
        hiddens.append(hidden)
        slopes.append(slope)
        weighted.append(out)
    part = weighted[1]
    me = f * 4 + lax.axis_index(TENSOR)
    probs_own = lax.dynamic_index_in_dim(probs_all, me, 0, False)

    valid_rows = valid_mask[0].astype(WIDE)[:, None]
    scale = jnp.full((8, 128), total_tokens / valid_total, WIDE)
    result, final_grad, group_grad, loss = combine(
        heads, part.reshape(2, 2, 2, rows, width), residual, teacher[0], valid_rows, scale
    )
    loss_terms = (jnp.sum(loss) * (total_images / (valid_total * width)))[None]

    grads_in = group_grad.reshape(2, group_rows, width)
    pres_near, pres_far, out_grads, extras = [], [], [], []
    for n, skip in enumerate(halves):
        pre, out_grad, extra = local_call(
            hidden_back_kernel,
            part_size,
            scalars,
            [
                (pick_near, *slot_block((capacity, group_rows), skip)),
                (grads_in, None, None),
                (expert_down, *held_expert((hidden_width, half), 0, skip)),
                (down_far, *per_expert((hidden_width, half), skip)),
                (hiddens[n], *a_hidden),
                (slopes[n], *a_hidden),
                (gates, *per_expert((pair, 1), skip)),
            ],
            [
                (shape((part_size, pair, hidden_width)), *a_hidden),
                (shape((part_size, pair, width)), *per_expert((pair, width))),
                (shape((2, part_size, group_rows), WIDE), None, None),
            ],
            [pltpu.VMEM((pair, width), LOW)],
        )
        pre, scalars = lax.optimization_barrier((pre, scalars))
        pres_near.append(pre)
        pres_far.append(swap(pre))
        out_grads.append(out_grad)
        extras.append(extra)
    down_shape = shape(expert_down.shape, WIDE)
    up_shape = shape(expert_up.shape, WIDE)
    down_grad, sends = None, []
    pieces = ((0, 0, part_size), (1, 0, part_size - 1), (1, part_size - 1, 1))
    for n, skip, size in pieces:
        ins = [
            (hiddens[n], *per_expert((pair, hidden_width), skip)),
            (out_grads[n], *per_expert((pair, width), skip)),
        ]
        if sends:
            ins.append((down_grad, pl.ANY, None))
        first = n * part_size + skip
        down_grad, send = local_call(
            down_grad_kernel,
            size,
            scalars,
            ins,
            [
                (down_shape, *held_expert((hidden_width, half), 0, first)),
                (shape((size, hidden_width, half)), *per_expert((hidden_width, half))),
            ],
            aliases={3: 0} if sends else None,
            microseconds=2 * size,
        )
        sends.append(send)
    down_others = [swap(send) for send in sends[:2]]
    up_grad, rows_near = None, []
    for n, skip in enumerate(halves):
        ins = [
            (buffer_near, *per_expert((pair, half), skip)),
            (pres_near[n], *a_hidden),
            (expert_up, *held_expert((half, hidden_width), 0, skip)),
        ]
        if n:
            ins.append((up_grad, pl.ANY, None))
        up_grad, out = local_call(
            up_back_kernel,
            part_size,
            scalars,
            ins,
            [
                (up_shape, *held_expert((half, hidden_width), 0, skip)),
                (shape((2, part_size * capacity, half)), *slot_block((capacity, half))),
            ],
            aliases={4: 0} if n else None,
        )
        rows_near.append(out)
    rows_near = jnp.concatenate(rows_near, 1)

    def far_ins(n, skip):
        return [
            (buffers_far[n], *per_expert((pair, half))),
            (pres_far[n], *a_hidden),
            (expert_up, *held_expert((half, hidden_width), 1, skip)),
        ]

    up_grad, rows_far = local_call(
        up_back_kernel,
        part_size,
        scalars,
        [*far_ins(0, 0), (up_grad, pl.ANY, None)],
        [
            (up_shape, *held_expert((half, hidden_width), 1)),
            (shape((2, part_size * capacity, half)), *slot_block((capacity, half))),
        ],
        aliases={4: 0},
    )
    up_grad, back_part = local_call(
        far_up_last_kernel,
        part_size,
        scalars,
        [
            *far_ins(1, part_size),
            (rows_near, None, None),
            (rows_far, None, None),
            (pick_near, None, None),
            (jnp.concatenate(picks_far, 1), None, None),
            (up_grad, pl.ANY, None),
        ],
        [
            (up_shape, *held_expert((half, hidden_width), 1, part_size)),
            (shape((2, group_rows, half)), None, None),
        ],
        [pltpu.VMEM((2, part_size * capacity, half), LOW)],
        aliases={8: 0},
    )
    back_part = back_part.reshape(2, 2, 2, rows, half)

    attended, logit_grads, residual_grad, gain_two_part = back_through_norm(
        heads,
        back_part,
        extras[0],
        extras[1],
        residual,
        gain_b,
        router_wide[:, :expert_count].T,
        probs_own,
        final_grad,
    )

    attended, last_send = lax.optimization_barrier((attended, sends[2]))
    down_others.append(swap(last_send))
    attended_grad = attended.reshape(rows, width)
    wo_own = lax.dynamic_index_in_dim(wo_all, z, 1, False).reshape(width, -1)
    mixed_grad = (
        jnp.dot(attended_grad, wo_own, preferred_element_type=WIDE)
        .astype(LOW)
        .reshape(rows, head_count, head_dim)
    )
    scores = scores_now()
    probs = jnp.exp(scores - logarithm_total)
    prob_part = jnp.einsum("qhe,khe->hqk", mixed_grad, values, preferred_element_type=WIDE)
    score_grad = (probs * (prob_part - jnp.sum(probs * prob_part, -1, keepdims=True))).astype(LOW)
    query_grad = (
        jnp.einsum("hqk,khe->qhe", score_grad, key_rows, preferred_element_type=WIDE) * score_scale
    )
    key_grad = (
        jnp.einsum("hqk,qhe->khe", score_grad, queries, preferred_element_type=WIDE) * score_scale
    )
    value_grad = jnp.einsum(
        "hqk,qhe->khe", probs.astype(LOW), mixed_grad, preferred_element_type=WIDE
    )
    projected_grad = (
        jnp.concatenate([query_grad, key_grad, value_grad], -1)
        .astype(LOW)
        .reshape(rows, qkv_width)
    )
    first_part = lax.dot_general(
        projected_grad, qkv_full, (((1,), (1,)), ((), ())), preferred_element_type=WIDE
    )
    gain_one_part = jnp.sum(first_part * normed_one, 0)
    qkv_grad = jnp.einsum("sd,se->de", first_in, projected_grad, preferred_element_type=WIDE)
    out_grad_t = jnp.einsum("sd,se->de", attended_grad, mixed, preferred_element_type=WIDE)
    router_grad = dot(second_in, logit_grads, (0, 1))
    spare = jnp.zeros((width, -(qkv_width + out_grad_t.shape[1] + expert_count) % 128), WIDE)
    dense = jnp.concatenate([qkv_grad, out_grad_t, router_grad, spare], 1).astype(LOW)
    gain_parts = jnp.stack([gain_one_part, jnp.sum(gain_two_part, 0)], 0).reshape(2, 8, block)
    gain_parts = jnp.pad(jnp.swapaxes(gain_parts, 0, 1), ((0, 0), (0, 6), (0, 128 - block)))
    tokens_grad, dense_out, gain_out = last_sums(
        heads,
        first_part.astype(LOW).reshape(heads, rows // heads, width),
        dense.reshape(8, block, -1),
        tokens[0],
        gain_a,
        residual_grad,
        gain_parts,
    )
    for arrived, (n, skip, size) in zip(down_others, pieces):
        (down_grad,) = local_call(
            widen_kernel,
            size,
            scalars,
            [(arrived, *per_expert((hidden_width, half))), (down_grad, pl.ANY, None)],
            [(down_shape, *held_expert((hidden_width, half), 1, n * part_size + skip))],
            aliases={2: 0},
            microseconds=2 * size,
        )
    out_width = head_count * head_dim
    return (
        result.reshape(1, rows, width),
        loss_terms,
        tokens_grad.reshape(1, rows, width),
        gain_out[0, :block],
        dense_out[:, :qkv_width].reshape(block, head_count, qkv_dim),
        dense_out[:, qkv_width : qkv_width + out_width].T.reshape(head_count, head_dim, block),
        gain_out[1, :block],
        dense_out[:, qkv_width + out_width : qkv_width + out_width + expert_count],
        up_grad,
        down_grad,
    )


def local(sizes, *args):
    tokens, routes, up = args[0], args[2], args[9]
    fits = (
        sizes[FSDP] == 2
        and sizes[TENSOR] == 4
        and sizes[HEADS] % 2 == 0
        and tokens.shape[0] == 1
        and up.shape[0] % 8 == 0
        and tokens.shape[1] % (32 * sizes[HEADS]) == 0
        and tokens.shape[2] % 256 == 0
        and routes.shape[2] <= 8
        and up.shape[0] * sizes[HEADS] <= 126
    )
    return fast(*args) if fits else general(*args)


def solution(mesh):
    sizes = dict(mesh.shape)
    program = functools.partial(local, sizes)
    in_specs = (
        P((FSDP, TENSOR), None, None),
        P((FSDP, TENSOR), None),
        P(FSDP, None, None),
        P((FSDP, TENSOR), None, None),
        P((FSDP, TENSOR)),
        P((FSDP, TENSOR), HEADS, None),
        P(HEADS, None, (FSDP, TENSOR)),
        P((FSDP, TENSOR)),
        P((FSDP, TENSOR), None),
        P(HEADS, FSDP, TENSOR),
        P(HEADS, TENSOR, FSDP),
    )
    out_specs = (
        P((FSDP, TENSOR), None, None),
        P((FSDP, TENSOR)),
        P((FSDP, TENSOR), None, None),
        P((FSDP, TENSOR)),
        P((FSDP, TENSOR), HEADS, None),
        P(HEADS, None, (FSDP, TENSOR)),
        P((FSDP, TENSOR)),
        P((FSDP, TENSOR), None),
        P(HEADS, FSDP, TENSOR),
        P(HEADS, TENSOR, FSDP),
    )
    return jax.shard_map(program, mesh=mesh, in_specs=in_specs, out_specs=out_specs, check_vma=False)
```

```python
import functools
import types

import jax
import jax.numpy as jnp
from jax import lax
from jax.experimental import pallas as pl
from jax.experimental.pallas import tpu as pltpu
from jax.sharding import PartitionSpec as P

FSDP, HEADS, TENSOR = "fsdp", "heads", "tensor"
EPSILON = 1e-06
MASKED = -1e30
ROOT_HALF = 0.7071067811865476
DENSITY = 0.3989422804014327


def normalize(values):
    center = values - jnp.mean(values, -1, keepdims=True)
    inv_std = lax.rsqrt(jnp.mean(center * center, -1, keepdims=True) + EPSILON)
    return (center * inv_std, inv_std)


def norm_back(gradient, normed, inv_std, gain_vector):
    weighted = gradient * gain_vector
    gain_grad = jnp.sum(gradient * normed, axis=(0, 1))
    inner = (
        weighted
        - jnp.mean(weighted, -1, keepdims=True)
        - normed * jnp.mean(weighted * normed, -1, keepdims=True)
    )
    return (inner * inv_std, gain_grad)


def scores_of(queries, key_rows, keys_ok, score_scale):
    raw_scores = (
        jnp.einsum("iqhe,ikhe->ihqk", queries, key_rows, preferred_element_type=jnp.float32)
        * score_scale
    )
    return jnp.where(keys_ok, raw_scores, MASKED)


def gather_weights(
    gain_one, qkv_weight, out_weight, gain_two, router_weight, expert_up, expert_down
):
    dense_set = (
        lax.all_gather(qkv_weight, (FSDP, TENSOR), axis=0, tiled=True),
        lax.all_gather(out_weight, (FSDP, TENSOR), axis=2, tiled=True),
        lax.all_gather(router_weight, (FSDP, TENSOR), axis=0, tiled=True),
        lax.all_gather(gain_one, (FSDP, TENSOR), axis=0, tiled=True),
        lax.all_gather(gain_two, (FSDP, TENSOR), axis=0, tiled=True),
    )
    expert_set = (
        lax.all_gather(expert_up, FSDP, axis=1, tiled=True),
        lax.all_gather(expert_down, FSDP, axis=2, tiled=True),
    )
    return (dense_set, expert_set)


def reduce_expert_grads(up_grad, down_grad):
    return (
        lax.psum_scatter(up_grad, FSDP, scatter_dimension=1, tiled=True),
        lax.psum_scatter(down_grad, FSDP, scatter_dimension=2, tiled=True),
    )


def general(
    tokens,
    valid_mask,
    routes,
    teacher,
    gain_one,
    qkv_weight,
    out_weight,
    gain_two,
    router_weight,
    expert_up,
    expert_down,
):
    valid_total = lax.psum(jnp.sum(valid_mask.astype(jnp.float32)), (FSDP, TENSOR))
    dense_set, expert_set = gather_weights(
        gain_one, qkv_weight, out_weight, gain_two, router_weight, expert_up, expert_down
    )
    qkv_full, output_complete, router_full, gain_a, gain_b = dense_set
    up_full, down_full = expert_set
    image_count, token_slots, model_width = tokens.shape
    head_dim = qkv_full.shape[2] // 3
    local_experts = expert_up.shape[0]
    tensor_size = lax.axis_size(TENSOR)
    group_images = image_count * tensor_size
    group_rows = group_images * token_slots
    top_choices = routes.shape[2]
    expert_count = local_experts * lax.axis_size(HEADS)
    capacity = 2 * top_choices * group_rows // expert_count
    slot_count = local_experts * capacity
    total_tokens = image_count * token_slots * lax.axis_size(FSDP) * tensor_size
    total_images = image_count * lax.axis_size(FSDP) * tensor_size
    score_scale = head_dim ** (-0.5)
    inputs = tokens.astype(jnp.float32)
    normed_one, spread_one = normalize(inputs)
    first_in = (normed_one * gain_a.astype(jnp.float32)).astype(jnp.bfloat16)
    projected = jnp.einsum(
        "isd,dhe->ishe", first_in, qkv_full, preferred_element_type=jnp.float32
    ).astype(jnp.bfloat16)
    queries = projected[..., :head_dim]
    key_rows = projected[..., head_dim : 2 * head_dim]
    values = projected[..., 2 * head_dim :]
    keys_ok = (valid_mask > 0)[:, None, None, :]
    scores = scores_of(queries, key_rows, keys_ok, score_scale)
    peak_score = jnp.max(scores, -1, keepdims=True)
    exp_scores = jnp.exp(scores - peak_score)
    score_total = jnp.sum(exp_scores, -1, keepdims=True)
    logarithm_total = peak_score + jnp.log(score_total)
    attention = (exp_scores / score_total).astype(jnp.bfloat16)
    combined_heads = jnp.einsum(
        "ihqk,ikhe->iqhe", attention, values, preferred_element_type=jnp.float32
    ).astype(jnp.bfloat16)
    attn_part = jnp.einsum(
        "iqhe,hed->iqd", combined_heads, output_complete, preferred_element_type=jnp.float32
    )
    attended = lax.psum(attn_part, HEADS)
    residual = inputs + attended
    normed_two, spread_two = normalize(residual)
    second_in = (normed_two * gain_b.astype(jnp.float32)).astype(jnp.bfloat16)
    group_in = lax.all_gather(second_in, TENSOR, axis=0, tiled=True)
    rows_in = group_in.reshape(group_rows, model_width)
    logits = jnp.dot(rows_in, router_full, preferred_element_type=jnp.float32)
    peak_logit = jnp.max(logits, -1, keepdims=True)
    exponent_logits = jnp.exp(logits - peak_logit)
    router_probs = exponent_logits / jnp.sum(exponent_logits, -1, keepdims=True)
    expert_ids = jnp.arange(expert_count, dtype=jnp.int32)
    route_pairs = routes.reshape(group_rows, top_choices)
    picked_hot = (route_pairs[:, :, None] == expert_ids[None, None, :]).astype(jnp.float32)
    gate_weight_values = jnp.sum(router_probs[:, None, :] * picked_hot, -1)
    flat_routes = route_pairs.reshape(group_rows * top_choices)
    route_hot = (flat_routes[:, None] == expert_ids[None, :]).astype(jnp.int32)
    order = jnp.arange(group_rows * top_choices, dtype=jnp.int32)
    before = (order[None, :] < order[:, None]).astype(jnp.bfloat16)
    earlier = jnp.dot(
        before, route_hot.astype(jnp.bfloat16), preferred_element_type=jnp.float32
    ).astype(jnp.int32)
    slot_index = jnp.sum(earlier * route_hot, 1)
    first_expert = lax.axis_index(HEADS) * local_experts
    is_local = (flat_routes >= first_expert) & (flat_routes < first_expert + local_experts)
    target = jnp.where(is_local, (flat_routes - first_expert) * capacity + slot_index, slot_count)
    owner_row = jnp.arange(group_rows * top_choices, dtype=jnp.int32) // top_choices
    source = jnp.zeros((slot_count,), jnp.int32).at[target].set(owner_row, mode="drop")
    slot_gate = (
        jnp.zeros((slot_count,), jnp.float32)
        .at[target]
        .set(gate_weight_values.reshape(-1), mode="drop")
    )
    slot_pick = jnp.minimum(target, slot_count - 1)
    retain_mask = is_local.astype(jnp.float32)
    dispatched = rows_in[source].reshape(local_experts, capacity, model_width)
    before_gelu = jnp.einsum(
        "ecd,edf->ecf", dispatched, up_full, preferred_element_type=jnp.float32
    )
    hidden = jax.nn.gelu(before_gelu, approximate=False).astype(jnp.bfloat16)
    expert_out = jnp.einsum(
        "ecf,efd->ecd", hidden, down_full, preferred_element_type=jnp.float32
    ).reshape(slot_count, model_width)
    weighted = expert_out * slot_gate[:, None]
    moe_part = jnp.sum(
        (weighted[slot_pick] * retain_mask[:, None]).reshape(group_rows, top_choices, model_width),
        1,
    )
    moe_part = moe_part.reshape(group_images, token_slots, model_width)
    expert_sum = lax.psum(
        lax.psum_scatter(moe_part, TENSOR, scatter_dimension=0, tiled=True), HEADS
    )
    final = residual + expert_sum
    valid_rows = valid_mask.astype(jnp.float32)[..., None]
    difference = (final - teacher.astype(jnp.float32)) * valid_rows
    loss_terms = jnp.sum(difference * difference, axis=(1, 2)) * (
        total_images / (valid_total * model_width)
    )
    final_grad = difference * (total_tokens / valid_total)
    dense_set, expert_set = gather_weights(
        gain_one, qkv_weight, out_weight, gain_two, router_weight, expert_up, expert_down
    )
    qkv_full, output_complete, router_full, gain_a, gain_b = dense_set
    up_full, down_full = expert_set
    moe_grad = final_grad.astype(jnp.bfloat16)
    group_grad = lax.all_gather(moe_grad, TENSOR, axis=0, tiled=True).reshape(
        group_rows, model_width
    )
    slot_grad = group_grad[source].astype(jnp.float32)
    gate_slot_grad = jnp.sum(slot_grad * expert_out, -1)
    out_grad = (
        (slot_grad * slot_gate[:, None])
        .astype(jnp.bfloat16)
        .reshape(local_experts, capacity, model_width)
    )
    expert_down_grad = jnp.einsum(
        "ecf,ecd->efd", hidden, out_grad, preferred_element_type=jnp.float32
    )
    hidden_grad = jnp.einsum(
        "ecd,efd->ecf", out_grad, down_full, preferred_element_type=jnp.float32
    )
    normal_cdf = 0.5 * (1.0 + lax.erf(before_gelu * ROOT_HALF))
    slope = normal_cdf + before_gelu * DENSITY * jnp.exp(-0.5 * before_gelu * before_gelu)
    pre_grad = (hidden_grad * slope).astype(jnp.bfloat16)
    expert_up_grad = jnp.einsum(
        "ecd,ecf->edf", dispatched, pre_grad, preferred_element_type=jnp.float32
    )
    row_grad = jnp.einsum(
        "ecf,edf->ecd", pre_grad, up_full, preferred_element_type=jnp.float32
    ).reshape(slot_count, model_width)
    rows_part = jnp.sum(
        (row_grad[slot_pick] * retain_mask[:, None]).reshape(group_rows, top_choices, model_width),
        1,
    )
    rows_part = rows_part.reshape(group_images, token_slots, model_width)
    gate_part = (gate_slot_grad[slot_pick] * retain_mask).reshape(
        group_images, token_slots, top_choices
    )
    rows_share, gate_share = (
        lax.psum_scatter(rows_part, TENSOR, scatter_dimension=0, tiled=True),
        lax.psum_scatter(gate_part, TENSOR, scatter_dimension=0, tiled=True),
    )
    second_grad, gate_grad = lax.psum((rows_share, gate_share), HEADS)
    own_start = lax.axis_index(TENSOR) * image_count * token_slots
    own_rows = image_count * token_slots
    own_probs = lax.dynamic_slice_in_dim(router_probs, own_start, own_rows, 0).reshape(
        image_count, token_slots, expert_count
    )
    own_hot = lax.dynamic_slice_in_dim(picked_hot, own_start, own_rows, 0).reshape(
        image_count, token_slots, top_choices, expert_count
    )
    prob_grad = jnp.sum(gate_grad[..., None] * own_hot, 2)
    logit_grad = (
        own_probs * (prob_grad - jnp.sum(own_probs * prob_grad, -1, keepdims=True))
    ).astype(jnp.bfloat16)
    router_grad = jnp.einsum(
        "isd,ise->de", second_in, logit_grad, preferred_element_type=jnp.float32
    )
    second_grad = second_grad + jnp.einsum(
        "ise,de->isd", logit_grad, router_full, preferred_element_type=jnp.float32
    )
    residual_norm, gain_two_grad = norm_back(
        second_grad, normed_two, spread_two, gain_b.astype(jnp.float32)
    )
    residual_grad = final_grad + residual_norm
    attended_output_gradient = residual_grad.astype(jnp.bfloat16)
    out_weight_grad = jnp.einsum(
        "iqhe,iqd->hed",
        combined_heads,
        attended_output_gradient,
        preferred_element_type=jnp.float32,
    )
    mixed_grad = jnp.einsum(
        "iqd,hed->iqhe",
        attended_output_gradient,
        output_complete,
        preferred_element_type=jnp.float32,
    ).astype(jnp.bfloat16)
    scores = scores_of(queries, key_rows, keys_ok, score_scale)
    probs = jnp.exp(scores - logarithm_total)
    probs_low = probs.astype(jnp.bfloat16)
    prob_part = jnp.einsum(
        "iqhe,ikhe->ihqk", mixed_grad, values, preferred_element_type=jnp.float32
    )
    score_grad = (probs * (prob_part - jnp.sum(probs * prob_part, -1, keepdims=True))).astype(
        jnp.bfloat16
    )
    query_grad = (
        jnp.einsum("ihqk,ikhe->iqhe", score_grad, key_rows, preferred_element_type=jnp.float32)
        * score_scale
    )
    key_grad = (
        jnp.einsum("ihqk,iqhe->ikhe", score_grad, queries, preferred_element_type=jnp.float32)
        * score_scale
    )
    value_grad = jnp.einsum(
        "ihqk,iqhe->ikhe", probs_low, mixed_grad, preferred_element_type=jnp.float32
    )
    projected_grad = jnp.concatenate([query_grad, key_grad, value_grad], -1).astype(jnp.bfloat16)
    qkv_grad = jnp.einsum(
        "isd,ishe->dhe", first_in, projected_grad, preferred_element_type=jnp.float32
    )
    first_part = jnp.einsum(
        "ishe,dhe->isd", projected_grad, qkv_full, preferred_element_type=jnp.float32
    )
    first_grad = lax.psum(first_part, HEADS)
    input_norm, gain_one_grad = norm_back(
        first_grad, normed_one, spread_one, gain_a.astype(jnp.float32)
    )
    tokens_grad = residual_grad + input_norm
    dense_grads = (
        lax.psum_scatter(qkv_grad, (FSDP, TENSOR), scatter_dimension=0, tiled=True),
        lax.psum_scatter(out_weight_grad, (FSDP, TENSOR), scatter_dimension=2, tiled=True),
        lax.psum_scatter(router_grad, (FSDP, TENSOR), scatter_dimension=0, tiled=True),
        lax.psum_scatter(gain_one_grad, (FSDP, TENSOR), scatter_dimension=0, tiled=True),
        lax.psum_scatter(gain_two_grad, (FSDP, TENSOR), scatter_dimension=0, tiled=True),
    )
    expert_grads = reduce_expert_grads(expert_up_grad, expert_down_grad)
    return (
        final.astype(jnp.bfloat16),
        loss_terms,
        tokens_grad,
        dense_grads[3],
        dense_grads[0],
        dense_grads[1],
        dense_grads[4],
        dense_grads[2],
        expert_grads[0],
        expert_grads[1],
    )


MESH = pl.DeviceIdType.MESH
LOW = jnp.bfloat16
WIDE = jnp.float32


class Links:
    def __init__(self, send_sems, recv_sems):
        self.send_sems, self.recv_sems = send_sems, recv_sems
        self.copies, self.gone = [], []

    def send(self, src, dst, device):
        k = len(self.copies)
        copy = pltpu.make_async_remote_copy(
            src_ref=src,
            dst_ref=dst,
            send_sem=self.send_sems.at[k],
            recv_sem=self.recv_sems.at[k],
            device_id=device,
            device_id_type=MESH,
        )
        copy.start()
        self.copies.append(copy)
        return copy

    def left(self, copies):
        for copy in copies:
            copy.wait_send()
            self.gone.append(copy)

    def drain(self):
        for copy in self.copies:
            if not any(copy is other for other in self.gone):
                copy.wait_send()


class Place:
    def __init__(self, heads):
        self.f = lax.axis_index(FSDP)
        t = lax.axis_index(TENSOR)
        self.y, self.c = t // 2, lax.rem(t, 2)
        self.z = lax.axis_index(HEADS)
        self.heads = heads
        self.x_peer = {FSDP: 1 - self.f}
        self.y_peer = {TENSOR: 2 * (1 - self.y) + self.c}
        self.core_peer = {TENSOR: 2 * self.y + 1 - self.c}
        self.z_peers = [{HEADS: lax.rem(self.z + k, heads)} for k in range(1, heads)]
        self.plane_peers = []
        for a in range(2):
            for k in range(4):
                if a or k:
                    where = {TENSOR: lax.rem(t + k, 4)}
                    if a:
                        where[FSDP] = 1 - self.f
                    self.plane_peers.append(where)

    def image(self, df, dy, dc):
        f = 1 - self.f if df else self.f
        y = 1 - self.y if dy else self.y
        c = 1 - self.c if dc else self.c
        return f * 4 + 2 * y + c

    def greet(self, devices):
        barrier = pltpu.get_barrier_semaphore()
        for device in devices:
            pl.semaphore_signal(barrier, inc=1, device_id=device, device_id_type=MESH)
        pl.semaphore_wait(barrier, len(devices))

    def tensor_peers(self):
        t = 2 * self.y + self.c
        return [{TENSOR: lax.rem(t + k, 4)} for k in range(1, 4)]

    def owners(self):
        return [
            {FSDP: 1 - self.f if a else self.f, HEADS: lax.rem(self.z + k, self.heads)}
            for k in range(self.heads)
            for a in range(2)
            if a or k
        ]

    def everyone(self):
        t = 2 * self.y + self.c
        corners = [{FSDP: 1 - self.f, TENSOR: lax.rem(t + k, 4)} for k in range(1, 4)]
        return self.tensor_peers() + self.owners() + corners

    def axis_peers(self):
        return [self.x_peer, self.y_peer, self.core_peer]


class PlaneGather:
    def __init__(self, links, place, first, second, whole):
        self.links, self.place = links, place
        self.first, self.second, self.whole = first, second, whole

    def go(self, part, image, device):
        return self.links.send(part(image), part(image), device)

    def start(self):
        p, me = self.place, self.place.image(0, 0, 0)
        self.xa = self.go(self.first, me, p.x_peer)
        self.yb = self.go(self.second, me, p.y_peer)
        self.own = self.go(self.whole, me, p.core_peer)
        self.xb = self.go(self.second, me, p.x_peer)
        self.ya = self.go(self.first, me, p.y_peer)

    def forward(self):
        p = self.place
        self.xa.wait_recv()
        self.fa = self.go(self.first, p.image(1, 0, 0), p.y_peer)
        self.yb.wait_recv()
        self.fb = self.go(self.second, p.image(0, 1, 0), p.x_peer)

    def share(self):
        p = self.place
        self.xb.wait_recv()
        self.c1 = self.go(self.whole, p.image(1, 0, 0), p.core_peer)
        self.ya.wait_recv()
        self.c2 = self.go(self.whole, p.image(0, 1, 0), p.core_peer)

    def finish(self):
        p = self.place
        self.fa.wait_recv()
        self.fb.wait_recv()
        self.c3 = self.go(self.whole, p.image(1, 1, 0), p.core_peer)
        for copy in (self.own, self.c1, self.c2, self.c3):
            copy.wait_recv()

    def run(self):
        self.start()
        self.forward()
        self.share()
        self.finish()


GATHER_COPIES = 10


def in_rows(rows, step, body):
    def one(i, carry):
        body(pl.ds(pl.multiple_of(i * step, step), step))
        return carry

    lax.fori_loop(0, rows // step, one, 0)


class PlaneSum:
    def __init__(self, links, place, part, core_in, xa, ya, yb, xb, cut, step):
        self.links, self.place, self.part, self.core_in = links, place, part, core_in
        self.xa, self.ya, self.yb, self.xb, self.cut, self.step = xa, ya, yb, xb, cut, step
        self.rows, self.width = part.shape[1], part.shape[2]
        self.a, self.b = pl.ds(0, cut), pl.ds(cut, self.width - cut)

    def start(self):
        p = self.place
        self.order = [(1, 1), (1, 0), (0, 1), (0, 0)]
        self.into = {}
        for df, dy in self.order:
            f = 1 - p.f if df else p.f
            y = 1 - p.y if dy else p.y
            self.into[df, dy] = self.links.send(
                self.part.at[p.image(df, dy, 1)], self.core_in.at[2 * f + y], p.core_peer
            )

    def slot(self, df, dy):
        p = self.place
        return 2 * (1 - p.f if df else p.f) + (1 - p.y if dy else p.y)

    def cores(self):
        p, rc = self.place, self.core_in
        self.got = {}
        for df, dy in self.order:
            self.into[df, dy].wait_recv()
            j, mine = self.slot(df, dy), p.image(df, dy, 0)

            def add(rows, j=j, mine=mine):
                both = rc[j, rows, :].astype(WIDE) + self.part[mine, rows, :].astype(WIDE)
                rc[j, rows, :] = both.astype(LOW)

            in_rows(self.rows, self.step, add)
            y = 1 - p.y if dy else p.y
            f = 1 - p.f if df else p.f
            if df:
                self.got["x", dy] = self.links.send(rc.at[j, :, self.a], self.xa.at[y], p.x_peer)
            if dy:
                self.got["y", df] = self.links.send(rc.at[j, :, self.b], self.yb.at[f], p.y_peer)

    def cross(self):
        p, rc, xa, yb = self.place, self.core_in, self.xa, self.yb
        self.got["x", 1].wait_recv()
        j, other = self.slot(0, 1), 1 - p.y

        def add_a(rows):
            both = xa[other, rows, :].astype(WIDE) + rc[j, rows, self.a].astype(WIDE)
            xa[other, rows, :] = both.astype(LOW)

        in_rows(self.rows, self.step, add_a)
        self.last_a = self.links.send(xa.at[other], self.ya, p.y_peer)
        self.got["y", 1].wait_recv()
        k, away = self.slot(1, 0), 1 - p.f

        def add_b(rows):
            both = yb[away, rows, :].astype(WIDE) + rc[k, rows, self.b].astype(WIDE)
            yb[away, rows, :] = both.astype(LOW)

        in_rows(self.rows, self.step, add_b)
        self.last_b = self.links.send(yb.at[away], self.xb, p.x_peer)

    def finish(self, take):
        p, rc = self.place, self.core_in
        self.got["x", 0].wait_recv()
        self.got["y", 0].wait_recv()
        self.last_a.wait_recv()
        self.last_b.wait_recv()
        j, y, f = self.slot(0, 0), p.y, p.f

        def add(rows):
            first = rc[j, rows, self.a].astype(WIDE) + self.xa[y, rows, :].astype(WIDE)
            second = rc[j, rows, self.b].astype(WIDE) + self.yb[f, rows, :].astype(WIDE)
            take(rows, self.a, first + self.ya[rows, :].astype(WIDE))
            take(rows, self.b, second + self.xb[rows, :].astype(WIDE))

        in_rows(self.rows, self.step, add)


SUM_COPIES = 10


def sum_scratch(rows, width, cut):
    return [
        pltpu.VMEM((4, rows, width), LOW),
        pltpu.VMEM((2, rows, cut), LOW),
        pltpu.VMEM((rows, cut), LOW),
        pltpu.VMEM((2, rows, width - cut), LOW),
        pltpu.VMEM((rows, width - cut), LOW),
    ]


def all_heads(links, place, make):
    copies = []
    for k, device in enumerate(place.z_peers):
        src, dst = make(k, device[HEADS])
        copies.append(links.send(src, dst, device))
    return copies


def spends(microseconds):
    return pl.CostEstimate(flops=0, bytes_accessed=microseconds * 3_000_000, transcendentals=0)


def remote_call(
    kernel,
    outs,
    ins,
    scratch,
    copies,
    collective_id,
    vmem_mib,
    microseconds,
    in_hbm=(),
    out_hbm=(),
):
    vmem, hbm = pl.BlockSpec(memory_space=pltpu.VMEM), pl.BlockSpec(memory_space=pltpu.HBM)
    return pl.pallas_call(
        kernel,
        out_shape=outs,
        in_specs=[hbm if i in in_hbm else vmem for i in range(len(ins))],
        out_specs=[hbm if i in out_hbm else vmem for i in range(len(outs))],
        scratch_shapes=[
            *scratch,
            pltpu.SemaphoreType.DMA((copies,)),
            pltpu.SemaphoreType.DMA((copies,)),
        ],
        compiler_params=pltpu.CompilerParams(
            collective_id=collective_id,
            has_side_effects=True,
            vmem_limit_bytes=vmem_mib * 2**20,
        ),
        cost_estimate=spends(microseconds),
    )(*ins)


def shape(dims, dtype=LOW):
    return jax.ShapeDtypeStruct(dims, dtype)


def weights_kernel(heads, wq, wo, count, route, oq, oo, counts, far_route, ss, rs):
    place = Place(heads)
    links = Links(ss, rs)
    me = place.image(0, 0, 0)
    place.greet(place.plane_peers + place.z_peers)
    oq[me] = wq[...]
    oo[me, place.z] = wo[...]
    counts[me] = count[...]
    half = wq.shape[1] // 2
    mid = heads // 2
    main = PlaneGather(
        links,
        place,
        lambda i: oq.at[i, :, pl.ds(0, half)],
        lambda i: oq.at[i, :, pl.ds(half, half)],
        lambda i: oq.at[i],
    )
    side = PlaneGather(
        links,
        place,
        lambda i: oo.at[i, pl.ds(0, mid)],
        lambda i: oo.at[i, pl.ds(mid, heads - mid)],
        lambda i: oo.at[i],
    )
    main.start()
    along = all_heads(
        links, place, lambda k, z: (oo.at[me, place.z], oo.at[me, place.z])
    )
    small = [links.send(counts.at[me], counts.at[me], d) for d in place.plane_peers]
    small.append(links.send(route, far_route, place.x_peer))
    main.forward()
    for copy in along:
        copy.wait_recv()
    side.start()
    main.share()
    main.finish()
    side.forward()
    side.share()
    side.finish()
    for copy in small:
        copy.wait_recv()
    links.drain()


def gather_weights_fast(heads, wq, wo, count, route):
    outs = [
        shape((8, *wq.shape)),
        shape((8, heads, *wo.shape)),
        shape((8, *count.shape), jnp.int32),
        shape(route.shape, jnp.int32),
    ]
    copies = 2 * GATHER_COPIES + heads - 1 + 7 + 1
    return remote_call(
        functools.partial(weights_kernel, heads),
        outs,
        [wq, wo, count, route],
        [],
        copies,
        1,
        32,
        20,
    )


def mix_kernel(
    heads,
    experts,
    skip,
    mixed,
    wo,
    tokens,
    gain,
    router,
    near_route,
    far_route,
    down,
    residual,
    second,
    group,
    probs,
    slots,
    arrived,
    everyone,
    other_half,
    ss,
    rs,
):
    place = Place(heads)
    links = Links(ss, rs)
    me = place.image(0, 0, 0)
    place.greet(place.plane_peers + place.z_peers)
    everyone[place.z] = mixed[...]
    along = all_heads(links, place, lambda k, z: (everyone.at[place.z], everyone.at[place.z]))
    local_experts = slots.shape[0] // 2
    ids = place.z * local_experts + lax.broadcasted_iota(jnp.int32, (local_experts, 1), 0)
    first = place.f == 0
    near, far = near_route[...], far_route[...]
    both = [jnp.where(first, near, far), jnp.where(first, far, near)]
    chosen = jnp.concatenate([(r[0:1] == ids) | (r[1:2] == ids) for r in both], 0)
    count = chosen.astype(WIDE)
    before = lax.broadcasted_iota(jnp.int32, (128, 128), 0)
    before = (before < lax.broadcasted_iota(jnp.int32, (128, 128), 1)).astype(LOW)
    running = jnp.zeros((2 * local_experts, 1), WIDE)
    for b in range(slots.shape[1] // 128):
        columns = slice(b * 128, (b + 1) * 128)
        here = count[:, columns]
        slot = dot(here.astype(LOW), before) + running
        slots[:, columns] = jnp.where(chosen[:, columns], slot, -1.0).astype(jnp.int32)
        running = running + jnp.sum(here, -1, keepdims=True)
    for copy in along:
        copy.wait_recv()
    rows_all, width = tokens.shape
    half = width // 2
    total = jnp.zeros((rows_all, width), WIDE)
    for z in range(heads):
        weight = wo[:, z].reshape(width, wo.shape[3])
        total = total + lax.dot_general(
            everyone[z], weight, (((1,), (1,)), ((), ())), preferred_element_type=WIDE
        )
    residual[...] = total

    def norm(rows):
        values = tokens[rows, :].astype(WIDE) + residual[rows, :]
        residual[rows, :] = values
        normed, _ = normalize(values)
        second[rows, :] = (normed * gain[...]).astype(LOW)

    in_rows(rows_all, 64, norm)
    low, high = second[:, :half], second[:, half:]
    group[me] = jnp.where(first, low, high)
    other_half[...] = jnp.where(first, high, low)
    x1 = links.send(other_half, group.at[me], place.x_peer)
    theirs = pl.ds((1 - place.f) * (local_experts // 2) + skip, arrived.shape[0])
    bulk = links.send(down.at[theirs], arrived, place.x_peer)
    y1 = links.send(group.at[me], group.at[me], place.y_peer)
    shared = [links.send(group.at[me], group.at[me], place.core_peer)]
    logits = lax.dot_general(
        router[...], second[...], (((0,), (1,)), ((), ())), preferred_element_type=WIDE
    )[:experts]
    powers = jnp.exp(logits - jnp.max(logits, 0, keepdims=True))
    probs[me] = powers / jnp.sum(powers, 0, keepdims=True)
    small = [links.send(probs.at[me], probs.at[me], d) for d in place.plane_peers]
    across, beside, corner = place.image(1, 0, 0), place.image(0, 1, 0), place.image(1, 1, 0)
    x1.wait_recv()
    y2 = links.send(group.at[across], group.at[across], place.y_peer)
    shared.append(links.send(group.at[across], group.at[across], place.core_peer))
    y1.wait_recv()
    shared.append(links.send(group.at[beside], group.at[beside], place.core_peer))
    y2.wait_recv()
    shared.append(links.send(group.at[corner], group.at[corner], place.core_peer))
    for copy in shared + small + [bulk]:
        copy.wait_recv()
    links.drain()


def mix_heads(
    heads, experts, skip, mixed, wo, tokens, gain, router, near_route, far_route, down
):
    rows, width = tokens.shape
    late = down.shape[0] // 2 - skip
    return remote_call(
        functools.partial(mix_kernel, heads, experts, skip),
        [
            shape((rows, width), WIDE),
            shape((rows, width)),
            shape((8, rows, width // 2)),
            shape((8, experts, rows), WIDE),
            shape((2 * experts // heads, near_route.shape[1]), jnp.int32),
            shape((late, *down.shape[1:])),
        ],
        [mixed, wo, tokens, gain, router, near_route, far_route, down],
        [pltpu.VMEM((heads, *mixed.shape), LOW), pltpu.VMEM((rows, width // 2), LOW)],
        heads - 1 + 7 + 8,
        2,
        48,
        26,
        in_hbm=(7,),
        out_hbm=(5,),
    )


class ChunkSum:
    def __init__(self, links, place, part, columns, core_in, xa, ya, yb, xb):
        self.links, self.place, self.part, self.columns = links, place, part, columns
        self.core_in, self.xa, self.ya, self.yb, self.xb = core_in, xa, ya, yb, xb
        self.rows, self.half = core_in.shape[2], core_in.shape[3] // 2
        self.a, self.b = pl.ds(0, self.half), pl.ds(self.half, self.half)

    def start(self):
        p = self.place
        self.into = self.links.send(
            self.part.at[:, :, 1 - p.c, :, self.columns], self.core_in, p.core_peer
        )

    def cores(self):
        p, rc = self.place, self.core_in
        self.into.wait_recv()

        def add(rows):
            here = self.part[:, :, p.c, rows, self.columns].astype(WIDE)
            rc[:, :, rows, :] = (rc[:, :, rows, :].astype(WIDE) + here).astype(LOW)

        in_rows(self.rows, 32, add)
        self.to_x = self.links.send(rc.at[1 - p.f, :, :, self.a], self.xa, p.x_peer)
        self.to_y = self.links.send(rc.at[:, 1 - p.y, :, self.b], self.yb, p.y_peer)

    def cross(self):
        p, rc, xa, yb = self.place, self.core_in, self.xa, self.yb
        self.to_x.wait_recv()
        y, f = 1 - p.y, 1 - p.f

        def add_a(rows):
            both = xa[y, rows, :].astype(WIDE) + rc[p.f, y, rows, self.a].astype(WIDE)
            xa[y, rows, :] = both.astype(LOW)

        in_rows(self.rows, 64, add_a)
        self.last_a = self.links.send(xa.at[y], self.ya, p.y_peer)
        self.to_y.wait_recv()

        def add_b(rows):
            both = yb[f, rows, :].astype(WIDE) + rc[f, p.y, rows, self.b].astype(WIDE)
            yb[f, rows, :] = both.astype(LOW)

        in_rows(self.rows, 64, add_b)
        self.last_b = self.links.send(yb.at[f], self.xb, p.x_peer)

    def finish(self, take):
        p, rc = self.place, self.core_in
        self.last_a.wait_recv()
        self.last_b.wait_recv()

        def add(rows):
            first = rc[p.f, p.y, rows, self.a].astype(WIDE) + self.xa[p.y, rows, :].astype(WIDE)
            second = rc[p.f, p.y, rows, self.b].astype(WIDE) + self.yb[p.f, rows, :].astype(WIDE)
            take(rows, 0, first + self.ya[rows, :].astype(WIDE))
            take(rows, 1, second + self.xb[rows, :].astype(WIDE))

        in_rows(self.rows, 64, add)


def skewed(chunks, stages):
    for step in range(chunks + len(stages) - 1):
        for k in range(chunks):
            if 0 <= step - k < len(stages):
                stages[step - k](k)


def combine_part(place, links, chunks, r):
    heads, z, me = place.heads, place.z, place.image(0, 0, 0)
    part, residual, teacher, valid, scale = r.part, r.residual, r.teacher, r.valid, r.scale
    result, final_grad, group, loss = r.result, r.final_grad, r.group, r.loss
    image_sum, far = r.image_sum, r.image_far
    rows_all, width = residual.shape
    own = rows_all // heads
    wide = width // chunks
    half = wide // 2
    mine = pl.ds(pl.multiple_of(z * own, own), own)
    columns = [pl.ds(k * wide, wide) for k in range(chunks)]
    adders = [
        ChunkSum(
            links,
            place,
            part,
            columns[k],
            r.sum_core.at[k],
            r.sum_xa.at[k],
            r.sum_ya.at[k],
            r.sum_yb.at[k],
            r.sum_xb.at[k],
        )
        for k in range(chunks)
    ]
    for adder in adders:
        adder.start()
    along, spread, squares = {}, {}, []
    gathers = [
        PlaneGather(
            links,
            place,
            lambda i, k=k: group.at[i, :, pl.ds(k * wide, half)],
            lambda i, k=k: group.at[i, :, pl.ds(k * wide + half, half)],
            lambda i, k=k: group.at[i, :, columns[k]],
        )
        for k in range(chunks)
    ]

    def to_heads(k):
        def keep(rows, part_of, values):
            image_sum[k, rows, pl.ds(part_of * half, half)] = values.astype(LOW)

        adders[k].finish(keep)
        along[k] = all_heads(
            links,
            place,
            lambda n, to: (
                image_sum.at[k, pl.ds(pl.multiple_of(to * own, own), own)],
                far.at[k, n],
            ),
        )

    def final(k):
        for copy in along[k]:
            copy.wait_recv()
        total = image_sum[k, mine, :].astype(WIDE)
        for n in range(heads - 1):
            total = total + far[k, n].astype(WIDE)
        values = residual[mine, columns[k]] + total
        result[z, :, columns[k]] = values.astype(LOW)
        error = (values - teacher[mine, columns[k]].astype(WIDE)) * valid[mine, :]
        grad = error * scale[0:1, 0:1]
        final_grad[:, columns[k]] = grad
        group[me, mine, columns[k]] = grad.astype(LOW)
        block = group.at[me, mine, columns[k]]
        spread[k] = all_heads(links, place, lambda n, to: (block, block))
        square = jnp.sum((error * error).reshape(own // 8, 8, wide), axis=0)
        squares.extend(square[:, i * 128 : (i + 1) * 128] for i in range(wide // 128))

    def to_plane(k):
        for copy in spread[k]:
            copy.wait_recv()
        gathers[k].start()

    def forward(k):
        gathers[k].forward()
        gathers[k].share()

    skewed(
        chunks,
        [
            lambda k: adders[k].cores(),
            lambda k: adders[k].cross(),
            to_heads,
            final,
            to_plane,
            forward,
        ],
    )
    loss[z] = sum(squares)
    extra = all_heads(links, place, lambda k, to: (result.at[z], result.at[z]))
    extra += all_heads(links, place, lambda k, to: (loss.at[z], loss.at[z]))
    for gather in gathers:
        gather.finish()
    return extra


def dot(a, b, over=(1, 0)):
    return lax.dot_general(a, b, (((over[0],), (over[1],)), ((), ())), preferred_element_type=WIDE)


def one_hot(slots, row, capacity):
    places = lax.broadcasted_iota(jnp.int32, (capacity, slots.shape[1]), 0)
    return places == slots[pl.ds(row, 1), :]


class Loads:
    def __init__(self, sems):
        self.sems, self.count = sems, 0

    def start(self, src, dst):
        copy = pltpu.make_async_copy(src, dst, self.sems.at[self.count])
        self.count += 1
        copy.start()
        return copy


def gelu_parts(values):
    cdf = 0.5 * (1.0 + lax.erf(values * ROOT_HALF))
    return values * cdf, cdf + values * DENSITY * jnp.exp(-0.5 * values * values)


def experts_part(place, links, loads, pieces, r):
    slots, x, probs, up, down = r.slots, r.x, r.probs, r.up, r.down
    pick_near, pick_far, gates, hidden = r.pick_near, r.pick_far, r.gates, r.hidden
    buffer_near, buffer_far, own, weighted = r.buffer_near, r.buffer_far, r.own, r.weighted
    away, arrived, w_up, w_near, w_far = r.away, r.arrived, r.w_up, r.w_near, r.w_far
    kept, pair, _ = own.shape
    capacity, half = pair // 2, x.shape[2]
    local_experts = 2 * kept
    mine, theirs = place.f * kept, (1 - place.f) * kept
    ups = {}
    for far in (1, 0):
        for i in range(kept):
            source = (theirs if far else mine) + i
            ups[far, i] = loads.start(up.at[source], w_up.at[far, i])
    nears = [loads.start(down.at[mine + i], w_near.at[i]) for i in range(kept)]
    fars, at = [], 0
    for piece in pieces:
        size = piece.shape[0]
        fars.append(loads.start(piece, w_far.at[pl.ds(at, size)]))
        at += size
    place.greet(place.everyone())
    sent = []
    for i in range(kept):
        for g in range(2):
            rows = slice(i * capacity, (i + 1) * capacity)
            hot = one_hot(slots, g * local_experts + theirs + i, capacity).astype(LOW)
            pick_far[g, rows] = hot
            buffer_far[i, g * capacity : (g + 1) * capacity] = dot(hot, x[g]).astype(LOW)
        ups[1, i].wait()
        away[i] = dot(buffer_far[i], w_up[1, i]).astype(LOW)
        sent.append(links.send(away.at[i], arrived.at[i], place.x_peer))
    late = [
        links.send(down.at[theirs + i], w_far.at[i], place.x_peer) for i in range(at, kept)
    ]
    for i in range(kept):
        expert = place.z * local_experts + mine + i
        for g in range(2):
            rows = slice(i * capacity, (i + 1) * capacity)
            into = slice(g * capacity, (g + 1) * capacity)
            hot = one_hot(slots, g * local_experts + mine + i, capacity)
            chances = [probs[4 * g + k, pl.ds(expert, 1), :] for k in range(4)]
            chances = jnp.concatenate(chances, 1)
            gates[i, into] = jnp.sum(jnp.where(hot, chances, 0.0), -1, keepdims=True)
            pick_near[g, rows] = hot.astype(LOW)
            buffer_near[i, into] = dot(hot.astype(LOW), x[g]).astype(LOW)
        ups[0, i].wait()
        own[i] = dot(buffer_near[i], w_up[0, i])
    for copy in nears + fars:
        copy.wait()
    for i in range(kept):
        sent[i].wait_recv()
        if i >= at:
            late[i - at].wait_recv()
        values, slopes = gelu_parts(own[i] + arrived[i].astype(WIDE))
        hidden[i] = values.astype(LOW)
        own[i] = slopes
        for weight, f in ((w_near, place.f), (w_far, 1 - place.f)):
            out = (dot(hidden[i], weight[i]) * gates[i]).astype(LOW)
            columns = pl.ds(pl.multiple_of(f * half, half), half)
            for g in range(2):
                rows = slice(i * capacity, (i + 1) * capacity)
                weighted[g, rows, columns] = out[g * capacity : (g + 1) * capacity]
    for g in range(2):
        total = dot(pick_near[g], weighted[g], (0, 0)).astype(LOW)
        r.part[g] = total.reshape(r.part.shape[1:])
    links.left(sent)


def experts_back_part(place, links, loads, r):
    pick_near, pick_far, hidden, slope, gates = r.pick_near, r.pick_far, r.hidden, r.own, r.gates
    w_up, w_near, w_far, group = r.w_up, r.w_near, r.w_far, r.group
    pre_near, pre_far, out_grad = r.away, r.arrived, r.out_grad
    side = r.weighted.shape[2] // 2
    rows_near = r.weighted.at[:, :, pl.ds(0, side)]
    rows_far = r.weighted.at[:, :, pl.ds(side, side)]
    send_held = r.w_far
    kept, pair, width = out_grad.shape
    capacity, half = pair // 2, width // 2
    first = pl.ds(pl.multiple_of(place.f * half, half), half)
    second = pl.ds(pl.multiple_of((1 - place.f) * half, half), half)
    sent = []
    for i in range(kept):
        rows = slice(i * capacity, (i + 1) * capacity)
        for g in range(2):
            rows_in = group[4 * g : 4 * g + 4].reshape(pick_near.shape[2], width)
            r.slot_rows[g * capacity : (g + 1) * capacity] = dot(
                pick_near[g, rows], rows_in
            ).astype(LOW)
        raw = dot(r.slot_rows[:, first], w_near[i], (1, 1))
        raw = raw + dot(r.slot_rows[:, second], w_far[i], (1, 1))
        pre_near[i] = (raw * gates[i] * slope[i]).astype(LOW)
        sent.append(links.send(pre_near.at[i], pre_far.at[i], place.x_peer))
        out_grad[i] = (r.slot_rows[...].astype(WIDE) * gates[i]).astype(LOW)
        gate_grad = jnp.sum(raw * hidden[i].astype(WIDE), -1, keepdims=True)
        for g in range(2):
            terms = gate_grad[g * capacity : (g + 1) * capacity]
            terms = terms * pick_near[g, rows].astype(WIDE)
            r.gate_rows[g, i : i + 1] = jnp.sum(terms, 0, keepdims=True)
    bulk = []
    for i in range(kept):
        send_held[i] = dot(hidden[i], out_grad[i, :, second], (0, 0)).astype(LOW)
    early = pl.ds(0, kept // 2)
    bulk = [links.send(send_held.at[early], r.down_far.at[early], place.x_peer)]
    stores = [
        loads.start(r.hidden, r.hidden_out),
        loads.start(r.buffer_near, r.near_out),
        loads.start(r.buffer_far, r.far_out),
        loads.start(pre_near, r.near_pre),
        loads.start(out_grad, r.grad_out),
    ]

    def through_up(far, i, pre, rows_out):
        back = dot(pre[i], w_up[far, i], (1, 1)).astype(LOW)
        rows = slice(i * capacity, (i + 1) * capacity)
        for g in range(2):
            rows_out[g, rows] = back[g * capacity : (g + 1) * capacity]

    for i in range(kept):
        through_up(0, i, pre_near, rows_near)
    for i in range(kept):
        sent[i].wait_recv()
        through_up(1, i, pre_far, rows_far)
    stores.append(loads.start(pre_far, r.far_pre))
    for g in range(2):
        near = dot(pick_near[g], rows_near[g], (0, 0))
        both = (near + dot(pick_far[g], rows_far[g], (0, 0))).astype(LOW)
        r.back_part[g] = both.reshape(r.back_part.shape[1:])
    return stores, bulk


def back_part(place, links, chunks, bulk, r):
    heads, f, y, z = place.heads, place.f, place.y, place.z
    t, me = 2 * y + place.c, place.image(0, 0, 0)
    part, gate_part, probs, valid = r.back_part, r.gate_rows, r.probs_own, r.valid_row
    residual, gain, router, final_grad, tokens = (r.residual, r.gain, r.router, r.final_grad, r.tokens)
    gain_one, second_in, projected, log_total, mixed = (r.gain_one, r.second_in, r.projected, r.log_total, r.mixed)
    qkv, wo, tokens_grad, dense_out, gain_out = (r.qkv, r.wo, r.tokens_grad, r.dense_out, r.gain_out)
    core_in, y_in, far, pair, x_in = (r.core_in, r.y_in, r.far, r.pair, r.x_in)
    gate_in, gate_sum, gate_all, logit_rows, logit_grads = (r.gate_in, r.gate_sum, r.gate_all, r.logit_rows, r.logit_grads)
    attended, first_in, projected_grad, first_part, dense = (r.attended, r.first_in, r.projected_grad, r.first_part, r.dense)
    dense_core, xa, ya, yb, xb = (r.dense_core, r.xa, r.ya, r.yb, r.xb)
    first_far, rounded, gain_part, gain_plane, gain_heads = (r.first_far, r.rounded, r.gain_part, r.gain_plane, r.gain_heads)
    tensor_peers, owners = place.tensor_peers(), place.owners()
    rows_all, width = residual.shape
    half = width // 2
    own = rows_all // heads
    into, beside, along, cross = {}, {}, {}, {}
    for k in range(chunks):
        source = part.at[:, :, 1 - place.c, :, pl.ds(k * 128, 128)]
        into[k] = links.send(source, core_in.at[k], place.core_peer)
    gate_in[t] = gate_part[...]
    shared = [links.send(gate_part, gate_in.at[t], d) for d in tensor_peers]
    mine = pl.ds(pl.multiple_of(z * own, own), own)

    def to_y(k):
        into[k].wait_recv()
        rc = core_in.at[k]

        def add(rows):
            here = part[:, :, place.c, rows, pl.ds(k * 128, 128)].astype(WIDE)
            rc[:, :, rows, :] = (rc[:, :, rows, :].astype(WIDE) + here).astype(LOW)

        in_rows(rows_all, 32, add)
        beside[k] = links.send(rc.at[:, 1 - y], y_in.at[k], place.y_peer)

    def to_heads(k):
        beside[k].wait_recv()

        def add(rows):
            both = y_in[k, :, rows, :].astype(WIDE) + core_in[k, :, y, rows, :].astype(WIDE)
            y_in[k, :, rows, :] = both.astype(LOW)

        in_rows(rows_all, 64, add)
        along[k] = all_heads(
            links,
            place,
            lambda n, to: (
                y_in.at[k, :, pl.ds(pl.multiple_of(to * own, own), own)],
                far.at[k, n],
            ),
        )

    def to_x(k):
        for copy in along[k]:
            copy.wait_recv()
        total = y_in[k, :, mine, :].astype(WIDE)
        for n in range(heads - 1):
            total = total + far[k, n].astype(WIDE)
        pair[k] = total.astype(LOW)
        cross[k] = links.send(pair.at[k, 1 - f], x_in.at[k], place.x_peer)

    to_y(0)
    for copy in shared:
        copy.wait_recv()
    gate_sum[...] = sum(gate_in[k] for k in range(4))
    kept = gate_sum.shape[1]
    rows_of = pl.ds(pl.multiple_of(t * rows_all, rows_all), rows_all)
    gate_all[z, f] = gate_sum[f, :, rows_of]
    spread = [
        links.send(gate_sum.at[d[FSDP], :, rows_of], gate_all.at[z, f], d) for d in owners
    ]
    to_y(1)
    to_heads(0)
    for k in range(2, chunks):
        to_y(k)
        to_heads(k - 1)
        to_x(k - 2)
    for copy in spread:
        copy.wait_recv()
    chances = probs[...]
    prob_grad = gate_all[...].reshape(2 * heads * kept, rows_all)
    logit_grad = chances * (prob_grad - jnp.sum(chances * prob_grad, 0, keepdims=True))
    logit_grads[...] = logit_grad.astype(LOW)
    logit_rows[...] = dot(logit_grads[...], router[...], (0, 0))
    normed, spread_two = normalize(residual[mine, :])
    router_grad = dot(second_in[...], logit_grads[...], (0, 1))
    spare = jnp.zeros((width, 128 - router_grad.shape[1]), WIDE)
    router_grad = jnp.concatenate([router_grad, spare], 1).astype(LOW)
    blocks, block = dense.shape[:2]
    qkv_width = projected.shape[1]
    dense_width = dense.shape[2]
    dense[:, :, pl.ds(dense_width - 128, 128)] = router_grad.reshape(blocks, block, 128)

    def first_norm(rows):
        again, _ = normalize(tokens[rows, :].astype(WIDE))
        first_in[rows, :] = (again * gain_one[...]).astype(LOW)

    in_rows(rows_all, 64, first_norm)
    to_heads(chunks - 1)
    to_x(chunks - 2)
    to_x(chunks - 1)
    early = r.w_far.shape[0] // 2
    late = pl.ds(early, r.w_far.shape[0] - early)
    bulk.append(links.send(r.w_far.at[late], r.down_far.at[late], place.x_peer))
    near = jnp.concatenate([pair[k, f].astype(WIDE) for k in range(chunks)], 1)
    for k in range(chunks):
        cross[k].wait_recv()
    away = jnp.concatenate([x_in[k].astype(WIDE) for k in range(chunks)], 1)
    first = f == 0
    rows_grad = jnp.concatenate([jnp.where(first, near, away), jnp.where(first, away, near)], 1)
    second_grad = rows_grad + logit_rows[mine, :]
    weighted = second_grad * gain[...]
    gain_part[1:2, :] = jnp.sum(second_grad * normed, 0, keepdims=True)
    inner = (
        weighted
        - jnp.mean(weighted, -1, keepdims=True)
        - normed * jnp.mean(weighted * normed, -1, keepdims=True)
    )
    total_grad = final_grad[...] + inner * spread_two
    attended[mine, :] = total_grad.astype(LOW)
    for copy in all_heads(
        links, place, lambda k, to: (attended.at[mine], attended.at[mine])
    ):
        copy.wait_recv()

    mixed_grad = dot(attended[...], wo[...].reshape(width, wo.shape[2])).astype(LOW)
    head_count = log_total.shape[1]
    size = qkv_width // head_count // 3
    score_scale = size ** (-0.5)
    keys_ok = valid[...] > 0
    grads = []
    for h in range(head_count):
        at = 3 * h * size
        query, key, value = (projected[:, at + n * size : at + (n + 1) * size] for n in range(3))
        above = mixed_grad[:, h * size : (h + 1) * size]
        scores = jnp.where(keys_ok, dot(query, key, (1, 1)) * score_scale, MASKED)
        chances = jnp.exp(scores - log_total[:, h : h + 1])
        prob_part = dot(above, value, (1, 1))
        inner = jnp.sum(chances * prob_part, -1, keepdims=True)
        score_grad = (chances * (prob_part - inner)).astype(LOW)
        grads.append(dot(score_grad, key) * score_scale)
        grads.append(dot(score_grad, query, (0, 0)) * score_scale)
        grads.append(dot(chances.astype(LOW), above, (0, 0)))
    projected_grad[...] = jnp.concatenate(grads, 1).astype(LOW)
    weight = qkv[:, :, pl.ds(128, qkv_width)].reshape(width, qkv_width)
    back = dot(projected_grad[...], weight, (1, 1))
    first_part[...] = back.astype(LOW).reshape(heads, own, width)
    along = all_heads(links, place, lambda n, to: (first_part.at[to], first_far.at[n]))
    dense_now = jnp.concatenate(
        [
            dot(first_in[...], projected_grad[...], (0, 0)).astype(LOW),
            dot(attended[...], mixed[...], (0, 0)).astype(LOW),
        ],
        1,
    )
    dense[:, :, pl.ds(0, dense_width - 128)] = dense_now.reshape(blocks, block, dense_width - 128)
    adder = PlaneSum(links, place, dense, dense_core, xa, ya, yb, xb, xa.shape[2], 32)
    adder.start()
    gain_part[0:1, :] = jnp.sum(back * normalize(tokens[...].astype(WIDE))[0], 0, keepdims=True)
    gain_plane[me] = gain_part[...]
    small = [links.send(gain_part, gain_plane.at[me], d) for d in place.plane_peers]
    adder.cores()
    adder.cross()
    for copy in small:
        copy.wait_recv()
    gain_heads[z] = sum(gain_plane[i] for i in range(8))
    gains = all_heads(links, place, lambda n, to: (gain_heads.at[z], gain_heads.at[z]))
    normed, spread_one = normalize(tokens[mine, :].astype(WIDE))
    for copy in along:
        copy.wait_recv()
    first_grad = first_part[z].astype(WIDE)
    for n in range(heads - 1):
        first_grad = first_grad + first_far[n].astype(WIDE)
    weighted = first_grad * gain_one[...]
    inner = (
        weighted
        - jnp.mean(weighted, -1, keepdims=True)
        - normed * jnp.mean(weighted * normed, -1, keepdims=True)
    )
    rounded[z] = (total_grad + inner * spread_one).astype(LOW)
    along = all_heads(links, place, lambda n, to: (rounded.at[z], rounded.at[z]))

    def keep(rows, columns, values):
        dense_out[rows, columns] = values

    adder.finish(keep)
    for copy in gains:
        copy.wait_recv()
    gain_out[...] = sum(gain_heads[i] for i in range(heads))
    for copy in along:
        copy.wait_recv()
    for i in range(heads):
        tokens_grad[i] = rounded[i].astype(WIDE)
    for copy in bulk:
        copy.wait_recv()


def layer_kernel(heads, chunks, names, piece_names, *refs):
    r = types.SimpleNamespace(**dict(zip(names, refs)))
    place = Place(heads)
    links = Links(r.send_sems, r.recv_sems)
    loads = Loads(r.load_sems)
    experts_part(place, links, loads, [getattr(r, n) for n in piece_names], r)
    extra = combine_part(place, links, chunks, r)
    stores, bulk = experts_back_part(place, links, loads, r)
    for copy in extra:
        copy.wait_recv()
    back_part(place, links, chunks, bulk, r)
    for copy in stores:
        copy.wait()
    links.drain()


def named_call(kernel, ins, outs, scratch, copies, loads, collective_id, vmem_mib, microseconds):
    spaces = {False: pltpu.VMEM, True: pltpu.HBM}
    names = [*ins, *outs, *scratch, "load_sems", "send_sems", "recv_sems"]
    made = pl.pallas_call(
        functools.partial(kernel, names),
        out_shape=[o[0] for o in outs.values()],
        in_specs=[pl.BlockSpec(memory_space=spaces[a[1]]) for a in ins.values()],
        out_specs=[pl.BlockSpec(memory_space=spaces[o[1]]) for o in outs.values()],
        scratch_shapes=[
            *scratch.values(),
            pltpu.SemaphoreType.DMA((loads,)),
            pltpu.SemaphoreType.DMA((copies,)),
            pltpu.SemaphoreType.DMA((copies,)),
        ],
        compiler_params=pltpu.CompilerParams(
            collective_id=collective_id,
            has_side_effects=True,
            vmem_limit_bytes=vmem_mib * 2**20,
        ),
        cost_estimate=spends(microseconds),
    )(*[a[0] for a in ins.values()])
    return types.SimpleNamespace(**dict(zip(outs, made)))


def layer(heads, capacity, head_count, pieces, vmem, hbm):
    rows, width = vmem["residual"].shape
    own, half, chunks = rows // heads, width // 2, width // 256
    local_experts, _, hidden_width = hbm["up"].shape
    kept, pair, group_rows = local_experts // 2, 2 * capacity, 4 * rows
    block = width // 8
    qkv_width, mixed_width = vmem["projected"].shape[1], vmem["mixed"].shape[1]
    dense_width = qkv_width + mixed_width + 128
    cut = 128 * ((dense_width // 128 + 1) // 2)
    late = kept - sum(piece.shape[0] for piece in pieces)
    piece_names = [f"piece{n}" for n in range(len(pieces))]
    ins = {name: (array, False) for name, array in vmem.items()}
    ins.update({name: (array, True) for name, array in hbm.items()})
    ins.update({name: (array, True) for name, array in zip(piece_names, pieces)})
    outs = {
        "result": (shape((heads, own, width)), False),
        "loss": (shape((heads, 8, 128), WIDE), False),
        "tokens_grad": (shape((heads, own, width), WIDE), False),
        "dense_out": (shape((block, dense_width), WIDE), False),
        "gain_out": (shape((2, width), WIDE), False),
        "down_far": (shape((kept, hidden_width, half)), True),
        "hidden_out": (shape((kept, pair, hidden_width)), True),
        "near_out": (shape((kept, pair, half)), True),
        "far_out": (shape((kept, pair, half)), True),
        "near_pre": (shape((kept, pair, hidden_width)), True),
        "far_pre": (shape((kept, pair, hidden_width)), True),
        "grad_out": (shape((kept, pair, width)), True),
    }
    low = {
        "pick_near": (2, kept * capacity, group_rows),
        "pick_far": (2, kept * capacity, group_rows),
        "buffer_near": (kept, pair, half),
        "buffer_far": (kept, pair, half),
        "hidden": (kept, pair, hidden_width),
        "weighted": (2, kept * capacity, width),
        "away": (kept, pair, hidden_width),
        "arrived": (kept, pair, hidden_width),
        "w_up": (2, kept, half, hidden_width),
        "w_near": (kept, hidden_width, half),
        "w_far": (kept, hidden_width, half),
        "part": (2, 2, 2, rows, width),
        "group": (8, rows, width),
        "sum_core": (chunks, 2, 2, rows, 256),
        "sum_xa": (chunks, 2, rows, 128),
        "sum_ya": (chunks, rows, 128),
        "sum_yb": (chunks, 2, rows, 128),
        "sum_xb": (chunks, rows, 128),
        "image_sum": (chunks, rows, 256),
        "image_far": (chunks, heads - 1, own, 256),
        "out_grad": (kept, pair, width),
        "slot_rows": (pair, width),
        "back_part": (2, 2, 2, rows, half),
        "core_in": (chunks, 2, 2, rows, 128),
        "y_in": (chunks, 2, rows, 128),
        "far": (chunks, heads - 1, 2, own, 128),
        "pair": (chunks, 2, own, 128),
        "x_in": (chunks, own, 128),
        "logit_grads": vmem["probs_own"].shape,
        "attended": (rows, width),
        "first_in": (rows, width),
        "projected_grad": (rows, qkv_width),
        "first_part": (heads, own, width),
        "dense": (8, block, dense_width),
        "dense_core": (4, block, dense_width),
        "xa": (2, block, cut),
        "ya": (block, cut),
        "yb": (2, block, dense_width - cut),
        "xb": (block, dense_width - cut),
        "first_far": (heads - 1, own, width),
        "rounded": (heads, own, width),
    }
    wide = {
        "gates": (kept, pair, 1),
        "own": (kept, pair, hidden_width),
        "final_grad": (own, width),
        "gate_rows": (2, kept, group_rows),
        "gate_in": (4, 2, kept, group_rows),
        "gate_sum": (2, kept, group_rows),
        "gate_all": (heads, 2, kept, rows),
        "logit_rows": (rows, width),
        "gain_part": (2, width),
        "gain_plane": (8, 2, width),
        "gain_heads": (heads, 2, width),
    }
    scratch = {name: pltpu.VMEM(dims, LOW) for name, dims in low.items()}
    scratch.update({name: pltpu.VMEM(dims, WIDE) for name, dims in wide.items()})
    copies = kept + late + chunks * (5 + GATHER_COPIES + 2 * (heads - 1)) + 2 * (heads - 1)
    copies += kept + 2 + chunks * (3 + heads - 1) + 3 + 2 * heads - 1 + heads - 1
    copies += SUM_COPIES + 3 * (heads - 1) + 7
    return named_call(
        lambda names, *refs: layer_kernel(heads, chunks, names, piece_names, *refs),
        ins,
        outs,
        scratch,
        copies,
        3 * kept + len(pieces) + 6,
        3,
        54,
        190,
    )


def finish_kernel(s, near, near_pre, far, far_pre, hidden, out_grad, *refs):
    pieces, (up, down) = refs[:-2], refs[-2:]
    i = pl.program_id(0)
    kept, half = pl.num_programs(0) // 2, down.shape[2]
    j = i - s[1]
    held = (j >= 0) & (j < kept)

    @pl.when(held)
    def _():
        up[0] = dot(near[0], near_pre[0], (0, 0))
        columns = pl.ds(pl.multiple_of(s[0] * half, half), half)
        down[0] = dot(hidden[0], out_grad[0, :, columns], (0, 0))

    @pl.when(jnp.logical_not(held))
    def _():
        up[0] = dot(far[0], far_pre[0], (0, 0))

    at = 0
    for piece in pieces:
        for k in range(piece.shape[0]):

            @pl.when(i - s[2] == at + k)
            def _(piece=piece, k=k):
                down[0] = piece[k].astype(WIDE)

        at += piece.shape[0]


def finish(scalars, near, near_pre, far, far_pre, hidden, out_grad, arrived):
    kept, _, half = near.shape
    hidden_width = near_pre.shape[2]

    def of(array, which):
        return pl.BlockSpec(
            (1, *array.shape[1:]), lambda i, s: (jnp.clip(i - s[which], 0, kept - 1), 0, 0)
        )

    def all_of(array):
        return pl.BlockSpec(array.shape, lambda i, s: (0, 0, 0))

    ins = [(near, 1), (near_pre, 1), (far, 2), (far_pre, 2), (hidden, 1), (out_grad, 1)]
    return pl.pallas_call(
        finish_kernel,
        out_shape=[
            shape((2 * kept, half, hidden_width), WIDE),
            shape((2 * kept, hidden_width, half), WIDE),
        ],
        grid_spec=pltpu.PrefetchScalarGridSpec(
            num_scalar_prefetch=1,
            grid=(2 * kept,),
            in_specs=[of(*a) for a in ins] + [all_of(piece) for piece in arrived],
            out_specs=[
                pl.BlockSpec((1, half, hidden_width), lambda i, s: (i, 0, 0)),
                pl.BlockSpec((1, hidden_width, half), lambda i, s: (i, 0, 0)),
            ],
        ),
        compiler_params=pltpu.CompilerParams(vmem_limit_bytes=60 * 2**20),
        cost_estimate=spends(8),
    )(scalars, *[a[0] for a in ins], *arrived)


def swap(values):
    return lax.ppermute(values, FSDP, [(0, 1), (1, 0)])


def fast(
    tokens,
    valid_mask,
    routes,
    teacher,
    gain_one,
    qkv_weight,
    out_weight,
    gain_two,
    router_weight,
    expert_up,
    expert_down,
):
    heads = lax.axis_size(HEADS)
    f, z = lax.axis_index(FSDP), lax.axis_index(HEADS)
    _, rows, width = tokens.shape
    block, head_count, qkv_dim = qkv_weight.shape
    head_dim = qkv_dim // 3
    local_experts = expert_up.shape[0]
    kept = local_experts // 2
    expert_count = local_experts * heads
    group_rows = 4 * rows
    capacity = 2 * routes.shape[2] * group_rows // expert_count
    total_tokens, total_images = 8 * rows, 8
    score_scale = head_dim ** (-0.5)

    mine, theirs = f * kept, (1 - f) * kept
    half = width // 2
    first_chunk, second_chunk = kept // 4, kept // 2
    down_a = lax.dynamic_slice_in_dim(expert_down, theirs, first_chunk, 0)
    down_a, qkv_weight = lax.optimization_barrier((down_a, qkv_weight))
    down_a = swap(down_a)

    qkv_width = head_count * qkv_dim
    pad = -(128 + qkv_width) % 256
    wq = jnp.concatenate(
        [
            router_weight,
            gain_one[:, None],
            gain_two[:, None],
            jnp.zeros((block, 128 - expert_count - 2), LOW),
            qkv_weight.reshape(block, qkv_width),
            jnp.zeros((block, pad), LOW),
        ],
        1,
    )
    wo = out_weight.reshape(head_count * head_dim, block).T
    count = jnp.full((8, 128), jnp.sum(valid_mask), jnp.int32)
    near_route = jnp.pad(routes.reshape(group_rows, -1).T, ((0, 8 - routes.shape[2]), (0, 0)))
    count, down_a = lax.optimization_barrier((count, down_a))
    gathered, wo_all, counts, far_route = gather_weights_fast(heads, wq, wo, count, near_route)
    gathered, down_b = lax.optimization_barrier(
        (gathered, lax.dynamic_slice_in_dim(expert_down, theirs + first_chunk, second_chunk, 0))
    )
    down_b = swap(down_b)
    gathered_blocks = gathered
    gathered = gathered.reshape(width, -1)
    qkv_full = gathered[:, 128 : 128 + qkv_width]
    lanes = jnp.arange(128)
    router_wide = jnp.where(lanes < expert_count, gathered[:, :128], 0)
    gain_a = gathered[:, expert_count].astype(WIDE)[None]
    gain_b = gathered[:, expert_count + 1].astype(WIDE)[None]
    valid_total = jnp.sum(counts[:, 0, 0]).astype(WIDE)

    inputs = tokens[0].astype(WIDE)
    normed_one, _ = normalize(inputs)
    first_in = (normed_one * gain_a).astype(LOW)
    projected = (
        jnp.dot(first_in, qkv_full, preferred_element_type=WIDE)
        .astype(LOW)
        .reshape(rows, head_count, qkv_dim)
    )
    queries = projected[..., :head_dim]
    key_rows = projected[..., head_dim : 2 * head_dim]
    values = projected[..., 2 * head_dim :]
    keys_ok = (valid_mask > 0)[0][None, None, :]

    def scores_now():
        raw = jnp.einsum("qhe,khe->hqk", queries, key_rows, preferred_element_type=WIDE)
        return jnp.where(keys_ok, raw * score_scale, MASKED)

    scores = scores_now()
    peak_score = jnp.max(scores, -1, keepdims=True)
    exp_scores = jnp.exp(scores - peak_score)
    score_total = jnp.sum(exp_scores, -1, keepdims=True)
    logarithm_total = peak_score + jnp.log(score_total)
    attention = (exp_scores / score_total).astype(LOW)
    mixed = (
        jnp.einsum("hqk,khe->qhe", attention, values, preferred_element_type=WIDE)
        .astype(LOW)
        .reshape(rows, head_count * head_dim)
    )
    residual, second_in, group_in, probs_all, slots, down_c = mix_heads(
        heads,
        expert_count,
        first_chunk + second_chunk,
        mixed,
        wo_all,
        tokens[0],
        gain_b,
        router_wide,
        near_route,
        far_route,
        expert_down,
    )
    group_in, down_b = lax.optimization_barrier((group_in, down_b))

    rows_in = group_in.reshape(2, group_rows, half)
    pieces = [down_a, down_b, down_c]
    me = f * 4 + lax.axis_index(TENSOR)
    valid_rows = valid_mask[0].astype(WIDE)[:, None]
    vmem = {
        "slots": slots,
        "x": rows_in,
        "probs": probs_all,
        "residual": residual,
        "teacher": teacher[0],
        "valid": valid_rows,
        "scale": jnp.full((8, 128), total_tokens / valid_total, WIDE),
        "gain": gain_b,
        "router": router_wide[:, :expert_count].T,
        "probs_own": lax.dynamic_index_in_dim(probs_all, me, 0, False),
        "tokens": tokens[0],
        "gain_one": gain_a,
        "second_in": second_in,
        "projected": projected.reshape(rows, qkv_width),
        "log_total": logarithm_total.reshape(head_count, rows).T,
        "mixed": mixed,
        "valid_row": valid_mask,
        "qkv": gathered_blocks,
        "wo": lax.dynamic_index_in_dim(wo_all, z, 1, False),
    }
    hbm = {"up": expert_up, "down": expert_down}
    made = layer(heads, capacity, head_count, pieces, vmem, hbm)
    result, tokens_grad, dense_out = made.result, made.tokens_grad, made.dense_out
    loss_terms = (jnp.sum(made.loss) * (total_images / (valid_total * width)))[None]
    own_gains = lax.dynamic_slice_in_dim(made.gain_out, me * block, block, 1)
    scalars = jnp.stack([f, mine, theirs]).astype(jnp.int32)
    up_grad, down_grad = finish(
        scalars,
        made.near_out,
        made.near_pre,
        made.far_out,
        made.far_pre,
        made.hidden_out,
        made.grad_out,
        [made.down_far],
    )
    out_width = head_count * head_dim
    return (
        result.reshape(1, rows, width),
        loss_terms,
        tokens_grad.reshape(1, rows, width),
        own_gains[0],
        dense_out[:, :qkv_width].reshape(block, head_count, qkv_dim),
        dense_out[:, qkv_width : qkv_width + out_width].T.reshape(head_count, head_dim, block),
        own_gains[1],
        dense_out[:, qkv_width + out_width :][:, :expert_count],
        up_grad,
        down_grad,
    )


def local(sizes, *args):
    tokens, routes, up = args[0], args[2], args[9]
    fits = (
        sizes[FSDP] == 2
        and sizes[TENSOR] == 4
        and sizes[HEADS] % 2 == 0
        and tokens.shape[0] == 1
        and up.shape[0] % 8 == 0
        and tokens.shape[1] % (32 * sizes[HEADS]) == 0
        and tokens.shape[2] % 256 == 0
        and routes.shape[2] <= 8
        and up.shape[0] * sizes[HEADS] <= 126
    )
    return fast(*args) if fits else general(*args)


def solution(mesh):
    sizes = dict(mesh.shape)
    program = functools.partial(local, sizes)
    in_specs = (
        P((FSDP, TENSOR), None, None),
        P((FSDP, TENSOR), None),
        P(FSDP, None, None),
        P((FSDP, TENSOR), None, None),
        P((FSDP, TENSOR)),
        P((FSDP, TENSOR), HEADS, None),
        P(HEADS, None, (FSDP, TENSOR)),
        P((FSDP, TENSOR)),
        P((FSDP, TENSOR), None),
        P(HEADS, FSDP, TENSOR),
        P(HEADS, TENSOR, FSDP),
    )
    out_specs = (
        P((FSDP, TENSOR), None, None),
        P((FSDP, TENSOR)),
        P((FSDP, TENSOR), None, None),
        P((FSDP, TENSOR)),
        P((FSDP, TENSOR), HEADS, None),
        P(HEADS, None, (FSDP, TENSOR)),
        P((FSDP, TENSOR)),
        P((FSDP, TENSOR), None),
        P(HEADS, FSDP, TENSOR),
        P(HEADS, TENSOR, FSDP),
    )
    return jax.shard_map(program, mesh=mesh, in_specs=in_specs, out_specs=out_specs, check_vma=False)
```

```python
import functools
import types

import jax
import jax.numpy as jnp
from jax import lax
from jax.experimental import pallas as pl
from jax.experimental.pallas import tpu as pltpu
from jax.sharding import PartitionSpec as P

FSDP, HEADS, TENSOR = "fsdp", "heads", "tensor"
EPSILON = 1e-06
MASKED = -1e30
ROOT_HALF = 0.7071067811865476
DENSITY = 0.3989422804014327


def normalize(values):
    center = values - jnp.mean(values, -1, keepdims=True)
    inv_std = lax.rsqrt(jnp.mean(center * center, -1, keepdims=True) + EPSILON)
    return (center * inv_std, inv_std)


def norm_back(gradient, normed, inv_std, gain_vector):
    weighted = gradient * gain_vector
    gain_grad = jnp.sum(gradient * normed, axis=(0, 1))
    inner = (
        weighted
        - jnp.mean(weighted, -1, keepdims=True)
        - normed * jnp.mean(weighted * normed, -1, keepdims=True)
    )
    return (inner * inv_std, gain_grad)


def scores_of(queries, key_rows, keys_ok, score_scale):
    raw_scores = (
        jnp.einsum("iqhe,ikhe->ihqk", queries, key_rows, preferred_element_type=jnp.float32)
        * score_scale
    )
    return jnp.where(keys_ok, raw_scores, MASKED)


def gather_weights(
    gain_one, qkv_weight, out_weight, gain_two, router_weight, expert_up, expert_down
):
    dense_set = (
        lax.all_gather(qkv_weight, (FSDP, TENSOR), axis=0, tiled=True),
        lax.all_gather(out_weight, (FSDP, TENSOR), axis=2, tiled=True),
        lax.all_gather(router_weight, (FSDP, TENSOR), axis=0, tiled=True),
        lax.all_gather(gain_one, (FSDP, TENSOR), axis=0, tiled=True),
        lax.all_gather(gain_two, (FSDP, TENSOR), axis=0, tiled=True),
    )
    expert_set = (
        lax.all_gather(expert_up, FSDP, axis=1, tiled=True),
        lax.all_gather(expert_down, FSDP, axis=2, tiled=True),
    )
    return (dense_set, expert_set)


def reduce_expert_grads(up_grad, down_grad):
    return (
        lax.psum_scatter(up_grad, FSDP, scatter_dimension=1, tiled=True),
        lax.psum_scatter(down_grad, FSDP, scatter_dimension=2, tiled=True),
    )


def general(
    tokens,
    valid_mask,
    routes,
    teacher,
    gain_one,
    qkv_weight,
    out_weight,
    gain_two,
    router_weight,
    expert_up,
    expert_down,
):
    valid_total = lax.psum(jnp.sum(valid_mask.astype(jnp.float32)), (FSDP, TENSOR))
    dense_set, expert_set = gather_weights(
        gain_one, qkv_weight, out_weight, gain_two, router_weight, expert_up, expert_down
    )
    qkv_full, output_complete, router_full, gain_a, gain_b = dense_set
    up_full, down_full = expert_set
    image_count, token_slots, model_width = tokens.shape
    head_dim = qkv_full.shape[2] // 3
    local_experts = expert_up.shape[0]
    tensor_size = lax.axis_size(TENSOR)
    group_images = image_count * tensor_size
    group_rows = group_images * token_slots
    top_choices = routes.shape[2]
    expert_count = local_experts * lax.axis_size(HEADS)
    capacity = 2 * top_choices * group_rows // expert_count
    slot_count = local_experts * capacity
    total_tokens = image_count * token_slots * lax.axis_size(FSDP) * tensor_size
    total_images = image_count * lax.axis_size(FSDP) * tensor_size
    score_scale = head_dim ** (-0.5)
    inputs = tokens.astype(jnp.float32)
    normed_one, spread_one = normalize(inputs)
    first_in = (normed_one * gain_a.astype(jnp.float32)).astype(jnp.bfloat16)
    projected = jnp.einsum(
        "isd,dhe->ishe", first_in, qkv_full, preferred_element_type=jnp.float32
    ).astype(jnp.bfloat16)
    queries = projected[..., :head_dim]
    key_rows = projected[..., head_dim : 2 * head_dim]
    values = projected[..., 2 * head_dim :]
    keys_ok = (valid_mask > 0)[:, None, None, :]
    scores = scores_of(queries, key_rows, keys_ok, score_scale)
    peak_score = jnp.max(scores, -1, keepdims=True)
    exp_scores = jnp.exp(scores - peak_score)
    score_total = jnp.sum(exp_scores, -1, keepdims=True)
    logarithm_total = peak_score + jnp.log(score_total)
    attention = (exp_scores / score_total).astype(jnp.bfloat16)
    combined_heads = jnp.einsum(
        "ihqk,ikhe->iqhe", attention, values, preferred_element_type=jnp.float32
    ).astype(jnp.bfloat16)
    attn_part = jnp.einsum(
        "iqhe,hed->iqd", combined_heads, output_complete, preferred_element_type=jnp.float32
    )
    attended = lax.psum(attn_part, HEADS)
    residual = inputs + attended
    normed_two, spread_two = normalize(residual)
    second_in = (normed_two * gain_b.astype(jnp.float32)).astype(jnp.bfloat16)
    group_in = lax.all_gather(second_in, TENSOR, axis=0, tiled=True)
    rows_in = group_in.reshape(group_rows, model_width)
    logits = jnp.dot(rows_in, router_full, preferred_element_type=jnp.float32)
    peak_logit = jnp.max(logits, -1, keepdims=True)
    exponent_logits = jnp.exp(logits - peak_logit)
    router_probs = exponent_logits / jnp.sum(exponent_logits, -1, keepdims=True)
    expert_ids = jnp.arange(expert_count, dtype=jnp.int32)
    route_pairs = routes.reshape(group_rows, top_choices)
    picked_hot = (route_pairs[:, :, None] == expert_ids[None, None, :]).astype(jnp.float32)
    gate_weight_values = jnp.sum(router_probs[:, None, :] * picked_hot, -1)
    flat_routes = route_pairs.reshape(group_rows * top_choices)
    route_hot = (flat_routes[:, None] == expert_ids[None, :]).astype(jnp.int32)
    order = jnp.arange(group_rows * top_choices, dtype=jnp.int32)
    before = (order[None, :] < order[:, None]).astype(jnp.bfloat16)
    earlier = jnp.dot(
        before, route_hot.astype(jnp.bfloat16), preferred_element_type=jnp.float32
    ).astype(jnp.int32)
    slot_index = jnp.sum(earlier * route_hot, 1)
    first_expert = lax.axis_index(HEADS) * local_experts
    is_local = (flat_routes >= first_expert) & (flat_routes < first_expert + local_experts)
    target = jnp.where(is_local, (flat_routes - first_expert) * capacity + slot_index, slot_count)
    owner_row = jnp.arange(group_rows * top_choices, dtype=jnp.int32) // top_choices
    source = jnp.zeros((slot_count,), jnp.int32).at[target].set(owner_row, mode="drop")
    slot_gate = (
        jnp.zeros((slot_count,), jnp.float32)
        .at[target]
        .set(gate_weight_values.reshape(-1), mode="drop")
    )
    slot_pick = jnp.minimum(target, slot_count - 1)
    retain_mask = is_local.astype(jnp.float32)
    dispatched = rows_in[source].reshape(local_experts, capacity, model_width)
    before_gelu = jnp.einsum(
        "ecd,edf->ecf", dispatched, up_full, preferred_element_type=jnp.float32
    )
    hidden = jax.nn.gelu(before_gelu, approximate=False).astype(jnp.bfloat16)
    expert_out = jnp.einsum(
        "ecf,efd->ecd", hidden, down_full, preferred_element_type=jnp.float32
    ).reshape(slot_count, model_width)
    weighted = expert_out * slot_gate[:, None]
    moe_part = jnp.sum(
        (weighted[slot_pick] * retain_mask[:, None]).reshape(group_rows, top_choices, model_width),
        1,
    )
    moe_part = moe_part.reshape(group_images, token_slots, model_width)
    expert_sum = lax.psum(
        lax.psum_scatter(moe_part, TENSOR, scatter_dimension=0, tiled=True), HEADS
    )
    final = residual + expert_sum
    valid_rows = valid_mask.astype(jnp.float32)[..., None]
    difference = (final - teacher.astype(jnp.float32)) * valid_rows
    loss_terms = jnp.sum(difference * difference, axis=(1, 2)) * (
        total_images / (valid_total * model_width)
    )
    final_grad = difference * (total_tokens / valid_total)
    dense_set, expert_set = gather_weights(
        gain_one, qkv_weight, out_weight, gain_two, router_weight, expert_up, expert_down
    )
    qkv_full, output_complete, router_full, gain_a, gain_b = dense_set
    up_full, down_full = expert_set
    moe_grad = final_grad.astype(jnp.bfloat16)
    group_grad = lax.all_gather(moe_grad, TENSOR, axis=0, tiled=True).reshape(
        group_rows, model_width
    )
    slot_grad = group_grad[source].astype(jnp.float32)
    gate_slot_grad = jnp.sum(slot_grad * expert_out, -1)
    out_grad = (
        (slot_grad * slot_gate[:, None])
        .astype(jnp.bfloat16)
        .reshape(local_experts, capacity, model_width)
    )
    expert_down_grad = jnp.einsum(
        "ecf,ecd->efd", hidden, out_grad, preferred_element_type=jnp.float32
    )
    hidden_grad = jnp.einsum(
        "ecd,efd->ecf", out_grad, down_full, preferred_element_type=jnp.float32
    )
    normal_cdf = 0.5 * (1.0 + lax.erf(before_gelu * ROOT_HALF))
    slope = normal_cdf + before_gelu * DENSITY * jnp.exp(-0.5 * before_gelu * before_gelu)
    pre_grad = (hidden_grad * slope).astype(jnp.bfloat16)
    expert_up_grad = jnp.einsum(
        "ecd,ecf->edf", dispatched, pre_grad, preferred_element_type=jnp.float32
    )
    row_grad = jnp.einsum(
        "ecf,edf->ecd", pre_grad, up_full, preferred_element_type=jnp.float32
    ).reshape(slot_count, model_width)
    rows_part = jnp.sum(
        (row_grad[slot_pick] * retain_mask[:, None]).reshape(group_rows, top_choices, model_width),
        1,
    )
    rows_part = rows_part.reshape(group_images, token_slots, model_width)
    gate_part = (gate_slot_grad[slot_pick] * retain_mask).reshape(
        group_images, token_slots, top_choices
    )
    rows_share, gate_share = (
        lax.psum_scatter(rows_part, TENSOR, scatter_dimension=0, tiled=True),
        lax.psum_scatter(gate_part, TENSOR, scatter_dimension=0, tiled=True),
    )
    second_grad, gate_grad = lax.psum((rows_share, gate_share), HEADS)
    own_start = lax.axis_index(TENSOR) * image_count * token_slots
    own_rows = image_count * token_slots
    own_probs = lax.dynamic_slice_in_dim(router_probs, own_start, own_rows, 0).reshape(
        image_count, token_slots, expert_count
    )
    own_hot = lax.dynamic_slice_in_dim(picked_hot, own_start, own_rows, 0).reshape(
        image_count, token_slots, top_choices, expert_count
    )
    prob_grad = jnp.sum(gate_grad[..., None] * own_hot, 2)
    logit_grad = (
        own_probs * (prob_grad - jnp.sum(own_probs * prob_grad, -1, keepdims=True))
    ).astype(jnp.bfloat16)
    router_grad = jnp.einsum(
        "isd,ise->de", second_in, logit_grad, preferred_element_type=jnp.float32
    )
    second_grad = second_grad + jnp.einsum(
        "ise,de->isd", logit_grad, router_full, preferred_element_type=jnp.float32
    )
    residual_norm, gain_two_grad = norm_back(
        second_grad, normed_two, spread_two, gain_b.astype(jnp.float32)
    )
    residual_grad = final_grad + residual_norm
    attended_output_gradient = residual_grad.astype(jnp.bfloat16)
    out_weight_grad = jnp.einsum(
        "iqhe,iqd->hed",
        combined_heads,
        attended_output_gradient,
        preferred_element_type=jnp.float32,
    )
    mixed_grad = jnp.einsum(
        "iqd,hed->iqhe",
        attended_output_gradient,
        output_complete,
        preferred_element_type=jnp.float32,
    ).astype(jnp.bfloat16)
    scores = scores_of(queries, key_rows, keys_ok, score_scale)
    probs = jnp.exp(scores - logarithm_total)
    probs_low = probs.astype(jnp.bfloat16)
    prob_part = jnp.einsum(
        "iqhe,ikhe->ihqk", mixed_grad, values, preferred_element_type=jnp.float32
    )
    score_grad = (probs * (prob_part - jnp.sum(probs * prob_part, -1, keepdims=True))).astype(
        jnp.bfloat16
    )
    query_grad = (
        jnp.einsum("ihqk,ikhe->iqhe", score_grad, key_rows, preferred_element_type=jnp.float32)
        * score_scale
    )
    key_grad = (
        jnp.einsum("ihqk,iqhe->ikhe", score_grad, queries, preferred_element_type=jnp.float32)
        * score_scale
    )
    value_grad = jnp.einsum(
        "ihqk,iqhe->ikhe", probs_low, mixed_grad, preferred_element_type=jnp.float32
    )
    projected_grad = jnp.concatenate([query_grad, key_grad, value_grad], -1).astype(jnp.bfloat16)
    qkv_grad = jnp.einsum(
        "isd,ishe->dhe", first_in, projected_grad, preferred_element_type=jnp.float32
    )
    first_part = jnp.einsum(
        "ishe,dhe->isd", projected_grad, qkv_full, preferred_element_type=jnp.float32
    )
    first_grad = lax.psum(first_part, HEADS)
    input_norm, gain_one_grad = norm_back(
        first_grad, normed_one, spread_one, gain_a.astype(jnp.float32)
    )
    tokens_grad = residual_grad + input_norm
    dense_grads = (
        lax.psum_scatter(qkv_grad, (FSDP, TENSOR), scatter_dimension=0, tiled=True),
        lax.psum_scatter(out_weight_grad, (FSDP, TENSOR), scatter_dimension=2, tiled=True),
        lax.psum_scatter(router_grad, (FSDP, TENSOR), scatter_dimension=0, tiled=True),
        lax.psum_scatter(gain_one_grad, (FSDP, TENSOR), scatter_dimension=0, tiled=True),
        lax.psum_scatter(gain_two_grad, (FSDP, TENSOR), scatter_dimension=0, tiled=True),
    )
    expert_grads = reduce_expert_grads(expert_up_grad, expert_down_grad)
    return (
        final.astype(jnp.bfloat16),
        loss_terms,
        tokens_grad,
        dense_grads[3],
        dense_grads[0],
        dense_grads[1],
        dense_grads[4],
        dense_grads[2],
        expert_grads[0],
        expert_grads[1],
    )


MESH = pl.DeviceIdType.MESH
LOW = jnp.bfloat16
WIDE = jnp.float32


class Links:
    def __init__(self, send_sems, recv_sems):
        self.send_sems, self.recv_sems = send_sems, recv_sems
        self.copies, self.gone = [], []

    def send(self, src, dst, device):
        k = len(self.copies)
        assert k < self.send_sems.shape[0]
        copy = pltpu.make_async_remote_copy(
            src_ref=src,
            dst_ref=dst,
            send_sem=self.send_sems.at[k],
            recv_sem=self.recv_sems.at[k],
            device_id=device,
            device_id_type=MESH,
        )
        copy.start()
        self.copies.append(copy)
        return copy

    def left(self, copies):
        for copy in copies:
            copy.wait_send()
            self.gone.append(copy)

    def drain(self):
        for copy in self.copies:
            if not any(copy is other for other in self.gone):
                copy.wait_send()


class Place:
    def __init__(self, heads):
        self.f = lax.axis_index(FSDP)
        t = lax.axis_index(TENSOR)
        self.y, self.c = t // 2, lax.rem(t, 2)
        self.z = lax.axis_index(HEADS)
        self.heads = heads
        self.x_peer = {FSDP: 1 - self.f}
        self.y_peer = {TENSOR: 2 * (1 - self.y) + self.c}
        self.core_peer = {TENSOR: 2 * self.y + 1 - self.c}
        self.z_peers = [{HEADS: lax.rem(self.z + k, heads)} for k in range(1, heads)]
        self.plane_peers = []
        for a in range(2):
            for k in range(4):
                if a or k:
                    where = {TENSOR: lax.rem(t + k, 4)}
                    if a:
                        where[FSDP] = 1 - self.f
                    self.plane_peers.append(where)

    def image(self, df, dy, dc):
        f = 1 - self.f if df else self.f
        y = 1 - self.y if dy else self.y
        c = 1 - self.c if dc else self.c
        return f * 4 + 2 * y + c

    def greet(self, devices):
        barrier = pltpu.get_barrier_semaphore()
        for device in devices:
            pl.semaphore_signal(barrier, inc=1, device_id=device, device_id_type=MESH)
        pl.semaphore_wait(barrier, len(devices))

    def tensor_peers(self):
        t = 2 * self.y + self.c
        return [{TENSOR: lax.rem(t + k, 4)} for k in range(1, 4)]

    def owners(self):
        return [
            {FSDP: 1 - self.f if a else self.f, HEADS: lax.rem(self.z + k, self.heads)}
            for k in range(self.heads)
            for a in range(2)
            if a or k
        ]

    def everyone(self):
        t = 2 * self.y + self.c
        corners = [{FSDP: 1 - self.f, TENSOR: lax.rem(t + k, 4)} for k in range(1, 4)]
        return self.tensor_peers() + self.owners() + corners

    def axis_peers(self):
        return [self.x_peer, self.y_peer, self.core_peer]


class PlaneGather:
    def __init__(self, links, place, first, second, whole):
        self.links, self.place = links, place
        self.first, self.second, self.whole = first, second, whole

    def go(self, part, image, device):
        return self.links.send(part(image), part(image), device)

    def start(self):
        p, me = self.place, self.place.image(0, 0, 0)
        self.xa = self.go(self.first, me, p.x_peer)
        self.yb = self.go(self.second, me, p.y_peer)
        self.own = self.go(self.whole, me, p.core_peer)
        self.xb = self.go(self.second, me, p.x_peer)
        self.ya = self.go(self.first, me, p.y_peer)

    def forward(self):
        p = self.place
        self.xa.wait_recv()
        self.fa = self.go(self.first, p.image(1, 0, 0), p.y_peer)
        self.yb.wait_recv()
        self.fb = self.go(self.second, p.image(0, 1, 0), p.x_peer)

    def share(self):
        p = self.place
        self.xb.wait_recv()
        self.c1 = self.go(self.whole, p.image(1, 0, 0), p.core_peer)
        self.ya.wait_recv()
        self.c2 = self.go(self.whole, p.image(0, 1, 0), p.core_peer)

    def finish(self):
        p = self.place
        self.fa.wait_recv()
        self.fb.wait_recv()
        self.c3 = self.go(self.whole, p.image(1, 1, 0), p.core_peer)
        for copy in (self.own, self.c1, self.c2, self.c3):
            copy.wait_recv()

    def run(self):
        self.start()
        self.forward()
        self.share()
        self.finish()


GATHER_COPIES = 10


def in_rows(rows, step, body):
    def one(i, carry):
        body(pl.ds(pl.multiple_of(i * step, step), step))
        return carry

    lax.fori_loop(0, rows // step, one, 0)


class PlaneSum:
    def __init__(self, links, place, part, core_in, xa, ya, yb, xb, cut, step):
        self.links, self.place, self.part, self.core_in = links, place, part, core_in
        self.xa, self.ya, self.yb, self.xb, self.cut, self.step = xa, ya, yb, xb, cut, step
        self.rows, self.width = part.shape[1], part.shape[2]
        self.a, self.b = pl.ds(0, cut), pl.ds(cut, self.width - cut)

    def start(self):
        p = self.place
        self.order = [(1, 1), (1, 0), (0, 1), (0, 0)]
        self.into = {}
        for df, dy in self.order:
            f = 1 - p.f if df else p.f
            y = 1 - p.y if dy else p.y
            self.into[df, dy] = self.links.send(
                self.part.at[p.image(df, dy, 1)], self.core_in.at[2 * f + y], p.core_peer
            )

    def slot(self, df, dy):
        p = self.place
        return 2 * (1 - p.f if df else p.f) + (1 - p.y if dy else p.y)

    def cores(self):
        p, rc = self.place, self.core_in
        self.got = {}
        for df, dy in self.order:
            self.into[df, dy].wait_recv()
            j, mine = self.slot(df, dy), p.image(df, dy, 0)

            def add(rows, j=j, mine=mine):
                both = rc[j, rows, :].astype(WIDE) + self.part[mine, rows, :].astype(WIDE)
                rc[j, rows, :] = both.astype(LOW)

            in_rows(self.rows, self.step, add)
            y = 1 - p.y if dy else p.y
            f = 1 - p.f if df else p.f
            if df:
                self.got["x", dy] = self.links.send(rc.at[j, :, self.a], self.xa.at[y], p.x_peer)
            if dy:
                self.got["y", df] = self.links.send(rc.at[j, :, self.b], self.yb.at[f], p.y_peer)

    def cross(self):
        p, rc, xa, yb = self.place, self.core_in, self.xa, self.yb
        self.got["x", 1].wait_recv()
        j, other = self.slot(0, 1), 1 - p.y

        def add_a(rows):
            both = xa[other, rows, :].astype(WIDE) + rc[j, rows, self.a].astype(WIDE)
            xa[other, rows, :] = both.astype(LOW)

        in_rows(self.rows, self.step, add_a)
        self.last_a = self.links.send(xa.at[other], self.ya, p.y_peer)
        self.got["y", 1].wait_recv()
        k, away = self.slot(1, 0), 1 - p.f

        def add_b(rows):
            both = yb[away, rows, :].astype(WIDE) + rc[k, rows, self.b].astype(WIDE)
            yb[away, rows, :] = both.astype(LOW)

        in_rows(self.rows, self.step, add_b)
        self.last_b = self.links.send(yb.at[away], self.xb, p.x_peer)

    def finish(self, take):
        p, rc = self.place, self.core_in
        self.got["x", 0].wait_recv()
        self.got["y", 0].wait_recv()
        self.last_a.wait_recv()
        self.last_b.wait_recv()
        j, y, f = self.slot(0, 0), p.y, p.f

        def add(rows):
            first = rc[j, rows, self.a].astype(WIDE) + self.xa[y, rows, :].astype(WIDE)
            second = rc[j, rows, self.b].astype(WIDE) + self.yb[f, rows, :].astype(WIDE)
            take(rows, self.a, first + self.ya[rows, :].astype(WIDE))
            take(rows, self.b, second + self.xb[rows, :].astype(WIDE))

        in_rows(self.rows, self.step, add)


SUM_COPIES = 10


def sum_scratch(rows, width, cut):
    return [
        pltpu.VMEM((4, rows, width), LOW),
        pltpu.VMEM((2, rows, cut), LOW),
        pltpu.VMEM((rows, cut), LOW),
        pltpu.VMEM((2, rows, width - cut), LOW),
        pltpu.VMEM((rows, width - cut), LOW),
    ]


def all_heads(links, place, make):
    copies = []
    for k, device in enumerate(place.z_peers):
        src, dst = make(k, device[HEADS])
        copies.append(links.send(src, dst, device))
    return copies


def spends(microseconds):
    return pl.CostEstimate(flops=0, bytes_accessed=microseconds * 3_000_000, transcendentals=0)


def shape(dims, dtype=LOW):
    return jax.ShapeDtypeStruct(dims, dtype)


class ChunkSum:
    def __init__(self, links, place, part, columns, core_in, xa, ya, yb, xb):
        self.links, self.place, self.part, self.columns = links, place, part, columns
        self.core_in, self.xa, self.ya, self.yb, self.xb = core_in, xa, ya, yb, xb
        self.rows, self.half = core_in.shape[2], core_in.shape[3] // 2
        self.a, self.b = pl.ds(0, self.half), pl.ds(self.half, self.half)

    def start(self):
        p = self.place
        self.into = self.links.send(
            self.part.at[:, :, 1 - p.c, :, self.columns], self.core_in, p.core_peer
        )

    def cores(self):
        p, rc = self.place, self.core_in
        self.into.wait_recv()

        def add(rows):
            here = self.part[:, :, p.c, rows, self.columns].astype(WIDE)
            rc[:, :, rows, :] = (rc[:, :, rows, :].astype(WIDE) + here).astype(LOW)

        in_rows(self.rows, 32, add)
        self.to_x = self.links.send(rc.at[1 - p.f, :, :, self.a], self.xa, p.x_peer)
        self.to_y = self.links.send(rc.at[:, 1 - p.y, :, self.b], self.yb, p.y_peer)

    def cross(self):
        p, rc, xa, yb = self.place, self.core_in, self.xa, self.yb
        self.to_x.wait_recv()
        y, f = 1 - p.y, 1 - p.f

        def add_a(rows):
            both = xa[y, rows, :].astype(WIDE) + rc[p.f, y, rows, self.a].astype(WIDE)
            xa[y, rows, :] = both.astype(LOW)

        in_rows(self.rows, 64, add_a)
        self.last_a = self.links.send(xa.at[y], self.ya, p.y_peer)
        self.to_y.wait_recv()

        def add_b(rows):
            both = yb[f, rows, :].astype(WIDE) + rc[f, p.y, rows, self.b].astype(WIDE)
            yb[f, rows, :] = both.astype(LOW)

        in_rows(self.rows, 64, add_b)
        self.last_b = self.links.send(yb.at[f], self.xb, p.x_peer)

    def finish(self, take):
        p, rc = self.place, self.core_in
        self.last_a.wait_recv()
        self.last_b.wait_recv()

        def add(rows):
            first = rc[p.f, p.y, rows, self.a].astype(WIDE) + self.xa[p.y, rows, :].astype(WIDE)
            second = rc[p.f, p.y, rows, self.b].astype(WIDE) + self.yb[p.f, rows, :].astype(WIDE)
            take(rows, 0, first + self.ya[rows, :].astype(WIDE))
            take(rows, 1, second + self.xb[rows, :].astype(WIDE))

        in_rows(self.rows, 64, add)


def skewed(chunks, stages):
    for step in range(chunks + len(stages) - 1):
        for k in range(chunks):
            if 0 <= step - k < len(stages):
                stages[step - k](k)


def combine_part(place, links, chunks, r):
    heads, z, me = place.heads, place.z, place.image(0, 0, 0)
    part, residual, teacher, valid, scale = r.part, r.residual, r.teacher, r.valid, r.scale
    result, final_grad, group, loss = r.result, r.final_grad, r.group, r.loss
    image_sum, far = r.image_sum, r.image_far
    rows_all, width = residual.shape
    own = rows_all // heads
    wide = width // chunks
    half = wide // 2
    mine = pl.ds(pl.multiple_of(z * own, own), own)
    columns = [pl.ds(k * wide, wide) for k in range(chunks)]
    adders = [
        ChunkSum(
            links,
            place,
            part,
            columns[k],
            r.sum_core.at[k],
            r.sum_xa.at[k],
            r.sum_ya.at[k],
            r.sum_yb.at[k],
            r.sum_xb.at[k],
        )
        for k in range(chunks)
    ]
    for adder in adders:
        adder.start()
    along, spread, squares = {}, {}, []
    gathers = [
        PlaneGather(
            links,
            place,
            lambda i, k=k: group.at[i, :, pl.ds(k * wide, half)],
            lambda i, k=k: group.at[i, :, pl.ds(k * wide + half, half)],
            lambda i, k=k: group.at[i, :, columns[k]],
        )
        for k in range(chunks)
    ]

    def to_heads(k):
        def keep(rows, part_of, values):
            image_sum[k, rows, pl.ds(part_of * half, half)] = values.astype(LOW)

        adders[k].finish(keep)
        along[k] = all_heads(
            links,
            place,
            lambda n, to: (
                image_sum.at[k, pl.ds(pl.multiple_of(to * own, own), own)],
                far.at[k, n],
            ),
        )

    def final(k):
        for copy in along[k]:
            copy.wait_recv()
        total = image_sum[k, mine, :].astype(WIDE)
        for n in range(heads - 1):
            total = total + far[k, n].astype(WIDE)
        values = residual[mine, columns[k]] + total
        result[z, :, columns[k]] = values.astype(LOW)
        error = (values - teacher[mine, columns[k]].astype(WIDE)) * valid[mine, 0:1]
        grad = error * scale[0:1, 0:1]
        final_grad[:, columns[k]] = grad
        group[me, mine, columns[k]] = grad.astype(LOW)
        block = group.at[me, mine, columns[k]]
        spread[k] = all_heads(links, place, lambda n, to: (block, block))
        square = jnp.sum((error * error).reshape(own // 8, 8, wide), axis=0)
        squares.extend(square[:, i * 128 : (i + 1) * 128] for i in range(wide // 128))

    def to_plane(k):
        for copy in spread[k]:
            copy.wait_recv()
        gathers[k].start()

    def forward(k):
        gathers[k].forward()
        gathers[k].share()

    skewed(
        chunks,
        [
            lambda k: adders[k].cores(),
            lambda k: adders[k].cross(),
            to_heads,
            final,
            to_plane,
            forward,
        ],
    )
    loss[z] = sum(squares) * r.loss_scale[0:1, 0:1]
    extra = all_heads(links, place, lambda k, to: (result.at[z], result.at[z]))
    extra += all_heads(links, place, lambda k, to: (loss.at[z], loss.at[z]))
    for gather in gathers:
        gather.finish()
    return extra


def dot(a, b, over=(1, 0)):
    return lax.dot_general(a, b, (((over[0],), (over[1],)), ((), ())), preferred_element_type=WIDE)


def one_hot(slots, row, capacity):
    places = lax.broadcasted_iota(jnp.int32, (capacity, slots.shape[1]), 0)
    return places == slots[pl.ds(row, 1), :]


class Loads:
    def __init__(self, sems):
        self.sems, self.count = sems, 0

    def start(self, src, dst):
        assert self.count < self.sems.shape[0]
        copy = pltpu.make_async_copy(src, dst, self.sems.at[self.count])
        self.count += 1
        copy.start()
        return copy


def gelu_parts(values):
    cdf = 0.5 * (1.0 + lax.erf(values * ROOT_HALF))
    return values * cdf, cdf + values * DENSITY * jnp.exp(-0.5 * values * values)


def front_part(place, links, r):
    heads, f, z, me = place.heads, place.f, place.z, place.image(0, 0, 0)
    oq, oo, counts, slots = r.qkv, r.wo_all, r.counts, r.slots
    kept = r.w_far.shape[0]
    theirs = (1 - f) * kept
    oq[me] = r.shard[...]
    oo[me, z] = r.wo_shard[...]
    counts[me] = jnp.broadcast_to(jnp.sum(r.valid_row[...].astype(WIDE), -1, keepdims=True), (8, 128))
    half, mid = oq.shape[2] // 2, heads // 2
    main = PlaneGather(
        links,
        place,
        lambda i: oq.at[i, :, pl.ds(0, half)],
        lambda i: oq.at[i, :, pl.ds(half, half)],
        lambda i: oq.at[i],
    )
    side = PlaneGather(
        links,
        place,
        lambda i: oo.at[i, pl.ds(0, mid)],
        lambda i: oo.at[i, pl.ds(mid, heads - mid)],
        lambda i: oo.at[i],
    )

    def bulk(i):
        return links.send(r.down.at[theirs + i], r.w_far.at[i], place.x_peer)

    main.start()
    along = all_heads(links, place, lambda k, to: (oo.at[me, z], oo.at[me, z]))
    small = [links.send(counts.at[me], counts.at[me], d) for d in place.plane_peers]
    small.append(links.send(r.near_route, r.far_route, place.x_peer))
    main.forward()
    for copy in along:
        copy.wait_recv()
    side.start()
    down = [bulk(0)]
    main.share()
    main.finish()
    width = r.tokens.shape[1]
    experts = r.probs.shape[1]
    narrow = oq[:, :, 0:128].reshape(width, 128).astype(WIDE)
    turned = jnp.transpose(narrow)
    r.router[...] = turned[:experts].astype(LOW)
    r.gain_one[...] = turned[experts : experts + 1]
    r.gain[...] = turned[experts + 1 : experts + 2]
    rows_all = r.tokens.shape[0]

    def first_norm(rows):
        normed, _ = normalize(r.tokens[rows, :].astype(WIDE))
        r.first_in[rows, :] = (normed * r.gain_one[...]).astype(LOW)

    in_rows(rows_all, 64, first_norm)
    qkv_width = r.projected.shape[1]
    weight = oq[:, :, pl.ds(128, qkv_width)].reshape(width, qkv_width)
    r.projected[...] = dot(r.first_in[...], weight).astype(LOW)
    side.forward()
    down.append(bulk(1))
    head_count = r.log_total.shape[1]
    size = qkv_width // head_count // 3
    keys_ok = r.valid_row[...] > 0
    mixed = []
    for h in range(head_count):
        at = 3 * h * size
        query, key, value = (r.projected[:, at + n * size : at + (n + 1) * size] for n in range(3))
        scores = jnp.where(keys_ok, dot(query, key, (1, 1)) * size ** (-0.5), MASKED)
        peak = jnp.max(scores, -1, keepdims=True)
        powers = jnp.exp(scores - peak)
        total = jnp.sum(powers, -1, keepdims=True)
        r.log_total[:, h : h + 1] = peak + jnp.log(total)
        mixed.append(dot((powers / total).astype(LOW), value).astype(LOW))
    r.mixed[...] = jnp.concatenate(mixed, 1)
    everyone = r.all_mixed
    everyone[z] = r.mixed[...]
    along = all_heads(links, place, lambda k, to: (everyone.at[z], everyone.at[z]))
    side.share()
    for copy in small:
        copy.wait_recv()
    valid_total = sum(counts[i] for i in range(8))[0:1, 0:1]
    r.scale[...] = jnp.broadcast_to(8 * rows_all / valid_total, (8, 128))
    r.loss_scale[...] = jnp.broadcast_to(8 / (valid_total * width), (8, 128))
    column = jnp.broadcast_to(r.valid_row[...].astype(WIDE), (8, rows_all))
    r.valid[...] = jnp.transpose(column)
    local_experts = 2 * kept
    ids = z * local_experts + lax.broadcasted_iota(jnp.int32, (local_experts, 1), 0)
    first = f == 0
    near, far = r.near_route[...], r.far_route[...]
    both = [jnp.where(first, near, far), jnp.where(first, far, near)]
    chosen = []
    for route in both:
        hits = route[0:1] == ids
        for c in range(1, r.choices):
            hits = hits | (route[c : c + 1] == ids)
        chosen.append(hits)
    chosen = jnp.concatenate(chosen, 0)
    count = chosen.astype(WIDE)
    before = lax.broadcasted_iota(jnp.int32, (128, 128), 0)
    before = (before < lax.broadcasted_iota(jnp.int32, (128, 128), 1)).astype(LOW)
    running = jnp.zeros((2 * local_experts, 1), WIDE)
    for b in range(slots.shape[1] // 128):
        columns = slice(b * 128, (b + 1) * 128)
        here = count[:, columns]
        slot = dot(here.astype(LOW), before) + running
        slots[:, columns] = jnp.where(chosen[:, columns], slot, -1.0).astype(jnp.int32)
        running = running + jnp.sum(here, -1, keepdims=True)
    for copy in along:
        copy.wait_recv()
    side.finish()
    half = width // 2
    total = jnp.zeros((rows_all, width), WIDE)
    for n in range(heads):
        weight = oo[:, n].reshape(width, oo.shape[3])
        total = total + dot(everyone[n], weight, (1, 1))
    r.residual[...] = total

    def norm(rows):
        values = r.tokens[rows, :].astype(WIDE) + r.residual[rows, :]
        r.residual[rows, :] = values
        normed, _ = normalize(values)
        r.second_in[rows, :] = (normed * r.gain[...]).astype(LOW)

    in_rows(rows_all, 64, norm)
    low, high = r.second_in[:, :half], r.second_in[:, half:]

    def part_of(df, dy, dc):
        return r.x.at[
            1 - f if df else f, 1 - place.y if dy else place.y, 1 - place.c if dc else place.c
        ]

    mine, across, beside, corner = (
        part_of(0, 0, 0),
        part_of(1, 0, 0),
        part_of(0, 1, 0),
        part_of(1, 1, 0),
    )
    mine[...] = jnp.where(first, low, high)
    r.other_half[...] = jnp.where(first, high, low)
    x1 = links.send(r.other_half, mine, place.x_peer)
    y1 = links.send(mine, mine, place.y_peer)
    shared = [links.send(mine, mine, place.core_peer)]
    down.append(bulk(2))
    logits = dot(r.router[...], r.second_in[...], (1, 1))
    powers = jnp.exp(logits - jnp.max(logits, 0, keepdims=True))
    probs = powers / jnp.sum(powers, 0, keepdims=True)
    r.probs_own[...] = probs
    r.probs[me] = probs
    small = [links.send(r.probs.at[me], r.probs.at[me], d) for d in place.plane_peers]
    x1.wait_recv()
    y2 = links.send(across, across, place.y_peer)
    shared.append(links.send(across, across, place.core_peer))
    y1.wait_recv()
    shared.append(links.send(beside, beside, place.core_peer))
    y2.wait_recv()
    shared.append(links.send(corner, corner, place.core_peer))
    for copy in shared + small:
        copy.wait_recv()
    return [y1, y2, *shared], down


FRONT_COPIES = 2 * GATHER_COPIES + 7 + 1 + 1 + 2 + 4 + 7


def experts_part(place, links, loads, weights, down_far, r):
    slots, probs = r.slots, r.probs
    pick_near, pick_far, gates, hidden = r.pick_near, r.pick_far, r.gates, r.hidden
    buffer_near, buffer_far, own, weighted = r.buffer_near, r.buffer_far, r.own, r.weighted
    away, arrived, w_up, w_near, w_far = r.away, r.arrived, r.w_up, r.w_near, r.w_far
    kept, pair, _ = own.shape
    capacity, half = pair // 2, r.x.shape[4]
    group_rows = slots.shape[1]
    stores = []

    def kept_rows(i, buffer, target):
        stores.append(loads.start(buffer.at[i % 2], target.at[i]))

    local_experts = 2 * kept
    mine, theirs = place.f * kept, (1 - place.f) * kept
    ups, nears = weights
    sent = []
    for i in range(kept):
        if i > 1:
            stores[i - 2].wait()
        for g in range(2):
            rows = slice(i * capacity, (i + 1) * capacity)
            hot = one_hot(slots, g * local_experts + theirs + i, capacity).astype(LOW)
            pick_far[g, rows] = hot
            x = r.x[g].reshape(group_rows, half)
            buffer_far[i % 2, g * capacity : (g + 1) * capacity] = dot(hot, x).astype(LOW)
        ups[1, i].wait()
        kept_rows(i, buffer_far, r.far_out)
        away[i] = dot(buffer_far[i % 2], w_up[1, i]).astype(LOW)
        sent.append(links.send(away.at[i], arrived.at[i], place.x_peer))
    down_far = [
        *down_far,
        *(
            links.send(r.down.at[theirs + i], w_far.at[i], place.x_peer)
            for i in range(len(down_far), kept)
        ),
    ]
    for i in range(kept):
        expert = place.z * local_experts + mine + i
        if i > 1:
            stores[kept + i - 2].wait()
        for g in range(2):
            rows = slice(i * capacity, (i + 1) * capacity)
            into = slice(g * capacity, (g + 1) * capacity)
            hot = one_hot(slots, g * local_experts + mine + i, capacity)
            chances = [probs[4 * g + k, pl.ds(expert, 1), :] for k in range(4)]
            chances = jnp.concatenate(chances, 1)
            gates[i, into] = jnp.sum(jnp.where(hot, chances, 0.0), -1, keepdims=True)
            pick_near[g, rows] = hot.astype(LOW)
            x = r.x[g].reshape(group_rows, half)
            buffer_near[i % 2, into] = dot(hot.astype(LOW), x).astype(LOW)
        ups[0, i].wait()
        kept_rows(i, buffer_near, r.near_out)
        own[i] = dot(buffer_near[i % 2], w_up[0, i])
    for copy in nears:
        copy.wait()
    for i in range(kept):
        sent[i].wait_recv()
        down_far[i].wait_recv()
        values, slopes = gelu_parts(own[i] + arrived[i].astype(WIDE))
        hidden[i] = values.astype(LOW)
        own[i] = slopes
        for weight, f in ((w_near, place.f), (w_far, 1 - place.f)):
            out = (dot(hidden[i], weight[i]) * gates[i]).astype(LOW)
            columns = pl.ds(pl.multiple_of(f * half, half), half)
            for g in range(2):
                rows = slice(i * capacity, (i + 1) * capacity)
                weighted[g, rows, columns] = out[g * capacity : (g + 1) * capacity]
    for g in range(2):
        total = dot(pick_near[g], weighted[g], (0, 0)).astype(LOW)
        r.part[g] = total.reshape(r.part.shape[1:])
    links.left(sent)
    return stores[kept - 2 : kept] + stores[2 * kept - 2 :]


def experts_back_part(place, links, loads, r):
    pick_near, pick_far, hidden, slope, gates = r.pick_near, r.pick_far, r.hidden, r.own, r.gates
    w_up, w_near, w_far, group = r.w_up, r.w_near, r.w_far, r.group
    pre_near, pre_far, out_grad = r.away, r.arrived, r.out_grad
    side = r.weighted.shape[2] // 2
    rows_near = r.weighted.at[:, :, pl.ds(0, side)]
    rows_far = r.weighted.at[:, :, pl.ds(side, side)]
    send_held = r.w_far
    kept, pair, width = out_grad.shape
    capacity, half = pair // 2, width // 2
    first = pl.ds(pl.multiple_of(place.f * half, half), half)
    second = pl.ds(pl.multiple_of((1 - place.f) * half, half), half)
    sent = []
    for i in range(kept):
        rows = slice(i * capacity, (i + 1) * capacity)
        for g in range(2):
            rows_in = group[4 * g : 4 * g + 4].reshape(pick_near.shape[2], width)
            r.slot_rows[g * capacity : (g + 1) * capacity] = dot(
                pick_near[g, rows], rows_in
            ).astype(LOW)
        raw = dot(r.slot_rows[:, first], w_near[i], (1, 1))
        raw = raw + dot(r.slot_rows[:, second], w_far[i], (1, 1))
        pre_near[i] = (raw * gates[i] * slope[i]).astype(LOW)
        sent.append(links.send(pre_near.at[i], pre_far.at[i], place.x_peer))
        out_grad[i] = (r.slot_rows[...].astype(WIDE) * gates[i]).astype(LOW)
        gate_grad = jnp.sum(raw * hidden[i].astype(WIDE), -1, keepdims=True)
        for g in range(2):
            terms = gate_grad[g * capacity : (g + 1) * capacity]
            terms = terms * pick_near[g, rows].astype(WIDE)
            r.gate_rows[g, i : i + 1] = jnp.sum(terms, 0, keepdims=True)
    bulk = []
    for i in range(kept):
        send_held[i] = dot(hidden[i], out_grad[i, :, second], (0, 0)).astype(LOW)
    early = pl.ds(0, kept // 2)
    bulk = [links.send(send_held.at[early], r.down_far.at[early], place.x_peer)]
    stores = [
        loads.start(r.hidden, r.hidden_out),
        loads.start(pre_near, r.near_pre),
        loads.start(out_grad, r.grad_out),
    ]

    def through_up(far, i, pre, rows_out):
        back = dot(pre[i], w_up[far, i], (1, 1)).astype(LOW)
        rows = slice(i * capacity, (i + 1) * capacity)
        for g in range(2):
            rows_out[g, rows] = back[g * capacity : (g + 1) * capacity]

    for i in range(kept):
        through_up(0, i, pre_near, rows_near)
    for i in range(kept):
        sent[i].wait_recv()
        through_up(1, i, pre_far, rows_far)
    stores.append(loads.start(pre_far, r.far_pre))
    for g in range(2):
        near = dot(pick_near[g], rows_near[g], (0, 0))
        both = (near + dot(pick_far[g], rows_far[g], (0, 0))).astype(LOW)
        r.x[g] = both.reshape(r.x.shape[1:])
    return stores, bulk


def back_part(place, links, chunks, bulk, r):
    heads, f, y, z = place.heads, place.f, place.y, place.z
    t, me = 2 * y + place.c, place.image(0, 0, 0)
    part, gate_part, probs, valid = r.x, r.gate_rows, r.probs_own, r.valid_row
    residual, gain, router, final_grad, tokens = (r.residual, r.gain, r.router, r.final_grad, r.tokens)
    gain_one, second_in, projected, log_total, mixed = (r.gain_one, r.second_in, r.projected, r.log_total, r.mixed)
    qkv, wo, tokens_grad, dense_out, gain_out = (r.qkv, r.wo_all, r.tokens_grad, r.dense_out, r.gain_out)
    core_in, y_in, far, pair, x_in = (r.core_in, r.y_in, r.far, r.pair, r.x_in)
    gate_in, gate_sum, gate_all, logit_rows, logit_grads = (r.gate_in, r.gate_sum, r.gate_all, r.logit_rows, r.logit_grads)
    attended, first_in, projected_grad, first_part, dense = (r.attended, r.first_in, r.projected_grad, r.first_part, r.dense)
    dense_core, xa, ya, yb, xb = (r.dense_core, r.xa, r.ya, r.yb, r.xb)
    first_far, rounded, gain_part, gain_plane, gain_heads = (r.first_far, r.rounded, r.gain_part, r.gain_plane, r.gain_heads)
    tensor_peers, owners = place.tensor_peers(), place.owners()
    rows_all, width = residual.shape
    half = width // 2
    own = rows_all // heads
    into, beside, along, cross = {}, {}, {}, {}
    for k in range(chunks):
        source = part.at[:, :, 1 - place.c, :, pl.ds(k * 128, 128)]
        into[k] = links.send(source, core_in.at[k], place.core_peer)
    gate_in[t] = gate_part[...]
    shared = [links.send(gate_part, gate_in.at[t], d) for d in tensor_peers]
    mine = pl.ds(pl.multiple_of(z * own, own), own)

    def to_y(k):
        into[k].wait_recv()
        rc = core_in.at[k]

        def add(rows):
            here = part[:, :, place.c, rows, pl.ds(k * 128, 128)].astype(WIDE)
            rc[:, :, rows, :] = (rc[:, :, rows, :].astype(WIDE) + here).astype(LOW)

        in_rows(rows_all, 32, add)
        beside[k] = links.send(rc.at[:, 1 - y], y_in.at[k], place.y_peer)

    def to_heads(k):
        beside[k].wait_recv()

        def add(rows):
            both = y_in[k, :, rows, :].astype(WIDE) + core_in[k, :, y, rows, :].astype(WIDE)
            y_in[k, :, rows, :] = both.astype(LOW)

        in_rows(rows_all, 64, add)
        along[k] = all_heads(
            links,
            place,
            lambda n, to: (
                y_in.at[k, :, pl.ds(pl.multiple_of(to * own, own), own)],
                far.at[k, n],
            ),
        )

    def to_x(k):
        for copy in along[k]:
            copy.wait_recv()
        total = y_in[k, :, mine, :].astype(WIDE)
        for n in range(heads - 1):
            total = total + far[k, n].astype(WIDE)
        pair[k] = total.astype(LOW)
        cross[k] = links.send(pair.at[k, 1 - f], x_in.at[k], place.x_peer)

    to_y(0)
    for copy in shared:
        copy.wait_recv()
    gate_sum[...] = sum(gate_in[k] for k in range(4))
    kept = gate_sum.shape[1]
    rows_of = pl.ds(pl.multiple_of(t * rows_all, rows_all), rows_all)
    gate_all[z, f] = gate_sum[f, :, rows_of]
    spread = [
        links.send(gate_sum.at[d[FSDP], :, rows_of], gate_all.at[z, f], d) for d in owners
    ]
    to_y(1)
    to_heads(0)
    for k in range(2, chunks):
        to_y(k)
        to_heads(k - 1)
        to_x(k - 2)
    for copy in spread:
        copy.wait_recv()
    chances = probs[...]
    prob_grad = gate_all[...].reshape(2 * heads * kept, rows_all)
    logit_grad = chances * (prob_grad - jnp.sum(chances * prob_grad, 0, keepdims=True))
    logit_grads[...] = logit_grad.astype(LOW)
    logit_rows[...] = dot(logit_grads[...], router[...], (0, 0))
    normed, spread_two = normalize(residual[mine, :])
    router_grad = dot(second_in[...], logit_grads[...], (0, 1))
    spare = jnp.zeros((width, 128 - router_grad.shape[1]), WIDE)
    router_grad = jnp.concatenate([router_grad, spare], 1).astype(LOW)
    blocks, block = dense.shape[:2]
    qkv_width = projected.shape[1]
    dense_width = dense.shape[2]
    dense[:, :, pl.ds(dense_width - 128, 128)] = router_grad.reshape(blocks, block, 128)

    to_heads(chunks - 1)
    to_x(chunks - 2)
    to_x(chunks - 1)
    early = r.w_far.shape[0] // 2
    late = pl.ds(early, r.w_far.shape[0] - early)
    bulk.append(links.send(r.w_far.at[late], r.down_far.at[late], place.x_peer))
    near = jnp.concatenate([pair[k, f].astype(WIDE) for k in range(chunks)], 1)
    for k in range(chunks):
        cross[k].wait_recv()
    away = jnp.concatenate([x_in[k].astype(WIDE) for k in range(chunks)], 1)
    first = f == 0
    rows_grad = jnp.concatenate([jnp.where(first, near, away), jnp.where(first, away, near)], 1)
    second_grad = rows_grad + logit_rows[mine, :]
    weighted = second_grad * gain[...]
    gain_part[1:2, :] = jnp.sum(second_grad * normed, 0, keepdims=True)
    inner = (
        weighted
        - jnp.mean(weighted, -1, keepdims=True)
        - normed * jnp.mean(weighted * normed, -1, keepdims=True)
    )
    total_grad = final_grad[...] + inner * spread_two
    attended[mine, :] = total_grad.astype(LOW)
    for copy in all_heads(
        links, place, lambda k, to: (attended.at[mine], attended.at[mine])
    ):
        copy.wait_recv()

    mixed_grad = dot(attended[...], wo[:, z].reshape(width, wo.shape[3])).astype(LOW)
    head_count = log_total.shape[1]
    size = qkv_width // head_count // 3
    score_scale = size ** (-0.5)
    keys_ok = valid[...] > 0
    grads = []
    for h in range(head_count):
        at = 3 * h * size
        query, key, value = (projected[:, at + n * size : at + (n + 1) * size] for n in range(3))
        above = mixed_grad[:, h * size : (h + 1) * size]
        scores = jnp.where(keys_ok, dot(query, key, (1, 1)) * score_scale, MASKED)
        chances = jnp.exp(scores - log_total[:, h : h + 1])
        prob_part = dot(above, value, (1, 1))
        inner = jnp.sum(chances * prob_part, -1, keepdims=True)
        score_grad = (chances * (prob_part - inner)).astype(LOW)
        grads.append(dot(score_grad, key) * score_scale)
        grads.append(dot(score_grad, query, (0, 0)) * score_scale)
        grads.append(dot(chances.astype(LOW), above, (0, 0)))
    projected_grad[...] = jnp.concatenate(grads, 1).astype(LOW)
    weight = qkv[:, :, pl.ds(128, qkv_width)].reshape(width, qkv_width)
    back = dot(projected_grad[...], weight, (1, 1))
    first_part[...] = back.astype(LOW).reshape(heads, own, width)
    along = all_heads(links, place, lambda n, to: (first_part.at[to], first_far.at[n]))
    dense_now = jnp.concatenate(
        [
            dot(first_in[...], projected_grad[...], (0, 0)).astype(LOW),
            dot(attended[...], mixed[...], (0, 0)).astype(LOW),
        ],
        1,
    )
    dense[:, :, pl.ds(0, dense_width - 128)] = dense_now.reshape(blocks, block, dense_width - 128)
    adder = PlaneSum(links, place, dense, dense_core, xa, ya, yb, xb, xa.shape[2], 32)
    adder.start()
    gain_part[0:1, :] = jnp.sum(back * normalize(tokens[...].astype(WIDE))[0], 0, keepdims=True)
    gain_plane[me] = gain_part[...]
    small = [links.send(gain_part, gain_plane.at[me], d) for d in place.plane_peers]
    adder.cores()
    adder.cross()
    for copy in small:
        copy.wait_recv()
    gain_heads[z] = sum(gain_plane[i] for i in range(8))
    gains = all_heads(links, place, lambda n, to: (gain_heads.at[z], gain_heads.at[z]))
    normed, spread_one = normalize(tokens[mine, :].astype(WIDE))
    for copy in along:
        copy.wait_recv()
    first_grad = first_part[z].astype(WIDE)
    for n in range(heads - 1):
        first_grad = first_grad + first_far[n].astype(WIDE)
    weighted = first_grad * gain_one[...]
    inner = (
        weighted
        - jnp.mean(weighted, -1, keepdims=True)
        - normed * jnp.mean(weighted * normed, -1, keepdims=True)
    )
    rounded[z] = (total_grad + inner * spread_one).astype(LOW)
    along = all_heads(links, place, lambda n, to: (rounded.at[z], rounded.at[z]))

    def keep(rows, columns, values):
        dense_out[rows, columns] = values

    adder.finish(keep)
    for copy in gains:
        copy.wait_recv()
    gain_out[...] = sum(gain_heads[i] for i in range(heads))
    for copy in along:
        copy.wait_recv()
    for i in range(heads):
        tokens_grad[i] = rounded[i].astype(WIDE)
    for copy in bulk:
        copy.wait_recv()


def layer_kernel(heads, chunks, choices, names, *refs):
    r = types.SimpleNamespace(**dict(zip(names, refs)), choices=choices)
    place = Place(heads)
    links = Links(r.send_sems, r.recv_sems)
    loads = Loads(r.load_sems)
    kept = r.w_far.shape[0]
    mine, theirs = place.f * kept, (1 - place.f) * kept
    ups = {}
    for far in (1, 0):
        for i in range(kept):
            source = (theirs if far else mine) + i
            ups[far, i] = loads.start(r.up.at[source], r.w_up.at[far, i])
    nears = [loads.start(r.down.at[mine + i], r.w_near.at[i]) for i in range(kept)]
    place.greet(place.everyone())
    from_x, down_far = front_part(place, links, r)
    held = experts_part(place, links, loads, (ups, nears), down_far, r)
    extra = combine_part(place, links, chunks, r)
    links.left(from_x)
    stores, bulk = experts_back_part(place, links, loads, r)
    for copy in extra:
        copy.wait_recv()
    back_part(place, links, chunks, bulk, r)
    for copy in held + stores:
        copy.wait()
    links.drain()


def named_call(kernel, ins, outs, scratch, copies, loads, collective_id, vmem_mib, microseconds):
    spaces = {False: pltpu.VMEM, True: pltpu.HBM}
    names = [*ins, *outs, *scratch, "load_sems", "send_sems", "recv_sems"]
    made = pl.pallas_call(
        functools.partial(kernel, names),
        out_shape=[o[0] for o in outs.values()],
        in_specs=[pl.BlockSpec(memory_space=spaces[a[1]]) for a in ins.values()],
        out_specs=[pl.BlockSpec(memory_space=spaces[o[1]]) for o in outs.values()],
        scratch_shapes=[
            *scratch.values(),
            pltpu.SemaphoreType.DMA((loads,)),
            pltpu.SemaphoreType.DMA((copies,)),
            pltpu.SemaphoreType.DMA((copies,)),
        ],
        compiler_params=pltpu.CompilerParams(
            collective_id=collective_id,
            has_side_effects=True,
            vmem_limit_bytes=vmem_mib * 2**20,
        ),
        cost_estimate=spends(microseconds),
    )(*[a[0] for a in ins.values()])
    return types.SimpleNamespace(**dict(zip(outs, made)))


def layer(heads, experts, capacity, choices, head_count, vmem, hbm):
    rows, width = vmem["tokens"].shape
    own, half, chunks = rows // heads, width // 2, width // 256
    local_experts, _, hidden_width = hbm["up"].shape
    kept, pair, group_rows = local_experts // 2, 2 * capacity, 4 * rows
    block, mixed_width = vmem["wo_shard"].shape
    qkv_width = 3 * mixed_width
    dense_width = qkv_width + mixed_width + 128
    cut = 128 * ((dense_width // 128 + 1) // 2)
    ins = {name: (array, False) for name, array in vmem.items()}
    ins.update({name: (array, True) for name, array in hbm.items()})
    outs = {
        "result": (shape((heads, own, width)), False),
        "loss": (shape((heads, 8, 128), WIDE), False),
        "tokens_grad": (shape((heads, own, width), WIDE), False),
        "dense_out": (shape((block, dense_width), WIDE), False),
        "gain_out": (shape((2, width), WIDE), False),
        "down_far": (shape((kept, hidden_width, half)), True),
        "hidden_out": (shape((kept, pair, hidden_width)), True),
        "near_out": (shape((kept, pair, half)), True),
        "far_out": (shape((kept, pair, half)), True),
        "near_pre": (shape((kept, pair, hidden_width)), True),
        "far_pre": (shape((kept, pair, hidden_width)), True),
        "grad_out": (shape((kept, pair, width)), True),
    }
    low = {
        "pick_near": (2, kept * capacity, group_rows),
        "pick_far": (2, kept * capacity, group_rows),
        "buffer_near": (2, pair, half),
        "buffer_far": (2, pair, half),
        "hidden": (kept, pair, hidden_width),
        "weighted": (2, kept * capacity, width),
        "away": (kept, pair, hidden_width),
        "arrived": (kept, pair, hidden_width),
        "w_up": (2, kept, half, hidden_width),
        "w_near": (kept, hidden_width, half),
        "w_far": (kept, hidden_width, half),
        "part": (2, 2, 2, rows, width),
        "group": (8, rows, width),
        "sum_core": (chunks, 2, 2, rows, 256),
        "sum_xa": (chunks, 2, rows, 128),
        "sum_ya": (chunks, rows, 128),
        "sum_yb": (chunks, 2, rows, 128),
        "sum_xb": (chunks, rows, 128),
        "image_sum": (chunks, rows, 256),
        "image_far": (chunks, heads - 1, own, 256),
        "out_grad": (kept, pair, width),
        "slot_rows": (pair, width),
        "x": (2, 2, 2, rows, half),
        "other_half": (rows, half),
        "qkv": (8, *vmem["shard"].shape),
        "wo_all": (8, heads, block, mixed_width),
        "router": (experts, width),
        "projected": (rows, qkv_width),
        "mixed": (rows, mixed_width),
        "all_mixed": (heads, rows, mixed_width),
        "second_in": (rows, width),
        "core_in": (chunks, 2, 2, rows, 128),
        "y_in": (chunks, 2, rows, 128),
        "far": (chunks, heads - 1, 2, own, 128),
        "pair": (chunks, 2, own, 128),
        "x_in": (chunks, own, 128),
        "logit_grads": (experts, rows),
        "attended": (rows, width),
        "first_in": (rows, width),
        "projected_grad": (rows, qkv_width),
        "first_part": (heads, own, width),
        "dense": (8, block, dense_width),
        "dense_core": (4, block, dense_width),
        "xa": (2, block, cut),
        "ya": (block, cut),
        "yb": (2, block, dense_width - cut),
        "xb": (block, dense_width - cut),
        "first_far": (heads - 1, own, width),
        "rounded": (heads, own, width),
    }
    wide = {
        "gates": (kept, pair, 1),
        "counts": (8, 8, 128),
        "scale": (8, 128),
        "loss_scale": (8, 128),
        "valid": (rows, 8),
        "gain_one": (1, width),
        "gain": (1, width),
        "log_total": (rows, head_count),
        "residual": (rows, width),
        "probs": (8, experts, rows),
        "probs_own": (experts, rows),
        "own": (kept, pair, hidden_width),
        "final_grad": (own, width),
        "gate_rows": (2, kept, group_rows),
        "gate_in": (4, 2, kept, group_rows),
        "gate_sum": (2, kept, group_rows),
        "gate_all": (heads, 2, kept, rows),
        "logit_rows": (rows, width),
        "gain_part": (2, width),
        "gain_plane": (8, 2, width),
        "gain_heads": (heads, 2, width),
    }
    scratch = {name: pltpu.VMEM(dims, LOW) for name, dims in low.items()}
    scratch.update({name: pltpu.VMEM(dims, WIDE) for name, dims in wide.items()})
    whole = {"far_route": (8, group_rows), "slots": (2 * local_experts, group_rows)}
    scratch.update({name: pltpu.VMEM(dims, jnp.int32) for name, dims in whole.items()})
    copies = FRONT_COPIES + 2 * (heads - 1) + 2 * kept + chunks * (5 + GATHER_COPIES + 2 * (heads - 1)) + 2 * (heads - 1)
    copies += kept + 2 + chunks * (3 + heads - 1) + 3 + 2 * heads - 1 + heads - 1
    copies += SUM_COPIES + 3 * (heads - 1) + 7
    return named_call(
        functools.partial(layer_kernel, heads, chunks, choices),
        ins,
        outs,
        scratch,
        copies,
        5 * kept + 6,
        1,
        59,
        280,
    )


def finish_kernel(s, near, near_pre, far, far_pre, hidden, out_grad, *refs):
    pieces, (up, down) = refs[:-2], refs[-2:]
    i = pl.program_id(0)
    kept, half = pl.num_programs(0) // 2, down.shape[2]
    j = i - s[1]
    held = (j >= 0) & (j < kept)

    @pl.when(held)
    def _():
        up[0] = dot(near[0], near_pre[0], (0, 0))
        columns = pl.ds(pl.multiple_of(s[0] * half, half), half)
        down[0] = dot(hidden[0], out_grad[0, :, columns], (0, 0))

    @pl.when(jnp.logical_not(held))
    def _():
        up[0] = dot(far[0], far_pre[0], (0, 0))

    at = 0
    for piece in pieces:
        for k in range(piece.shape[0]):

            @pl.when(i - s[2] == at + k)
            def _(piece=piece, k=k):
                down[0] = piece[k].astype(WIDE)

        at += piece.shape[0]


def finish(scalars, near, near_pre, far, far_pre, hidden, out_grad, arrived):
    kept, _, half = near.shape
    hidden_width = near_pre.shape[2]

    def of(array, which):
        return pl.BlockSpec(
            (1, *array.shape[1:]), lambda i, s: (jnp.clip(i - s[which], 0, kept - 1), 0, 0)
        )

    def all_of(array):
        return pl.BlockSpec(array.shape, lambda i, s: (0, 0, 0))

    ins = [(near, 1), (near_pre, 1), (far, 2), (far_pre, 2), (hidden, 1), (out_grad, 1)]
    return pl.pallas_call(
        finish_kernel,
        out_shape=[
            shape((2 * kept, half, hidden_width), WIDE),
            shape((2 * kept, hidden_width, half), WIDE),
        ],
        grid_spec=pltpu.PrefetchScalarGridSpec(
            num_scalar_prefetch=1,
            grid=(2 * kept,),
            in_specs=[of(*a) for a in ins] + [all_of(piece) for piece in arrived],
            out_specs=[
                pl.BlockSpec((1, half, hidden_width), lambda i, s: (i, 0, 0)),
                pl.BlockSpec((1, hidden_width, half), lambda i, s: (i, 0, 0)),
            ],
        ),
        compiler_params=pltpu.CompilerParams(vmem_limit_bytes=60 * 2**20),
        cost_estimate=spends(8),
    )(scalars, *[a[0] for a in ins], *arrived)


def swap(values):
    return lax.ppermute(values, FSDP, [(0, 1), (1, 0)])


def fast(
    tokens,
    valid_mask,
    routes,
    teacher,
    gain_one,
    qkv_weight,
    out_weight,
    gain_two,
    router_weight,
    expert_up,
    expert_down,
):
    heads = lax.axis_size(HEADS)
    f, z = lax.axis_index(FSDP), lax.axis_index(HEADS)
    _, rows, width = tokens.shape
    block, head_count, qkv_dim = qkv_weight.shape
    head_dim = qkv_dim // 3
    local_experts = expert_up.shape[0]
    kept = local_experts // 2
    expert_count = local_experts * heads
    group_rows = 4 * rows
    capacity = 2 * routes.shape[2] * group_rows // expert_count
    mine, theirs = f * kept, (1 - f) * kept
    half = width // 2
    qkv_width = head_count * qkv_dim
    pad = -(128 + qkv_width) % 256
    wq = jnp.concatenate(
        [
            router_weight,
            gain_one[:, None],
            gain_two[:, None],
            jnp.zeros((block, 128 - expert_count - 2), LOW),
            qkv_weight.reshape(block, qkv_width),
            jnp.zeros((block, pad), LOW),
        ],
        1,
    )
    wo = out_weight.reshape(head_count * head_dim, block).T
    near_route = jnp.pad(routes.reshape(group_rows, -1).T, ((0, 8 - routes.shape[2]), (0, 0)))
    vmem = {
        "shard": wq,
        "wo_shard": wo,
        "near_route": near_route,
        "tokens": tokens[0],
        "teacher": teacher[0],
        "valid_row": valid_mask,
    }
    hbm = {"up": expert_up, "down": expert_down}
    made = layer(heads, expert_count, capacity, routes.shape[2], head_count, vmem, hbm)
    me = f * 4 + lax.axis_index(TENSOR)
    result, tokens_grad, dense_out = made.result, made.tokens_grad, made.dense_out
    loss_terms = jnp.sum(made.loss)[None]
    own_gains = lax.dynamic_slice_in_dim(made.gain_out, me * block, block, 1)
    scalars = jnp.stack([f, mine, theirs]).astype(jnp.int32)
    up_grad, down_grad = finish(
        scalars,
        made.near_out,
        made.near_pre,
        made.far_out,
        made.far_pre,
        made.hidden_out,
        made.grad_out,
        [made.down_far],
    )
    out_width = head_count * head_dim
    return (
        result.reshape(1, rows, width),
        loss_terms,
        tokens_grad.reshape(1, rows, width),
        own_gains[0],
        dense_out[:, :qkv_width].reshape(block, head_count, qkv_dim),
        dense_out[:, qkv_width : qkv_width + out_width].T.reshape(head_count, head_dim, block),
        own_gains[1],
        dense_out[:, qkv_width + out_width :][:, :expert_count],
        up_grad,
        down_grad,
    )


def local(sizes, *args):
    tokens, routes, up = args[0], args[2], args[9]
    fits = (
        sizes[FSDP] == 2
        and sizes[TENSOR] == 4
        and sizes[HEADS] % 2 == 0
        and tokens.shape[0] == 1
        and up.shape[0] % 8 == 0
        and tokens.shape[1] % (32 * sizes[HEADS]) == 0
        and tokens.shape[2] % 256 == 0
        and routes.shape[2] <= 8
        and up.shape[0] * sizes[HEADS] <= 126
    )
    return fast(*args) if fits else general(*args)


def solution(mesh):
    sizes = dict(mesh.shape)
    program = functools.partial(local, sizes)
    in_specs = (
        P((FSDP, TENSOR), None, None),
        P((FSDP, TENSOR), None),
        P(FSDP, None, None),
        P((FSDP, TENSOR), None, None),
        P((FSDP, TENSOR)),
        P((FSDP, TENSOR), HEADS, None),
        P(HEADS, None, (FSDP, TENSOR)),
        P((FSDP, TENSOR)),
        P((FSDP, TENSOR), None),
        P(HEADS, FSDP, TENSOR),
        P(HEADS, TENSOR, FSDP),
    )
    out_specs = (
        P((FSDP, TENSOR), None, None),
        P((FSDP, TENSOR)),
        P((FSDP, TENSOR), None, None),
        P((FSDP, TENSOR)),
        P((FSDP, TENSOR), HEADS, None),
        P(HEADS, None, (FSDP, TENSOR)),
        P((FSDP, TENSOR)),
        P((FSDP, TENSOR), None),
        P(HEADS, FSDP, TENSOR),
        P(HEADS, TENSOR, FSDP),
    )
    return jax.shard_map(program, mesh=mesh, in_specs=in_specs, out_specs=out_specs, check_vma=False)
```

```python
import functools
import types

import jax
import jax.numpy as jnp
from jax import lax
from jax.experimental import pallas as pl
from jax.experimental.pallas import tpu as pltpu
from jax.sharding import PartitionSpec as P

FSDP, HEADS, TENSOR = "fsdp", "heads", "tensor"
EPSILON = 1e-06
MASKED = -1e30
ROOT_HALF = 0.7071067811865476
DENSITY = 0.3989422804014327


def normalize(values):
    center = values - jnp.mean(values, -1, keepdims=True)
    inv_std = lax.rsqrt(jnp.mean(center * center, -1, keepdims=True) + EPSILON)
    return (center * inv_std, inv_std)


def norm_back(gradient, normed, inv_std, gain_vector):
    weighted = gradient * gain_vector
    gain_grad = jnp.sum(gradient * normed, axis=(0, 1))
    inner = (
        weighted
        - jnp.mean(weighted, -1, keepdims=True)
        - normed * jnp.mean(weighted * normed, -1, keepdims=True)
    )
    return (inner * inv_std, gain_grad)


def scores_of(queries, key_rows, keys_ok, score_scale):
    raw_scores = (
        jnp.einsum("iqhe,ikhe->ihqk", queries, key_rows, preferred_element_type=jnp.float32)
        * score_scale
    )
    return jnp.where(keys_ok, raw_scores, MASKED)


def gather_weights(
    gain_one, qkv_weight, out_weight, gain_two, router_weight, expert_up, expert_down
):
    dense_set = (
        lax.all_gather(qkv_weight, (FSDP, TENSOR), axis=0, tiled=True),
        lax.all_gather(out_weight, (FSDP, TENSOR), axis=2, tiled=True),
        lax.all_gather(router_weight, (FSDP, TENSOR), axis=0, tiled=True),
        lax.all_gather(gain_one, (FSDP, TENSOR), axis=0, tiled=True),
        lax.all_gather(gain_two, (FSDP, TENSOR), axis=0, tiled=True),
    )
    expert_set = (
        lax.all_gather(expert_up, FSDP, axis=1, tiled=True),
        lax.all_gather(expert_down, FSDP, axis=2, tiled=True),
    )
    return (dense_set, expert_set)


def reduce_expert_grads(up_grad, down_grad):
    return (
        lax.psum_scatter(up_grad, FSDP, scatter_dimension=1, tiled=True),
        lax.psum_scatter(down_grad, FSDP, scatter_dimension=2, tiled=True),
    )


def general(
    tokens,
    valid_mask,
    routes,
    teacher,
    gain_one,
    qkv_weight,
    out_weight,
    gain_two,
    router_weight,
    expert_up,
    expert_down,
):
    valid_total = lax.psum(jnp.sum(valid_mask.astype(jnp.float32)), (FSDP, TENSOR))
    dense_set, expert_set = gather_weights(
        gain_one, qkv_weight, out_weight, gain_two, router_weight, expert_up, expert_down
    )
    qkv_full, output_complete, router_full, gain_a, gain_b = dense_set
    up_full, down_full = expert_set
    image_count, token_slots, model_width = tokens.shape
    head_dim = qkv_full.shape[2] // 3
    local_experts = expert_up.shape[0]
    tensor_size = lax.axis_size(TENSOR)
    group_images = image_count * tensor_size
    group_rows = group_images * token_slots
    top_choices = routes.shape[2]
    expert_count = local_experts * lax.axis_size(HEADS)
    capacity = 2 * top_choices * group_rows // expert_count
    slot_count = local_experts * capacity
    total_tokens = image_count * token_slots * lax.axis_size(FSDP) * tensor_size
    total_images = image_count * lax.axis_size(FSDP) * tensor_size
    score_scale = head_dim ** (-0.5)
    inputs = tokens.astype(jnp.float32)
    normed_one, spread_one = normalize(inputs)
    first_in = (normed_one * gain_a.astype(jnp.float32)).astype(jnp.bfloat16)
    projected = jnp.einsum(
        "isd,dhe->ishe", first_in, qkv_full, preferred_element_type=jnp.float32
    ).astype(jnp.bfloat16)
    queries = projected[..., :head_dim]
    key_rows = projected[..., head_dim : 2 * head_dim]
    values = projected[..., 2 * head_dim :]
    keys_ok = (valid_mask > 0)[:, None, None, :]
    scores = scores_of(queries, key_rows, keys_ok, score_scale)
    peak_score = jnp.max(scores, -1, keepdims=True)
    exp_scores = jnp.exp(scores - peak_score)
    score_total = jnp.sum(exp_scores, -1, keepdims=True)
    logarithm_total = peak_score + jnp.log(score_total)
    attention = (exp_scores / score_total).astype(jnp.bfloat16)
    combined_heads = jnp.einsum(
        "ihqk,ikhe->iqhe", attention, values, preferred_element_type=jnp.float32
    ).astype(jnp.bfloat16)
    attn_part = jnp.einsum(
        "iqhe,hed->iqd", combined_heads, output_complete, preferred_element_type=jnp.float32
    )
    attended = lax.psum(attn_part, HEADS)
    residual = inputs + attended
    normed_two, spread_two = normalize(residual)
    second_in = (normed_two * gain_b.astype(jnp.float32)).astype(jnp.bfloat16)
    group_in = lax.all_gather(second_in, TENSOR, axis=0, tiled=True)
    rows_in = group_in.reshape(group_rows, model_width)
    logits = jnp.dot(rows_in, router_full, preferred_element_type=jnp.float32)
    peak_logit = jnp.max(logits, -1, keepdims=True)
    exponent_logits = jnp.exp(logits - peak_logit)
    router_probs = exponent_logits / jnp.sum(exponent_logits, -1, keepdims=True)
    expert_ids = jnp.arange(expert_count, dtype=jnp.int32)
    route_pairs = routes.reshape(group_rows, top_choices)
    picked_hot = (route_pairs[:, :, None] == expert_ids[None, None, :]).astype(jnp.float32)
    gate_weight_values = jnp.sum(router_probs[:, None, :] * picked_hot, -1)
    flat_routes = route_pairs.reshape(group_rows * top_choices)
    route_hot = (flat_routes[:, None] == expert_ids[None, :]).astype(jnp.int32)
    order = jnp.arange(group_rows * top_choices, dtype=jnp.int32)
    before = (order[None, :] < order[:, None]).astype(jnp.bfloat16)
    earlier = jnp.dot(
        before, route_hot.astype(jnp.bfloat16), preferred_element_type=jnp.float32
    ).astype(jnp.int32)
    slot_index = jnp.sum(earlier * route_hot, 1)
    first_expert = lax.axis_index(HEADS) * local_experts
    is_local = (flat_routes >= first_expert) & (flat_routes < first_expert + local_experts)
    target = jnp.where(is_local, (flat_routes - first_expert) * capacity + slot_index, slot_count)
    owner_row = jnp.arange(group_rows * top_choices, dtype=jnp.int32) // top_choices
    source = jnp.zeros((slot_count,), jnp.int32).at[target].set(owner_row, mode="drop")
    slot_gate = (
        jnp.zeros((slot_count,), jnp.float32)
        .at[target]
        .set(gate_weight_values.reshape(-1), mode="drop")
    )
    slot_pick = jnp.minimum(target, slot_count - 1)
    retain_mask = is_local.astype(jnp.float32)
    dispatched = rows_in[source].reshape(local_experts, capacity, model_width)
    before_gelu = jnp.einsum(
        "ecd,edf->ecf", dispatched, up_full, preferred_element_type=jnp.float32
    )
    hidden = jax.nn.gelu(before_gelu, approximate=False).astype(jnp.bfloat16)
    expert_out = jnp.einsum(
        "ecf,efd->ecd", hidden, down_full, preferred_element_type=jnp.float32
    ).reshape(slot_count, model_width)
    weighted = expert_out * slot_gate[:, None]
    moe_part = jnp.sum(
        (weighted[slot_pick] * retain_mask[:, None]).reshape(group_rows, top_choices, model_width),
        1,
    )
    moe_part = moe_part.reshape(group_images, token_slots, model_width)
    expert_sum = lax.psum(
        lax.psum_scatter(moe_part, TENSOR, scatter_dimension=0, tiled=True), HEADS
    )
    final = residual + expert_sum
    valid_rows = valid_mask.astype(jnp.float32)[..., None]
    difference = (final - teacher.astype(jnp.float32)) * valid_rows
    loss_terms = jnp.sum(difference * difference, axis=(1, 2)) * (
        total_images / (valid_total * model_width)
    )
    final_grad = difference * (total_tokens / valid_total)
    dense_set, expert_set = gather_weights(
        gain_one, qkv_weight, out_weight, gain_two, router_weight, expert_up, expert_down
    )
    qkv_full, output_complete, router_full, gain_a, gain_b = dense_set
    up_full, down_full = expert_set
    moe_grad = final_grad.astype(jnp.bfloat16)
    group_grad = lax.all_gather(moe_grad, TENSOR, axis=0, tiled=True).reshape(
        group_rows, model_width
    )
    slot_grad = group_grad[source].astype(jnp.float32)
    gate_slot_grad = jnp.sum(slot_grad * expert_out, -1)
    out_grad = (
        (slot_grad * slot_gate[:, None])
        .astype(jnp.bfloat16)
        .reshape(local_experts, capacity, model_width)
    )
    expert_down_grad = jnp.einsum(
        "ecf,ecd->efd", hidden, out_grad, preferred_element_type=jnp.float32
    )
    hidden_grad = jnp.einsum(
        "ecd,efd->ecf", out_grad, down_full, preferred_element_type=jnp.float32
    )
    normal_cdf = 0.5 * (1.0 + lax.erf(before_gelu * ROOT_HALF))
    slope = normal_cdf + before_gelu * DENSITY * jnp.exp(-0.5 * before_gelu * before_gelu)
    pre_grad = (hidden_grad * slope).astype(jnp.bfloat16)
    expert_up_grad = jnp.einsum(
        "ecd,ecf->edf", dispatched, pre_grad, preferred_element_type=jnp.float32
    )
    row_grad = jnp.einsum(
        "ecf,edf->ecd", pre_grad, up_full, preferred_element_type=jnp.float32
    ).reshape(slot_count, model_width)
    rows_part = jnp.sum(
        (row_grad[slot_pick] * retain_mask[:, None]).reshape(group_rows, top_choices, model_width),
        1,
    )
    rows_part = rows_part.reshape(group_images, token_slots, model_width)
    gate_part = (gate_slot_grad[slot_pick] * retain_mask).reshape(
        group_images, token_slots, top_choices
    )
    rows_share, gate_share = (
        lax.psum_scatter(rows_part, TENSOR, scatter_dimension=0, tiled=True),
        lax.psum_scatter(gate_part, TENSOR, scatter_dimension=0, tiled=True),
    )
    second_grad, gate_grad = lax.psum((rows_share, gate_share), HEADS)
    own_start = lax.axis_index(TENSOR) * image_count * token_slots
    own_rows = image_count * token_slots
    own_probs = lax.dynamic_slice_in_dim(router_probs, own_start, own_rows, 0).reshape(
        image_count, token_slots, expert_count
    )
    own_hot = lax.dynamic_slice_in_dim(picked_hot, own_start, own_rows, 0).reshape(
        image_count, token_slots, top_choices, expert_count
    )
    prob_grad = jnp.sum(gate_grad[..., None] * own_hot, 2)
    logit_grad = (
        own_probs * (prob_grad - jnp.sum(own_probs * prob_grad, -1, keepdims=True))
    ).astype(jnp.bfloat16)
    router_grad = jnp.einsum(
        "isd,ise->de", second_in, logit_grad, preferred_element_type=jnp.float32
    )
    second_grad = second_grad + jnp.einsum(
        "ise,de->isd", logit_grad, router_full, preferred_element_type=jnp.float32
    )
    residual_norm, gain_two_grad = norm_back(
        second_grad, normed_two, spread_two, gain_b.astype(jnp.float32)
    )
    residual_grad = final_grad + residual_norm
    attended_output_gradient = residual_grad.astype(jnp.bfloat16)
    out_weight_grad = jnp.einsum(
        "iqhe,iqd->hed",
        combined_heads,
        attended_output_gradient,
        preferred_element_type=jnp.float32,
    )
    mixed_grad = jnp.einsum(
        "iqd,hed->iqhe",
        attended_output_gradient,
        output_complete,
        preferred_element_type=jnp.float32,
    ).astype(jnp.bfloat16)
    scores = scores_of(queries, key_rows, keys_ok, score_scale)
    probs = jnp.exp(scores - logarithm_total)
    probs_low = probs.astype(jnp.bfloat16)
    prob_part = jnp.einsum(
        "iqhe,ikhe->ihqk", mixed_grad, values, preferred_element_type=jnp.float32
    )
    score_grad = (probs * (prob_part - jnp.sum(probs * prob_part, -1, keepdims=True))).astype(
        jnp.bfloat16
    )
    query_grad = (
        jnp.einsum("ihqk,ikhe->iqhe", score_grad, key_rows, preferred_element_type=jnp.float32)
        * score_scale
    )
    key_grad = (
        jnp.einsum("ihqk,iqhe->ikhe", score_grad, queries, preferred_element_type=jnp.float32)
        * score_scale
    )
    value_grad = jnp.einsum(
        "ihqk,iqhe->ikhe", probs_low, mixed_grad, preferred_element_type=jnp.float32
    )
    projected_grad = jnp.concatenate([query_grad, key_grad, value_grad], -1).astype(jnp.bfloat16)
    qkv_grad = jnp.einsum(
        "isd,ishe->dhe", first_in, projected_grad, preferred_element_type=jnp.float32
    )
    first_part = jnp.einsum(
        "ishe,dhe->isd", projected_grad, qkv_full, preferred_element_type=jnp.float32
    )
    first_grad = lax.psum(first_part, HEADS)
    input_norm, gain_one_grad = norm_back(
        first_grad, normed_one, spread_one, gain_a.astype(jnp.float32)
    )
    tokens_grad = residual_grad + input_norm
    dense_grads = (
        lax.psum_scatter(qkv_grad, (FSDP, TENSOR), scatter_dimension=0, tiled=True),
        lax.psum_scatter(out_weight_grad, (FSDP, TENSOR), scatter_dimension=2, tiled=True),
        lax.psum_scatter(router_grad, (FSDP, TENSOR), scatter_dimension=0, tiled=True),
        lax.psum_scatter(gain_one_grad, (FSDP, TENSOR), scatter_dimension=0, tiled=True),
        lax.psum_scatter(gain_two_grad, (FSDP, TENSOR), scatter_dimension=0, tiled=True),
    )
    expert_grads = reduce_expert_grads(expert_up_grad, expert_down_grad)
    return (
        final.astype(jnp.bfloat16),
        loss_terms,
        tokens_grad,
        dense_grads[3],
        dense_grads[0],
        dense_grads[1],
        dense_grads[4],
        dense_grads[2],
        expert_grads[0],
        expert_grads[1],
    )


MESH = pl.DeviceIdType.MESH
LOW = jnp.bfloat16
WIDE = jnp.float32


class Links:
    def __init__(self, send_sems, recv_sems):
        self.send_sems, self.recv_sems = send_sems, recv_sems
        self.copies, self.gone = [], []

    def send(self, src, dst, device):
        k = len(self.copies)
        assert k < self.send_sems.shape[0]
        copy = pltpu.make_async_remote_copy(
            src_ref=src,
            dst_ref=dst,
            send_sem=self.send_sems.at[k],
            recv_sem=self.recv_sems.at[k],
            device_id=device,
            device_id_type=MESH,
        )
        copy.start()
        self.copies.append(copy)
        return copy

    def left(self, copies):
        for copy in copies:
            copy.wait_send()
            self.gone.append(copy)

    def drain(self):
        for copy in self.copies:
            if not any(copy is other for other in self.gone):
                copy.wait_send()


class Place:
    def __init__(self, heads):
        self.f = lax.axis_index(FSDP)
        t = lax.axis_index(TENSOR)
        self.y, self.c = t // 2, lax.rem(t, 2)
        self.z = lax.axis_index(HEADS)
        self.heads = heads
        self.x_peer = {FSDP: 1 - self.f}
        self.y_peer = {TENSOR: 2 * (1 - self.y) + self.c}
        self.core_peer = {TENSOR: 2 * self.y + 1 - self.c}
        self.z_peers = [{HEADS: lax.rem(self.z + k, heads)} for k in range(1, heads)]
        self.plane_peers = []
        for a in range(2):
            for k in range(4):
                if a or k:
                    where = {TENSOR: lax.rem(t + k, 4)}
                    if a:
                        where[FSDP] = 1 - self.f
                    self.plane_peers.append(where)

    def image(self, df, dy, dc):
        f = 1 - self.f if df else self.f
        y = 1 - self.y if dy else self.y
        c = 1 - self.c if dc else self.c
        return f * 4 + 2 * y + c

    def greet(self, devices):
        barrier = pltpu.get_barrier_semaphore()
        for device in devices:
            pl.semaphore_signal(barrier, inc=1, device_id=device, device_id_type=MESH)
        pl.semaphore_wait(barrier, len(devices))

    def tensor_peers(self):
        t = 2 * self.y + self.c
        return [{TENSOR: lax.rem(t + k, 4)} for k in range(1, 4)]

    def owners(self):
        return [
            {FSDP: 1 - self.f if a else self.f, HEADS: lax.rem(self.z + k, self.heads)}
            for k in range(self.heads)
            for a in range(2)
            if a or k
        ]

    def everyone(self):
        t = 2 * self.y + self.c
        corners = [{FSDP: 1 - self.f, TENSOR: lax.rem(t + k, 4)} for k in range(1, 4)]
        return self.tensor_peers() + self.owners() + corners

    def axis_peers(self):
        return [self.x_peer, self.y_peer, self.core_peer]


class PlaneGather:
    def __init__(self, links, place, first, second, whole):
        self.links, self.place = links, place
        self.first, self.second, self.whole = first, second, whole

    def go(self, part, image, device):
        return self.links.send(part(image), part(image), device)

    def start(self):
        p, me = self.place, self.place.image(0, 0, 0)
        self.xa = self.go(self.first, me, p.x_peer)
        self.yb = self.go(self.second, me, p.y_peer)
        self.own = self.go(self.whole, me, p.core_peer)
        self.xb = self.go(self.second, me, p.x_peer)
        self.ya = self.go(self.first, me, p.y_peer)

    def forward(self):
        p = self.place
        self.xa.wait_recv()
        self.fa = self.go(self.first, p.image(1, 0, 0), p.y_peer)
        self.yb.wait_recv()
        self.fb = self.go(self.second, p.image(0, 1, 0), p.x_peer)

    def share(self):
        p = self.place
        self.xb.wait_recv()
        self.c1 = self.go(self.whole, p.image(1, 0, 0), p.core_peer)
        self.ya.wait_recv()
        self.c2 = self.go(self.whole, p.image(0, 1, 0), p.core_peer)

    def finish(self):
        p = self.place
        self.fa.wait_recv()
        self.fb.wait_recv()
        self.c3 = self.go(self.whole, p.image(1, 1, 0), p.core_peer)
        for copy in (self.own, self.c1, self.c2, self.c3):
            copy.wait_recv()

    def run(self):
        self.start()
        self.forward()
        self.share()
        self.finish()


GATHER_COPIES = 10


def in_rows(rows, step, body):
    def one(i, carry):
        body(pl.ds(pl.multiple_of(i * step, step), step))
        return carry

    lax.fori_loop(0, rows // step, one, 0)


class PlaneSum:
    def __init__(self, links, place, part, core_in, xa, ya, yb, xb, cut, step):
        self.links, self.place, self.part, self.core_in = links, place, part, core_in
        self.xa, self.ya, self.yb, self.xb, self.cut, self.step = xa, ya, yb, xb, cut, step
        self.rows, self.width = part.shape[1], part.shape[2]
        self.a, self.b = pl.ds(0, cut), pl.ds(cut, self.width - cut)

    def start(self):
        p = self.place
        self.order = [(1, 1), (1, 0), (0, 1), (0, 0)]
        self.into = {}
        for df, dy in self.order:
            f = 1 - p.f if df else p.f
            y = 1 - p.y if dy else p.y
            self.into[df, dy] = self.links.send(
                self.part.at[p.image(df, dy, 1)], self.core_in.at[2 * f + y], p.core_peer
            )

    def slot(self, df, dy):
        p = self.place
        return 2 * (1 - p.f if df else p.f) + (1 - p.y if dy else p.y)

    def cores(self):
        p, rc = self.place, self.core_in
        self.got = {}
        for df, dy in self.order:
            self.into[df, dy].wait_recv()
            j, mine = self.slot(df, dy), p.image(df, dy, 0)

            def add(rows, j=j, mine=mine):
                both = rc[j, rows, :].astype(WIDE) + self.part[mine, rows, :].astype(WIDE)
                rc[j, rows, :] = both.astype(LOW)

            in_rows(self.rows, self.step, add)
            y = 1 - p.y if dy else p.y
            f = 1 - p.f if df else p.f
            if df:
                self.got["x", dy] = self.links.send(rc.at[j, :, self.a], self.xa.at[y], p.x_peer)
            if dy:
                self.got["y", df] = self.links.send(rc.at[j, :, self.b], self.yb.at[f], p.y_peer)

    def cross(self):
        p, rc, xa, yb = self.place, self.core_in, self.xa, self.yb
        self.got["x", 1].wait_recv()
        j, other = self.slot(0, 1), 1 - p.y

        def add_a(rows):
            both = xa[other, rows, :].astype(WIDE) + rc[j, rows, self.a].astype(WIDE)
            xa[other, rows, :] = both.astype(LOW)

        in_rows(self.rows, self.step, add_a)
        self.last_a = self.links.send(xa.at[other], self.ya, p.y_peer)
        self.got["y", 1].wait_recv()
        k, away = self.slot(1, 0), 1 - p.f

        def add_b(rows):
            both = yb[away, rows, :].astype(WIDE) + rc[k, rows, self.b].astype(WIDE)
            yb[away, rows, :] = both.astype(LOW)

        in_rows(self.rows, self.step, add_b)
        self.last_b = self.links.send(yb.at[away], self.xb, p.x_peer)

    def finish(self, take):
        p, rc = self.place, self.core_in
        self.got["x", 0].wait_recv()
        self.got["y", 0].wait_recv()
        self.last_a.wait_recv()
        self.last_b.wait_recv()
        j, y, f = self.slot(0, 0), p.y, p.f

        def add(rows):
            first = rc[j, rows, self.a].astype(WIDE) + self.xa[y, rows, :].astype(WIDE)
            second = rc[j, rows, self.b].astype(WIDE) + self.yb[f, rows, :].astype(WIDE)
            take(rows, self.a, first + self.ya[rows, :].astype(WIDE))
            take(rows, self.b, second + self.xb[rows, :].astype(WIDE))

        in_rows(self.rows, self.step, add)


SUM_COPIES = 10


def sum_scratch(rows, width, cut):
    return [
        pltpu.VMEM((4, rows, width), LOW),
        pltpu.VMEM((2, rows, cut), LOW),
        pltpu.VMEM((rows, cut), LOW),
        pltpu.VMEM((2, rows, width - cut), LOW),
        pltpu.VMEM((rows, width - cut), LOW),
    ]


def all_heads(links, place, make):
    copies = []
    for k, device in enumerate(place.z_peers):
        src, dst = make(k, device[HEADS])
        copies.append(links.send(src, dst, device))
    return copies


def spends(microseconds):
    return pl.CostEstimate(flops=0, bytes_accessed=microseconds * 3_000_000, transcendentals=0)


def shape(dims, dtype=LOW):
    return jax.ShapeDtypeStruct(dims, dtype)


class ChunkSum:
    def __init__(self, links, place, part, columns, core_in, xa, ya, yb, xb):
        self.links, self.place, self.part, self.columns = links, place, part, columns
        self.core_in, self.xa, self.ya, self.yb, self.xb = core_in, xa, ya, yb, xb
        self.rows, self.half = core_in.shape[2], core_in.shape[3] // 2
        self.a, self.b = pl.ds(0, self.half), pl.ds(self.half, self.half)

    def start(self):
        p = self.place
        self.into = self.links.send(
            self.part.at[:, :, 1 - p.c, :, self.columns], self.core_in, p.core_peer
        )

    def cores(self):
        p, rc = self.place, self.core_in
        self.into.wait_recv()

        def add(rows):
            here = self.part[:, :, p.c, rows, self.columns].astype(WIDE)
            rc[:, :, rows, :] = (rc[:, :, rows, :].astype(WIDE) + here).astype(LOW)

        in_rows(self.rows, 32, add)
        self.to_x = self.links.send(rc.at[1 - p.f, :, :, self.a], self.xa, p.x_peer)
        self.to_y = self.links.send(rc.at[:, 1 - p.y, :, self.b], self.yb, p.y_peer)

    def cross(self):
        p, rc, xa, yb = self.place, self.core_in, self.xa, self.yb
        self.to_x.wait_recv()
        y, f = 1 - p.y, 1 - p.f

        def add_a(rows):
            both = xa[y, rows, :].astype(WIDE) + rc[p.f, y, rows, self.a].astype(WIDE)
            xa[y, rows, :] = both.astype(LOW)

        in_rows(self.rows, 64, add_a)
        self.last_a = self.links.send(xa.at[y], self.ya, p.y_peer)
        self.to_y.wait_recv()

        def add_b(rows):
            both = yb[f, rows, :].astype(WIDE) + rc[f, p.y, rows, self.b].astype(WIDE)
            yb[f, rows, :] = both.astype(LOW)

        in_rows(self.rows, 64, add_b)
        self.last_b = self.links.send(yb.at[f], self.xb, p.x_peer)

    def finish(self, take):
        p, rc = self.place, self.core_in
        self.last_a.wait_recv()
        self.last_b.wait_recv()

        def add(rows):
            first = rc[p.f, p.y, rows, self.a].astype(WIDE) + self.xa[p.y, rows, :].astype(WIDE)
            second = rc[p.f, p.y, rows, self.b].astype(WIDE) + self.yb[p.f, rows, :].astype(WIDE)
            take(rows, 0, first + self.ya[rows, :].astype(WIDE))
            take(rows, 1, second + self.xb[rows, :].astype(WIDE))

        in_rows(self.rows, 64, add)


def skewed(chunks, stages):
    for step in range(chunks + len(stages) - 1):
        for k in range(chunks):
            if 0 <= step - k < len(stages):
                stages[step - k](k)


def combine_part(place, links, chunks, r):
    heads, z, me = place.heads, place.z, place.image(0, 0, 0)
    part, residual, teacher, valid, scale = r.part, r.residual, r.teacher, r.valid, r.scale
    result, final_grad, group, loss = r.result, r.final_grad, r.group, r.loss
    image_sum, far = r.image_sum, r.image_far
    rows_all, width = residual.shape
    own = rows_all // heads
    wide = width // chunks
    half = wide // 2
    mine = pl.ds(pl.multiple_of(z * own, own), own)
    columns = [pl.ds(k * wide, wide) for k in range(chunks)]
    adders = [
        ChunkSum(
            links,
            place,
            part,
            columns[k],
            r.sum_core.at[k],
            r.sum_xa.at[k],
            r.sum_ya.at[k],
            r.sum_yb.at[k],
            r.sum_xb.at[k],
        )
        for k in range(chunks)
    ]
    for adder in adders:
        adder.start()
    along, spread, squares = {}, {}, []
    gathers = [
        PlaneGather(
            links,
            place,
            lambda i, k=k: group.at[i, :, pl.ds(k * wide, half)],
            lambda i, k=k: group.at[i, :, pl.ds(k * wide + half, half)],
            lambda i, k=k: group.at[i, :, columns[k]],
        )
        for k in range(chunks)
    ]

    def to_heads(k):
        if k == chunks - 1:
            r.hidden_copies.append(send_hidden(place, links, r, 1))

        def keep(rows, part_of, values):
            image_sum[k, rows, pl.ds(part_of * half, half)] = values.astype(LOW)

        adders[k].finish(keep)
        along[k] = all_heads(
            links,
            place,
            lambda n, to: (
                image_sum.at[k, pl.ds(pl.multiple_of(to * own, own), own)],
                far.at[k, n],
            ),
        )

    def final(k):
        for copy in along[k]:
            copy.wait_recv()
        total = image_sum[k, mine, :].astype(WIDE)
        for n in range(heads - 1):
            total = total + far[k, n].astype(WIDE)
        values = residual[mine, columns[k]] + total
        result[z, :, columns[k]] = values.astype(LOW)
        error = (values - teacher[mine, columns[k]].astype(WIDE)) * valid[mine, 0:1]
        grad = error * scale[0:1, 0:1]
        final_grad[:, columns[k]] = grad
        group[me, mine, columns[k]] = grad.astype(LOW)
        block = group.at[me, mine, columns[k]]
        spread[k] = all_heads(links, place, lambda n, to: (block, block))
        square = jnp.sum((error * error).reshape(own // 8, 8, wide), axis=0)
        squares.extend(square[:, i * 128 : (i + 1) * 128] for i in range(wide // 128))

    def to_plane(k):
        for copy in spread[k]:
            copy.wait_recv()
        gathers[k].start()

    def forward(k):
        gathers[k].forward()
        gathers[k].share()

    skewed(
        chunks,
        [
            lambda k: adders[k].cores(),
            lambda k: adders[k].cross(),
            to_heads,
            final,
            to_plane,
            forward,
        ],
    )
    loss[z] = sum(squares) * r.loss_scale[0:1, 0:1]
    extra = all_heads(links, place, lambda k, to: (result.at[z], result.at[z]))
    extra += all_heads(links, place, lambda k, to: (loss.at[z], loss.at[z]))
    for gather in gathers:
        gather.finish()
    return extra


def dot(a, b, over=(1, 0)):
    return lax.dot_general(a, b, (((over[0],), (over[1],)), ((), ())), preferred_element_type=WIDE)


def one_hot(slots, row, capacity):
    places = lax.broadcasted_iota(jnp.int32, (capacity, slots.shape[1]), 0)
    return places == slots[pl.ds(row, 1), :]


class Loads:
    def __init__(self, sems):
        self.sems, self.count = sems, 0

    def start(self, src, dst):
        assert self.count < self.sems.shape[0]
        copy = pltpu.make_async_copy(src, dst, self.sems.at[self.count])
        self.count += 1
        copy.start()
        return copy


def gelu_parts(values):
    cdf = 0.5 * (1.0 + lax.erf(values * ROOT_HALF))
    return values * cdf, cdf + values * DENSITY * jnp.exp(-0.5 * values * values)


def front_part(place, links, r):
    heads, f, z, me = place.heads, place.f, place.z, place.image(0, 0, 0)
    oq, oo, counts, slots = r.qkv, r.wo_all, r.counts, r.slots
    kept = r.w_far.shape[0]
    theirs = (1 - f) * kept
    rows = [r.router_in[...], r.gain_one_in[...], r.gain_two_in[...]]
    rows = [row.astype(WIDE) for row in rows]
    block = oq.shape[1]
    rows.append(jnp.zeros((128 - sum(row.shape[0] for row in rows), block), WIDE))
    oq[me, :, 0:128] = jnp.transpose(jnp.concatenate(rows, 0)).astype(LOW)
    qkv = jnp.concatenate([r.qkv_in[h] for h in range(r.qkv_in.shape[0])], 1)
    oq[me, :, pl.ds(128, qkv.shape[1])] = qkv
    rest = oq.shape[2] - 128 - qkv.shape[1]
    if rest:
        oq[me, :, pl.ds(128 + qkv.shape[1], rest)] = jnp.zeros((block, rest), LOW)
    oo[me, z] = jnp.transpose(r.out_in[...].astype(WIDE)).astype(LOW)
    counts[me] = jnp.broadcast_to(jnp.sum(r.valid_row[...].astype(WIDE), -1, keepdims=True), (8, 128))
    half, mid = oq.shape[2] // 2, heads // 2
    main = PlaneGather(
        links,
        place,
        lambda i: oq.at[i, :, pl.ds(0, half)],
        lambda i: oq.at[i, :, pl.ds(half, half)],
        lambda i: oq.at[i],
    )
    side = PlaneGather(
        links,
        place,
        lambda i: oo.at[i, pl.ds(0, mid)],
        lambda i: oo.at[i, pl.ds(mid, heads - mid)],
        lambda i: oo.at[i],
    )

    def bulk(i):
        return links.send(r.down.at[theirs + i], r.w_far.at[i], place.x_peer)

    main.start()
    along = all_heads(links, place, lambda k, to: (oo.at[me, z], oo.at[me, z]))
    small = [links.send(counts.at[me], counts.at[me], d) for d in place.plane_peers]
    small.append(links.send(r.near_route, r.far_route, place.x_peer))
    main.forward()
    for copy in along:
        copy.wait_recv()
    side.start()
    down = [bulk(0)]
    main.share()
    main.finish()
    width = r.tokens.shape[1]
    experts = r.probs.shape[1]
    narrow = oq[:, :, 0:128].reshape(width, 128).astype(WIDE)
    turned = jnp.transpose(narrow)
    r.router[...] = turned[:experts].astype(LOW)
    r.gain_one[...] = turned[experts : experts + 1]
    r.gain[...] = turned[experts + 1 : experts + 2]
    rows_all = r.tokens.shape[0]

    def first_norm(rows):
        normed, _ = normalize(r.tokens[rows, :].astype(WIDE))
        r.first_in[rows, :] = (normed * r.gain_one[...]).astype(LOW)

    in_rows(rows_all, 64, first_norm)
    qkv_width = r.projected.shape[1]
    weight = oq[:, :, pl.ds(128, qkv_width)].reshape(width, qkv_width)
    r.projected[...] = dot(r.first_in[...], weight).astype(LOW)
    side.forward()
    down.append(bulk(1))
    head_count = r.log_total.shape[1]
    size = qkv_width // head_count // 3
    keys_ok = r.valid_row[...] > 0
    mixed = []
    for h in range(head_count):
        at = 3 * h * size
        query, key, value = (r.projected[:, at + n * size : at + (n + 1) * size] for n in range(3))
        scores = jnp.where(keys_ok, dot(query, key, (1, 1)) * size ** (-0.5), MASKED)
        peak = jnp.max(scores, -1, keepdims=True)
        powers = jnp.exp(scores - peak)
        total = jnp.sum(powers, -1, keepdims=True)
        r.log_total[:, h : h + 1] = peak + jnp.log(total)
        mixed.append(dot((powers / total).astype(LOW), value).astype(LOW))
    r.mixed[...] = jnp.concatenate(mixed, 1)
    everyone = r.all_mixed
    everyone[z] = r.mixed[...]
    along = all_heads(links, place, lambda k, to: (everyone.at[z], everyone.at[z]))
    side.share()
    for copy in small:
        copy.wait_recv()
    valid_total = sum(counts[i] for i in range(8))[0:1, 0:1]
    r.scale[...] = jnp.broadcast_to(8 * rows_all / valid_total, (8, 128))
    r.loss_scale[...] = jnp.broadcast_to(8 / (valid_total * width), (8, 128))
    column = jnp.broadcast_to(r.valid_row[...].astype(WIDE), (8, rows_all))
    r.valid[...] = jnp.transpose(column)
    local_experts = 2 * kept
    ids = z * local_experts + lax.broadcasted_iota(jnp.int32, (local_experts, 1), 0)
    first = f == 0
    near, far = r.near_route[...], r.far_route[...]
    both = [jnp.where(first, near, far), jnp.where(first, far, near)]
    chosen = []
    for route in both:
        hits = []
        for c in range(route.shape[1]):
            row = jnp.concatenate([route[k, c : c + 1] for k in range(4)], 1)
            hits.append(row == ids)
        chosen.append(functools.reduce(jnp.logical_or, hits))
    chosen = jnp.concatenate(chosen, 0)
    count = chosen.astype(WIDE)
    before = lax.broadcasted_iota(jnp.int32, (128, 128), 0)
    before = (before < lax.broadcasted_iota(jnp.int32, (128, 128), 1)).astype(LOW)
    running = jnp.zeros((2 * local_experts, 1), WIDE)
    for b in range(slots.shape[1] // 128):
        columns = slice(b * 128, (b + 1) * 128)
        here = count[:, columns]
        slot = dot(here.astype(LOW), before) + running
        slots[:, columns] = jnp.where(chosen[:, columns], slot, -1.0).astype(jnp.int32)
        running = running + jnp.sum(here, -1, keepdims=True)
    for copy in along:
        copy.wait_recv()
    side.finish()
    half = width // 2
    total = jnp.zeros((rows_all, width), WIDE)
    for n in range(heads):
        weight = oo[:, n].reshape(width, oo.shape[3])
        total = total + dot(everyone[n], weight, (1, 1))
    r.residual[...] = total

    def norm(rows):
        values = r.tokens[rows, :].astype(WIDE) + r.residual[rows, :]
        r.residual[rows, :] = values
        normed, _ = normalize(values)
        r.second_in[rows, :] = (normed * r.gain[...]).astype(LOW)

    in_rows(rows_all, 64, norm)
    low, high = r.second_in[:, :half], r.second_in[:, half:]

    def part_of(df, dy, dc):
        return r.x.at[
            1 - f if df else f, 1 - place.y if dy else place.y, 1 - place.c if dc else place.c
        ]

    mine, across, beside, corner = (
        part_of(0, 0, 0),
        part_of(1, 0, 0),
        part_of(0, 1, 0),
        part_of(1, 1, 0),
    )
    mine[...] = jnp.where(first, low, high)
    r.other_half[...] = jnp.where(first, high, low)
    x1 = links.send(r.other_half, mine, place.x_peer)
    y1 = links.send(mine, mine, place.y_peer)
    shared = [links.send(mine, mine, place.core_peer)]
    down.append(bulk(2))
    logits = dot(r.router[...], r.second_in[...], (1, 1))
    powers = jnp.exp(logits - jnp.max(logits, 0, keepdims=True))
    probs = powers / jnp.sum(powers, 0, keepdims=True)
    r.probs_own[...] = probs
    r.probs[me] = probs
    small = [links.send(r.probs.at[me], r.probs.at[me], d) for d in place.plane_peers]
    x1.wait_recv()
    y2 = links.send(across, across, place.y_peer)
    shared.append(links.send(across, across, place.core_peer))
    y1.wait_recv()
    shared.append(links.send(beside, beside, place.core_peer))
    y2.wait_recv()
    shared.append(links.send(corner, corner, place.core_peer))
    for copy in shared + small:
        copy.wait_recv()
    return [y1, y2, *shared], down


FRONT_COPIES = 2 * GATHER_COPIES + 7 + 1 + 1 + 2 + 4 + 7


def send_hidden(place, links, r, i):
    return links.send(r.hidden.at[i], r.far_hidden.at[i], place.x_peer)


def experts_part(place, links, loads, weights, down_far, r):
    slots, probs = r.slots, r.probs
    pick_near, pick_far, gates, hidden = r.pick_near, r.pick_far, r.gates, r.hidden
    buffer_near, buffer_far, own, weighted = r.buffer_near, r.buffer_far, r.own, r.weighted
    away, arrived, w_up, w_near, w_far = r.away, r.arrived, r.w_up, r.w_near, r.w_far
    kept, pair, _ = own.shape
    capacity, half = pair // 2, r.x.shape[4]
    group_rows = slots.shape[1]
    stores = []

    def kept_rows(i, buffer, target):
        stores.append(loads.start(buffer.at[i % 2], target.at[i]))

    local_experts = 2 * kept
    mine, theirs = place.f * kept, (1 - place.f) * kept
    ups, nears = weights
    sent = []
    for i in range(kept):
        if i > 1:
            stores[i - 2].wait()
        for g in range(2):
            rows = slice(i * capacity, (i + 1) * capacity)
            hot = one_hot(slots, g * local_experts + theirs + i, capacity).astype(LOW)
            pick_far[g, rows] = hot
            x = r.x[g].reshape(group_rows, half)
            buffer_far[i % 2, g * capacity : (g + 1) * capacity] = dot(hot, x).astype(LOW)
        ups[1, i].wait()
        kept_rows(i, buffer_far, r.far_out)
        away[i] = dot(buffer_far[i % 2], w_up[1, i]).astype(LOW)
        sent.append(links.send(away.at[i], arrived.at[i], place.x_peer))
    down_far = [
        *down_far,
        *(
            links.send(r.down.at[theirs + i], w_far.at[i], place.x_peer)
            for i in range(len(down_far), kept)
        ),
    ]
    for i in range(kept):
        expert = place.z * local_experts + mine + i
        if i > 1:
            stores[kept + i - 2].wait()
        for g in range(2):
            rows = slice(i * capacity, (i + 1) * capacity)
            into = slice(g * capacity, (g + 1) * capacity)
            hot = one_hot(slots, g * local_experts + mine + i, capacity)
            chances = [probs[4 * g + k, pl.ds(expert, 1), :] for k in range(4)]
            chances = jnp.concatenate(chances, 1)
            gates[i, into] = jnp.sum(jnp.where(hot, chances, 0.0), -1, keepdims=True)
            pick_near[g, rows] = hot.astype(LOW)
            x = r.x[g].reshape(group_rows, half)
            buffer_near[i % 2, into] = dot(hot.astype(LOW), x).astype(LOW)
        ups[0, i].wait()
        kept_rows(i, buffer_near, r.near_out)
        own[i] = dot(buffer_near[i % 2], w_up[0, i])
    for copy in nears:
        copy.wait()
    for i in range(kept):
        sent[i].wait_recv()
        down_far[i].wait_recv()
        values, slopes = gelu_parts(own[i] + arrived[i].astype(WIDE))
        hidden[i] = values.astype(LOW)
        if i == 0:
            r.hidden_copies.append(send_hidden(place, links, r, 0))
        own[i] = slopes
        for weight, f in ((w_near, place.f), (w_far, 1 - place.f)):
            out = (dot(hidden[i], weight[i]) * gates[i]).astype(LOW)
            columns = pl.ds(pl.multiple_of(f * half, half), half)
            for g in range(2):
                rows = slice(i * capacity, (i + 1) * capacity)
                weighted[g, rows, columns] = out[g * capacity : (g + 1) * capacity]
    for g in range(2):
        total = dot(pick_near[g], weighted[g], (0, 0)).astype(LOW)
        r.part[g] = total.reshape(r.part.shape[1:])
    links.left(sent)
    return stores[kept - 2 : kept] + stores[2 * kept - 2 :]


def experts_back_part(place, links, loads, chunks, r):
    pick_near, pick_far, hidden, slope, gates = r.pick_near, r.pick_far, r.hidden, r.own, r.gates
    w_up, w_near, w_far, group = r.w_up, r.w_near, r.w_far, r.group
    pre_near, pre_far, out_grad = r.away, r.arrived, r.out_grad
    side = r.weighted.shape[2] // 2
    rows_near = r.weighted.at[:, :, pl.ds(0, side)]
    rows_far = r.weighted.at[:, :, pl.ds(side, side)]
    kept, pair, half = out_grad.shape
    capacity, width = pair // 2, 2 * half
    first = pl.ds(pl.multiple_of(place.f * half, half), half)
    second = pl.ds(pl.multiple_of((1 - place.f) * half, half), half)
    sent = {}

    def send(g, i):
        piece = pl.ds(g * capacity, capacity)
        sent[g, i] = links.send(pre_near.at[i, piece], pre_far.at[i, piece], place.x_peer)

    for i in range(kept):
        rows = slice(i * capacity, (i + 1) * capacity)
        for g in range(2):
            rows_in = group[4 * g : 4 * g + 4].reshape(pick_near.shape[2], width)
            r.slot_rows[g * capacity : (g + 1) * capacity] = dot(
                pick_near[g, rows], rows_in
            ).astype(LOW)
        raw = dot(r.slot_rows[:, first], w_near[i], (1, 1))
        raw = raw + dot(r.slot_rows[:, second], w_far[i], (1, 1))
        pre_near[i] = (raw * gates[i] * slope[i]).astype(LOW)
        send(0, i)
        out_grad[i] = (r.slot_rows[:, first].astype(WIDE) * gates[i]).astype(LOW)
        gate_grad = jnp.sum(raw * hidden[i].astype(WIDE), -1, keepdims=True)
        for g in range(2):
            terms = gate_grad[g * capacity : (g + 1) * capacity]
            terms = terms * pick_near[g, rows].astype(WIDE)
            r.gate_rows[g, i : i + 1] = jnp.sum(terms, 0, keepdims=True)
    for i in range(kept):
        send(1, i)
    t = 2 * place.y + place.c
    r.gate_in[t] = r.gate_rows[...]
    shared = [
        links.send(r.gate_rows, r.gate_in.at[t], d) for d in place.tensor_peers()
    ]
    stores = [
        loads.start(r.hidden, r.near_hidden),
        loads.start(pre_near, r.near_pre),
        loads.start(out_grad, r.near_grad),
    ]

    for i in range(kept):
        back = dot(pre_near[i], w_up[0, i], (1, 1)).astype(LOW)
        rows = slice(i * capacity, (i + 1) * capacity)
        for g in range(2):
            rows_near[g, rows] = back[g * capacity : (g + 1) * capacity]
    for copy in shared:
        copy.wait_recv()
    spread = share_gates(place, links, r)
    experts = place.z * 2 * kept + (1 - place.f) * kept
    for i in range(kept):
        rows = slice(i * capacity, (i + 1) * capacity)
        for g in range(2):
            hot = pick_far[g, rows]
            chances = [r.probs[4 * g + k, pl.ds(experts + i, 1), :] for k in range(4)]
            chances = jnp.concatenate(chances, 1)
            gate = jnp.sum(hot.astype(WIDE) * chances, -1, keepdims=True)
            rows_in = group[4 * g : 4 * g + 4, :, first].reshape(pick_far.shape[2], half)
            into = slice(g * capacity, (g + 1) * capacity)
            r.far_held[i, into] = (dot(hot, rows_in) * gate).astype(LOW)
    stores.append(loads.start(r.far_held, r.far_grad))
    for i in range(2, kept):
        r.hidden_copies.append(send_hidden(place, links, r, i))
    sums = RowSum(links, place, r)
    sums.spread = spread
    steps = {0: sums.to_y, 1: sums.to_heads, kept - 1: sums.total}
    for g in range(2):
        into = slice(g * capacity, (g + 1) * capacity)
        for i in range(kept):
            sent[g, i].wait_recv()
            back = dot(pre_far[i, into], w_up[1, i], (1, 1)).astype(LOW)
            rows_far[g, i * capacity : (i + 1) * capacity] = back
            if g and i in steps:
                for k in range(chunks):
                    steps[i](0, k)
        near = dot(pick_near[g], rows_near[g], (0, 0))
        both = (near + dot(pick_far[g], rows_far[g], (0, 0))).astype(LOW)
        r.x[g] = both.reshape(r.x.shape[1:])
        for k in range(chunks):
            sums.start(g, k)
    stores.append(loads.start(pre_far, r.far_pre))
    return stores, sums


def share_gates(place, links, r):
    t = 2 * place.y + place.c
    r.gate_sum[...] = sum(r.gate_in[k] for k in range(4))
    rows_all = r.probs_own.shape[1]
    rows_of = pl.ds(pl.multiple_of(t * rows_all, rows_all), rows_all)
    r.gate_all[place.z, place.f] = r.gate_sum[place.f, :, rows_of]
    return [
        links.send(r.gate_sum.at[d[FSDP], :, rows_of], r.gate_all.at[place.z, place.f], d)
        for d in place.owners()
    ]


def router_back(r):
    experts, rows_all = r.probs_own.shape
    width = r.residual.shape[1]
    chances = r.probs_own[...]
    prob_grad = r.gate_all[...].reshape(experts, rows_all)
    logit_grad = chances * (prob_grad - jnp.sum(chances * prob_grad, 0, keepdims=True))
    r.logit_grads[...] = logit_grad.astype(LOW)
    r.logit_rows[...] = dot(r.logit_grads[...], r.router[...], (0, 0))
    router_grad = dot(r.second_in[...], r.logit_grads[...], (0, 1))
    spare = jnp.zeros((width, 128 - experts), WIDE)
    router_grad = jnp.concatenate([router_grad, spare], 1).astype(LOW)
    blocks, block, dense_width = r.dense.shape
    r.dense[:, :, pl.ds(dense_width - 128, 128)] = router_grad.reshape(blocks, block, 128)


class RowSum:
    def __init__(self, links, place, r):
        self.links, self.place, self.r = links, place, r
        self.into, self.beside, self.along, self.cross = {}, {}, {}, {}
        self.rows = r.x.shape[3]
        self.own = self.rows // place.heads

    def start(self, g, k):
        source = self.r.x.at[g, :, 1 - self.place.c, :, pl.ds(k * 128, 128)]
        self.into[g, k] = self.links.send(
            source, self.r.core_in.at[k, g], self.place.core_peer
        )

    def to_y(self, g, k):
        self.into[g, k].wait_recv()
        rc, c, y = self.r.core_in.at[k, g], self.place.c, self.place.y

        def add(rows):
            here = self.r.x[g, :, c, rows, pl.ds(k * 128, 128)].astype(WIDE)
            rc[:, rows, :] = (rc[:, rows, :].astype(WIDE) + here).astype(LOW)

        in_rows(self.rows, 64, add)
        self.beside[g, k] = self.links.send(
            rc.at[1 - y], self.r.y_in.at[k, g], self.place.y_peer
        )

    def to_heads(self, g, k):
        self.beside[g, k].wait_recv()
        y_in, core_in = self.r.y_in.at[k, g], self.r.core_in.at[k, g, self.place.y]

        def add(rows):
            both = y_in[rows, :].astype(WIDE) + core_in[rows, :].astype(WIDE)
            y_in[rows, :] = both.astype(LOW)

        in_rows(self.rows, 64, add)
        own = self.own
        self.along[g, k] = all_heads(
            self.links,
            self.place,
            lambda n, to: (
                y_in.at[pl.ds(pl.multiple_of(to * own, own), own)],
                self.r.far.at[k, n, g],
            ),
        )

    def total(self, g, k):
        for copy in self.along[g, k]:
            copy.wait_recv()
        z, own = self.place.z, self.own
        total = self.r.y_in[k, g, pl.ds(pl.multiple_of(z * own, own), own), :].astype(WIDE)
        for n in range(self.place.heads - 1):
            total = total + self.r.far[k, n, g].astype(WIDE)
        self.r.pair[k, g] = total.astype(LOW)

    def to_x(self, k):
        self.cross[k] = self.links.send(
            self.r.pair.at[k, 1 - self.place.f], self.r.x_in.at[k], self.place.x_peer
        )


def back_part(place, links, chunks, sums, r):
    heads, f, y, z = place.heads, place.f, place.y, place.z
    me, valid = place.image(0, 0, 0), r.valid_row
    residual, gain, final_grad, tokens = r.residual, r.gain, r.final_grad, r.tokens
    gain_one, projected, log_total, mixed = r.gain_one, r.projected, r.log_total, r.mixed
    qkv, wo, tokens_grad, dense_out, gain_out = (
        r.qkv,
        r.wo_all,
        r.tokens_grad,
        r.dense_out,
        r.gain_out,
    )
    pair, x_in, logit_rows, attended, first_in = (
        r.pair,
        r.x_in,
        r.logit_rows,
        r.attended,
        r.first_in,
    )
    projected_grad, first_part, dense, dense_core = (
        r.projected_grad,
        r.first_part,
        r.dense,
        r.dense_core,
    )
    xa, ya, yb, xb, first_far, rounded = r.xa, r.ya, r.yb, r.xb, r.first_far, r.rounded
    gain_part, gain_plane, gain_heads = r.gain_part, r.gain_plane, r.gain_heads
    rows_all, width = residual.shape
    half = width // 2
    own = rows_all // heads
    mine = pl.ds(pl.multiple_of(z * own, own), own)
    blocks, block, dense_width = dense.shape
    qkv_width = projected.shape[1]
    for step in range(chunks + 2):
        if step == 2:
            for copy in sums.spread:
                copy.wait_recv()
            router_back(r)
        for k in range(chunks):
            if step == k:
                sums.to_y(1, k)
            if step == k + 1:
                sums.to_heads(1, k)
            if step == k + 2:
                sums.total(1, k)
                sums.to_x(k)
    normed, spread_two = normalize(residual[mine, :])
    cross = sums.cross
    near = jnp.concatenate([pair[k, f].astype(WIDE) for k in range(chunks)], 1)
    for k in range(chunks):
        cross[k].wait_recv()
    away = jnp.concatenate([x_in[k].astype(WIDE) for k in range(chunks)], 1)
    first = f == 0
    rows_grad = jnp.concatenate([jnp.where(first, near, away), jnp.where(first, away, near)], 1)
    second_grad = rows_grad + logit_rows[mine, :]
    weighted = second_grad * gain[...]
    gain_part[1:2, :] = jnp.sum(second_grad * normed, 0, keepdims=True)
    inner = (
        weighted
        - jnp.mean(weighted, -1, keepdims=True)
        - normed * jnp.mean(weighted * normed, -1, keepdims=True)
    )
    total_grad = final_grad[...] + inner * spread_two
    attended[mine, :] = total_grad.astype(LOW)
    for copy in all_heads(
        links, place, lambda k, to: (attended.at[mine], attended.at[mine])
    ):
        copy.wait_recv()

    mixed_grad = dot(attended[...], wo[:, z].reshape(width, wo.shape[3])).astype(LOW)
    head_count = log_total.shape[1]
    size = qkv_width // head_count // 3
    score_scale = size ** (-0.5)
    keys_ok = valid[...] > 0
    grads = []
    for h in range(head_count):
        at = 3 * h * size
        query, key, value = (projected[:, at + n * size : at + (n + 1) * size] for n in range(3))
        above = mixed_grad[:, h * size : (h + 1) * size]
        scores = jnp.where(keys_ok, dot(query, key, (1, 1)) * score_scale, MASKED)
        chances = jnp.exp(scores - log_total[:, h : h + 1])
        prob_part = dot(above, value, (1, 1))
        inner = jnp.sum(chances * prob_part, -1, keepdims=True)
        score_grad = (chances * (prob_part - inner)).astype(LOW)
        grads.append(dot(score_grad, key) * score_scale)
        grads.append(dot(score_grad, query, (0, 0)) * score_scale)
        grads.append(dot(chances.astype(LOW), above, (0, 0)))
    projected_grad[...] = jnp.concatenate(grads, 1).astype(LOW)
    weight = qkv[:, :, pl.ds(128, qkv_width)].reshape(width, qkv_width)
    back = dot(projected_grad[...], weight, (1, 1))
    first_part[...] = back.astype(LOW).reshape(heads, own, width)
    cuts = [pl.ds(q * own // 2, own // 2) for q in range(2)]
    along = [
        all_heads(links, place, lambda n, to: (first_part.at[to, q], first_far.at[n, q]))
        for q in cuts
    ]
    dense_now = jnp.concatenate(
        [
            dot(first_in[...], projected_grad[...], (0, 0)).astype(LOW),
            dot(attended[...], mixed[...], (0, 0)).astype(LOW),
        ],
        1,
    )
    dense[:, :, pl.ds(0, dense_width - 128)] = dense_now.reshape(blocks, block, dense_width - 128)
    adder = PlaneSum(links, place, dense, dense_core, xa, ya, yb, xb, xa.shape[2], 32)
    adder.start()
    gain_part[0:1, :] = jnp.sum(back * normalize(tokens[...].astype(WIDE))[0], 0, keepdims=True)
    gain_plane[me] = gain_part[...]
    small = [links.send(gain_part, gain_plane.at[me], d) for d in place.plane_peers]
    adder.cores()
    adder.cross()
    for copy in small:
        copy.wait_recv()
    gain_heads[z] = sum(gain_plane[i] for i in range(8))
    gains = all_heads(links, place, lambda n, to: (gain_heads.at[z], gain_heads.at[z]))
    ends = []
    for n_cut, q in enumerate(cuts):
        at = pl.ds(pl.multiple_of(z * own + n_cut * own // 2, own // 2), own // 2)
        normed, spread_one = normalize(tokens[at, :].astype(WIDE))
        for copy in along[n_cut]:
            copy.wait_recv()
        first_grad = first_part[z, q].astype(WIDE)
        for n in range(heads - 1):
            first_grad = first_grad + first_far[n, q].astype(WIDE)
        weighted = first_grad * gain_one[...]
        inner = (
            weighted
            - jnp.mean(weighted, -1, keepdims=True)
            - normed * jnp.mean(weighted * normed, -1, keepdims=True)
        )
        here = total_grad[n_cut * own // 2 : (n_cut + 1) * own // 2]
        rounded[z, q] = (here + inner * spread_one).astype(LOW)
        ends += all_heads(links, place, lambda n, to: (rounded.at[z, q], rounded.at[z, q]))

    def keep(rows, columns, values):
        dense_out[rows, columns] = values

    adder.finish(keep)
    for copy in gains:
        copy.wait_recv()
    gain_out[...] = sum(gain_heads[i] for i in range(heads))
    for copy in ends:
        copy.wait_recv()
    for i in range(heads):
        tokens_grad[i] = rounded[i].astype(WIDE)
    for copy in r.hidden_copies:
        copy.wait_recv()


def layer_kernel(heads, chunks, small, names, *refs):
    r = types.SimpleNamespace(**dict(zip(names, refs)), hidden_copies=[])
    place = Place(heads)
    links = Links(r.send_sems, r.recv_sems)
    loads = Loads(r.load_sems)
    kept = r.w_far.shape[0]
    mine, theirs = place.f * kept, (1 - place.f) * kept
    first = [loads.start(getattr(r, name + "_hbm"), getattr(r, name)) for name in small]
    ups = {}
    for far in (1, 0):
        for i in range(kept):
            source = (theirs if far else mine) + i
            ups[far, i] = loads.start(r.up.at[source], r.w_up.at[far, i])
    nears = [loads.start(r.down.at[mine + i], r.w_near.at[i]) for i in range(kept)]
    place.greet(place.everyone())
    for copy in first:
        copy.wait()
    from_x, down_far = front_part(place, links, r)
    held = experts_part(place, links, loads, (ups, nears), down_far, r)
    extra = combine_part(place, links, chunks, r)
    links.left(from_x)
    stores, sums = experts_back_part(place, links, loads, chunks, r)
    for copy in extra:
        copy.wait_recv()
    back_part(place, links, chunks, sums, r)
    for copy in held + stores:
        copy.wait()
    links.drain()


def named_call(kernel, ins, outs, scratch, copies, loads, collective_id, vmem_mib, microseconds):
    spaces = {False: pltpu.VMEM, True: pltpu.HBM}
    names = [*ins, *outs, *scratch, "load_sems", "send_sems", "recv_sems"]
    made = pl.pallas_call(
        functools.partial(kernel, names),
        out_shape=[o[0] for o in outs.values()],
        in_specs=[pl.BlockSpec(memory_space=spaces[a[1]]) for a in ins.values()],
        out_specs=[pl.BlockSpec(memory_space=spaces[o[1]]) for o in outs.values()],
        scratch_shapes=[
            *scratch.values(),
            pltpu.SemaphoreType.DMA((loads,)),
            pltpu.SemaphoreType.DMA((copies,)),
            pltpu.SemaphoreType.DMA((copies,)),
        ],
        compiler_params=pltpu.CompilerParams(
            collective_id=collective_id,
            has_side_effects=True,
            vmem_limit_bytes=vmem_mib * 2**20,
        ),
        cost_estimate=spends(microseconds),
    )(*[a[0] for a in ins.values()])
    return types.SimpleNamespace(**dict(zip(outs, made)))


def layer(heads, experts, capacity, small, hbm):
    rows, width = small["tokens"].shape
    own, half, chunks = rows // heads, width // 2, width // 256
    local_experts, _, hidden_width = hbm["up"].shape
    kept, pair, group_rows = local_experts // 2, 2 * capacity, 4 * rows
    mixed_width, block = small["out_in"].shape
    head_count = small["qkv_in"].shape[0]
    qkv_width = 3 * mixed_width
    gathered_width = 128 + qkv_width + -(128 + qkv_width) % 256
    dense_width = qkv_width + mixed_width + 128
    cut = 128 * ((dense_width // 128 + 1) // 2)
    ins = {name: (array, True) for name, array in hbm.items()}
    ins.update({name + "_hbm": (array, True) for name, array in small.items()})
    outs = dict(
        result=(shape((heads, own, width)), False),
        loss=(shape((heads, 8, 128), WIDE), False),
        tokens_grad=(shape((heads, own, width), WIDE), False),
        dense_out=(shape((block, dense_width), WIDE), False),
        gain_out=(shape((2, width), WIDE), False),
        near_out=(shape((kept, pair, half)), True),
        near_pre=(shape((kept, pair, hidden_width)), True),
        near_hidden=(shape((kept, pair, hidden_width)), True),
        near_grad=(shape((kept, pair, half)), True),
        far_out=(shape((kept, pair, half)), True),
        far_pre=(shape((kept, pair, hidden_width)), True),
        far_hidden=(shape((kept, pair, hidden_width)), True),
        far_grad=(shape((kept, pair, half)), True),
    )
    low = dict(
        pick_near=(2, kept * capacity, group_rows),
        pick_far=(2, kept * capacity, group_rows),
        buffer_near=(2, pair, half),
        buffer_far=(2, pair, half),
        hidden=(kept, pair, hidden_width),
        weighted=(2, kept * capacity, width),
        away=(kept, pair, hidden_width),
        arrived=(kept, pair, hidden_width),
        w_up=(2, kept, half, hidden_width),
        w_near=(kept, hidden_width, half),
        w_far=(kept, hidden_width, half),
        part=(2, 2, 2, rows, width),
        group=(8, rows, width),
        sum_core=(chunks, 2, 2, rows, 256),
        sum_xa=(chunks, 2, rows, 128),
        sum_ya=(chunks, rows, 128),
        sum_yb=(chunks, 2, rows, 128),
        sum_xb=(chunks, rows, 128),
        image_sum=(chunks, rows, 256),
        image_far=(chunks, heads - 1, own, 256),
        out_grad=(kept, pair, half),
        far_held=(kept, pair, half),
        slot_rows=(pair, width),
        x=(2, 2, 2, rows, half),
        other_half=(rows, half),
        qkv=(8, block, gathered_width),
        wo_all=(8, heads, block, mixed_width),
        router=(experts, width),
        projected=(rows, qkv_width),
        mixed=(rows, mixed_width),
        all_mixed=(heads, rows, mixed_width),
        second_in=(rows, width),
        core_in=(chunks, 2, 2, rows, 128),
        y_in=(chunks, 2, rows, 128),
        far=(chunks, heads - 1, 2, own, 128),
        pair=(chunks, 2, own, 128),
        x_in=(chunks, own, 128),
        logit_grads=(experts, rows),
        attended=(rows, width),
        first_in=(rows, width),
        projected_grad=(rows, qkv_width),
        first_part=(heads, own, width),
        dense=(8, block, dense_width),
        dense_core=(4, block, dense_width),
        xa=(2, block, cut),
        ya=(block, cut),
        yb=(2, block, dense_width - cut),
        xb=(block, dense_width - cut),
        first_far=(heads - 1, own, width),
        rounded=(heads, own, width),
    )
    wide = dict(
        gates=(kept, pair, 1),
        counts=(8, 8, 128),
        scale=(8, 128),
        loss_scale=(8, 128),
        valid=(rows, 8),
        gain_one=(1, width),
        gain=(1, width),
        log_total=(rows, head_count),
        residual=(rows, width),
        probs=(8, experts, rows),
        probs_own=(experts, rows),
        own=(kept, pair, hidden_width),
        final_grad=(own, width),
        gate_rows=(2, kept, group_rows),
        gate_in=(4, 2, kept, group_rows),
        gate_sum=(2, kept, group_rows),
        gate_all=(heads, 2, kept, rows),
        logit_rows=(rows, width),
        gain_part=(2, width),
        gain_plane=(8, 2, width),
        gain_heads=(heads, 2, width),
    )
    scratch = {name: pltpu.VMEM(dims, LOW) for name, dims in low.items()}
    scratch.update({name: pltpu.VMEM(dims, WIDE) for name, dims in wide.items()})
    whole = dict(
        far_route=small["near_route"].shape,
        slots=(2 * local_experts, group_rows),
    )
    scratch.update({name: pltpu.VMEM(a.shape, a.dtype) for name, a in small.items()})
    scratch.update({name: pltpu.VMEM(dims, jnp.int32) for name, dims in whole.items()})
    copies = FRONT_COPIES + 2 * (heads - 1) + 2 * kept + chunks * (5 + GATHER_COPIES + 2 * (heads - 1)) + 2 * (heads - 1)
    copies += 2 * kept + kept + 2 * chunks * (2 + heads - 1) + chunks + 3 + 2 * heads - 1
    copies += heads - 1 + SUM_COPIES + 5 * (heads - 1) + 7
    return named_call(
        functools.partial(layer_kernel, heads, chunks, tuple(small)),
        ins,
        outs,
        scratch,
        copies,
        5 * kept + 6 + len(small),
        1,
        59,
        280,
    )


def finish_kernel(s, *refs):
    sides, rest = (refs[:4], refs[4:8]), refs[8:]
    result_in, tokens_in, dense, gains, loss_in = rest[:5]
    up, down, result, tokens_grad, qkv_grad, out_grad, router_grad, gain_grads, loss = rest[5:]
    i = pl.program_id(0)
    kept = pl.num_programs(0) // 2
    for side, (rows, pre, hidden, grad) in enumerate(sides):
        j = i - s[side]

        @pl.when((j >= 0) & (j < kept))
        def _(rows=rows, pre=pre, hidden=hidden, grad=grad):
            up[0] = dot(rows[0], pre[0], (0, 0))
            down[0] = dot(hidden[0], grad[0], (0, 0))

    @pl.when(i == 0)
    def _():
        result[...] = result_in[...].reshape(result.shape)
        tokens_grad[...] = tokens_in[...].reshape(tokens_grad.shape)
        head_count, block, size = qkv_grad.shape
        for h in range(head_count):
            qkv_grad[h] = dense[:, h * size : (h + 1) * size]
        at = head_count * size
        mixed_width = out_grad.shape[0]
        out_grad[...] = jnp.transpose(dense[:, at : at + mixed_width])
        last = jnp.transpose(dense[:, at + mixed_width : at + mixed_width + 128])
        router_grad[...] = last[: router_grad.shape[0]]
        gain_grads[...] = sum(
            jnp.where(s[2] == b, gains[:, b * block : (b + 1) * block], 0.0) for b in range(8)
        )
        loss[...] = jnp.sum(jnp.sum(loss_in[...], 0), keepdims=True)


def finish(scalars, near, far, small, shapes):
    kept, _, half = near[0].shape
    hidden_width = near[1].shape[2]

    def of(array, which):
        return pl.BlockSpec(
            (1, *array.shape[1:]), lambda i, s: (jnp.clip(i - s[which], 0, kept - 1), 0, 0)
        )

    def all_of(array):
        return pl.BlockSpec(array.shape, lambda i, s, n=len(array.shape): (0,) * n)

    return pl.pallas_call(
        finish_kernel,
        out_shape=[
            shape((2 * kept, half, hidden_width), WIDE),
            shape((2 * kept, hidden_width, half), WIDE),
            *shapes,
        ],
        grid_spec=pltpu.PrefetchScalarGridSpec(
            num_scalar_prefetch=1,
            grid=(2 * kept,),
            in_specs=[of(array, 0) for array in near]
            + [of(array, 1) for array in far]
            + [all_of(array) for array in small],
            out_specs=[
                pl.BlockSpec((1, half, hidden_width), lambda i, s: (i, 0, 0)),
                pl.BlockSpec((1, hidden_width, half), lambda i, s: (i, 0, 0)),
                *[all_of(array) for array in shapes],
            ],
        ),
        compiler_params=pltpu.CompilerParams(vmem_limit_bytes=60 * 2**20),
        cost_estimate=spends(8),
    )(scalars, *near, *far, *small)


def fast(
    tokens,
    valid_mask,
    routes,
    teacher,
    gain_one,
    qkv_weight,
    out_weight,
    gain_two,
    router_weight,
    expert_up,
    expert_down,
):
    heads = lax.axis_size(HEADS)
    f, t = lax.axis_index(FSDP), lax.axis_index(TENSOR)
    _, rows, width = tokens.shape
    block, head_count, qkv_dim = qkv_weight.shape
    mixed_width = out_weight.shape[0] * out_weight.shape[1]
    local_experts = expert_up.shape[0]
    kept = local_experts // 2
    expert_count = local_experts * heads
    capacity = 2 * routes.shape[2] * 4 * rows // expert_count
    small = dict(
        router_in=router_weight.T,
        gain_one_in=gain_one[None],
        gain_two_in=gain_two[None],
        qkv_in=jnp.swapaxes(qkv_weight, 0, 1),
        out_in=out_weight.reshape(mixed_width, block),
        near_route=jnp.swapaxes(routes, 1, 2),
        tokens=tokens[0],
        teacher=teacher[0],
        valid_row=valid_mask,
    )
    made = layer(heads, expert_count, capacity, small, dict(up=expert_up, down=expert_down))
    scalars = jnp.stack([f * kept, (1 - f) * kept, f * 4 + t]).astype(jnp.int32)
    up_grad, down_grad, result, tokens_grad, qkv_grad, out_grad, router_grad, gains, loss = finish(
        scalars,
        [made.near_out, made.near_pre, made.near_hidden, made.near_grad],
        [made.far_out, made.far_pre, made.far_hidden, made.far_grad],
        [made.result, made.tokens_grad, made.dense_out, made.gain_out, made.loss],
        [
            shape((rows, width)),
            shape((rows, width), WIDE),
            shape((head_count, block, qkv_dim), WIDE),
            shape((mixed_width, block), WIDE),
            shape((expert_count, block), WIDE),
            shape((2, block), WIDE),
            shape((1, 1), WIDE),
        ],
    )
    return (
        result[None],
        loss.reshape(1),
        tokens_grad[None],
        gains[0],
        jnp.swapaxes(qkv_grad, 0, 1),
        out_grad.reshape(head_count, -1, block),
        gains[1],
        router_grad.T,
        up_grad,
        down_grad,
    )


def local(sizes, *args):
    tokens, routes, up = args[0], args[2], args[9]
    fits = (
        sizes[FSDP] == 2
        and sizes[TENSOR] == 4
        and sizes[HEADS] % 2 == 0
        and tokens.shape[0] == 1
        and up.shape[0] % 8 == 0
        and tokens.shape[1] % (32 * sizes[HEADS]) == 0
        and tokens.shape[2] % 256 == 0
        and routes.shape[2] <= 8
        and up.shape[0] * sizes[HEADS] <= 126
    )
    return fast(*args) if fits else general(*args)


def solution(mesh):
    sizes = dict(mesh.shape)
    program = functools.partial(local, sizes)
    in_specs = (
        P((FSDP, TENSOR), None, None),
        P((FSDP, TENSOR), None),
        P(FSDP, None, None),
        P((FSDP, TENSOR), None, None),
        P((FSDP, TENSOR)),
        P((FSDP, TENSOR), HEADS, None),
        P(HEADS, None, (FSDP, TENSOR)),
        P((FSDP, TENSOR)),
        P((FSDP, TENSOR), None),
        P(HEADS, FSDP, TENSOR),
        P(HEADS, TENSOR, FSDP),
    )
    out_specs = (
        P((FSDP, TENSOR), None, None),
        P((FSDP, TENSOR)),
        P((FSDP, TENSOR), None, None),
        P((FSDP, TENSOR)),
        P((FSDP, TENSOR), HEADS, None),
        P(HEADS, None, (FSDP, TENSOR)),
        P((FSDP, TENSOR)),
        P((FSDP, TENSOR), None),
        P(HEADS, FSDP, TENSOR),
        P(HEADS, TENSOR, FSDP),
    )
    return jax.shard_map(program, mesh=mesh, in_specs=in_specs, out_specs=out_specs, check_vma=False)
```

```python
import functools
import types

import jax
import jax.numpy as jnp
from jax import lax
from jax.experimental import pallas as pl
from jax.experimental.pallas import tpu as pltpu
from jax.sharding import PartitionSpec as P

FSDP, HEADS, TENSOR = "fsdp", "heads", "tensor"
EPSILON = 1e-06
MASKED = -1e30
ROOT_HALF = 0.7071067811865476
DENSITY = 0.3989422804014327


def normalize(values):
    center = values - jnp.mean(values, -1, keepdims=True)
    inv_std = lax.rsqrt(jnp.mean(center * center, -1, keepdims=True) + EPSILON)
    return (center * inv_std, inv_std)


def norm_back(gradient, normed, inv_std, gain_vector):
    weighted = gradient * gain_vector
    gain_grad = jnp.sum(gradient * normed, axis=(0, 1))
    inner = (
        weighted
        - jnp.mean(weighted, -1, keepdims=True)
        - normed * jnp.mean(weighted * normed, -1, keepdims=True)
    )
    return (inner * inv_std, gain_grad)


def scores_of(queries, key_rows, keys_ok, score_scale):
    raw_scores = (
        jnp.einsum("iqhe,ikhe->ihqk", queries, key_rows, preferred_element_type=jnp.float32)
        * score_scale
    )
    return jnp.where(keys_ok, raw_scores, MASKED)


def gather_weights(
    gain_one, qkv_weight, out_weight, gain_two, router_weight, expert_up, expert_down
):
    dense_set = (
        lax.all_gather(qkv_weight, (FSDP, TENSOR), axis=0, tiled=True),
        lax.all_gather(out_weight, (FSDP, TENSOR), axis=2, tiled=True),
        lax.all_gather(router_weight, (FSDP, TENSOR), axis=0, tiled=True),
        lax.all_gather(gain_one, (FSDP, TENSOR), axis=0, tiled=True),
        lax.all_gather(gain_two, (FSDP, TENSOR), axis=0, tiled=True),
    )
    expert_set = (
        lax.all_gather(expert_up, FSDP, axis=1, tiled=True),
        lax.all_gather(expert_down, FSDP, axis=2, tiled=True),
    )
    return (dense_set, expert_set)


def reduce_expert_grads(up_grad, down_grad):
    return (
        lax.psum_scatter(up_grad, FSDP, scatter_dimension=1, tiled=True),
        lax.psum_scatter(down_grad, FSDP, scatter_dimension=2, tiled=True),
    )


def general(
    tokens,
    valid_mask,
    routes,
    teacher,
    gain_one,
    qkv_weight,
    out_weight,
    gain_two,
    router_weight,
    expert_up,
    expert_down,
):
    valid_total = lax.psum(jnp.sum(valid_mask.astype(jnp.float32)), (FSDP, TENSOR))
    dense_set, expert_set = gather_weights(
        gain_one, qkv_weight, out_weight, gain_two, router_weight, expert_up, expert_down
    )
    qkv_full, output_complete, router_full, gain_a, gain_b = dense_set
    up_full, down_full = expert_set
    image_count, token_slots, model_width = tokens.shape
    head_dim = qkv_full.shape[2] // 3
    local_experts = expert_up.shape[0]
    tensor_size = lax.axis_size(TENSOR)
    group_images = image_count * tensor_size
    group_rows = group_images * token_slots
    top_choices = routes.shape[2]
    expert_count = local_experts * lax.axis_size(HEADS)
    capacity = 2 * top_choices * group_rows // expert_count
    slot_count = local_experts * capacity
    total_tokens = image_count * token_slots * lax.axis_size(FSDP) * tensor_size
    total_images = image_count * lax.axis_size(FSDP) * tensor_size
    score_scale = head_dim ** (-0.5)
    inputs = tokens.astype(jnp.float32)
    normed_one, spread_one = normalize(inputs)
    first_in = (normed_one * gain_a.astype(jnp.float32)).astype(jnp.bfloat16)
    projected = jnp.einsum(
        "isd,dhe->ishe", first_in, qkv_full, preferred_element_type=jnp.float32
    ).astype(jnp.bfloat16)
    queries = projected[..., :head_dim]
    key_rows = projected[..., head_dim : 2 * head_dim]
    values = projected[..., 2 * head_dim :]
    keys_ok = (valid_mask > 0)[:, None, None, :]
    scores = scores_of(queries, key_rows, keys_ok, score_scale)
    peak_score = jnp.max(scores, -1, keepdims=True)
    exp_scores = jnp.exp(scores - peak_score)
    score_total = jnp.sum(exp_scores, -1, keepdims=True)
    logarithm_total = peak_score + jnp.log(score_total)
    attention = (exp_scores / score_total).astype(jnp.bfloat16)
    combined_heads = jnp.einsum(
        "ihqk,ikhe->iqhe", attention, values, preferred_element_type=jnp.float32
    ).astype(jnp.bfloat16)
    attn_part = jnp.einsum(
        "iqhe,hed->iqd", combined_heads, output_complete, preferred_element_type=jnp.float32
    )
    attended = lax.psum(attn_part, HEADS)
    residual = inputs + attended
    normed_two, spread_two = normalize(residual)
    second_in = (normed_two * gain_b.astype(jnp.float32)).astype(jnp.bfloat16)
    group_in = lax.all_gather(second_in, TENSOR, axis=0, tiled=True)
    rows_in = group_in.reshape(group_rows, model_width)
    logits = jnp.dot(rows_in, router_full, preferred_element_type=jnp.float32)
    peak_logit = jnp.max(logits, -1, keepdims=True)
    exponent_logits = jnp.exp(logits - peak_logit)
    router_probs = exponent_logits / jnp.sum(exponent_logits, -1, keepdims=True)
    expert_ids = jnp.arange(expert_count, dtype=jnp.int32)
    route_pairs = routes.reshape(group_rows, top_choices)
    picked_hot = (route_pairs[:, :, None] == expert_ids[None, None, :]).astype(jnp.float32)
    gate_weight_values = jnp.sum(router_probs[:, None, :] * picked_hot, -1)
    flat_routes = route_pairs.reshape(group_rows * top_choices)
    route_hot = (flat_routes[:, None] == expert_ids[None, :]).astype(jnp.int32)
    order = jnp.arange(group_rows * top_choices, dtype=jnp.int32)
    before = (order[None, :] < order[:, None]).astype(jnp.bfloat16)
    earlier = jnp.dot(
        before, route_hot.astype(jnp.bfloat16), preferred_element_type=jnp.float32
    ).astype(jnp.int32)
    slot_index = jnp.sum(earlier * route_hot, 1)
    first_expert = lax.axis_index(HEADS) * local_experts
    is_local = (flat_routes >= first_expert) & (flat_routes < first_expert + local_experts)
    target = jnp.where(is_local, (flat_routes - first_expert) * capacity + slot_index, slot_count)
    owner_row = jnp.arange(group_rows * top_choices, dtype=jnp.int32) // top_choices
    source = jnp.zeros((slot_count,), jnp.int32).at[target].set(owner_row, mode="drop")
    slot_gate = (
        jnp.zeros((slot_count,), jnp.float32)
        .at[target]
        .set(gate_weight_values.reshape(-1), mode="drop")
    )
    slot_pick = jnp.minimum(target, slot_count - 1)
    retain_mask = is_local.astype(jnp.float32)
    dispatched = rows_in[source].reshape(local_experts, capacity, model_width)
    before_gelu = jnp.einsum(
        "ecd,edf->ecf", dispatched, up_full, preferred_element_type=jnp.float32
    )
    hidden = jax.nn.gelu(before_gelu, approximate=False).astype(jnp.bfloat16)
    expert_out = jnp.einsum(
        "ecf,efd->ecd", hidden, down_full, preferred_element_type=jnp.float32
    ).reshape(slot_count, model_width)
    weighted = expert_out * slot_gate[:, None]
    moe_part = jnp.sum(
        (weighted[slot_pick] * retain_mask[:, None]).reshape(group_rows, top_choices, model_width),
        1,
    )
    moe_part = moe_part.reshape(group_images, token_slots, model_width)
    expert_sum = lax.psum(
        lax.psum_scatter(moe_part, TENSOR, scatter_dimension=0, tiled=True), HEADS
    )
    final = residual + expert_sum
    valid_rows = valid_mask.astype(jnp.float32)[..., None]
    difference = (final - teacher.astype(jnp.float32)) * valid_rows
    loss_terms = jnp.sum(difference * difference, axis=(1, 2)) * (
        total_images / (valid_total * model_width)
    )
    final_grad = difference * (total_tokens / valid_total)
    dense_set, expert_set = gather_weights(
        gain_one, qkv_weight, out_weight, gain_two, router_weight, expert_up, expert_down
    )
    qkv_full, output_complete, router_full, gain_a, gain_b = dense_set
    up_full, down_full = expert_set
    moe_grad = final_grad.astype(jnp.bfloat16)
    group_grad = lax.all_gather(moe_grad, TENSOR, axis=0, tiled=True).reshape(
        group_rows, model_width
    )
    slot_grad = group_grad[source].astype(jnp.float32)
    gate_slot_grad = jnp.sum(slot_grad * expert_out, -1)
    out_grad = (
        (slot_grad * slot_gate[:, None])
        .astype(jnp.bfloat16)
        .reshape(local_experts, capacity, model_width)
    )
    expert_down_grad = jnp.einsum(
        "ecf,ecd->efd", hidden, out_grad, preferred_element_type=jnp.float32
    )
    hidden_grad = jnp.einsum(
        "ecd,efd->ecf", out_grad, down_full, preferred_element_type=jnp.float32
    )
    normal_cdf = 0.5 * (1.0 + lax.erf(before_gelu * ROOT_HALF))
    slope = normal_cdf + before_gelu * DENSITY * jnp.exp(-0.5 * before_gelu * before_gelu)
    pre_grad = (hidden_grad * slope).astype(jnp.bfloat16)
    expert_up_grad = jnp.einsum(
        "ecd,ecf->edf", dispatched, pre_grad, preferred_element_type=jnp.float32
    )
    row_grad = jnp.einsum(
        "ecf,edf->ecd", pre_grad, up_full, preferred_element_type=jnp.float32
    ).reshape(slot_count, model_width)
    rows_part = jnp.sum(
        (row_grad[slot_pick] * retain_mask[:, None]).reshape(group_rows, top_choices, model_width),
        1,
    )
    rows_part = rows_part.reshape(group_images, token_slots, model_width)
    gate_part = (gate_slot_grad[slot_pick] * retain_mask).reshape(
        group_images, token_slots, top_choices
    )
    rows_share, gate_share = (
        lax.psum_scatter(rows_part, TENSOR, scatter_dimension=0, tiled=True),
        lax.psum_scatter(gate_part, TENSOR, scatter_dimension=0, tiled=True),
    )
    second_grad, gate_grad = lax.psum((rows_share, gate_share), HEADS)
    own_start = lax.axis_index(TENSOR) * image_count * token_slots
    own_rows = image_count * token_slots
    own_probs = lax.dynamic_slice_in_dim(router_probs, own_start, own_rows, 0).reshape(
        image_count, token_slots, expert_count
    )
    own_hot = lax.dynamic_slice_in_dim(picked_hot, own_start, own_rows, 0).reshape(
        image_count, token_slots, top_choices, expert_count
    )
    prob_grad = jnp.sum(gate_grad[..., None] * own_hot, 2)
    logit_grad = (
        own_probs * (prob_grad - jnp.sum(own_probs * prob_grad, -1, keepdims=True))
    ).astype(jnp.bfloat16)
    router_grad = jnp.einsum(
        "isd,ise->de", second_in, logit_grad, preferred_element_type=jnp.float32
    )
    second_grad = second_grad + jnp.einsum(
        "ise,de->isd", logit_grad, router_full, preferred_element_type=jnp.float32
    )
    residual_norm, gain_two_grad = norm_back(
        second_grad, normed_two, spread_two, gain_b.astype(jnp.float32)
    )
    residual_grad = final_grad + residual_norm
    attended_output_gradient = residual_grad.astype(jnp.bfloat16)
    out_weight_grad = jnp.einsum(
        "iqhe,iqd->hed",
        combined_heads,
        attended_output_gradient,
        preferred_element_type=jnp.float32,
    )
    mixed_grad = jnp.einsum(
        "iqd,hed->iqhe",
        attended_output_gradient,
        output_complete,
        preferred_element_type=jnp.float32,
    ).astype(jnp.bfloat16)
    scores = scores_of(queries, key_rows, keys_ok, score_scale)
    probs = jnp.exp(scores - logarithm_total)
    probs_low = probs.astype(jnp.bfloat16)
    prob_part = jnp.einsum(
        "iqhe,ikhe->ihqk", mixed_grad, values, preferred_element_type=jnp.float32
    )
    score_grad = (probs * (prob_part - jnp.sum(probs * prob_part, -1, keepdims=True))).astype(
        jnp.bfloat16
    )
    query_grad = (
        jnp.einsum("ihqk,ikhe->iqhe", score_grad, key_rows, preferred_element_type=jnp.float32)
        * score_scale
    )
    key_grad = (
        jnp.einsum("ihqk,iqhe->ikhe", score_grad, queries, preferred_element_type=jnp.float32)
        * score_scale
    )
    value_grad = jnp.einsum(
        "ihqk,iqhe->ikhe", probs_low, mixed_grad, preferred_element_type=jnp.float32
    )
    projected_grad = jnp.concatenate([query_grad, key_grad, value_grad], -1).astype(jnp.bfloat16)
    qkv_grad = jnp.einsum(
        "isd,ishe->dhe", first_in, projected_grad, preferred_element_type=jnp.float32
    )
    first_part = jnp.einsum(
        "ishe,dhe->isd", projected_grad, qkv_full, preferred_element_type=jnp.float32
    )
    first_grad = lax.psum(first_part, HEADS)
    input_norm, gain_one_grad = norm_back(
        first_grad, normed_one, spread_one, gain_a.astype(jnp.float32)
    )
    tokens_grad = residual_grad + input_norm
    dense_grads = (
        lax.psum_scatter(qkv_grad, (FSDP, TENSOR), scatter_dimension=0, tiled=True),
        lax.psum_scatter(out_weight_grad, (FSDP, TENSOR), scatter_dimension=2, tiled=True),
        lax.psum_scatter(router_grad, (FSDP, TENSOR), scatter_dimension=0, tiled=True),
        lax.psum_scatter(gain_one_grad, (FSDP, TENSOR), scatter_dimension=0, tiled=True),
        lax.psum_scatter(gain_two_grad, (FSDP, TENSOR), scatter_dimension=0, tiled=True),
    )
    expert_grads = reduce_expert_grads(expert_up_grad, expert_down_grad)
    return (
        final.astype(jnp.bfloat16),
        loss_terms,
        tokens_grad,
        dense_grads[3],
        dense_grads[0],
        dense_grads[1],
        dense_grads[4],
        dense_grads[2],
        expert_grads[0],
        expert_grads[1],
    )


MESH = pl.DeviceIdType.MESH
LOW = jnp.bfloat16
WIDE = jnp.float32


class Links:
    def __init__(self, send_sems, recv_sems):
        self.send_sems, self.recv_sems = send_sems, recv_sems
        self.copies, self.gone = [], []

    def send(self, src, dst, device):
        k = len(self.copies)
        assert k < self.send_sems.shape[0]
        copy = pltpu.make_async_remote_copy(
            src_ref=src,
            dst_ref=dst,
            send_sem=self.send_sems.at[k],
            recv_sem=self.recv_sems.at[k],
            device_id=device,
            device_id_type=MESH,
        )
        copy.start()
        self.copies.append(copy)
        return copy

    def left(self, copies):
        for copy in copies:
            copy.wait_send()
            self.gone.append(copy)

    def drain(self):
        for copy in self.copies:
            if not any(copy is other for other in self.gone):
                copy.wait_send()


class Place:
    def __init__(self, heads):
        self.f = lax.axis_index(FSDP)
        t = lax.axis_index(TENSOR)
        self.y, self.c = t // 2, lax.rem(t, 2)
        self.z = lax.axis_index(HEADS)
        self.heads = heads
        self.x_peer = {FSDP: 1 - self.f}
        self.y_peer = {TENSOR: 2 * (1 - self.y) + self.c}
        self.core_peer = {TENSOR: 2 * self.y + 1 - self.c}
        self.z_peers = [{HEADS: lax.rem(self.z + k, heads)} for k in range(1, heads)]
        self.plane_peers = []
        for a in range(2):
            for k in range(4):
                if a or k:
                    where = {TENSOR: lax.rem(t + k, 4)}
                    if a:
                        where[FSDP] = 1 - self.f
                    self.plane_peers.append(where)

    def image(self, df, dy, dc):
        f = 1 - self.f if df else self.f
        y = 1 - self.y if dy else self.y
        c = 1 - self.c if dc else self.c
        return f * 4 + 2 * y + c

    def greet(self, devices):
        barrier = pltpu.get_barrier_semaphore()
        for device in devices:
            pl.semaphore_signal(barrier, inc=1, device_id=device, device_id_type=MESH)
        pl.semaphore_wait(barrier, len(devices))

    def tensor_peers(self):
        t = 2 * self.y + self.c
        return [{TENSOR: lax.rem(t + k, 4)} for k in range(1, 4)]

    def owners(self):
        return [
            {FSDP: 1 - self.f if a else self.f, HEADS: lax.rem(self.z + k, self.heads)}
            for k in range(self.heads)
            for a in range(2)
            if a or k
        ]

    def everyone(self):
        t = 2 * self.y + self.c
        corners = [{FSDP: 1 - self.f, TENSOR: lax.rem(t + k, 4)} for k in range(1, 4)]
        return self.tensor_peers() + self.owners() + corners

    def axis_peers(self):
        return [self.x_peer, self.y_peer, self.core_peer]


class PlaneGather:
    def __init__(self, links, place, first, second, whole):
        self.links, self.place = links, place
        self.first, self.second, self.whole = first, second, whole

    def go(self, part, image, device):
        return self.links.send(part(image), part(image), device)

    def start(self):
        p, me = self.place, self.place.image(0, 0, 0)
        self.xa = self.go(self.first, me, p.x_peer)
        self.yb = self.go(self.second, me, p.y_peer)
        self.own = self.go(self.whole, me, p.core_peer)
        self.xb = self.go(self.second, me, p.x_peer)
        self.ya = self.go(self.first, me, p.y_peer)

    def forward(self):
        p = self.place
        self.xa.wait_recv()
        self.fa = self.go(self.first, p.image(1, 0, 0), p.y_peer)
        self.yb.wait_recv()
        self.fb = self.go(self.second, p.image(0, 1, 0), p.x_peer)

    def share(self):
        p = self.place
        self.xb.wait_recv()
        self.c1 = self.go(self.whole, p.image(1, 0, 0), p.core_peer)
        self.ya.wait_recv()
        self.c2 = self.go(self.whole, p.image(0, 1, 0), p.core_peer)

    def finish(self):
        p = self.place
        self.fa.wait_recv()
        self.fb.wait_recv()
        self.c3 = self.go(self.whole, p.image(1, 1, 0), p.core_peer)
        for copy in (self.own, self.c1, self.c2, self.c3):
            copy.wait_recv()

    def run(self):
        self.start()
        self.forward()
        self.share()
        self.finish()


GATHER_COPIES = 10


def in_rows(rows, step, body):
    def one(i, carry):
        body(pl.ds(pl.multiple_of(i * step, step), step))
        return carry

    lax.fori_loop(0, rows // step, one, 0)


class PlaneSum:
    def __init__(self, links, place, part, core_in, xa, ya, yb, xb, cut, step):
        self.links, self.place, self.part, self.core_in = links, place, part, core_in
        self.xa, self.ya, self.yb, self.xb, self.cut, self.step = xa, ya, yb, xb, cut, step
        self.rows, self.width = part.shape[1], part.shape[2]
        self.a, self.b = pl.ds(0, cut), pl.ds(cut, self.width - cut)

    def start(self):
        p = self.place
        self.order = [(1, 1), (1, 0), (0, 1), (0, 0)]
        self.into = {}
        for df, dy in self.order:
            f = 1 - p.f if df else p.f
            y = 1 - p.y if dy else p.y
            self.into[df, dy] = self.links.send(
                self.part.at[p.image(df, dy, 1)], self.core_in.at[2 * f + y], p.core_peer
            )

    def slot(self, df, dy):
        p = self.place
        return 2 * (1 - p.f if df else p.f) + (1 - p.y if dy else p.y)

    def cores(self):
        p, rc = self.place, self.core_in
        self.got = {}
        for df, dy in self.order:
            self.into[df, dy].wait_recv()
            j, mine = self.slot(df, dy), p.image(df, dy, 0)

            def add(rows, j=j, mine=mine):
                both = rc[j, rows, :].astype(WIDE) + self.part[mine, rows, :].astype(WIDE)
                rc[j, rows, :] = both.astype(LOW)

            in_rows(self.rows, self.step, add)
            y = 1 - p.y if dy else p.y
            f = 1 - p.f if df else p.f
            if df:
                self.got["x", dy] = self.links.send(rc.at[j, :, self.a], self.xa.at[y], p.x_peer)
            if dy:
                self.got["y", df] = self.links.send(rc.at[j, :, self.b], self.yb.at[f], p.y_peer)

    def cross(self):
        p, rc, xa, yb = self.place, self.core_in, self.xa, self.yb
        self.got["x", 1].wait_recv()
        j, other = self.slot(0, 1), 1 - p.y

        def add_a(rows):
            both = xa[other, rows, :].astype(WIDE) + rc[j, rows, self.a].astype(WIDE)
            xa[other, rows, :] = both.astype(LOW)

        in_rows(self.rows, self.step, add_a)
        self.last_a = self.links.send(xa.at[other], self.ya, p.y_peer)
        self.got["y", 1].wait_recv()
        k, away = self.slot(1, 0), 1 - p.f

        def add_b(rows):
            both = yb[away, rows, :].astype(WIDE) + rc[k, rows, self.b].astype(WIDE)
            yb[away, rows, :] = both.astype(LOW)

        in_rows(self.rows, self.step, add_b)
        self.last_b = self.links.send(yb.at[away], self.xb, p.x_peer)

    def finish(self, take):
        p, rc = self.place, self.core_in
        self.got["x", 0].wait_recv()
        self.got["y", 0].wait_recv()
        self.last_a.wait_recv()
        self.last_b.wait_recv()
        j, y, f = self.slot(0, 0), p.y, p.f

        def add(rows):
            first = rc[j, rows, self.a].astype(WIDE) + self.xa[y, rows, :].astype(WIDE)
            second = rc[j, rows, self.b].astype(WIDE) + self.yb[f, rows, :].astype(WIDE)
            take(rows, self.a, first + self.ya[rows, :].astype(WIDE))
            take(rows, self.b, second + self.xb[rows, :].astype(WIDE))

        in_rows(self.rows, self.step, add)


SUM_COPIES = 10


def sum_scratch(rows, width, cut):
    return [
        pltpu.VMEM((4, rows, width), LOW),
        pltpu.VMEM((2, rows, cut), LOW),
        pltpu.VMEM((rows, cut), LOW),
        pltpu.VMEM((2, rows, width - cut), LOW),
        pltpu.VMEM((rows, width - cut), LOW),
    ]


def all_heads(links, place, make):
    copies = []
    for k, device in enumerate(place.z_peers):
        src, dst = make(k, device[HEADS])
        copies.append(links.send(src, dst, device))
    return copies


def spends(microseconds):
    return pl.CostEstimate(flops=0, bytes_accessed=microseconds * 3_000_000, transcendentals=0)


def shape(dims, dtype=LOW):
    return jax.ShapeDtypeStruct(dims, dtype)


class ChunkSum:
    def __init__(self, links, place, part, columns, core_in, xa, ya, yb, xb):
        self.links, self.place, self.part, self.columns = links, place, part, columns
        self.core_in, self.xa, self.ya, self.yb, self.xb = core_in, xa, ya, yb, xb
        self.rows, self.half = core_in.shape[2], core_in.shape[3] // 2
        self.a, self.b = pl.ds(0, self.half), pl.ds(self.half, self.half)

    def start(self):
        p = self.place
        self.into = self.links.send(
            self.part.at[:, :, 1 - p.c, :, self.columns], self.core_in, p.core_peer
        )

    def cores(self):
        p, rc = self.place, self.core_in
        self.into.wait_recv()

        def add(rows):
            here = self.part[:, :, p.c, rows, self.columns].astype(WIDE)
            rc[:, :, rows, :] = (rc[:, :, rows, :].astype(WIDE) + here).astype(LOW)

        in_rows(self.rows, 32, add)
        self.to_x = self.links.send(rc.at[1 - p.f, :, :, self.a], self.xa, p.x_peer)
        self.to_y = self.links.send(rc.at[:, 1 - p.y, :, self.b], self.yb, p.y_peer)

    def cross(self):
        p, rc, xa, yb = self.place, self.core_in, self.xa, self.yb
        self.to_x.wait_recv()
        y, f = 1 - p.y, 1 - p.f

        def add_a(rows):
            both = xa[y, rows, :].astype(WIDE) + rc[p.f, y, rows, self.a].astype(WIDE)
            xa[y, rows, :] = both.astype(LOW)

        in_rows(self.rows, 64, add_a)
        self.last_a = self.links.send(xa.at[y], self.ya, p.y_peer)
        self.to_y.wait_recv()

        def add_b(rows):
            both = yb[f, rows, :].astype(WIDE) + rc[f, p.y, rows, self.b].astype(WIDE)
            yb[f, rows, :] = both.astype(LOW)

        in_rows(self.rows, 64, add_b)
        self.last_b = self.links.send(yb.at[f], self.xb, p.x_peer)

    def finish(self, take):
        p, rc = self.place, self.core_in
        self.last_a.wait_recv()
        self.last_b.wait_recv()

        def add(rows):
            first = rc[p.f, p.y, rows, self.a].astype(WIDE) + self.xa[p.y, rows, :].astype(WIDE)
            second = rc[p.f, p.y, rows, self.b].astype(WIDE) + self.yb[p.f, rows, :].astype(WIDE)
            take(rows, 0, first + self.ya[rows, :].astype(WIDE))
            take(rows, 1, second + self.xb[rows, :].astype(WIDE))

        in_rows(self.rows, 64, add)


def skewed(chunks, stages):
    for step in range(chunks + len(stages) - 1):
        for k in range(chunks):
            if 0 <= step - k < len(stages):
                stages[step - k](k)


def combine_part(place, links, chunks, r):
    heads, z, me = place.heads, place.z, place.image(0, 0, 0)
    part, residual, teacher, valid, scale = r.part, r.residual, r.teacher, r.valid, r.scale
    result, final_grad, group, loss = r.result, r.final_grad, r.group, r.loss
    image_sum, far = r.image_sum, r.image_far
    rows_all, width = residual.shape
    own = rows_all // heads
    wide = width // chunks
    half = wide // 2
    mine = pl.ds(pl.multiple_of(z * own, own), own)
    columns = [pl.ds(k * wide, wide) for k in range(chunks)]
    adders = [
        ChunkSum(
            links,
            place,
            part,
            columns[k],
            r.sum_core.at[k],
            r.sum_xa.at[k],
            r.sum_ya.at[k],
            r.sum_yb.at[k],
            r.sum_xb.at[k],
        )
        for k in range(chunks)
    ]
    for adder in adders:
        adder.start()
    along, spread, squares = {}, {}, []
    gathers = [
        PlaneGather(
            links,
            place,
            lambda i, k=k: group.at[i, :, pl.ds(k * wide, half)],
            lambda i, k=k: group.at[i, :, pl.ds(k * wide + half, half)],
            lambda i, k=k: group.at[i, :, columns[k]],
        )
        for k in range(chunks)
    ]

    def to_heads(k):
        def keep(rows, part_of, values):
            image_sum[k, rows, pl.ds(part_of * half, half)] = values.astype(LOW)

        adders[k].finish(keep)
        along[k] = all_heads(
            links,
            place,
            lambda n, to: (
                image_sum.at[k, pl.ds(pl.multiple_of(to * own, own), own)],
                far.at[k, n],
            ),
        )

    def final(k):
        for copy in along[k]:
            copy.wait_recv()
        total = image_sum[k, mine, :].astype(WIDE)
        for n in range(heads - 1):
            total = total + far[k, n].astype(WIDE)
        values = residual[mine, columns[k]] + total
        result[z, :, columns[k]] = values.astype(LOW)
        error = (values - teacher[mine, columns[k]].astype(WIDE)) * valid[mine, 0:1]
        grad = error * scale[0:1, 0:1]
        final_grad[:, columns[k]] = grad
        group[me, mine, columns[k]] = grad.astype(LOW)
        block = group.at[me, mine, columns[k]]
        spread[k] = all_heads(links, place, lambda n, to: (block, block))
        square = jnp.sum((error * error).reshape(own // 8, 8, wide), axis=0)
        squares.extend(square[:, i * 128 : (i + 1) * 128] for i in range(wide // 128))

    def to_plane(k):
        for copy in spread[k]:
            copy.wait_recv()
        gathers[k].start()

    def forward(k):
        gathers[k].forward()
        gathers[k].share()

    skewed(
        chunks,
        [
            lambda k: adders[k].cores(),
            lambda k: adders[k].cross(),
            to_heads,
            final,
            to_plane,
            forward,
        ],
    )
    loss[z] = sum(squares) * r.loss_scale[0:1, 0:1]
    extra = all_heads(links, place, lambda k, to: (result.at[z], result.at[z]))
    extra += all_heads(links, place, lambda k, to: (loss.at[z], loss.at[z]))
    for gather in gathers:
        gather.finish()
    return extra


def dot(a, b, over=(1, 0)):
    return lax.dot_general(a, b, (((over[0],), (over[1],)), ((), ())), preferred_element_type=WIDE)


def one_hot(slots, row, capacity):
    places = lax.broadcasted_iota(jnp.int32, (capacity, slots.shape[1]), 0)
    return places == slots[pl.ds(row, 1), :]


class Loads:
    def __init__(self, sems):
        self.sems, self.count = sems, 0

    def start(self, src, dst):
        assert self.count < self.sems.shape[0]
        copy = pltpu.make_async_copy(src, dst, self.sems.at[self.count])
        self.count += 1
        copy.start()
        return copy


def gelu_parts(values):
    cdf = 0.5 * (1.0 + lax.erf(values * ROOT_HALF))
    return values * cdf, cdf + values * DENSITY * jnp.exp(-0.5 * values * values)


def front_part(place, links, r):
    heads, f, z, me = place.heads, place.f, place.z, place.image(0, 0, 0)
    oq, oo, counts, slots = r.qkv, r.wo_all, r.counts, r.slots
    kept = r.w_far.shape[0]
    theirs = (1 - f) * kept
    rows = [r.router_in[...], r.gain_one_in[...], r.gain_two_in[...]]
    rows = [row.astype(WIDE) for row in rows]
    block = oq.shape[1]
    rows.append(jnp.zeros((128 - sum(row.shape[0] for row in rows), block), WIDE))
    oq[me, :, 0:128] = jnp.transpose(jnp.concatenate(rows, 0)).astype(LOW)
    qkv = jnp.concatenate([r.qkv_in[h] for h in range(r.qkv_in.shape[0])], 1)
    oq[me, :, pl.ds(128, qkv.shape[1])] = qkv
    rest = oq.shape[2] - 128 - qkv.shape[1]
    if rest:
        oq[me, :, pl.ds(128 + qkv.shape[1], rest)] = jnp.zeros((block, rest), LOW)
    oo[me, z] = jnp.transpose(r.out_in[...].astype(WIDE)).astype(LOW)
    counts[me] = jnp.broadcast_to(jnp.sum(r.valid_row[...].astype(WIDE), -1, keepdims=True), (8, 128))
    half, mid = oq.shape[2] // 2, heads // 2
    main = PlaneGather(
        links,
        place,
        lambda i: oq.at[i, :, pl.ds(0, half)],
        lambda i: oq.at[i, :, pl.ds(half, half)],
        lambda i: oq.at[i],
    )
    side = PlaneGather(
        links,
        place,
        lambda i: oo.at[i, pl.ds(0, mid)],
        lambda i: oo.at[i, pl.ds(mid, heads - mid)],
        lambda i: oo.at[i],
    )

    def bulk(i):
        return links.send(r.down.at[theirs + i], r.w_far.at[i], place.x_peer)

    main.start()
    along = all_heads(links, place, lambda k, to: (oo.at[me, z], oo.at[me, z]))
    small = [links.send(counts.at[me], counts.at[me], d) for d in place.plane_peers]
    small.append(links.send(r.near_route, r.far_route, place.x_peer))
    main.forward()
    for copy in along:
        copy.wait_recv()
    side.start()
    down = [bulk(0)]
    main.share()
    main.finish()
    width = r.tokens.shape[1]
    experts = r.probs.shape[1]
    narrow = oq[:, :, 0:128].reshape(width, 128).astype(WIDE)
    turned = jnp.transpose(narrow)
    r.router[...] = turned[:experts].astype(LOW)
    r.gain_one[...] = turned[experts : experts + 1]
    r.gain[...] = turned[experts + 1 : experts + 2]
    rows_all = r.tokens.shape[0]

    def first_norm(rows):
        normed, _ = normalize(r.tokens[rows, :].astype(WIDE))
        r.first_in[rows, :] = (normed * r.gain_one[...]).astype(LOW)

    in_rows(rows_all, 64, first_norm)
    qkv_width = r.projected.shape[1]
    weight = oq[:, :, pl.ds(128, qkv_width)].reshape(width, qkv_width)
    r.projected[...] = dot(r.first_in[...], weight).astype(LOW)
    side.forward()
    down.append(bulk(1))
    head_count = r.log_total.shape[1]
    size = qkv_width // head_count // 3
    keys_ok = r.valid_row[...] > 0
    mixed = []
    for h in range(head_count):
        at = 3 * h * size
        query, key, value = (r.projected[:, at + n * size : at + (n + 1) * size] for n in range(3))
        scores = jnp.where(keys_ok, dot(query, key, (1, 1)) * size ** (-0.5), MASKED)
        peak = jnp.max(scores, -1, keepdims=True)
        powers = jnp.exp(scores - peak)
        total = jnp.sum(powers, -1, keepdims=True)
        r.log_total[:, h : h + 1] = peak + jnp.log(total)
        mixed.append(dot((powers / total).astype(LOW), value).astype(LOW))
    r.mixed[...] = jnp.concatenate(mixed, 1)
    everyone = r.all_mixed
    everyone[z] = r.mixed[...]
    along = all_heads(links, place, lambda k, to: (everyone.at[z], everyone.at[z]))
    side.share()
    for copy in small:
        copy.wait_recv()
    valid_total = sum(counts[i] for i in range(8))[0:1, 0:1]
    r.scale[...] = jnp.broadcast_to(8 * rows_all / valid_total, (8, 128))
    r.loss_scale[...] = jnp.broadcast_to(8 / (valid_total * width), (8, 128))
    column = jnp.broadcast_to(r.valid_row[...].astype(WIDE), (8, rows_all))
    r.valid[...] = jnp.transpose(column)
    local_experts = 2 * kept
    ids = z * local_experts + lax.broadcasted_iota(jnp.int32, (local_experts, 1), 0)
    first = f == 0
    near, far = r.near_route[...], r.far_route[...]
    both = [jnp.where(first, near, far), jnp.where(first, far, near)]
    chosen = []
    for route in both:
        hits = []
        for c in range(route.shape[1]):
            row = jnp.concatenate([route[k, c : c + 1] for k in range(4)], 1)
            hits.append(row == ids)
        chosen.append(functools.reduce(jnp.logical_or, hits))
    chosen = jnp.concatenate(chosen, 0)
    count = chosen.astype(WIDE)
    before = lax.broadcasted_iota(jnp.int32, (128, 128), 0)
    before = (before < lax.broadcasted_iota(jnp.int32, (128, 128), 1)).astype(LOW)
    running = jnp.zeros((2 * local_experts, 1), WIDE)
    for b in range(slots.shape[1] // 128):
        columns = slice(b * 128, (b + 1) * 128)
        here = count[:, columns]
        slot = dot(here.astype(LOW), before) + running
        slots[:, columns] = jnp.where(chosen[:, columns], slot, -1.0).astype(jnp.int32)
        running = running + jnp.sum(here, -1, keepdims=True)
    for copy in along:
        copy.wait_recv()
    side.finish()
    half = width // 2
    total = jnp.zeros((rows_all, width), WIDE)
    for n in range(heads):
        weight = oo[:, n].reshape(width, oo.shape[3])
        total = total + dot(everyone[n], weight, (1, 1))
    r.residual[...] = total

    def norm(rows):
        values = r.tokens[rows, :].astype(WIDE) + r.residual[rows, :]
        r.residual[rows, :] = values
        normed, _ = normalize(values)
        r.second_in[rows, :] = (normed * r.gain[...]).astype(LOW)

    in_rows(rows_all, 64, norm)
    low, high = r.second_in[:, :half], r.second_in[:, half:]

    def part_of(df, dy, dc):
        return r.x.at[
            1 - f if df else f, 1 - place.y if dy else place.y, 1 - place.c if dc else place.c
        ]

    mine, across, beside, corner = (
        part_of(0, 0, 0),
        part_of(1, 0, 0),
        part_of(0, 1, 0),
        part_of(1, 1, 0),
    )
    mine[...] = jnp.where(first, low, high)
    r.other_half[...] = jnp.where(first, high, low)
    x1 = links.send(r.other_half, mine, place.x_peer)
    y1 = links.send(mine, mine, place.y_peer)
    shared = [links.send(mine, mine, place.core_peer)]
    down.append(bulk(2))
    logits = dot(r.router[...], r.second_in[...], (1, 1))
    powers = jnp.exp(logits - jnp.max(logits, 0, keepdims=True))
    probs = powers / jnp.sum(powers, 0, keepdims=True)
    r.probs_own[...] = probs
    r.probs[me] = probs
    small = [links.send(r.probs.at[me], r.probs.at[me], d) for d in place.plane_peers]
    x1.wait_recv()
    y2 = links.send(across, across, place.y_peer)
    shared.append(links.send(across, across, place.core_peer))
    y1.wait_recv()
    shared.append(links.send(beside, beside, place.core_peer))
    y2.wait_recv()
    shared.append(links.send(corner, corner, place.core_peer))
    for copy in shared + small:
        copy.wait_recv()
    return [y1, y2, *shared], down


FRONT_COPIES = 2 * GATHER_COPIES + 7 + 1 + 1 + 2 + 4 + 7


def send_hidden(place, links, r, i):
    return links.send(r.hidden.at[i], r.far_hidden.at[i], place.x_peer)


def experts_part(place, links, loads, weights, down_far, r):
    slots, probs = r.slots, r.probs
    pick_near, pick_far, gates, hidden = r.pick_near, r.pick_far, r.gates, r.hidden
    buffer_near, buffer_far, own, weighted = r.buffer_near, r.buffer_far, r.own, r.weighted
    away, arrived, w_up, w_near, w_far = r.away, r.arrived, r.w_up, r.w_near, r.w_far
    kept, pair, _ = own.shape
    capacity, half = pair // 2, r.x.shape[4]
    group_rows = slots.shape[1]
    stores = []

    def kept_rows(i, buffer, target):
        stores.append(loads.start(buffer.at[i % 2], target.at[i]))

    local_experts = 2 * kept
    mine, theirs = place.f * kept, (1 - place.f) * kept
    ups, nears = weights
    sent = []
    for i in range(kept):
        if i > 1:
            stores[i - 2].wait()
        for g in range(2):
            rows = slice(i * capacity, (i + 1) * capacity)
            hot = one_hot(slots, g * local_experts + theirs + i, capacity).astype(LOW)
            pick_far[g, rows] = hot
            x = r.x[g].reshape(group_rows, half)
            buffer_far[i % 2, g * capacity : (g + 1) * capacity] = dot(hot, x).astype(LOW)
        ups[1, i].wait()
        kept_rows(i, buffer_far, r.far_out)
        away[i] = dot(buffer_far[i % 2], w_up[1, i]).astype(LOW)
        sent.append(links.send(away.at[i], arrived.at[i], place.x_peer))
    down_far = [
        *down_far,
        *(
            links.send(r.down.at[theirs + i], w_far.at[i], place.x_peer)
            for i in range(len(down_far), kept)
        ),
    ]
    for i in range(kept):
        expert = place.z * local_experts + mine + i
        if i > 1:
            stores[kept + i - 2].wait()
        for g in range(2):
            rows = slice(i * capacity, (i + 1) * capacity)
            into = slice(g * capacity, (g + 1) * capacity)
            hot = one_hot(slots, g * local_experts + mine + i, capacity)
            chances = [probs[4 * g + k, pl.ds(expert, 1), :] for k in range(4)]
            chances = jnp.concatenate(chances, 1)
            gates[i, into] = jnp.sum(jnp.where(hot, chances, 0.0), -1, keepdims=True)
            pick_near[g, rows] = hot.astype(LOW)
            x = r.x[g].reshape(group_rows, half)
            buffer_near[i % 2, into] = dot(hot.astype(LOW), x).astype(LOW)
        ups[0, i].wait()
        kept_rows(i, buffer_near, r.near_out)
        own[i] = dot(buffer_near[i % 2], w_up[0, i])
    for copy in nears:
        copy.wait()
    for i in range(kept):
        sent[i].wait_recv()
        down_far[i].wait_recv()
        values, slopes = gelu_parts(own[i] + arrived[i].astype(WIDE))
        hidden[i] = values.astype(LOW)
        if i == 0:
            r.hidden_copies.append(send_hidden(place, links, r, 0))
        own[i] = slopes
        for weight, f in ((w_near, place.f), (w_far, 1 - place.f)):
            out = (dot(hidden[i], weight[i]) * gates[i]).astype(LOW)
            columns = pl.ds(pl.multiple_of(f * half, half), half)
            for g in range(2):
                rows = slice(i * capacity, (i + 1) * capacity)
                weighted[g, rows, columns] = out[g * capacity : (g + 1) * capacity]
    for g in range(2):
        total = dot(pick_near[g], weighted[g], (0, 0)).astype(LOW)
        r.part[g] = total.reshape(r.part.shape[1:])
    links.left(sent)
    return stores[kept - 2 : kept] + stores[2 * kept - 2 :]


def experts_back_part(place, links, loads, chunks, r):
    pick_near, pick_far, hidden, slope, gates = r.pick_near, r.pick_far, r.hidden, r.own, r.gates
    w_up, w_near, w_far, group = r.w_up, r.w_near, r.w_far, r.group
    pre_near, pre_far, out_grad = r.away, r.arrived, r.out_grad
    side = r.weighted.shape[2] // 2
    rows_near = r.weighted.at[:, :, pl.ds(0, side)]
    rows_far = r.weighted.at[:, :, pl.ds(side, side)]
    kept, pair, half = out_grad.shape
    capacity, width = pair // 2, 2 * half
    first = pl.ds(pl.multiple_of(place.f * half, half), half)
    second = pl.ds(pl.multiple_of((1 - place.f) * half, half), half)
    sent = {}

    def send(g, i):
        piece = pl.ds(g * capacity, capacity)
        sent[g, i] = links.send(pre_near.at[i, piece], pre_far.at[i, piece], place.x_peer)

    for i in range(kept):
        rows = slice(i * capacity, (i + 1) * capacity)
        for g in range(2):
            rows_in = group[4 * g : 4 * g + 4].reshape(pick_near.shape[2], width)
            r.slot_rows[g * capacity : (g + 1) * capacity] = dot(
                pick_near[g, rows], rows_in
            ).astype(LOW)
        raw = dot(r.slot_rows[:, first], w_near[i], (1, 1))
        raw = raw + dot(r.slot_rows[:, second], w_far[i], (1, 1))
        pre_near[i] = (raw * gates[i] * slope[i]).astype(LOW)
        send(0, i)
        out_grad[i] = (r.slot_rows[:, first].astype(WIDE) * gates[i]).astype(LOW)
        gate_grad = jnp.sum(raw * hidden[i].astype(WIDE), -1, keepdims=True)
        for g in range(2):
            terms = gate_grad[g * capacity : (g + 1) * capacity]
            terms = terms * pick_near[g, rows].astype(WIDE)
            r.gate_rows[g, i : i + 1] = jnp.sum(terms, 0, keepdims=True)
    for i in range(kept):
        send(1, i)
    t = 2 * place.y + place.c
    r.gate_in[t] = r.gate_rows[...]
    shared = [
        links.send(r.gate_rows, r.gate_in.at[t], d) for d in place.tensor_peers()
    ]
    stores = [
        loads.start(r.hidden, r.near_hidden),
        loads.start(pre_near, r.near_pre),
        loads.start(out_grad, r.near_grad),
    ]

    for i in range(kept):
        back = dot(pre_near[i], w_up[0, i], (1, 1)).astype(LOW)
        rows = slice(i * capacity, (i + 1) * capacity)
        for g in range(2):
            rows_near[g, rows] = back[g * capacity : (g + 1) * capacity]
    for copy in shared:
        copy.wait_recv()
    spread = share_gates(place, links, r)
    experts = place.z * 2 * kept + (1 - place.f) * kept
    for i in range(kept):
        rows = slice(i * capacity, (i + 1) * capacity)
        for g in range(2):
            hot = pick_far[g, rows]
            chances = [r.probs[4 * g + k, pl.ds(experts + i, 1), :] for k in range(4)]
            chances = jnp.concatenate(chances, 1)
            gate = jnp.sum(hot.astype(WIDE) * chances, -1, keepdims=True)
            rows_in = group[4 * g : 4 * g + 4, :, first].reshape(pick_far.shape[2], half)
            into = slice(g * capacity, (g + 1) * capacity)
            r.far_held[i, into] = (dot(hot, rows_in) * gate).astype(LOW)
    stores.append(loads.start(r.far_held, r.far_grad))
    r.hidden_copies.append(send_hidden(place, links, r, 1))
    sums = RowSum(links, place, r)
    sums.spread = spread
    steps = {0: sums.to_y, 1: sums.to_heads, kept - 1: sums.total}
    for g in range(2):
        into = slice(g * capacity, (g + 1) * capacity)
        for i in range(kept):
            sent[g, i].wait_recv()
            back = dot(pre_far[i, into], w_up[1, i], (1, 1)).astype(LOW)
            rows_far[g, i * capacity : (i + 1) * capacity] = back
            if g and i in steps:
                for k in range(chunks):
                    steps[i](0, k)
        near = dot(pick_near[g], rows_near[g], (0, 0))
        both = (near + dot(pick_far[g], rows_far[g], (0, 0))).astype(LOW)
        r.x[g] = both.reshape(r.x.shape[1:])
        for k in range(chunks):
            sums.start(g, k)
    stores.append(loads.start(pre_far, r.far_pre))
    return stores, sums


def share_gates(place, links, r):
    t = 2 * place.y + place.c
    r.gate_sum[...] = sum(r.gate_in[k] for k in range(4))
    rows_all = r.probs_own.shape[1]
    rows_of = pl.ds(pl.multiple_of(t * rows_all, rows_all), rows_all)
    r.gate_all[place.z, place.f] = r.gate_sum[place.f, :, rows_of]
    return [
        links.send(r.gate_sum.at[d[FSDP], :, rows_of], r.gate_all.at[place.z, place.f], d)
        for d in place.owners()
    ]


def router_back(r):
    experts, rows_all = r.probs_own.shape
    width = r.residual.shape[1]
    chances = r.probs_own[...]
    prob_grad = r.gate_all[...].reshape(experts, rows_all)
    logit_grad = chances * (prob_grad - jnp.sum(chances * prob_grad, 0, keepdims=True))
    r.logit_grads[...] = logit_grad.astype(LOW)
    r.logit_rows[...] = dot(r.logit_grads[...], r.router[...], (0, 0))
    router_grad = dot(r.second_in[...], r.logit_grads[...], (0, 1))
    spare = jnp.zeros((width, 128 - experts), WIDE)
    router_grad = jnp.concatenate([router_grad, spare], 1).astype(LOW)
    blocks, block, dense_width = r.dense.shape
    r.dense[:, :, pl.ds(dense_width - 128, 128)] = router_grad.reshape(blocks, block, 128)


class RowSum:
    def __init__(self, links, place, r):
        self.links, self.place, self.r = links, place, r
        self.into, self.beside, self.along, self.cross = {}, {}, {}, {}
        self.rows = r.x.shape[3]
        self.own = self.rows // place.heads

    def start(self, g, k):
        source = self.r.x.at[g, :, 1 - self.place.c, :, pl.ds(k * 128, 128)]
        self.into[g, k] = self.links.send(
            source, self.r.core_in.at[k, g], self.place.core_peer
        )

    def to_y(self, g, k):
        self.into[g, k].wait_recv()
        rc, c, y = self.r.core_in.at[k, g], self.place.c, self.place.y

        def add(rows):
            here = self.r.x[g, :, c, rows, pl.ds(k * 128, 128)].astype(WIDE)
            rc[:, rows, :] = (rc[:, rows, :].astype(WIDE) + here).astype(LOW)

        in_rows(self.rows, 64, add)
        self.beside[g, k] = self.links.send(
            rc.at[1 - y], self.r.y_in.at[k, g], self.place.y_peer
        )

    def to_heads(self, g, k):
        self.beside[g, k].wait_recv()
        y_in, core_in = self.r.y_in.at[k, g], self.r.core_in.at[k, g, self.place.y]

        def add(rows):
            both = y_in[rows, :].astype(WIDE) + core_in[rows, :].astype(WIDE)
            y_in[rows, :] = both.astype(LOW)

        in_rows(self.rows, 64, add)
        own = self.own
        self.along[g, k] = all_heads(
            self.links,
            self.place,
            lambda n, to: (
                y_in.at[pl.ds(pl.multiple_of(to * own, own), own)],
                self.r.far.at[k, n, g],
            ),
        )

    def total(self, g, k):
        for copy in self.along[g, k]:
            copy.wait_recv()
        z, own = self.place.z, self.own
        total = self.r.y_in[k, g, pl.ds(pl.multiple_of(z * own, own), own), :].astype(WIDE)
        for n in range(self.place.heads - 1):
            total = total + self.r.far[k, n, g].astype(WIDE)
        self.r.pair[k, g] = total.astype(LOW)

    def to_x(self, k):
        self.cross[k] = self.links.send(
            self.r.pair.at[k, 1 - self.place.f], self.r.x_in.at[k], self.place.x_peer
        )


def back_part(place, links, chunks, sums, r):
    heads, f, y, z = place.heads, place.f, place.y, place.z
    me, valid = place.image(0, 0, 0), r.valid_row
    residual, gain, final_grad, tokens = r.residual, r.gain, r.final_grad, r.tokens
    gain_one, projected, log_total, mixed = r.gain_one, r.projected, r.log_total, r.mixed
    qkv, wo, tokens_grad, dense_out, gain_out = (
        r.qkv,
        r.wo_all,
        r.tokens_grad,
        r.dense_out,
        r.gain_out,
    )
    pair, x_in, logit_rows, attended, first_in = (
        r.pair,
        r.x_in,
        r.logit_rows,
        r.attended,
        r.first_in,
    )
    projected_grad, first_part, dense, dense_core = (
        r.projected_grad,
        r.first_part,
        r.dense,
        r.dense_core,
    )
    xa, ya, yb, xb, first_far, rounded = r.xa, r.ya, r.yb, r.xb, r.first_far, r.rounded
    gain_part, gain_plane, gain_heads = r.gain_part, r.gain_plane, r.gain_heads
    rows_all, width = residual.shape
    half = width // 2
    own = rows_all // heads
    mine = pl.ds(pl.multiple_of(z * own, own), own)
    blocks, block, dense_width = dense.shape
    qkv_width = projected.shape[1]
    for step in range(chunks + 2):
        if step == 2:
            for copy in sums.spread:
                copy.wait_recv()
            router_back(r)
        for k in range(chunks):
            if step == k:
                sums.to_y(1, k)
            if step == k + 1:
                sums.to_heads(1, k)
            if step == k + 2:
                sums.total(1, k)
                sums.to_x(k)
    for i in range(2, r.hidden.shape[0]):
        r.hidden_copies.append(send_hidden(place, links, r, i))
    normed, spread_two = normalize(residual[mine, :])
    cross = sums.cross
    near = jnp.concatenate([pair[k, f].astype(WIDE) for k in range(chunks)], 1)
    for k in range(chunks):
        cross[k].wait_recv()
    away = jnp.concatenate([x_in[k].astype(WIDE) for k in range(chunks)], 1)
    first = f == 0
    rows_grad = jnp.concatenate([jnp.where(first, near, away), jnp.where(first, away, near)], 1)
    second_grad = rows_grad + logit_rows[mine, :]
    weighted = second_grad * gain[...]
    gain_part[1:2, :] = jnp.sum(second_grad * normed, 0, keepdims=True)
    inner = (
        weighted
        - jnp.mean(weighted, -1, keepdims=True)
        - normed * jnp.mean(weighted * normed, -1, keepdims=True)
    )
    total_grad = final_grad[...] + inner * spread_two
    attended[mine, :] = total_grad.astype(LOW)
    for copy in all_heads(
        links, place, lambda k, to: (attended.at[mine], attended.at[mine])
    ):
        copy.wait_recv()

    mixed_grad = dot(attended[...], wo[:, z].reshape(width, wo.shape[3])).astype(LOW)
    head_count = log_total.shape[1]
    size = qkv_width // head_count // 3
    score_scale = size ** (-0.5)
    keys_ok = valid[...] > 0
    grads = []
    for h in range(head_count):
        at = 3 * h * size
        query, key, value = (projected[:, at + n * size : at + (n + 1) * size] for n in range(3))
        above = mixed_grad[:, h * size : (h + 1) * size]
        scores = jnp.where(keys_ok, dot(query, key, (1, 1)) * score_scale, MASKED)
        chances = jnp.exp(scores - log_total[:, h : h + 1])
        prob_part = dot(above, value, (1, 1))
        inner = jnp.sum(chances * prob_part, -1, keepdims=True)
        score_grad = (chances * (prob_part - inner)).astype(LOW)
        grads.append(dot(score_grad, key) * score_scale)
        grads.append(dot(score_grad, query, (0, 0)) * score_scale)
        grads.append(dot(chances.astype(LOW), above, (0, 0)))
    projected_grad[...] = jnp.concatenate(grads, 1).astype(LOW)
    weight = qkv[:, :, pl.ds(128, qkv_width)].reshape(width, qkv_width)
    back = dot(projected_grad[...], weight, (1, 1))
    first_part[...] = back.astype(LOW).reshape(heads, own, width)
    cuts = [pl.ds(q * own // 2, own // 2) for q in range(2)]
    along = [
        all_heads(links, place, lambda n, to: (first_part.at[to, q], first_far.at[n, q]))
        for q in cuts
    ]
    dense_now = jnp.concatenate(
        [
            dot(first_in[...], projected_grad[...], (0, 0)).astype(LOW),
            dot(attended[...], mixed[...], (0, 0)).astype(LOW),
        ],
        1,
    )
    dense[:, :, pl.ds(0, dense_width - 128)] = dense_now.reshape(blocks, block, dense_width - 128)
    adder = PlaneSum(links, place, dense, dense_core, xa, ya, yb, xb, xa.shape[2], 32)
    adder.start()
    gain_part[0:1, :] = jnp.sum(back * normalize(tokens[...].astype(WIDE))[0], 0, keepdims=True)
    gain_plane[me] = gain_part[...]
    small = [links.send(gain_part, gain_plane.at[me], d) for d in place.plane_peers]
    adder.cores()
    adder.cross()
    for copy in small:
        copy.wait_recv()
    gain_heads[z] = sum(gain_plane[i] for i in range(8))
    gains = all_heads(links, place, lambda n, to: (gain_heads.at[z], gain_heads.at[z]))
    ends = []
    for n_cut, q in enumerate(cuts):
        at = pl.ds(pl.multiple_of(z * own + n_cut * own // 2, own // 2), own // 2)
        normed, spread_one = normalize(tokens[at, :].astype(WIDE))
        for copy in along[n_cut]:
            copy.wait_recv()
        first_grad = first_part[z, q].astype(WIDE)
        for n in range(heads - 1):
            first_grad = first_grad + first_far[n, q].astype(WIDE)
        weighted = first_grad * gain_one[...]
        inner = (
            weighted
            - jnp.mean(weighted, -1, keepdims=True)
            - normed * jnp.mean(weighted * normed, -1, keepdims=True)
        )
        here = total_grad[n_cut * own // 2 : (n_cut + 1) * own // 2]
        rounded[z, q] = (here + inner * spread_one).astype(LOW)
        ends += all_heads(links, place, lambda n, to: (rounded.at[z, q], rounded.at[z, q]))

    def keep(rows, columns, values):
        dense_out[rows, columns] = values

    adder.finish(keep)
    for copy in gains:
        copy.wait_recv()
    gain_out[...] = sum(gain_heads[i] for i in range(heads))
    for copy in ends:
        copy.wait_recv()
    for i in range(heads):
        tokens_grad[i] = rounded[i].astype(WIDE)
    for copy in r.hidden_copies:
        copy.wait_recv()


def layer_kernel(heads, chunks, small, names, *refs):
    r = types.SimpleNamespace(**dict(zip(names, refs)), hidden_copies=[])
    place = Place(heads)
    links = Links(r.send_sems, r.recv_sems)
    loads = Loads(r.load_sems)
    kept = r.w_far.shape[0]
    mine, theirs = place.f * kept, (1 - place.f) * kept
    first = [loads.start(getattr(r, name + "_hbm"), getattr(r, name)) for name in small]
    ups = {}
    for far in (1, 0):
        for i in range(kept):
            source = (theirs if far else mine) + i
            ups[far, i] = loads.start(r.up.at[source], r.w_up.at[far, i])
    nears = [loads.start(r.down.at[mine + i], r.w_near.at[i]) for i in range(kept)]
    place.greet(place.everyone())
    for copy in first:
        copy.wait()
    from_x, down_far = front_part(place, links, r)
    held = experts_part(place, links, loads, (ups, nears), down_far, r)
    extra = combine_part(place, links, chunks, r)
    links.left(from_x)
    stores, sums = experts_back_part(place, links, loads, chunks, r)
    for copy in extra:
        copy.wait_recv()
    back_part(place, links, chunks, sums, r)
    for copy in held + stores:
        copy.wait()
    links.drain()


def named_call(kernel, ins, outs, scratch, copies, loads, collective_id, vmem_mib, microseconds):
    spaces = {False: pltpu.VMEM, True: pltpu.HBM}
    names = [*ins, *outs, *scratch, "load_sems", "send_sems", "recv_sems"]
    made = pl.pallas_call(
        functools.partial(kernel, names),
        out_shape=[o[0] for o in outs.values()],
        in_specs=[pl.BlockSpec(memory_space=spaces[a[1]]) for a in ins.values()],
        out_specs=[pl.BlockSpec(memory_space=spaces[o[1]]) for o in outs.values()],
        scratch_shapes=[
            *scratch.values(),
            pltpu.SemaphoreType.DMA((loads,)),
            pltpu.SemaphoreType.DMA((copies,)),
            pltpu.SemaphoreType.DMA((copies,)),
        ],
        compiler_params=pltpu.CompilerParams(
            collective_id=collective_id,
            has_side_effects=True,
            vmem_limit_bytes=vmem_mib * 2**20,
        ),
        cost_estimate=spends(microseconds),
    )(*[a[0] for a in ins.values()])
    return types.SimpleNamespace(**dict(zip(outs, made)))


def layer(heads, experts, capacity, small, hbm):
    rows, width = small["tokens"].shape
    own, half, chunks = rows // heads, width // 2, width // 256
    local_experts, _, hidden_width = hbm["up"].shape
    kept, pair, group_rows = local_experts // 2, 2 * capacity, 4 * rows
    mixed_width, block = small["out_in"].shape
    head_count = small["qkv_in"].shape[0]
    qkv_width = 3 * mixed_width
    gathered_width = 128 + qkv_width + -(128 + qkv_width) % 256
    dense_width = qkv_width + mixed_width + 128
    cut = 128 * ((dense_width // 128 + 1) // 2)
    ins = {name: (array, True) for name, array in hbm.items()}
    ins.update({name + "_hbm": (array, True) for name, array in small.items()})
    outs = dict(
        result=(shape((heads, own, width)), False),
        loss=(shape((heads, 8, 128), WIDE), False),
        tokens_grad=(shape((heads, own, width), WIDE), False),
        dense_out=(shape((block, dense_width), WIDE), False),
        gain_out=(shape((2, width), WIDE), False),
        near_out=(shape((kept, pair, half)), True),
        near_pre=(shape((kept, pair, hidden_width)), True),
        near_hidden=(shape((kept, pair, hidden_width)), True),
        near_grad=(shape((kept, pair, half)), True),
        far_out=(shape((kept, pair, half)), True),
        far_pre=(shape((kept, pair, hidden_width)), True),
        far_hidden=(shape((kept, pair, hidden_width)), True),
        far_grad=(shape((kept, pair, half)), True),
    )
    low = dict(
        pick_near=(2, kept * capacity, group_rows),
        pick_far=(2, kept * capacity, group_rows),
        buffer_near=(2, pair, half),
        buffer_far=(2, pair, half),
        hidden=(kept, pair, hidden_width),
        weighted=(2, kept * capacity, width),
        away=(kept, pair, hidden_width),
        arrived=(kept, pair, hidden_width),
        w_up=(2, kept, half, hidden_width),
        w_near=(kept, hidden_width, half),
        w_far=(kept, hidden_width, half),
        part=(2, 2, 2, rows, width),
        group=(8, rows, width),
        sum_core=(chunks, 2, 2, rows, 256),
        sum_xa=(chunks, 2, rows, 128),
        sum_ya=(chunks, rows, 128),
        sum_yb=(chunks, 2, rows, 128),
        sum_xb=(chunks, rows, 128),
        image_sum=(chunks, rows, 256),
        image_far=(chunks, heads - 1, own, 256),
        out_grad=(kept, pair, half),
        far_held=(kept, pair, half),
        slot_rows=(pair, width),
        x=(2, 2, 2, rows, half),
        other_half=(rows, half),
        qkv=(8, block, gathered_width),
        wo_all=(8, heads, block, mixed_width),
        router=(experts, width),
        projected=(rows, qkv_width),
        mixed=(rows, mixed_width),
        all_mixed=(heads, rows, mixed_width),
        second_in=(rows, width),
        core_in=(chunks, 2, 2, rows, 128),
        y_in=(chunks, 2, rows, 128),
        far=(chunks, heads - 1, 2, own, 128),
        pair=(chunks, 2, own, 128),
        x_in=(chunks, own, 128),
        logit_grads=(experts, rows),
        attended=(rows, width),
        first_in=(rows, width),
        projected_grad=(rows, qkv_width),
        first_part=(heads, own, width),
        dense=(8, block, dense_width),
        dense_core=(4, block, dense_width),
        xa=(2, block, cut),
        ya=(block, cut),
        yb=(2, block, dense_width - cut),
        xb=(block, dense_width - cut),
        first_far=(heads - 1, own, width),
        rounded=(heads, own, width),
    )
    wide = dict(
        gates=(kept, pair, 1),
        counts=(8, 8, 128),
        scale=(8, 128),
        loss_scale=(8, 128),
        valid=(rows, 8),
        gain_one=(1, width),
        gain=(1, width),
        log_total=(rows, head_count),
        residual=(rows, width),
        probs=(8, experts, rows),
        probs_own=(experts, rows),
        own=(kept, pair, hidden_width),
        final_grad=(own, width),
        gate_rows=(2, kept, group_rows),
        gate_in=(4, 2, kept, group_rows),
        gate_sum=(2, kept, group_rows),
        gate_all=(heads, 2, kept, rows),
        logit_rows=(rows, width),
        gain_part=(2, width),
        gain_plane=(8, 2, width),
        gain_heads=(heads, 2, width),
    )
    scratch = {name: pltpu.VMEM(dims, LOW) for name, dims in low.items()}
    scratch.update({name: pltpu.VMEM(dims, WIDE) for name, dims in wide.items()})
    whole = dict(
        far_route=small["near_route"].shape,
        slots=(2 * local_experts, group_rows),
    )
    scratch.update({name: pltpu.VMEM(a.shape, a.dtype) for name, a in small.items()})
    scratch.update({name: pltpu.VMEM(dims, jnp.int32) for name, dims in whole.items()})
    copies = FRONT_COPIES + 2 * (heads - 1) + 2 * kept + chunks * (5 + GATHER_COPIES + 2 * (heads - 1)) + 2 * (heads - 1)
    copies += 2 * kept + kept + 2 * chunks * (2 + heads - 1) + chunks + 3 + 2 * heads - 1
    copies += heads - 1 + SUM_COPIES + 5 * (heads - 1) + 7
    return named_call(
        functools.partial(layer_kernel, heads, chunks, tuple(small)),
        ins,
        outs,
        scratch,
        copies,
        5 * kept + 6 + len(small),
        1,
        59,
        280,
    )


def finish_kernel(s, *refs):
    sides, rest = (refs[:4], refs[4:8]), refs[8:]
    result_in, tokens_in, dense, gains, loss_in = rest[:5]
    up, down, result, tokens_grad, qkv_grad, out_grad, router_grad, gain_grads, loss = rest[5:]
    i = pl.program_id(0)
    kept = pl.num_programs(0) // 2
    for side, (rows, pre, hidden, grad) in enumerate(sides):
        j = i - s[side]

        @pl.when((j >= 0) & (j < kept))
        def _(rows=rows, pre=pre, hidden=hidden, grad=grad):
            up[0] = dot(rows[0], pre[0], (0, 0))
            down[0] = dot(hidden[0], grad[0], (0, 0))

    @pl.when(i == 0)
    def _():
        result[...] = result_in[...].reshape(result.shape)
        tokens_grad[...] = tokens_in[...].reshape(tokens_grad.shape)
        head_count, block, size = qkv_grad.shape
        for h in range(head_count):
            qkv_grad[h] = dense[:, h * size : (h + 1) * size]
        at = head_count * size
        mixed_width = out_grad.shape[0]
        out_grad[...] = jnp.transpose(dense[:, at : at + mixed_width])
        last = jnp.transpose(dense[:, at + mixed_width : at + mixed_width + 128])
        router_grad[...] = last[: router_grad.shape[0]]
        gain_grads[...] = sum(
            jnp.where(s[2] == b, gains[:, b * block : (b + 1) * block], 0.0) for b in range(8)
        )
        loss[...] = jnp.sum(jnp.sum(loss_in[...], 0), keepdims=True)


def finish(scalars, near, far, small, shapes):
    kept, _, half = near[0].shape
    hidden_width = near[1].shape[2]

    def of(array, which):
        return pl.BlockSpec(
            (1, *array.shape[1:]), lambda i, s: (jnp.clip(i - s[which], 0, kept - 1), 0, 0)
        )

    def all_of(array):
        return pl.BlockSpec(array.shape, lambda i, s, n=len(array.shape): (0,) * n)

    return pl.pallas_call(
        finish_kernel,
        out_shape=[
            shape((2 * kept, half, hidden_width), WIDE),
            shape((2 * kept, hidden_width, half), WIDE),
            *shapes,
        ],
        grid_spec=pltpu.PrefetchScalarGridSpec(
            num_scalar_prefetch=1,
            grid=(2 * kept,),
            in_specs=[of(array, 0) for array in near]
            + [of(array, 1) for array in far]
            + [all_of(array) for array in small],
            out_specs=[
                pl.BlockSpec((1, half, hidden_width), lambda i, s: (i, 0, 0)),
                pl.BlockSpec((1, hidden_width, half), lambda i, s: (i, 0, 0)),
                *[all_of(array) for array in shapes],
            ],
        ),
        compiler_params=pltpu.CompilerParams(vmem_limit_bytes=60 * 2**20),
        cost_estimate=spends(8),
    )(scalars, *near, *far, *small)


def fast(
    tokens,
    valid_mask,
    routes,
    teacher,
    gain_one,
    qkv_weight,
    out_weight,
    gain_two,
    router_weight,
    expert_up,
    expert_down,
):
    heads = lax.axis_size(HEADS)
    f, t = lax.axis_index(FSDP), lax.axis_index(TENSOR)
    _, rows, width = tokens.shape
    block, head_count, qkv_dim = qkv_weight.shape
    mixed_width = out_weight.shape[0] * out_weight.shape[1]
    local_experts = expert_up.shape[0]
    kept = local_experts // 2
    expert_count = local_experts * heads
    capacity = 2 * routes.shape[2] * 4 * rows // expert_count
    small = dict(
        router_in=router_weight.T,
        gain_one_in=gain_one[None],
        gain_two_in=gain_two[None],
        qkv_in=jnp.swapaxes(qkv_weight, 0, 1),
        out_in=out_weight.reshape(mixed_width, block),
        near_route=jnp.swapaxes(routes, 1, 2),
        tokens=tokens[0],
        teacher=teacher[0],
        valid_row=valid_mask,
    )
    made = layer(heads, expert_count, capacity, small, dict(up=expert_up, down=expert_down))
    scalars = jnp.stack([f * kept, (1 - f) * kept, f * 4 + t]).astype(jnp.int32)
    up_grad, down_grad, result, tokens_grad, qkv_grad, out_grad, router_grad, gains, loss = finish(
        scalars,
        [made.near_out, made.near_pre, made.near_hidden, made.near_grad],
        [made.far_out, made.far_pre, made.far_hidden, made.far_grad],
        [made.result, made.tokens_grad, made.dense_out, made.gain_out, made.loss],
        [
            shape((rows, width)),
            shape((rows, width), WIDE),
            shape((head_count, block, qkv_dim), WIDE),
            shape((mixed_width, block), WIDE),
            shape((expert_count, block), WIDE),
            shape((2, block), WIDE),
            shape((1, 1), WIDE),
        ],
    )
    return (
        result[None],
        loss.reshape(1),
        tokens_grad[None],
        gains[0],
        jnp.swapaxes(qkv_grad, 0, 1),
        out_grad.reshape(head_count, -1, block),
        gains[1],
        router_grad.T,
        up_grad,
        down_grad,
    )


def local(sizes, *args):
    tokens, routes, up = args[0], args[2], args[9]
    fits = (
        sizes[FSDP] == 2
        and sizes[TENSOR] == 4
        and sizes[HEADS] % 2 == 0
        and tokens.shape[0] == 1
        and up.shape[0] % 8 == 0
        and tokens.shape[1] % (32 * sizes[HEADS]) == 0
        and tokens.shape[2] % 256 == 0
        and routes.shape[2] <= 8
        and up.shape[0] * sizes[HEADS] <= 126
    )
    return fast(*args) if fits else general(*args)


def solution(mesh):
    sizes = dict(mesh.shape)
    program = functools.partial(local, sizes)
    in_specs = (
        P((FSDP, TENSOR), None, None),
        P((FSDP, TENSOR), None),
        P(FSDP, None, None),
        P((FSDP, TENSOR), None, None),
        P((FSDP, TENSOR)),
        P((FSDP, TENSOR), HEADS, None),
        P(HEADS, None, (FSDP, TENSOR)),
        P((FSDP, TENSOR)),
        P((FSDP, TENSOR), None),
        P(HEADS, FSDP, TENSOR),
        P(HEADS, TENSOR, FSDP),
    )
    out_specs = (
        P((FSDP, TENSOR), None, None),
        P((FSDP, TENSOR)),
        P((FSDP, TENSOR), None, None),
        P((FSDP, TENSOR)),
        P((FSDP, TENSOR), HEADS, None),
        P(HEADS, None, (FSDP, TENSOR)),
        P((FSDP, TENSOR)),
        P((FSDP, TENSOR), None),
        P(HEADS, FSDP, TENSOR),
        P(HEADS, TENSOR, FSDP),
    )
    return jax.shard_map(program, mesh=mesh, in_specs=in_specs, out_specs=out_specs, check_vma=False)
```

```python
import functools
import types

import jax
import jax.numpy as jnp
from jax import lax
from jax.experimental import pallas as pl
from jax.experimental.pallas import tpu as pltpu
from jax.sharding import PartitionSpec as P

FSDP, HEADS, TENSOR = "fsdp", "heads", "tensor"
EPSILON = 1e-06
MASKED = -1e30
ROOT_HALF = 0.7071067811865476
DENSITY = 0.3989422804014327


def normalize(values):
    center = values - jnp.mean(values, -1, keepdims=True)
    inv_std = lax.rsqrt(jnp.mean(center * center, -1, keepdims=True) + EPSILON)
    return (center * inv_std, inv_std)


def norm_back(gradient, normed, inv_std, gain_vector):
    weighted = gradient * gain_vector
    gain_grad = jnp.sum(gradient * normed, axis=(0, 1))
    inner = (
        weighted
        - jnp.mean(weighted, -1, keepdims=True)
        - normed * jnp.mean(weighted * normed, -1, keepdims=True)
    )
    return (inner * inv_std, gain_grad)


def scores_of(queries, key_rows, keys_ok, score_scale):
    raw_scores = (
        jnp.einsum("iqhe,ikhe->ihqk", queries, key_rows, preferred_element_type=jnp.float32)
        * score_scale
    )
    return jnp.where(keys_ok, raw_scores, MASKED)


def gather_weights(
    gain_one, qkv_weight, out_weight, gain_two, router_weight, expert_up, expert_down
):
    dense_set = (
        lax.all_gather(qkv_weight, (FSDP, TENSOR), axis=0, tiled=True),
        lax.all_gather(out_weight, (FSDP, TENSOR), axis=2, tiled=True),
        lax.all_gather(router_weight, (FSDP, TENSOR), axis=0, tiled=True),
        lax.all_gather(gain_one, (FSDP, TENSOR), axis=0, tiled=True),
        lax.all_gather(gain_two, (FSDP, TENSOR), axis=0, tiled=True),
    )
    expert_set = (
        lax.all_gather(expert_up, FSDP, axis=1, tiled=True),
        lax.all_gather(expert_down, FSDP, axis=2, tiled=True),
    )
    return (dense_set, expert_set)


def reduce_expert_grads(up_grad, down_grad):
    return (
        lax.psum_scatter(up_grad, FSDP, scatter_dimension=1, tiled=True),
        lax.psum_scatter(down_grad, FSDP, scatter_dimension=2, tiled=True),
    )


def general(
    tokens,
    valid_mask,
    routes,
    teacher,
    gain_one,
    qkv_weight,
    out_weight,
    gain_two,
    router_weight,
    expert_up,
    expert_down,
):
    valid_total = lax.psum(jnp.sum(valid_mask.astype(jnp.float32)), (FSDP, TENSOR))
    dense_set, expert_set = gather_weights(
        gain_one, qkv_weight, out_weight, gain_two, router_weight, expert_up, expert_down
    )
    qkv_full, output_complete, router_full, gain_a, gain_b = dense_set
    up_full, down_full = expert_set
    image_count, token_slots, model_width = tokens.shape
    head_dim = qkv_full.shape[2] // 3
    local_experts = expert_up.shape[0]
    tensor_size = lax.axis_size(TENSOR)
    group_images = image_count * tensor_size
    group_rows = group_images * token_slots
    top_choices = routes.shape[2]
    expert_count = local_experts * lax.axis_size(HEADS)
    capacity = 2 * top_choices * group_rows // expert_count
    slot_count = local_experts * capacity
    total_tokens = image_count * token_slots * lax.axis_size(FSDP) * tensor_size
    total_images = image_count * lax.axis_size(FSDP) * tensor_size
    score_scale = head_dim ** (-0.5)
    inputs = tokens.astype(jnp.float32)
    normed_one, spread_one = normalize(inputs)
    first_in = (normed_one * gain_a.astype(jnp.float32)).astype(jnp.bfloat16)
    projected = jnp.einsum(
        "isd,dhe->ishe", first_in, qkv_full, preferred_element_type=jnp.float32
    ).astype(jnp.bfloat16)
    queries = projected[..., :head_dim]
    key_rows = projected[..., head_dim : 2 * head_dim]
    values = projected[..., 2 * head_dim :]
    keys_ok = (valid_mask > 0)[:, None, None, :]
    scores = scores_of(queries, key_rows, keys_ok, score_scale)
    peak_score = jnp.max(scores, -1, keepdims=True)
    exp_scores = jnp.exp(scores - peak_score)
    score_total = jnp.sum(exp_scores, -1, keepdims=True)
    logarithm_total = peak_score + jnp.log(score_total)
    attention = (exp_scores / score_total).astype(jnp.bfloat16)
    combined_heads = jnp.einsum(
        "ihqk,ikhe->iqhe", attention, values, preferred_element_type=jnp.float32
    ).astype(jnp.bfloat16)
    attn_part = jnp.einsum(
        "iqhe,hed->iqd", combined_heads, output_complete, preferred_element_type=jnp.float32
    )
    attended = lax.psum(attn_part, HEADS)
    residual = inputs + attended
    normed_two, spread_two = normalize(residual)
    second_in = (normed_two * gain_b.astype(jnp.float32)).astype(jnp.bfloat16)
    group_in = lax.all_gather(second_in, TENSOR, axis=0, tiled=True)
    rows_in = group_in.reshape(group_rows, model_width)
    logits = jnp.dot(rows_in, router_full, preferred_element_type=jnp.float32)
    peak_logit = jnp.max(logits, -1, keepdims=True)
    exponent_logits = jnp.exp(logits - peak_logit)
    router_probs = exponent_logits / jnp.sum(exponent_logits, -1, keepdims=True)
    expert_ids = jnp.arange(expert_count, dtype=jnp.int32)
    route_pairs = routes.reshape(group_rows, top_choices)
    picked_hot = (route_pairs[:, :, None] == expert_ids[None, None, :]).astype(jnp.float32)
    gate_weight_values = jnp.sum(router_probs[:, None, :] * picked_hot, -1)
    flat_routes = route_pairs.reshape(group_rows * top_choices)
    route_hot = (flat_routes[:, None] == expert_ids[None, :]).astype(jnp.int32)
    order = jnp.arange(group_rows * top_choices, dtype=jnp.int32)
    before = (order[None, :] < order[:, None]).astype(jnp.bfloat16)
    earlier = jnp.dot(
        before, route_hot.astype(jnp.bfloat16), preferred_element_type=jnp.float32
    ).astype(jnp.int32)
    slot_index = jnp.sum(earlier * route_hot, 1)
    first_expert = lax.axis_index(HEADS) * local_experts
    is_local = (flat_routes >= first_expert) & (flat_routes < first_expert + local_experts)
    target = jnp.where(is_local, (flat_routes - first_expert) * capacity + slot_index, slot_count)
    owner_row = jnp.arange(group_rows * top_choices, dtype=jnp.int32) // top_choices
    source = jnp.zeros((slot_count,), jnp.int32).at[target].set(owner_row, mode="drop")
    slot_gate = (
        jnp.zeros((slot_count,), jnp.float32)
        .at[target]
        .set(gate_weight_values.reshape(-1), mode="drop")
    )
    slot_pick = jnp.minimum(target, slot_count - 1)
    retain_mask = is_local.astype(jnp.float32)
    dispatched = rows_in[source].reshape(local_experts, capacity, model_width)
    before_gelu = jnp.einsum(
        "ecd,edf->ecf", dispatched, up_full, preferred_element_type=jnp.float32
    )
    hidden = jax.nn.gelu(before_gelu, approximate=False).astype(jnp.bfloat16)
    expert_out = jnp.einsum(
        "ecf,efd->ecd", hidden, down_full, preferred_element_type=jnp.float32
    ).reshape(slot_count, model_width)
    weighted = expert_out * slot_gate[:, None]
    moe_part = jnp.sum(
        (weighted[slot_pick] * retain_mask[:, None]).reshape(group_rows, top_choices, model_width),
        1,
    )
    moe_part = moe_part.reshape(group_images, token_slots, model_width)
    expert_sum = lax.psum(
        lax.psum_scatter(moe_part, TENSOR, scatter_dimension=0, tiled=True), HEADS
    )
    final = residual + expert_sum
    valid_rows = valid_mask.astype(jnp.float32)[..., None]
    difference = (final - teacher.astype(jnp.float32)) * valid_rows
    loss_terms = jnp.sum(difference * difference, axis=(1, 2)) * (
        total_images / (valid_total * model_width)
    )
    final_grad = difference * (total_tokens / valid_total)
    dense_set, expert_set = gather_weights(
        gain_one, qkv_weight, out_weight, gain_two, router_weight, expert_up, expert_down
    )
    qkv_full, output_complete, router_full, gain_a, gain_b = dense_set
    up_full, down_full = expert_set
    moe_grad = final_grad.astype(jnp.bfloat16)
    group_grad = lax.all_gather(moe_grad, TENSOR, axis=0, tiled=True).reshape(
        group_rows, model_width
    )
    slot_grad = group_grad[source].astype(jnp.float32)
    gate_slot_grad = jnp.sum(slot_grad * expert_out, -1)
    out_grad = (
        (slot_grad * slot_gate[:, None])
        .astype(jnp.bfloat16)
        .reshape(local_experts, capacity, model_width)
    )
    expert_down_grad = jnp.einsum(
        "ecf,ecd->efd", hidden, out_grad, preferred_element_type=jnp.float32
    )
    hidden_grad = jnp.einsum(
        "ecd,efd->ecf", out_grad, down_full, preferred_element_type=jnp.float32
    )
    normal_cdf = 0.5 * (1.0 + lax.erf(before_gelu * ROOT_HALF))
    slope = normal_cdf + before_gelu * DENSITY * jnp.exp(-0.5 * before_gelu * before_gelu)
    pre_grad = (hidden_grad * slope).astype(jnp.bfloat16)
    expert_up_grad = jnp.einsum(
        "ecd,ecf->edf", dispatched, pre_grad, preferred_element_type=jnp.float32
    )
    row_grad = jnp.einsum(
        "ecf,edf->ecd", pre_grad, up_full, preferred_element_type=jnp.float32
    ).reshape(slot_count, model_width)
    rows_part = jnp.sum(
        (row_grad[slot_pick] * retain_mask[:, None]).reshape(group_rows, top_choices, model_width),
        1,
    )
    rows_part = rows_part.reshape(group_images, token_slots, model_width)
    gate_part = (gate_slot_grad[slot_pick] * retain_mask).reshape(
        group_images, token_slots, top_choices
    )
    rows_share, gate_share = (
        lax.psum_scatter(rows_part, TENSOR, scatter_dimension=0, tiled=True),
        lax.psum_scatter(gate_part, TENSOR, scatter_dimension=0, tiled=True),
    )
    second_grad, gate_grad = lax.psum((rows_share, gate_share), HEADS)
    own_start = lax.axis_index(TENSOR) * image_count * token_slots
    own_rows = image_count * token_slots
    own_probs = lax.dynamic_slice_in_dim(router_probs, own_start, own_rows, 0).reshape(
        image_count, token_slots, expert_count
    )
    own_hot = lax.dynamic_slice_in_dim(picked_hot, own_start, own_rows, 0).reshape(
        image_count, token_slots, top_choices, expert_count
    )
    prob_grad = jnp.sum(gate_grad[..., None] * own_hot, 2)
    logit_grad = (
        own_probs * (prob_grad - jnp.sum(own_probs * prob_grad, -1, keepdims=True))
    ).astype(jnp.bfloat16)
    router_grad = jnp.einsum(
        "isd,ise->de", second_in, logit_grad, preferred_element_type=jnp.float32
    )
    second_grad = second_grad + jnp.einsum(
        "ise,de->isd", logit_grad, router_full, preferred_element_type=jnp.float32
    )
    residual_norm, gain_two_grad = norm_back(
        second_grad, normed_two, spread_two, gain_b.astype(jnp.float32)
    )
    residual_grad = final_grad + residual_norm
    attended_output_gradient = residual_grad.astype(jnp.bfloat16)
    out_weight_grad = jnp.einsum(
        "iqhe,iqd->hed",
        combined_heads,
        attended_output_gradient,
        preferred_element_type=jnp.float32,
    )
    mixed_grad = jnp.einsum(
        "iqd,hed->iqhe",
        attended_output_gradient,
        output_complete,
        preferred_element_type=jnp.float32,
    ).astype(jnp.bfloat16)
    scores = scores_of(queries, key_rows, keys_ok, score_scale)
    probs = jnp.exp(scores - logarithm_total)
    probs_low = probs.astype(jnp.bfloat16)
    prob_part = jnp.einsum(
        "iqhe,ikhe->ihqk", mixed_grad, values, preferred_element_type=jnp.float32
    )
    score_grad = (probs * (prob_part - jnp.sum(probs * prob_part, -1, keepdims=True))).astype(
        jnp.bfloat16
    )
    query_grad = (
        jnp.einsum("ihqk,ikhe->iqhe", score_grad, key_rows, preferred_element_type=jnp.float32)
        * score_scale
    )
    key_grad = (
        jnp.einsum("ihqk,iqhe->ikhe", score_grad, queries, preferred_element_type=jnp.float32)
        * score_scale
    )
    value_grad = jnp.einsum(
        "ihqk,iqhe->ikhe", probs_low, mixed_grad, preferred_element_type=jnp.float32
    )
    projected_grad = jnp.concatenate([query_grad, key_grad, value_grad], -1).astype(jnp.bfloat16)
    qkv_grad = jnp.einsum(
        "isd,ishe->dhe", first_in, projected_grad, preferred_element_type=jnp.float32
    )
    first_part = jnp.einsum(
        "ishe,dhe->isd", projected_grad, qkv_full, preferred_element_type=jnp.float32
    )
    first_grad = lax.psum(first_part, HEADS)
    input_norm, gain_one_grad = norm_back(
        first_grad, normed_one, spread_one, gain_a.astype(jnp.float32)
    )
    tokens_grad = residual_grad + input_norm
    dense_grads = (
        lax.psum_scatter(qkv_grad, (FSDP, TENSOR), scatter_dimension=0, tiled=True),
        lax.psum_scatter(out_weight_grad, (FSDP, TENSOR), scatter_dimension=2, tiled=True),
        lax.psum_scatter(router_grad, (FSDP, TENSOR), scatter_dimension=0, tiled=True),
        lax.psum_scatter(gain_one_grad, (FSDP, TENSOR), scatter_dimension=0, tiled=True),
        lax.psum_scatter(gain_two_grad, (FSDP, TENSOR), scatter_dimension=0, tiled=True),
    )
    expert_grads = reduce_expert_grads(expert_up_grad, expert_down_grad)
    return (
        final.astype(jnp.bfloat16),
        loss_terms,
        tokens_grad,
        dense_grads[3],
        dense_grads[0],
        dense_grads[1],
        dense_grads[4],
        dense_grads[2],
        expert_grads[0],
        expert_grads[1],
    )


MESH = pl.DeviceIdType.MESH
LOW = jnp.bfloat16
WIDE = jnp.float32


class Links:
    def __init__(self, send_sems, recv_sems):
        self.send_sems, self.recv_sems = send_sems, recv_sems
        self.copies, self.gone = [], []

    def send(self, src, dst, device):
        k = len(self.copies)
        assert k < self.send_sems.shape[0]
        copy = pltpu.make_async_remote_copy(
            src_ref=src,
            dst_ref=dst,
            send_sem=self.send_sems.at[k],
            recv_sem=self.recv_sems.at[k],
            device_id=device,
            device_id_type=MESH,
        )
        copy.start()
        self.copies.append(copy)
        return copy

    def left(self, copies):
        for copy in copies:
            copy.wait_send()
            self.gone.append(copy)

    def drain(self):
        for copy in self.copies:
            if not any(copy is other for other in self.gone):
                copy.wait_send()


class Place:
    def __init__(self, heads):
        self.f = lax.axis_index(FSDP)
        t = lax.axis_index(TENSOR)
        self.y, self.c = t // 2, lax.rem(t, 2)
        self.z = lax.axis_index(HEADS)
        self.heads = heads
        self.x_peer = {FSDP: 1 - self.f}
        self.y_peer = {TENSOR: 2 * (1 - self.y) + self.c}
        self.core_peer = {TENSOR: 2 * self.y + 1 - self.c}
        self.z_peers = [{HEADS: lax.rem(self.z + k, heads)} for k in range(1, heads)]
        self.plane_peers = []
        for a in range(2):
            for k in range(4):
                if a or k:
                    where = {TENSOR: lax.rem(t + k, 4)}
                    if a:
                        where[FSDP] = 1 - self.f
                    self.plane_peers.append(where)

    def image(self, df, dy, dc):
        f = 1 - self.f if df else self.f
        y = 1 - self.y if dy else self.y
        c = 1 - self.c if dc else self.c
        return f * 4 + 2 * y + c

    def greet(self, devices):
        barrier = pltpu.get_barrier_semaphore()
        for device in devices:
            pl.semaphore_signal(barrier, inc=1, device_id=device, device_id_type=MESH)
        pl.semaphore_wait(barrier, len(devices))

    def tensor_peers(self):
        t = 2 * self.y + self.c
        return [{TENSOR: lax.rem(t + k, 4)} for k in range(1, 4)]

    def owners(self):
        return [
            {FSDP: 1 - self.f if a else self.f, HEADS: lax.rem(self.z + k, self.heads)}
            for k in range(self.heads)
            for a in range(2)
            if a or k
        ]

    def everyone(self):
        t = 2 * self.y + self.c
        corners = [{FSDP: 1 - self.f, TENSOR: lax.rem(t + k, 4)} for k in range(1, 4)]
        return self.tensor_peers() + self.owners() + corners

    def axis_peers(self):
        return [self.x_peer, self.y_peer, self.core_peer]


class PlaneGather:
    def __init__(self, links, place, first, second, whole):
        self.links, self.place = links, place
        self.first, self.second, self.whole = first, second, whole

    def go(self, part, image, device):
        return self.links.send(part(image), part(image), device)

    def start(self):
        p, me = self.place, self.place.image(0, 0, 0)
        self.xa = self.go(self.first, me, p.x_peer)
        self.yb = self.go(self.second, me, p.y_peer)
        self.own = self.go(self.whole, me, p.core_peer)
        self.xb = self.go(self.second, me, p.x_peer)
        self.ya = self.go(self.first, me, p.y_peer)

    def forward(self):
        p = self.place
        self.xa.wait_recv()
        self.fa = self.go(self.first, p.image(1, 0, 0), p.y_peer)
        self.yb.wait_recv()
        self.fb = self.go(self.second, p.image(0, 1, 0), p.x_peer)

    def share(self):
        p = self.place
        self.xb.wait_recv()
        self.c1 = self.go(self.whole, p.image(1, 0, 0), p.core_peer)
        self.ya.wait_recv()
        self.c2 = self.go(self.whole, p.image(0, 1, 0), p.core_peer)

    def finish(self):
        p = self.place
        self.fa.wait_recv()
        self.fb.wait_recv()
        self.c3 = self.go(self.whole, p.image(1, 1, 0), p.core_peer)
        for copy in (self.own, self.c1, self.c2, self.c3):
            copy.wait_recv()

    def run(self):
        self.start()
        self.forward()
        self.share()
        self.finish()


GATHER_COPIES = 10


def in_rows(rows, step, body):
    def one(i, carry):
        body(pl.ds(pl.multiple_of(i * step, step), step))
        return carry

    lax.fori_loop(0, rows // step, one, 0)


class PlaneSum:
    def __init__(self, links, place, part, core_in, xa, ya, yb, xb, cut, step):
        self.links, self.place, self.part, self.core_in = links, place, part, core_in
        self.xa, self.ya, self.yb, self.xb, self.cut, self.step = xa, ya, yb, xb, cut, step
        self.rows, self.width = part.shape[1], part.shape[2]
        self.a, self.b = pl.ds(0, cut), pl.ds(cut, self.width - cut)

    def start(self):
        p = self.place
        self.order = [(1, 1), (1, 0), (0, 1), (0, 0)]
        self.into = {}
        for df, dy in self.order:
            f = 1 - p.f if df else p.f
            y = 1 - p.y if dy else p.y
            self.into[df, dy] = self.links.send(
                self.part.at[p.image(df, dy, 1)], self.core_in.at[2 * f + y], p.core_peer
            )

    def slot(self, df, dy):
        p = self.place
        return 2 * (1 - p.f if df else p.f) + (1 - p.y if dy else p.y)

    def cores(self):
        p, rc = self.place, self.core_in
        self.got = {}
        for df, dy in self.order:
            self.into[df, dy].wait_recv()
            j, mine = self.slot(df, dy), p.image(df, dy, 0)

            def add(rows, j=j, mine=mine):
                both = rc[j, rows, :].astype(WIDE) + self.part[mine, rows, :].astype(WIDE)
                rc[j, rows, :] = both.astype(LOW)

            in_rows(self.rows, self.step, add)
            y = 1 - p.y if dy else p.y
            f = 1 - p.f if df else p.f
            if df:
                self.got["x", dy] = self.links.send(rc.at[j, :, self.a], self.xa.at[y], p.x_peer)
            if dy:
                self.got["y", df] = self.links.send(rc.at[j, :, self.b], self.yb.at[f], p.y_peer)

    def cross(self):
        p, rc, xa, yb = self.place, self.core_in, self.xa, self.yb
        self.got["x", 1].wait_recv()
        j, other = self.slot(0, 1), 1 - p.y

        def add_a(rows):
            both = xa[other, rows, :].astype(WIDE) + rc[j, rows, self.a].astype(WIDE)
            xa[other, rows, :] = both.astype(LOW)

        in_rows(self.rows, self.step, add_a)
        self.last_a = self.links.send(xa.at[other], self.ya, p.y_peer)
        self.got["y", 1].wait_recv()
        k, away = self.slot(1, 0), 1 - p.f

        def add_b(rows):
            both = yb[away, rows, :].astype(WIDE) + rc[k, rows, self.b].astype(WIDE)
            yb[away, rows, :] = both.astype(LOW)

        in_rows(self.rows, self.step, add_b)
        self.last_b = self.links.send(yb.at[away], self.xb, p.x_peer)

    def finish(self, take):
        p, rc = self.place, self.core_in
        self.got["x", 0].wait_recv()
        self.got["y", 0].wait_recv()
        self.last_a.wait_recv()
        self.last_b.wait_recv()
        j, y, f = self.slot(0, 0), p.y, p.f

        def add(rows):
            first = rc[j, rows, self.a].astype(WIDE) + self.xa[y, rows, :].astype(WIDE)
            second = rc[j, rows, self.b].astype(WIDE) + self.yb[f, rows, :].astype(WIDE)
            take(rows, self.a, first + self.ya[rows, :].astype(WIDE))
            take(rows, self.b, second + self.xb[rows, :].astype(WIDE))

        in_rows(self.rows, self.step, add)


SUM_COPIES = 10


def sum_scratch(rows, width, cut):
    return [
        pltpu.VMEM((4, rows, width), LOW),
        pltpu.VMEM((2, rows, cut), LOW),
        pltpu.VMEM((rows, cut), LOW),
        pltpu.VMEM((2, rows, width - cut), LOW),
        pltpu.VMEM((rows, width - cut), LOW),
    ]


def all_heads(links, place, make):
    copies = []
    for k, device in enumerate(place.z_peers):
        src, dst = make(k, device[HEADS])
        copies.append(links.send(src, dst, device))
    return copies


def spends(microseconds):
    return pl.CostEstimate(flops=0, bytes_accessed=microseconds * 3_000_000, transcendentals=0)


def shape(dims, dtype=LOW):
    return jax.ShapeDtypeStruct(dims, dtype)


class ChunkSum:
    def __init__(self, links, place, part, columns, core_in, xa, ya, yb, xb):
        self.links, self.place, self.part, self.columns = links, place, part, columns
        self.core_in, self.xa, self.ya, self.yb, self.xb = core_in, xa, ya, yb, xb
        self.rows, self.half = core_in.shape[2], core_in.shape[3] // 2
        self.a, self.b = pl.ds(0, self.half), pl.ds(self.half, self.half)

    def start(self):
        p = self.place
        self.into = self.links.send(
            self.part.at[:, :, 1 - p.c, :, self.columns], self.core_in, p.core_peer
        )

    def cores(self):
        p, rc = self.place, self.core_in
        self.into.wait_recv()

        def add(rows):
            here = self.part[:, :, p.c, rows, self.columns].astype(WIDE)
            rc[:, :, rows, :] = (rc[:, :, rows, :].astype(WIDE) + here).astype(LOW)

        in_rows(self.rows, 32, add)
        self.to_x = self.links.send(rc.at[1 - p.f, :, :, self.a], self.xa, p.x_peer)
        self.to_y = self.links.send(rc.at[:, 1 - p.y, :, self.b], self.yb, p.y_peer)

    def cross(self):
        p, rc, xa, yb = self.place, self.core_in, self.xa, self.yb
        self.to_x.wait_recv()
        y, f = 1 - p.y, 1 - p.f

        def add_a(rows):
            both = xa[y, rows, :].astype(WIDE) + rc[p.f, y, rows, self.a].astype(WIDE)
            xa[y, rows, :] = both.astype(LOW)

        in_rows(self.rows, 64, add_a)
        self.last_a = self.links.send(xa.at[y], self.ya, p.y_peer)
        self.to_y.wait_recv()

        def add_b(rows):
            both = yb[f, rows, :].astype(WIDE) + rc[f, p.y, rows, self.b].astype(WIDE)
            yb[f, rows, :] = both.astype(LOW)

        in_rows(self.rows, 64, add_b)
        self.last_b = self.links.send(yb.at[f], self.xb, p.x_peer)

    def finish(self, take):
        p, rc = self.place, self.core_in
        self.last_a.wait_recv()
        self.last_b.wait_recv()

        def add(rows):
            first = rc[p.f, p.y, rows, self.a].astype(WIDE) + self.xa[p.y, rows, :].astype(WIDE)
            second = rc[p.f, p.y, rows, self.b].astype(WIDE) + self.yb[p.f, rows, :].astype(WIDE)
            take(rows, 0, first + self.ya[rows, :].astype(WIDE))
            take(rows, 1, second + self.xb[rows, :].astype(WIDE))

        in_rows(self.rows, 64, add)


def skewed(chunks, stages):
    for step in range(chunks + len(stages) - 1):
        for k in range(chunks):
            if 0 <= step - k < len(stages):
                stages[step - k](k)


def combine_part(place, links, chunks, r):
    heads, z, me = place.heads, place.z, place.image(0, 0, 0)
    part, residual, teacher, valid, scale = r.part, r.residual, r.teacher, r.valid, r.scale
    result, final_grad, group, loss = r.result, r.final_grad, r.group, r.loss
    image_sum, far = r.image_sum, r.image_far
    rows_all, width = residual.shape
    own = rows_all // heads
    wide = width // chunks
    half = wide // 2
    mine = pl.ds(pl.multiple_of(z * own, own), own)
    columns = [pl.ds(k * wide, wide) for k in range(chunks)]
    adders = [
        ChunkSum(
            links,
            place,
            part,
            columns[k],
            r.sum_core.at[k],
            r.sum_xa.at[k],
            r.sum_ya.at[k],
            r.sum_yb.at[k],
            r.sum_xb.at[k],
        )
        for k in range(chunks)
    ]
    for adder in adders:
        adder.start()
    along, spread, squares = {}, {}, []
    gathers = [
        PlaneGather(
            links,
            place,
            lambda i, k=k: group.at[i, :, pl.ds(k * wide, half)],
            lambda i, k=k: group.at[i, :, pl.ds(k * wide + half, half)],
            lambda i, k=k: group.at[i, :, columns[k]],
        )
        for k in range(chunks)
    ]

    def to_heads(k):
        def keep(rows, part_of, values):
            image_sum[k, rows, pl.ds(part_of * half, half)] = values.astype(LOW)

        adders[k].finish(keep)
        along[k] = all_heads(
            links,
            place,
            lambda n, to: (
                image_sum.at[k, pl.ds(pl.multiple_of(to * own, own), own)],
                far.at[k, n],
            ),
        )

    def final(k):
        for copy in along[k]:
            copy.wait_recv()
        total = image_sum[k, mine, :].astype(WIDE)
        for n in range(heads - 1):
            total = total + far[k, n].astype(WIDE)
        values = residual[mine, columns[k]] + total
        result[z, :, columns[k]] = values.astype(LOW)
        error = (values - teacher[mine, columns[k]].astype(WIDE)) * valid[mine, 0:1]
        grad = error * scale[0:1, 0:1]
        final_grad[:, columns[k]] = grad
        group[me, mine, columns[k]] = grad.astype(LOW)
        block = group.at[me, mine, columns[k]]
        spread[k] = all_heads(links, place, lambda n, to: (block, block))
        square = jnp.sum((error * error).reshape(own // 8, 8, wide), axis=0)
        squares.extend(square[:, i * 128 : (i + 1) * 128] for i in range(wide // 128))

    def to_plane(k):
        for copy in spread[k]:
            copy.wait_recv()
        gathers[k].start()

    def forward(k):
        gathers[k].forward()
        gathers[k].share()

    skewed(
        chunks,
        [
            lambda k: adders[k].cores(),
            lambda k: adders[k].cross(),
            to_heads,
            final,
            to_plane,
            forward,
        ],
    )
    loss[z] = sum(squares) * r.loss_scale[0:1, 0:1]
    extra = all_heads(links, place, lambda k, to: (result.at[z], result.at[z]))
    extra += all_heads(links, place, lambda k, to: (loss.at[z], loss.at[z]))
    for gather in gathers:
        gather.finish()
    return extra


def dot(a, b, over=(1, 0)):
    return lax.dot_general(a, b, (((over[0],), (over[1],)), ((), ())), preferred_element_type=WIDE)


def one_hot(slots, row, capacity):
    places = lax.broadcasted_iota(jnp.int32, (capacity, slots.shape[1]), 0)
    return places == slots[pl.ds(row, 1), :]


class Loads:
    def __init__(self, sems):
        self.sems, self.count = sems, 0

    def start(self, src, dst):
        assert self.count < self.sems.shape[0]
        copy = pltpu.make_async_copy(src, dst, self.sems.at[self.count])
        self.count += 1
        copy.start()
        return copy


def gelu_parts(values):
    cdf = 0.5 * (1.0 + lax.erf(values * ROOT_HALF))
    return values * cdf, cdf + values * DENSITY * jnp.exp(-0.5 * values * values)


def front_part(place, links, r):
    heads, f, z, me = place.heads, place.f, place.z, place.image(0, 0, 0)
    oq, oo, counts, slots = r.qkv, r.wo_all, r.counts, r.slots
    kept = r.w_far.shape[0]
    theirs = (1 - f) * kept
    rows = [r.router_in[...], r.gain_one_in[...], r.gain_two_in[...]]
    rows = [row.astype(WIDE) for row in rows]
    block = oq.shape[1]
    rows.append(jnp.zeros((128 - sum(row.shape[0] for row in rows), block), WIDE))
    oq[me, :, 0:128] = jnp.transpose(jnp.concatenate(rows, 0)).astype(LOW)
    qkv = jnp.concatenate([r.qkv_in[h] for h in range(r.qkv_in.shape[0])], 1)
    oq[me, :, pl.ds(128, qkv.shape[1])] = qkv
    rest = oq.shape[2] - 128 - qkv.shape[1]
    if rest:
        oq[me, :, pl.ds(128 + qkv.shape[1], rest)] = jnp.zeros((block, rest), LOW)
    oo[me, z] = jnp.transpose(r.out_in[...].astype(WIDE)).astype(LOW)
    counts[me] = jnp.broadcast_to(jnp.sum(r.valid_row[...].astype(WIDE), -1, keepdims=True), (8, 128))
    half, mid = oq.shape[2] // 2, heads // 2
    main = PlaneGather(
        links,
        place,
        lambda i: oq.at[i, :, pl.ds(0, half)],
        lambda i: oq.at[i, :, pl.ds(half, half)],
        lambda i: oq.at[i],
    )
    side = PlaneGather(
        links,
        place,
        lambda i: oo.at[i, pl.ds(0, mid)],
        lambda i: oo.at[i, pl.ds(mid, heads - mid)],
        lambda i: oo.at[i],
    )

    def bulk(i):
        return links.send(r.down.at[theirs + i], r.w_far.at[i], place.x_peer)

    main.start()
    along = all_heads(links, place, lambda k, to: (oo.at[me, z], oo.at[me, z]))
    small = [links.send(counts.at[me], counts.at[me], d) for d in place.plane_peers]
    small.append(links.send(r.near_route, r.far_route, place.x_peer))
    main.forward()
    down = [bulk(0)]
    for copy in along:
        copy.wait_recv()
    side.start()
    main.share()
    main.finish()
    width = r.tokens.shape[1]
    experts = r.probs.shape[1]
    narrow = oq[:, :, 0:128].reshape(width, 128).astype(WIDE)
    turned = jnp.transpose(narrow)
    r.router[...] = turned[:experts].astype(LOW)
    r.gain_one[...] = turned[experts : experts + 1]
    r.gain[...] = turned[experts + 1 : experts + 2]
    rows_all = r.tokens.shape[0]

    def first_norm(rows):
        normed, _ = normalize(r.tokens[rows, :].astype(WIDE))
        r.first_in[rows, :] = (normed * r.gain_one[...]).astype(LOW)

    in_rows(rows_all, 64, first_norm)
    qkv_width = r.projected.shape[1]
    weight = oq[:, :, pl.ds(128, qkv_width)].reshape(width, qkv_width)
    r.projected[...] = dot(r.first_in[...], weight).astype(LOW)
    side.forward()
    down.append(bulk(1))
    head_count = r.log_total.shape[1]
    size = qkv_width // head_count // 3
    keys_ok = r.valid_row[...] > 0
    mixed = []
    for h in range(head_count):
        at = 3 * h * size
        query, key, value = (r.projected[:, at + n * size : at + (n + 1) * size] for n in range(3))
        scores = jnp.where(keys_ok, dot(query, key, (1, 1)) * size ** (-0.5), MASKED)
        peak = jnp.max(scores, -1, keepdims=True)
        powers = jnp.exp(scores - peak)
        total = jnp.sum(powers, -1, keepdims=True)
        r.log_total[:, h : h + 1] = peak + jnp.log(total)
        mixed.append(dot((powers / total).astype(LOW), value).astype(LOW))
    r.mixed[...] = jnp.concatenate(mixed, 1)
    everyone = r.all_mixed
    everyone[z] = r.mixed[...]
    along = all_heads(links, place, lambda k, to: (everyone.at[z], everyone.at[z]))
    side.share()
    for copy in small:
        copy.wait_recv()
    valid_total = sum(counts[i] for i in range(8))[0:1, 0:1]
    r.scale[...] = jnp.broadcast_to(8 * rows_all / valid_total, (8, 128))
    r.loss_scale[...] = jnp.broadcast_to(8 / (valid_total * width), (8, 128))
    column = jnp.broadcast_to(r.valid_row[...].astype(WIDE), (8, rows_all))
    r.valid[...] = jnp.transpose(column)
    local_experts = 2 * kept
    ids = z * local_experts + lax.broadcasted_iota(jnp.int32, (local_experts, 1), 0)
    first = f == 0
    near, far = r.near_route[...], r.far_route[...]
    both = [jnp.where(first, near, far), jnp.where(first, far, near)]
    chosen = []
    for route in both:
        hits = []
        for c in range(route.shape[1]):
            row = jnp.concatenate([route[k, c : c + 1] for k in range(4)], 1)
            hits.append(row == ids)
        chosen.append(functools.reduce(jnp.logical_or, hits))
    chosen = jnp.concatenate(chosen, 0)
    count = chosen.astype(WIDE)
    before = lax.broadcasted_iota(jnp.int32, (128, 128), 0)
    before = (before < lax.broadcasted_iota(jnp.int32, (128, 128), 1)).astype(LOW)
    running = jnp.zeros((2 * local_experts, 1), WIDE)
    for b in range(slots.shape[1] // 128):
        columns = slice(b * 128, (b + 1) * 128)
        here = count[:, columns]
        slot = dot(here.astype(LOW), before) + running
        slots[:, columns] = jnp.where(chosen[:, columns], slot, -1.0).astype(jnp.int32)
        running = running + jnp.sum(here, -1, keepdims=True)
    for copy in along:
        copy.wait_recv()
    side.finish()
    half = width // 2
    total = jnp.zeros((rows_all, width), WIDE)
    for n in range(heads):
        weight = oo[:, n].reshape(width, oo.shape[3])
        total = total + dot(everyone[n], weight, (1, 1))
    r.residual[...] = total

    def norm(rows):
        values = r.tokens[rows, :].astype(WIDE) + r.residual[rows, :]
        r.residual[rows, :] = values
        normed, _ = normalize(values)
        r.second_in[rows, :] = (normed * r.gain[...]).astype(LOW)

    in_rows(rows_all, 64, norm)
    low, high = r.second_in[:, :half], r.second_in[:, half:]

    def part_of(df, dy, dc):
        return r.x.at[
            1 - f if df else f, 1 - place.y if dy else place.y, 1 - place.c if dc else place.c
        ]

    mine, across, beside, corner = (
        part_of(0, 0, 0),
        part_of(1, 0, 0),
        part_of(0, 1, 0),
        part_of(1, 1, 0),
    )
    mine[...] = jnp.where(first, low, high)
    r.other_half[...] = jnp.where(first, high, low)
    x1 = links.send(r.other_half, mine, place.x_peer)
    y1 = links.send(mine, mine, place.y_peer)
    shared = [links.send(mine, mine, place.core_peer)]
    down.append(bulk(2))
    logits = dot(r.router[...], r.second_in[...], (1, 1))
    powers = jnp.exp(logits - jnp.max(logits, 0, keepdims=True))
    probs = powers / jnp.sum(powers, 0, keepdims=True)
    r.probs_own[...] = probs
    r.probs[me] = probs
    small = [links.send(r.probs.at[me], r.probs.at[me], d) for d in place.plane_peers]
    x1.wait_recv()
    y2 = links.send(across, across, place.y_peer)
    shared.append(links.send(across, across, place.core_peer))
    y1.wait_recv()
    shared.append(links.send(beside, beside, place.core_peer))
    y2.wait_recv()
    shared.append(links.send(corner, corner, place.core_peer))
    for copy in shared + small:
        copy.wait_recv()
    return [y1, y2, *shared], down


FRONT_COPIES = 2 * GATHER_COPIES + 7 + 1 + 1 + 2 + 4 + 7


def send_hidden(place, links, r, i):
    return links.send(r.hidden.at[i], r.far_hidden.at[i], place.x_peer)


def experts_part(place, links, loads, weights, down_far, r):
    slots, probs = r.slots, r.probs
    pick_near, pick_far, gates, hidden = r.pick_near, r.pick_far, r.gates, r.hidden
    buffer_near, buffer_far, own, weighted = r.buffer_near, r.buffer_far, r.own, r.weighted
    away, arrived, w_up, w_near, w_far = r.away, r.arrived, r.w_up, r.w_near, r.w_far
    kept, pair, _ = own.shape
    capacity, half = pair // 2, r.x.shape[4]
    group_rows = slots.shape[1]
    stores = []

    def kept_rows(i, buffer, target):
        stores.append(loads.start(buffer.at[i % 2], target.at[i]))

    local_experts = 2 * kept
    mine, theirs = place.f * kept, (1 - place.f) * kept
    ups, nears = weights
    sent = []
    for i in range(kept):
        if i > 1:
            stores[i - 2].wait()
        for g in range(2):
            rows = slice(i * capacity, (i + 1) * capacity)
            hot = one_hot(slots, g * local_experts + theirs + i, capacity).astype(LOW)
            pick_far[g, rows] = hot
            x = r.x[g].reshape(group_rows, half)
            buffer_far[i % 2, g * capacity : (g + 1) * capacity] = dot(hot, x).astype(LOW)
        ups[1, i].wait()
        kept_rows(i, buffer_far, r.far_out)
        away[i] = dot(buffer_far[i % 2], w_up[1, i]).astype(LOW)
        sent.append(links.send(away.at[i], arrived.at[i], place.x_peer))
    down_far = [
        *down_far,
        *(
            links.send(r.down.at[theirs + i], w_far.at[i], place.x_peer)
            for i in range(len(down_far), kept)
        ),
    ]
    for i in range(kept):
        expert = place.z * local_experts + mine + i
        if i > 1:
            stores[kept + i - 2].wait()
        for g in range(2):
            rows = slice(i * capacity, (i + 1) * capacity)
            into = slice(g * capacity, (g + 1) * capacity)
            hot = one_hot(slots, g * local_experts + mine + i, capacity)
            chances = [probs[4 * g + k, pl.ds(expert, 1), :] for k in range(4)]
            chances = jnp.concatenate(chances, 1)
            gates[i, into] = jnp.sum(jnp.where(hot, chances, 0.0), -1, keepdims=True)
            pick_near[g, rows] = hot.astype(LOW)
            x = r.x[g].reshape(group_rows, half)
            buffer_near[i % 2, into] = dot(hot.astype(LOW), x).astype(LOW)
        ups[0, i].wait()
        kept_rows(i, buffer_near, r.near_out)
        own[i] = dot(buffer_near[i % 2], w_up[0, i])
    for copy in nears:
        copy.wait()
    for i in range(kept):
        sent[i].wait_recv()
        down_far[i].wait_recv()
        values, slopes = gelu_parts(own[i] + arrived[i].astype(WIDE))
        hidden[i] = values.astype(LOW)
        if i == 0:
            r.hidden_copies.append(send_hidden(place, links, r, 0))
        own[i] = slopes
        for weight, f in ((w_near, place.f), (w_far, 1 - place.f)):
            out = (dot(hidden[i], weight[i]) * gates[i]).astype(LOW)
            columns = pl.ds(pl.multiple_of(f * half, half), half)
            for g in range(2):
                rows = slice(i * capacity, (i + 1) * capacity)
                weighted[g, rows, columns] = out[g * capacity : (g + 1) * capacity]
    for g in range(2):
        total = dot(pick_near[g], weighted[g], (0, 0)).astype(LOW)
        r.part[g] = total.reshape(r.part.shape[1:])
    links.left(sent)
    return stores[kept - 2 : kept] + stores[2 * kept - 2 :]


def experts_back_part(place, links, loads, chunks, r):
    pick_near, pick_far, hidden, slope, gates = r.pick_near, r.pick_far, r.hidden, r.own, r.gates
    w_up, w_near, w_far, group = r.w_up, r.w_near, r.w_far, r.group
    pre_near, pre_far, out_grad = r.away, r.arrived, r.out_grad
    side = r.weighted.shape[2] // 2
    rows_near = r.weighted.at[:, :, pl.ds(0, side)]
    rows_far = r.weighted.at[:, :, pl.ds(side, side)]
    kept, pair, half = out_grad.shape
    capacity, width = pair // 2, 2 * half
    first = pl.ds(pl.multiple_of(place.f * half, half), half)
    second = pl.ds(pl.multiple_of((1 - place.f) * half, half), half)
    sent = {}

    def send(g, i):
        piece = pl.ds(g * capacity, capacity)
        sent[g, i] = links.send(pre_near.at[i, piece], pre_far.at[i, piece], place.x_peer)

    for i in range(kept):
        rows = slice(i * capacity, (i + 1) * capacity)
        for g in range(2):
            rows_in = group[4 * g : 4 * g + 4].reshape(pick_near.shape[2], width)
            r.slot_rows[g * capacity : (g + 1) * capacity] = dot(
                pick_near[g, rows], rows_in
            ).astype(LOW)
        raw = dot(r.slot_rows[:, first], w_near[i], (1, 1))
        raw = raw + dot(r.slot_rows[:, second], w_far[i], (1, 1))
        pre_near[i] = (raw * gates[i] * slope[i]).astype(LOW)
        send(0, i)
        out_grad[i] = (r.slot_rows[:, first].astype(WIDE) * gates[i]).astype(LOW)
        gate_grad = jnp.sum(raw * hidden[i].astype(WIDE), -1, keepdims=True)
        for g in range(2):
            terms = gate_grad[g * capacity : (g + 1) * capacity]
            terms = terms * pick_near[g, rows].astype(WIDE)
            r.gate_rows[g, i : i + 1] = jnp.sum(terms, 0, keepdims=True)
    for i in range(kept):
        send(1, i)
    t = 2 * place.y + place.c
    r.gate_in[t] = r.gate_rows[...]
    shared = [
        links.send(r.gate_rows, r.gate_in.at[t], d) for d in place.tensor_peers()
    ]
    stores = [
        loads.start(r.hidden, r.near_hidden),
        loads.start(pre_near, r.near_pre),
        loads.start(out_grad, r.near_grad),
    ]

    for i in range(kept):
        back = dot(pre_near[i], w_up[0, i], (1, 1)).astype(LOW)
        rows = slice(i * capacity, (i + 1) * capacity)
        for g in range(2):
            rows_near[g, rows] = back[g * capacity : (g + 1) * capacity]
    for copy in shared:
        copy.wait_recv()
    spread = share_gates(place, links, r)
    experts = place.z * 2 * kept + (1 - place.f) * kept
    for i in range(kept):
        rows = slice(i * capacity, (i + 1) * capacity)
        for g in range(2):
            hot = pick_far[g, rows]
            chances = [r.probs[4 * g + k, pl.ds(experts + i, 1), :] for k in range(4)]
            chances = jnp.concatenate(chances, 1)
            gate = jnp.sum(hot.astype(WIDE) * chances, -1, keepdims=True)
            rows_in = group[4 * g : 4 * g + 4, :, first].reshape(pick_far.shape[2], half)
            into = slice(g * capacity, (g + 1) * capacity)
            r.far_held[i, into] = (dot(hot, rows_in) * gate).astype(LOW)
    stores.append(loads.start(r.far_held, r.far_grad))
    r.hidden_copies.append(send_hidden(place, links, r, 1))
    sums = RowSum(links, place, r)
    sums.spread = spread
    steps = {0: sums.to_y, 1: sums.to_heads, kept - 1: sums.total}
    for g in range(2):
        into = slice(g * capacity, (g + 1) * capacity)
        for i in range(kept):
            sent[g, i].wait_recv()
            back = dot(pre_far[i, into], w_up[1, i], (1, 1)).astype(LOW)
            rows_far[g, i * capacity : (i + 1) * capacity] = back
            if g and i in steps:
                for k in range(chunks):
                    steps[i](0, k)
        near = dot(pick_near[g], rows_near[g], (0, 0))
        both = (near + dot(pick_far[g], rows_far[g], (0, 0))).astype(LOW)
        r.x[g] = both.reshape(r.x.shape[1:])
        for k in range(chunks):
            sums.start(g, k)
    stores.append(loads.start(pre_far, r.far_pre))
    return stores, sums


def share_gates(place, links, r):
    t = 2 * place.y + place.c
    r.gate_sum[...] = sum(r.gate_in[k] for k in range(4))
    rows_all = r.probs_own.shape[1]
    rows_of = pl.ds(pl.multiple_of(t * rows_all, rows_all), rows_all)
    r.gate_all[place.z, place.f] = r.gate_sum[place.f, :, rows_of]
    return [
        links.send(r.gate_sum.at[d[FSDP], :, rows_of], r.gate_all.at[place.z, place.f], d)
        for d in place.owners()
    ]


def router_back(r):
    experts, rows_all = r.probs_own.shape
    width = r.residual.shape[1]
    chances = r.probs_own[...]
    prob_grad = r.gate_all[...].reshape(experts, rows_all)
    logit_grad = chances * (prob_grad - jnp.sum(chances * prob_grad, 0, keepdims=True))
    r.logit_grads[...] = logit_grad.astype(LOW)
    r.logit_rows[...] = dot(r.logit_grads[...], r.router[...], (0, 0))
    router_grad = dot(r.second_in[...], r.logit_grads[...], (0, 1))
    spare = jnp.zeros((width, 128 - experts), WIDE)
    router_grad = jnp.concatenate([router_grad, spare], 1).astype(LOW)
    blocks, block, dense_width = r.dense.shape
    r.dense[:, :, pl.ds(dense_width - 128, 128)] = router_grad.reshape(blocks, block, 128)


class RowSum:
    def __init__(self, links, place, r):
        self.links, self.place, self.r = links, place, r
        self.into, self.beside, self.along, self.cross = {}, {}, {}, {}
        self.rows = r.x.shape[3]
        self.own = self.rows // place.heads

    def start(self, g, k):
        source = self.r.x.at[g, :, 1 - self.place.c, :, pl.ds(k * 128, 128)]
        self.into[g, k] = self.links.send(
            source, self.r.core_in.at[k, g], self.place.core_peer
        )

    def to_y(self, g, k):
        self.into[g, k].wait_recv()
        rc, c, y = self.r.core_in.at[k, g], self.place.c, self.place.y

        def add(rows):
            here = self.r.x[g, :, c, rows, pl.ds(k * 128, 128)].astype(WIDE)
            rc[:, rows, :] = (rc[:, rows, :].astype(WIDE) + here).astype(LOW)

        in_rows(self.rows, 64, add)
        self.beside[g, k] = self.links.send(
            rc.at[1 - y], self.r.y_in.at[k, g], self.place.y_peer
        )

    def to_heads(self, g, k):
        self.beside[g, k].wait_recv()
        y_in, core_in = self.r.y_in.at[k, g], self.r.core_in.at[k, g, self.place.y]

        def add(rows):
            both = y_in[rows, :].astype(WIDE) + core_in[rows, :].astype(WIDE)
            y_in[rows, :] = both.astype(LOW)

        in_rows(self.rows, 64, add)
        own = self.own
        self.along[g, k] = all_heads(
            self.links,
            self.place,
            lambda n, to: (
                y_in.at[pl.ds(pl.multiple_of(to * own, own), own)],
                self.r.far.at[k, n, g],
            ),
        )

    def total(self, g, k):
        for copy in self.along[g, k]:
            copy.wait_recv()
        z, own = self.place.z, self.own
        total = self.r.y_in[k, g, pl.ds(pl.multiple_of(z * own, own), own), :].astype(WIDE)
        for n in range(self.place.heads - 1):
            total = total + self.r.far[k, n, g].astype(WIDE)
        self.r.pair[k, g] = total.astype(LOW)

    def to_x(self, k):
        self.cross[k] = self.links.send(
            self.r.pair.at[k, 1 - self.place.f], self.r.x_in.at[k], self.place.x_peer
        )


def back_part(place, links, chunks, sums, r):
    heads, f, y, z = place.heads, place.f, place.y, place.z
    me, valid = place.image(0, 0, 0), r.valid_row
    residual, gain, final_grad, tokens = r.residual, r.gain, r.final_grad, r.tokens
    gain_one, projected, log_total, mixed = r.gain_one, r.projected, r.log_total, r.mixed
    qkv, wo, tokens_grad, dense_out, gain_out = (
        r.qkv,
        r.wo_all,
        r.tokens_grad,
        r.dense_out,
        r.gain_out,
    )
    pair, x_in, logit_rows, attended, first_in = (
        r.pair,
        r.x_in,
        r.logit_rows,
        r.attended,
        r.first_in,
    )
    projected_grad, first_part, dense, dense_core = (
        r.projected_grad,
        r.first_part,
        r.dense,
        r.dense_core,
    )
    xa, ya, yb, xb, first_far, rounded = r.xa, r.ya, r.yb, r.xb, r.first_far, r.rounded
    gain_part, gain_plane, gain_heads = r.gain_part, r.gain_plane, r.gain_heads
    rows_all, width = residual.shape
    half = width // 2
    own = rows_all // heads
    mine = pl.ds(pl.multiple_of(z * own, own), own)
    blocks, block, dense_width = dense.shape
    qkv_width = projected.shape[1]
    for step in range(chunks + 2):
        if step == 2:
            for copy in sums.spread:
                copy.wait_recv()
            router_back(r)
        for k in range(chunks):
            if step == k:
                sums.to_y(1, k)
            if step == k + 1:
                sums.to_heads(1, k)
            if step == k + 2:
                sums.total(1, k)
                sums.to_x(k)
    for i in range(2, r.hidden.shape[0]):
        r.hidden_copies.append(send_hidden(place, links, r, i))
    normed, spread_two = normalize(residual[mine, :])
    cross = sums.cross
    near = jnp.concatenate([pair[k, f].astype(WIDE) for k in range(chunks)], 1)
    for k in range(chunks):
        cross[k].wait_recv()
    away = jnp.concatenate([x_in[k].astype(WIDE) for k in range(chunks)], 1)
    first = f == 0
    rows_grad = jnp.concatenate([jnp.where(first, near, away), jnp.where(first, away, near)], 1)
    second_grad = rows_grad + logit_rows[mine, :]
    weighted = second_grad * gain[...]
    gain_part[1:2, :] = jnp.sum(second_grad * normed, 0, keepdims=True)
    inner = (
        weighted
        - jnp.mean(weighted, -1, keepdims=True)
        - normed * jnp.mean(weighted * normed, -1, keepdims=True)
    )
    total_grad = final_grad[...] + inner * spread_two
    attended[mine, :] = total_grad.astype(LOW)
    for copy in all_heads(
        links, place, lambda k, to: (attended.at[mine], attended.at[mine])
    ):
        copy.wait_recv()

    mixed_grad = dot(attended[...], wo[:, z].reshape(width, wo.shape[3])).astype(LOW)
    head_count = log_total.shape[1]
    size = qkv_width // head_count // 3
    score_scale = size ** (-0.5)
    keys_ok = valid[...] > 0
    grads = []
    for h in range(head_count):
        at = 3 * h * size
        query, key, value = (projected[:, at + n * size : at + (n + 1) * size] for n in range(3))
        above = mixed_grad[:, h * size : (h + 1) * size]
        scores = jnp.where(keys_ok, dot(query, key, (1, 1)) * score_scale, MASKED)
        chances = jnp.exp(scores - log_total[:, h : h + 1])
        prob_part = dot(above, value, (1, 1))
        inner = jnp.sum(chances * prob_part, -1, keepdims=True)
        score_grad = (chances * (prob_part - inner)).astype(LOW)
        grads.append(dot(score_grad, key) * score_scale)
        grads.append(dot(score_grad, query, (0, 0)) * score_scale)
        grads.append(dot(chances.astype(LOW), above, (0, 0)))
    projected_grad[...] = jnp.concatenate(grads, 1).astype(LOW)
    weight = qkv[:, :, pl.ds(128, qkv_width)].reshape(width, qkv_width)
    back = dot(projected_grad[...], weight, (1, 1))
    first_part[...] = back.astype(LOW).reshape(heads, own, width)
    cuts = [pl.ds(q * own // 2, own // 2) for q in range(2)]
    along = [
        all_heads(links, place, lambda n, to: (first_part.at[to, q], first_far.at[n, q]))
        for q in cuts
    ]
    dense_now = jnp.concatenate(
        [
            dot(first_in[...], projected_grad[...], (0, 0)).astype(LOW),
            dot(attended[...], mixed[...], (0, 0)).astype(LOW),
        ],
        1,
    )
    dense[:, :, pl.ds(0, dense_width - 128)] = dense_now.reshape(blocks, block, dense_width - 128)
    adder = PlaneSum(links, place, dense, dense_core, xa, ya, yb, xb, xa.shape[2], 32)
    adder.start()
    gain_part[0:1, :] = jnp.sum(back * normalize(tokens[...].astype(WIDE))[0], 0, keepdims=True)
    gain_plane[me] = gain_part[...]
    small = [links.send(gain_part, gain_plane.at[me], d) for d in place.plane_peers]
    adder.cores()
    adder.cross()
    for copy in small:
        copy.wait_recv()
    gain_heads[z] = sum(gain_plane[i] for i in range(8))
    gains = all_heads(links, place, lambda n, to: (gain_heads.at[z], gain_heads.at[z]))
    ends = []
    for n_cut, q in enumerate(cuts):
        at = pl.ds(pl.multiple_of(z * own + n_cut * own // 2, own // 2), own // 2)
        normed, spread_one = normalize(tokens[at, :].astype(WIDE))
        for copy in along[n_cut]:
            copy.wait_recv()
        first_grad = first_part[z, q].astype(WIDE)
        for n in range(heads - 1):
            first_grad = first_grad + first_far[n, q].astype(WIDE)
        weighted = first_grad * gain_one[...]
        inner = (
            weighted
            - jnp.mean(weighted, -1, keepdims=True)
            - normed * jnp.mean(weighted * normed, -1, keepdims=True)
        )
        here = total_grad[n_cut * own // 2 : (n_cut + 1) * own // 2]
        rounded[z, q] = (here + inner * spread_one).astype(LOW)
        ends += all_heads(links, place, lambda n, to: (rounded.at[z, q], rounded.at[z, q]))

    def keep(rows, columns, values):
        dense_out[rows, columns] = values

    adder.finish(keep)
    for copy in gains:
        copy.wait_recv()
    gain_out[...] = sum(gain_heads[i] for i in range(heads))
    for copy in ends:
        copy.wait_recv()
    for i in range(heads):
        tokens_grad[i] = rounded[i].astype(WIDE)
    for copy in r.hidden_copies:
        copy.wait_recv()


def layer_kernel(heads, chunks, small, names, *refs):
    r = types.SimpleNamespace(**dict(zip(names, refs)), hidden_copies=[])
    place = Place(heads)
    links = Links(r.send_sems, r.recv_sems)
    loads = Loads(r.load_sems)
    kept = r.w_far.shape[0]
    mine, theirs = place.f * kept, (1 - place.f) * kept
    first = [loads.start(getattr(r, name + "_hbm"), getattr(r, name)) for name in small]
    ups = {}
    for far in (1, 0):
        for i in range(kept):
            source = (theirs if far else mine) + i
            ups[far, i] = loads.start(r.up.at[source], r.w_up.at[far, i])
    nears = [loads.start(r.down.at[mine + i], r.w_near.at[i]) for i in range(kept)]
    place.greet(place.everyone())
    for copy in first:
        copy.wait()
    from_x, down_far = front_part(place, links, r)
    held = experts_part(place, links, loads, (ups, nears), down_far, r)
    extra = combine_part(place, links, chunks, r)
    links.left(from_x)
    stores, sums = experts_back_part(place, links, loads, chunks, r)
    for copy in extra:
        copy.wait_recv()
    back_part(place, links, chunks, sums, r)
    for copy in held + stores:
        copy.wait()
    links.drain()


def named_call(kernel, ins, outs, scratch, copies, loads, collective_id, vmem_mib, microseconds):
    spaces = {False: pltpu.VMEM, True: pltpu.HBM}
    names = [*ins, *outs, *scratch, "load_sems", "send_sems", "recv_sems"]
    made = pl.pallas_call(
        functools.partial(kernel, names),
        out_shape=[o[0] for o in outs.values()],
        in_specs=[pl.BlockSpec(memory_space=spaces[a[1]]) for a in ins.values()],
        out_specs=[pl.BlockSpec(memory_space=spaces[o[1]]) for o in outs.values()],
        scratch_shapes=[
            *scratch.values(),
            pltpu.SemaphoreType.DMA((loads,)),
            pltpu.SemaphoreType.DMA((copies,)),
            pltpu.SemaphoreType.DMA((copies,)),
        ],
        compiler_params=pltpu.CompilerParams(
            collective_id=collective_id,
            has_side_effects=True,
            vmem_limit_bytes=vmem_mib * 2**20,
        ),
        cost_estimate=spends(microseconds),
    )(*[a[0] for a in ins.values()])
    return types.SimpleNamespace(**dict(zip(outs, made)))


def layer(heads, experts, capacity, small, hbm):
    rows, width = small["tokens"].shape
    own, half, chunks = rows // heads, width // 2, width // 256
    local_experts, _, hidden_width = hbm["up"].shape
    kept, pair, group_rows = local_experts // 2, 2 * capacity, 4 * rows
    mixed_width, block = small["out_in"].shape
    head_count = small["qkv_in"].shape[0]
    qkv_width = 3 * mixed_width
    gathered_width = 128 + qkv_width + -(128 + qkv_width) % 256
    dense_width = qkv_width + mixed_width + 128
    cut = 128 * ((dense_width // 128 + 1) // 2)
    ins = {name: (array, True) for name, array in hbm.items()}
    ins.update({name + "_hbm": (array, True) for name, array in small.items()})
    outs = dict(
        result=(shape((heads, own, width)), False),
        loss=(shape((heads, 8, 128), WIDE), False),
        tokens_grad=(shape((heads, own, width), WIDE), False),
        dense_out=(shape((block, dense_width), WIDE), False),
        gain_out=(shape((2, width), WIDE), False),
        near_out=(shape((kept, pair, half)), True),
        near_pre=(shape((kept, pair, hidden_width)), True),
        near_hidden=(shape((kept, pair, hidden_width)), True),
        near_grad=(shape((kept, pair, half)), True),
        far_out=(shape((kept, pair, half)), True),
        far_pre=(shape((kept, pair, hidden_width)), True),
        far_hidden=(shape((kept, pair, hidden_width)), True),
        far_grad=(shape((kept, pair, half)), True),
    )
    low = dict(
        pick_near=(2, kept * capacity, group_rows),
        pick_far=(2, kept * capacity, group_rows),
        buffer_near=(2, pair, half),
        buffer_far=(2, pair, half),
        hidden=(kept, pair, hidden_width),
        weighted=(2, kept * capacity, width),
        away=(kept, pair, hidden_width),
        arrived=(kept, pair, hidden_width),
        w_up=(2, kept, half, hidden_width),
        w_near=(kept, hidden_width, half),
        w_far=(kept, hidden_width, half),
        part=(2, 2, 2, rows, width),
        group=(8, rows, width),
        sum_core=(chunks, 2, 2, rows, 256),
        sum_xa=(chunks, 2, rows, 128),
        sum_ya=(chunks, rows, 128),
        sum_yb=(chunks, 2, rows, 128),
        sum_xb=(chunks, rows, 128),
        image_sum=(chunks, rows, 256),
        image_far=(chunks, heads - 1, own, 256),
        out_grad=(kept, pair, half),
        far_held=(kept, pair, half),
        slot_rows=(pair, width),
        x=(2, 2, 2, rows, half),
        other_half=(rows, half),
        qkv=(8, block, gathered_width),
        wo_all=(8, heads, block, mixed_width),
        router=(experts, width),
        projected=(rows, qkv_width),
        mixed=(rows, mixed_width),
        all_mixed=(heads, rows, mixed_width),
        second_in=(rows, width),
        core_in=(chunks, 2, 2, rows, 128),
        y_in=(chunks, 2, rows, 128),
        far=(chunks, heads - 1, 2, own, 128),
        pair=(chunks, 2, own, 128),
        x_in=(chunks, own, 128),
        logit_grads=(experts, rows),
        attended=(rows, width),
        first_in=(rows, width),
        projected_grad=(rows, qkv_width),
        first_part=(heads, own, width),
        dense=(8, block, dense_width),
        dense_core=(4, block, dense_width),
        xa=(2, block, cut),
        ya=(block, cut),
        yb=(2, block, dense_width - cut),
        xb=(block, dense_width - cut),
        first_far=(heads - 1, own, width),
        rounded=(heads, own, width),
    )
    wide = dict(
        gates=(kept, pair, 1),
        counts=(8, 8, 128),
        scale=(8, 128),
        loss_scale=(8, 128),
        valid=(rows, 8),
        gain_one=(1, width),
        gain=(1, width),
        log_total=(rows, head_count),
        residual=(rows, width),
        probs=(8, experts, rows),
        probs_own=(experts, rows),
        own=(kept, pair, hidden_width),
        final_grad=(own, width),
        gate_rows=(2, kept, group_rows),
        gate_in=(4, 2, kept, group_rows),
        gate_sum=(2, kept, group_rows),
        gate_all=(heads, 2, kept, rows),
        logit_rows=(rows, width),
        gain_part=(2, width),
        gain_plane=(8, 2, width),
        gain_heads=(heads, 2, width),
    )
    scratch = {name: pltpu.VMEM(dims, LOW) for name, dims in low.items()}
    scratch.update({name: pltpu.VMEM(dims, WIDE) for name, dims in wide.items()})
    whole = dict(
        far_route=small["near_route"].shape,
        slots=(2 * local_experts, group_rows),
    )
    scratch.update({name: pltpu.VMEM(a.shape, a.dtype) for name, a in small.items()})
    scratch.update({name: pltpu.VMEM(dims, jnp.int32) for name, dims in whole.items()})
    copies = FRONT_COPIES + 2 * (heads - 1) + 2 * kept + chunks * (5 + GATHER_COPIES + 2 * (heads - 1)) + 2 * (heads - 1)
    copies += 2 * kept + kept + 2 * chunks * (2 + heads - 1) + chunks + 3 + 2 * heads - 1
    copies += heads - 1 + SUM_COPIES + 5 * (heads - 1) + 7
    return named_call(
        functools.partial(layer_kernel, heads, chunks, tuple(small)),
        ins,
        outs,
        scratch,
        copies,
        5 * kept + 6 + len(small),
        1,
        59,
        280,
    )


def finish_kernel(s, *refs):
    sides, rest = (refs[:4], refs[4:8]), refs[8:]
    result_in, tokens_in, dense, gains, loss_in = rest[:5]
    up, down, result, tokens_grad, qkv_grad, out_grad, router_grad, gain_grads, loss = rest[5:]
    i = pl.program_id(0)
    kept = pl.num_programs(0) // 2
    for side, (rows, pre, hidden, grad) in enumerate(sides):
        j = i - s[side]

        @pl.when((j >= 0) & (j < kept))
        def _(rows=rows, pre=pre, hidden=hidden, grad=grad):
            up[0] = dot(rows[0], pre[0], (0, 0))
            down[0] = dot(hidden[0], grad[0], (0, 0))

    @pl.when(i == 0)
    def _():
        result[...] = result_in[...].reshape(result.shape)
        tokens_grad[...] = tokens_in[...].reshape(tokens_grad.shape)
        head_count, block, size = qkv_grad.shape
        for h in range(head_count):
            qkv_grad[h] = dense[:, h * size : (h + 1) * size]
        at = head_count * size
        mixed_width = out_grad.shape[0]
        out_grad[...] = jnp.transpose(dense[:, at : at + mixed_width])
        last = jnp.transpose(dense[:, at + mixed_width : at + mixed_width + 128])
        router_grad[...] = last[: router_grad.shape[0]]
        gain_grads[...] = sum(
            jnp.where(s[2] == b, gains[:, b * block : (b + 1) * block], 0.0) for b in range(8)
        )
        loss[...] = jnp.sum(jnp.sum(loss_in[...], 0), keepdims=True)


def finish(scalars, near, far, small, shapes):
    kept, _, half = near[0].shape
    hidden_width = near[1].shape[2]

    def of(array, which):
        return pl.BlockSpec(
            (1, *array.shape[1:]), lambda i, s: (jnp.clip(i - s[which], 0, kept - 1), 0, 0)
        )

    def all_of(array):
        return pl.BlockSpec(array.shape, lambda i, s, n=len(array.shape): (0,) * n)

    return pl.pallas_call(
        finish_kernel,
        out_shape=[
            shape((2 * kept, half, hidden_width), WIDE),
            shape((2 * kept, hidden_width, half), WIDE),
            *shapes,
        ],
        grid_spec=pltpu.PrefetchScalarGridSpec(
            num_scalar_prefetch=1,
            grid=(2 * kept,),
            in_specs=[of(array, 0) for array in near]
            + [of(array, 1) for array in far]
            + [all_of(array) for array in small],
            out_specs=[
                pl.BlockSpec((1, half, hidden_width), lambda i, s: (i, 0, 0)),
                pl.BlockSpec((1, hidden_width, half), lambda i, s: (i, 0, 0)),
                *[all_of(array) for array in shapes],
            ],
        ),
        compiler_params=pltpu.CompilerParams(vmem_limit_bytes=60 * 2**20),
        cost_estimate=spends(8),
    )(scalars, *near, *far, *small)


def fast(
    tokens,
    valid_mask,
    routes,
    teacher,
    gain_one,
    qkv_weight,
    out_weight,
    gain_two,
    router_weight,
    expert_up,
    expert_down,
):
    heads = lax.axis_size(HEADS)
    f, t = lax.axis_index(FSDP), lax.axis_index(TENSOR)
    _, rows, width = tokens.shape
    block, head_count, qkv_dim = qkv_weight.shape
    mixed_width = out_weight.shape[0] * out_weight.shape[1]
    local_experts = expert_up.shape[0]
    kept = local_experts // 2
    expert_count = local_experts * heads
    capacity = 2 * routes.shape[2] * 4 * rows // expert_count
    small = dict(
        router_in=router_weight.T,
        gain_one_in=gain_one[None],
        gain_two_in=gain_two[None],
        qkv_in=jnp.swapaxes(qkv_weight, 0, 1),
        out_in=out_weight.reshape(mixed_width, block),
        near_route=jnp.swapaxes(routes, 1, 2),
        tokens=tokens[0],
        teacher=teacher[0],
        valid_row=valid_mask,
    )
    made = layer(heads, expert_count, capacity, small, dict(up=expert_up, down=expert_down))
    scalars = jnp.stack([f * kept, (1 - f) * kept, f * 4 + t]).astype(jnp.int32)
    up_grad, down_grad, result, tokens_grad, qkv_grad, out_grad, router_grad, gains, loss = finish(
        scalars,
        [made.near_out, made.near_pre, made.near_hidden, made.near_grad],
        [made.far_out, made.far_pre, made.far_hidden, made.far_grad],
        [made.result, made.tokens_grad, made.dense_out, made.gain_out, made.loss],
        [
            shape((rows, width)),
            shape((rows, width), WIDE),
            shape((head_count, block, qkv_dim), WIDE),
            shape((mixed_width, block), WIDE),
            shape((expert_count, block), WIDE),
            shape((2, block), WIDE),
            shape((1, 1), WIDE),
        ],
    )
    return (
        result[None],
        loss.reshape(1),
        tokens_grad[None],
        gains[0],
        jnp.swapaxes(qkv_grad, 0, 1),
        out_grad.reshape(head_count, -1, block),
        gains[1],
        router_grad.T,
        up_grad,
        down_grad,
    )


def local(sizes, *args):
    tokens, routes, up = args[0], args[2], args[9]
    fits = (
        sizes[FSDP] == 2
        and sizes[TENSOR] == 4
        and sizes[HEADS] % 2 == 0
        and tokens.shape[0] == 1
        and up.shape[0] % 8 == 0
        and tokens.shape[1] % (32 * sizes[HEADS]) == 0
        and tokens.shape[2] % 256 == 0
        and routes.shape[2] <= 8
        and up.shape[0] * sizes[HEADS] <= 126
    )
    return fast(*args) if fits else general(*args)


def solution(mesh):
    sizes = dict(mesh.shape)
    program = functools.partial(local, sizes)
    in_specs = (
        P((FSDP, TENSOR), None, None),
        P((FSDP, TENSOR), None),
        P(FSDP, None, None),
        P((FSDP, TENSOR), None, None),
        P((FSDP, TENSOR)),
        P((FSDP, TENSOR), HEADS, None),
        P(HEADS, None, (FSDP, TENSOR)),
        P((FSDP, TENSOR)),
        P((FSDP, TENSOR), None),
        P(HEADS, FSDP, TENSOR),
        P(HEADS, TENSOR, FSDP),
    )
    out_specs = (
        P((FSDP, TENSOR), None, None),
        P((FSDP, TENSOR)),
        P((FSDP, TENSOR), None, None),
        P((FSDP, TENSOR)),
        P((FSDP, TENSOR), HEADS, None),
        P(HEADS, None, (FSDP, TENSOR)),
        P((FSDP, TENSOR)),
        P((FSDP, TENSOR), None),
        P(HEADS, FSDP, TENSOR),
        P(HEADS, TENSOR, FSDP),
    )
    return jax.shard_map(program, mesh=mesh, in_specs=in_specs, out_specs=out_specs, check_vma=False)
```
